32 devices in a mesh: ctx: 8 (over z, x), fsdp: 4 (over y, core).
Axes of the slice: x: 2, y: 2, z: 4, core: 2. Of those that a mesh axis runs over, the one named last changes fastest.
Arguments:
- hidden: bfloat16 [4, 1024, 768], P('fsdp', 'ctx'), may hold values from -6 to 6
- project_in: bfloat16 [768, 2304], P('fsdp', 'ctx'), may hold values from -0.21875 to 0.21875
- project_out: bfloat16 [768, 768], P('fsdp', 'ctx'), may hold values from -3.5 to 3.5
- expand_weight: bfloat16 [768, 3072], P('fsdp', 'ctx'), may hold values from -0.21875 to 0.21875
- shrink_weight: bfloat16 [3072, 768], P('fsdp', 'ctx'), may hold values from -0.109375 to 0.109375
- biases: bfloat16 [6, 768], P(None, 'ctx'), may hold values from -3 to 3
- gains: bfloat16 [2, 768], P(None, 'ctx'), may hold values from 0.5 to 1.5
- expand_bias: bfloat16 [3072], P('ctx'), may hold values from -3 to 3
- random_blocks: int32 [4, 16, 3], P('fsdp', 'ctx'), may hold values from 0 to 15
- global_blocks: int32 [4, 2], P('fsdp'), may hold values from 0 to 15
- document_lengths: int32 [4, 8], P('fsdp'), may hold values from 1 to 897, as said below
- cotangent: bfloat16 [4, 1024, 768], P('fsdp', 'ctx'), may hold values from -6 to 6
Outputs:
- output: bfloat16 [4, 1024, 768], P('fsdp', 'ctx')
- grad_hidden: bfloat16 [4, 1024, 768], P('fsdp', 'ctx')
- grad_project_in: float32 [768, 2304], P('fsdp', 'ctx')
- grad_project_out: float32 [768, 768], P('fsdp', 'ctx')
- grad_expand: float32 [768, 3072], P('fsdp', 'ctx')
- grad_shrink: float32 [3072, 768], P('fsdp', 'ctx')
- grad_biases: float32 [6, 768], P(None, 'ctx')
- grad_gains: float32 [2, 768], P(None, 'ctx')
- grad_expand_bias: float32 [3072], P('ctx')
The draws below stay inside these ranges and needn't reach their ends.
Inputs may be any that keep to these rules, and one draw needn't show every extreme that they name: `document_lengths`: each sequence's 8 lengths add up to 1024; exactly one document has the largest length, 897, and the others together have 128 - 1 tokens.
All inputs are finite; a program needn't handle non-finite values.
Results may differ from the reference program's by a relative error of at most 0.015.
Values may be sent and summed in bfloat16 or wider, within the bound.
A program may use at most 192 MiB of HBM per device.

```python
import jax
import jax.numpy as jnp
from jax import lax

D = 768
FF = 3072
HEAD_DIM = 64
BLOCK = 64
RAND_LINKS = 3
GLOBAL_LINKS = 2
NDOC = 8
TOK_DEV = 128
HEADS = 12
SEQ = 1024
NBLK = 16
SEQS = 4


def draw_document_lengths(key, part):
    key = jax.random.fold_in(key, 11)
    first_key, second_key = jax.random.split(key)
    ceiling = (TOK_DEV - 1) // (NDOC - 1)
    drawn = jax.random.randint(first_key, (SEQS, NDOC - 2), 1, ceiling + 1)
    drawn = jnp.concatenate([jnp.ones((SEQS, 1), jnp.int32), drawn[:, 1:].astype(jnp.int32)], axis=1)
    remainder = TOK_DEV - 1 - jnp.sum(drawn, axis=1, keepdims=True)
    smaller = jnp.concatenate([drawn, remainder.astype(jnp.int32)], axis=1)
    where_big = jax.random.randint(second_key, (SEQS, 1), 0, NDOC)
    largest = SEQ - TOK_DEV + 1
    placed = jnp.arange(NDOC, dtype=jnp.int32)[None, :]
    source = jnp.clip(jnp.where(placed < where_big, placed, placed - 1), 0, NDOC - 2)
    picked = jnp.take_along_axis(smaller, jnp.broadcast_to(source, (SEQS, NDOC)), axis=1)
    return jnp.where(placed == where_big, largest, picked).astype(jnp.int32)


def plant(values, key, least, high):
    longest = values.shape.index(max(values.shape))
    spots = []
    for shift in (0, 1):
        where = [jax.random.randint(jax.random.fold_in(key, axis), (), 0, length) for axis, length in enumerate(values.shape)]
        where[longest] = (where[longest] + shift) % values.shape[longest]
        spots.append(tuple(where))
    return values.at[spots[0]].set(least).at[spots[1]].set(high)


def levels(own_key, extent, cuts, low, high):
    level, own = 1.0, jax.random.fold_in(own_key, 6)
    for dim, blocks in cuts:
        draws = jnp.exp(jax.random.uniform(jax.random.fold_in(own, dim), (blocks,), jnp.float32, low / len(cuts), high / len(cuts)))
        level = level * jnp.repeat(draws, extent[dim] // blocks).reshape([-1 if axis == dim else 1 for axis in range(len(extent))])
    return level


def centred(own_key, dims, scale, reach, cuts=(), kind=jnp.bfloat16):
    factor_of = levels(own_key, dims, cuts, -0.22, 0.18) if cuts else 1.0
    array = jax.random.normal(own_key, dims, jnp.float32) * scale * factor_of
    return jnp.minimum(jnp.maximum(array, -reach), reach).astype(kind)


def setup_inputs(seed: int = 0) -> dict:
    keys = jax.random.split(jax.random.key(seed), 13)
    return {
        "hidden": centred(keys[0], (SEQS, SEQ, D), 1.0, 6.0, ((0, 4), (1, 8))),
        "project_in": centred(keys[1], (D, 3 * D), D ** -0.5, 0.21875, ((0, 4), (1, 8))),
        "project_out": centred(keys[2], (D, D), (max(D // 256, 1)) ** -0.5, 3.5, ((0, 4), (1, 8))),
        "expand_weight": centred(keys[3], (D, FF), D ** -0.5, 0.21875, ((0, 4), (1, 8))),
        "shrink_weight": centred(keys[4], (FF, D), FF ** -0.5, 0.109375, ((0, 4), (1, 8))),
        "biases": centred(keys[5], (6, D), 0.5, 3.0, ((1, 8),)),
        "gains": jnp.clip(1.0 + 0.1 * jax.random.normal(keys[6], (2, D), jnp.float32), 0.5, 1.5).astype(jnp.bfloat16),
        "expand_bias": centred(keys[7], (FF,), 0.5, 3.0, ((0, 8),)),
        "random_blocks": plant(jax.random.randint(keys[8], (SEQS, NBLK, RAND_LINKS), 0, NBLK), jax.random.fold_in(keys[8], 1), 0, NBLK - 1).astype(jnp.int32),
        "global_blocks": plant(jax.random.randint(keys[9], (SEQS, GLOBAL_LINKS), 0, NBLK), jax.random.fold_in(keys[9], 1), 0, NBLK - 1).astype(jnp.int32),
        "document_lengths": draw_document_lengths(jax.random.fold_in(keys[12], 71), 0),
        "cotangent": centred(keys[11], (SEQS, SEQ, D), 1.0, 6.0, ((0, 4), (1, 8))),
    }


precise = lax.Precision.HIGHEST

@jax.custom_vjp
def low(v):
    return lax.optimization_barrier(v.astype(jnp.bfloat16)).astype(jnp.float32)

@jax.custom_vjp
def low_back(v):
    return v

def low_keep(v):
    return (low(v), None)

def low_pass(kept, grad):
    return (grad,)

def back_keep(v):
    return (v, None)

def back_low(kept, grad):
    return (low(grad),)
low.defvjp(low_keep, low_pass)
low_back.defvjp(back_keep, back_low)

def segment_of(positions, bounds):
    return lax.optimization_barrier(jnp.sum((positions[..., None] >= bounds).astype(jnp.int32), axis=-1))

def link_table(random_rows, global_row):
    blocks = jnp.arange(NBLK, dtype=jnp.int32)
    window = jnp.stack([jnp.maximum(blocks - 1, 0), blocks, jnp.minimum(blocks + 1, NBLK - 1)], axis=1)
    global_links = jnp.broadcast_to(global_row[None, :], (NBLK, GLOBAL_LINKS))
    return jnp.concatenate([window, random_rows, global_links], axis=1).astype(jnp.int32)

def layer_norm(values, gain_row, shift_row):
    centre = values - lax.optimization_barrier(jnp.mean(values, axis=-1, keepdims=True))
    spread = lax.optimization_barrier(jnp.mean(centre * centre, axis=-1, keepdims=True))
    return centre * lax.rsqrt(spread + 1e-05) * gain_row + shift_row

def matmul(left_side, right_side):
    return jnp.dot(left_side, right_side, precision=precise, preferred_element_type=jnp.float32)

def forward(inputs, project_in, project_out, expand_weight, shrink_weight, biases, gains, expand_bias, linked_ids, segments):
    width = inputs.shape[1]
    group_size = 8
    mixed_qkv = low_back(matmul(inputs, project_in)) + jnp.concatenate([biases[0], jnp.zeros_like(biases[0]), biases[1]])
    mixed_qkv = low(mixed_qkv)
    queries = mixed_qkv[:, :width]
    blocks_kv = mixed_qkv[:, width:].reshape(NBLK, BLOCK, 2 * width)
    block_seg = segments.reshape(NBLK, BLOCK)

    def attend_group(pieces):
        query_block, link_block, seg_block = pieces
        linked = blocks_kv[link_block].reshape(group_size, -1, 2 * width)
        key_seg = block_seg[link_block].reshape(group_size, -1)
        query_heads = query_block.reshape(group_size, BLOCK, HEADS, HEAD_DIM)
        key_heads = linked[..., :width].reshape(group_size, -1, HEADS, HEAD_DIM)
        value_heads = linked[..., width:].reshape(group_size, -1, HEADS, HEAD_DIM)
        scores = low_back(jnp.einsum('bqhd,bkhd->bhqk', query_heads, key_heads, precision=precise)) * 0.125
        allowed = seg_block[:, None, :, None] == key_seg[:, None, None, :]
        scores = jnp.where(allowed, scores, -1e+30)
        top_score = lax.optimization_barrier(jnp.max(scores, axis=-1, keepdims=True))
        exponent = jnp.exp(scores - top_score)
        attention = exponent / lax.optimization_barrier(jnp.sum(exponent, axis=-1, keepdims=True))
        attended = jnp.einsum('bhqk,bkhd->bqhd', low(attention), value_heads, precision=precise)
        return attended.reshape(group_size, BLOCK, width)
    attended = lax.map(jax.checkpoint(attend_group), (queries.reshape(NBLK // group_size, group_size, BLOCK, width), linked_ids.reshape(NBLK // group_size, group_size, -1), block_seg.reshape(NBLK // group_size, group_size, BLOCK)))
    attended = low(low_back(attended.reshape(-1, width)))
    hidden_one = layer_norm(inputs + low_back(matmul(attended, project_out)) + biases[2], gains[0], biases[3])
    inner_pre = low_back(matmul(low(hidden_one), expand_weight)) + expand_bias
    outer = low_back(matmul(low(jax.nn.gelu(inner_pre, approximate=False)), shrink_weight)) + biases[4]
    return layer_norm(hidden_one + outer, gains[1], biases[5])

def reference(hidden, project_in, project_out, expand_weight, shrink_weight, biases, gains, expand_bias, random_blocks, global_blocks, document_lengths, cotangent):
    float_params = tuple((weight.astype(jnp.float32) for weight in (project_in, project_out, expand_weight, shrink_weight, biases, gains, expand_bias)))
    positions = jnp.arange(SEQ, dtype=jnp.int32)

    def one_sequence(totals, pieces):
        inputs, random_rows, global_row, lengths, upstream = pieces
        bounds = jnp.cumsum(lengths).astype(jnp.int32)[:-1]
        segments = segment_of(positions, bounds)
        linked_ids = link_table(random_rows, global_row)

        def apply_layer(inputs_float, *weights):
            return forward(inputs_float, *weights, linked_ids, segments)
        result, pull = jax.vjp(apply_layer, inputs.astype(jnp.float32), *float_params)
        gradients = pull(upstream.astype(jnp.float32))
        totals = tuple((running + fresh_grad for running, fresh_grad in zip(totals, gradients[1:])))
        return (totals, (result.astype(jnp.bfloat16), gradients[0].astype(jnp.bfloat16)))
    zeros_start = tuple((jnp.zeros_like(weight) for weight in float_params))
    totals, outputs = lax.scan(one_sequence, zeros_start, (hidden, random_blocks, global_blocks, document_lengths, cotangent))
    return (outputs[0], outputs[1], totals[0], totals[1], totals[2], totals[3], totals[4], totals[5], totals[6])
```

```python
import jax
import jax.numpy as jnp
from jax import lax
from jax.sharding import PartitionSpec as P

HEAD_DIM = 64
BLOCK = 64


def segment_of(positions, bounds):
    return jnp.sum((positions[..., None] >= bounds).astype(jnp.int32), axis=-1)


def layer_norm_parts(values, gain_row, shift_row):
    centre = values - jnp.mean(values, axis=-1, keepdims=True)
    inverse = lax.rsqrt(jnp.mean(centre * centre, axis=-1, keepdims=True) + 1e-05)
    normed = centre * inverse
    return (normed * gain_row + shift_row, normed, inverse)


def layer_norm_back(upstream, normed, inverse, gain_row):
    scaled = upstream * gain_row
    return inverse * (
        scaled
        - jnp.mean(scaled, axis=-1, keepdims=True)
        - normed * jnp.mean(scaled * normed, axis=-1, keepdims=True)
    )


def matmul(left_side, right_side):
    return jnp.dot(left_side, right_side, preferred_element_type=jnp.float32)


def matmul_left_t(left_side, right_side):
    return lax.dot_general(
        left_side, right_side, (((0,), (0,)), ((), ())), preferred_element_type=jnp.float32
    )


def matmul_right_t(left_side, right_side):
    return lax.dot_general(
        left_side, right_side, (((1,), (1,)), ((), ())), preferred_element_type=jnp.float32
    )


def over_cols(qkv_grad, out_grad, expand_grad, shrink_grad, vector_grad, gain_grad, inner_grad):
    return (
        lax.psum_scatter(qkv_grad, "ctx", scatter_dimension=1, tiled=True),
        lax.psum_scatter(out_grad, "ctx", scatter_dimension=1, tiled=True),
        lax.psum_scatter(expand_grad, "ctx", scatter_dimension=1, tiled=True),
        lax.psum_scatter(shrink_grad, "ctx", scatter_dimension=1, tiled=True),
        lax.psum_scatter(vector_grad, "ctx", scatter_dimension=1, tiled=True),
        lax.psum_scatter(gain_grad, "ctx", scatter_dimension=1, tiled=True),
        lax.psum_scatter(inner_grad, "ctx", scatter_dimension=1, tiled=True),
    )


def over_rows(qkv_grad, out_grad, expand_grad, shrink_grad):
    return (
        lax.psum_scatter(
            qkv_grad.astype(jnp.bfloat16), "fsdp", scatter_dimension=0, tiled=True
        ).astype(jnp.float32),
        lax.psum_scatter(
            out_grad.astype(jnp.bfloat16), "fsdp", scatter_dimension=0, tiled=True
        ).astype(jnp.float32),
        lax.psum_scatter(
            expand_grad.astype(jnp.bfloat16), "fsdp", scatter_dimension=0, tiled=True
        ).astype(jnp.float32),
        lax.psum_scatter(
            shrink_grad.astype(jnp.bfloat16), "fsdp", scatter_dimension=0, tiled=True
        ).astype(jnp.float32),
    )


def scatter_rows(link_ids, link_grads, row_count, feature_width):
    block_count = row_count // BLOCK
    inside = (link_ids >= 0) & (link_ids < block_count)
    target = jnp.where(inside, link_ids, block_count).reshape(-1)
    partial_value = jnp.zeros((block_count, BLOCK, feature_width), jnp.float32)
    partial_value = partial_value.at[target].add(
        link_grads.reshape(-1, BLOCK, feature_width), mode="drop"
    )
    return partial_value.reshape(row_count, feature_width)


def shards(
    hidden,
    project_in,
    project_out,
    expand_weight,
    shrink_weight,
    biases,
    gains,
    expand_bias,
    random_blocks,
    global_blocks,
    document_lengths,
    cotangent,
):
    inputs = hidden[0]
    tokens_here = inputs.shape[0]
    width = inputs.shape[1]
    head_count = width // HEAD_DIM
    blocks_here = tokens_here // BLOCK
    rand_count = random_blocks.shape[2]
    link_count = 3 + rand_count + global_blocks.shape[1]
    ctx_rank = lax.axis_index("ctx")
    last_block = tokens_here * lax.axis_size("ctx") // BLOCK - 1
    col_full = (
        lax.all_gather(project_in, "ctx", axis=1, tiled=True),
        lax.all_gather(project_out, "ctx", axis=1, tiled=True),
        lax.all_gather(expand_weight, "ctx", axis=1, tiled=True),
        lax.all_gather(shrink_weight, "ctx", axis=1, tiled=True),
        lax.all_gather(biases, "ctx", axis=1, tiled=True),
        lax.all_gather(gains, "ctx", axis=1, tiled=True),
        lax.all_gather(expand_bias.reshape(1, -1), "ctx", axis=1, tiled=True),
    )
    full_qkv, full_out, full_expand, full_shrink = (
        lax.all_gather(col_full[0], "fsdp", axis=0, tiled=True),
        lax.all_gather(col_full[1], "fsdp", axis=0, tiled=True),
        lax.all_gather(col_full[2], "fsdp", axis=0, tiled=True),
        lax.all_gather(col_full[3], "fsdp", axis=0, tiled=True),
    )
    vectors = col_full[4].astype(jnp.float32)
    gain_rows = col_full[5].astype(jnp.float32)
    inner_bias = col_full[6][0].astype(jnp.float32)
    block_ids = ctx_rank * blocks_here + jnp.arange(blocks_here, dtype=jnp.int32)
    window = jnp.stack(
        [jnp.maximum(block_ids - 1, 0), block_ids, jnp.minimum(block_ids + 1, last_block)], axis=1
    )
    global_links = jnp.broadcast_to(
        global_blocks[0][None, :], (blocks_here, global_blocks.shape[1])
    )
    linked_ids = jnp.concatenate([window, random_blocks[0], global_links], axis=1)
    lengths = document_lengths[0]
    doc_order = jnp.arange(lengths.shape[0], dtype=jnp.int32)
    bounds = jnp.sum(
        jnp.where(doc_order[None, :] <= doc_order[:-1, None], lengths[None, :], 0), axis=1
    )
    query_pos = (ctx_rank * tokens_here + jnp.arange(tokens_here, dtype=jnp.int32)).reshape(
        blocks_here, BLOCK
    )
    query_seg = segment_of(query_pos, bounds)
    key_pos = linked_ids[:, :, None] * BLOCK + jnp.arange(BLOCK, dtype=jnp.int32)[None, None, :]
    key_seg = segment_of(key_pos, bounds).reshape(blocks_here, -1)
    allowed = query_seg[:, None, :, None] == key_seg[:, None, None, :]
    zero_row = jnp.zeros((width,), jnp.float32)
    mixed_qkv = (
        matmul(inputs, full_qkv) + jnp.concatenate([vectors[0], zero_row, vectors[1]])
    ).astype(jnp.bfloat16)
    queries = mixed_qkv[:, :width]
    keyvals = mixed_qkv[:, width:]
    shard_piece = lax.all_gather(keyvals, "ctx", axis=0, tiled=True)
    block_count = shard_piece.shape[0] // BLOCK
    stacked = shard_piece.reshape(block_count, BLOCK, shard_piece.shape[1])
    picks = (
        linked_ids.reshape(-1)[:, None] == jnp.arange(block_count, dtype=jnp.int32)[None, :]
    ).astype(jnp.bfloat16)
    linked = jnp.einsum("lb,bkd->lkd", picks, stacked).reshape(
        blocks_here, link_count, BLOCK, 2 * width
    )
    query_heads = queries.reshape(blocks_here, BLOCK, head_count, HEAD_DIM)
    key_heads = linked[..., :width].reshape(blocks_here, link_count * BLOCK, head_count, HEAD_DIM)
    value_heads = linked[..., width:].reshape(blocks_here, link_count * BLOCK, head_count, HEAD_DIM)

    def score_parts():
        raw_scores = (
            jnp.einsum(
                "bqhd,bkhd->bhqk", query_heads, key_heads, preferred_element_type=jnp.float32
            )
            * 0.125
        )
        return jnp.where(allowed, raw_scores, -1e30)

    scores = score_parts()
    top_score = jnp.max(scores, axis=-1, keepdims=True)
    exp_total = jnp.sum(jnp.exp(scores - top_score), axis=-1, keepdims=True)
    attention = jnp.exp(scores - top_score) / exp_total
    attended = jnp.einsum(
        "bhqk,bkhd->bqhd",
        attention.astype(jnp.bfloat16),
        value_heads,
        preferred_element_type=jnp.float32,
    )
    attended = attended.reshape(tokens_here, width).astype(jnp.bfloat16)
    residual_one = inputs.astype(jnp.float32) + matmul(attended, full_out) + vectors[2]
    hidden_one, normed_one, inverse_one = layer_norm_parts(residual_one, gain_rows[0], vectors[3])
    hidden_low = hidden_one.astype(jnp.bfloat16)
    inner_pre = matmul(hidden_low, full_expand) + inner_bias
    activated, gelu_pull = jax.vjp(
        lambda argument: jax.nn.gelu(argument, approximate=False), inner_pre
    )
    active_low = activated.astype(jnp.bfloat16)
    residual_two = hidden_one + matmul(active_low, full_shrink) + vectors[4]
    result, normed_two, inverse_two = layer_norm_parts(residual_two, gain_rows[1], vectors[5])
    upstream = cotangent[0].astype(jnp.float32)
    grad_gain_two = jnp.sum(upstream * normed_two, axis=0)
    grad_shift_two = jnp.sum(upstream, axis=0)
    grad_two = layer_norm_back(upstream, normed_two, inverse_two, gain_rows[1])
    grad_bias_back = jnp.sum(grad_two, axis=0)
    grad_two_low = grad_two.astype(jnp.bfloat16)
    again_cols = (
        lax.all_gather(project_in, "ctx", axis=1, tiled=True),
        lax.all_gather(project_out, "ctx", axis=1, tiled=True),
        lax.all_gather(expand_weight, "ctx", axis=1, tiled=True),
        lax.all_gather(shrink_weight, "ctx", axis=1, tiled=True),
    )
    back_weights = (
        lax.all_gather(again_cols[0], "fsdp", axis=0, tiled=True),
        lax.all_gather(again_cols[1], "fsdp", axis=0, tiled=True),
        lax.all_gather(again_cols[2], "fsdp", axis=0, tiled=True),
        lax.all_gather(again_cols[3], "fsdp", axis=0, tiled=True),
    )
    back_qkv, back_out, back_expand, back_shrink = back_weights
    grad_shrink_w = matmul_left_t(active_low, grad_two_low)
    grad_active = matmul_right_t(grad_two_low, back_shrink)
    grad_inner = gelu_pull(grad_active)[0]
    grad_inner_bias = jnp.sum(grad_inner, axis=0)
    grad_inner_low = grad_inner.astype(jnp.bfloat16)
    grad_expand_w = matmul_left_t(hidden_low, grad_inner_low)
    grad_hidden_one = grad_two + matmul_right_t(grad_inner_low, back_expand)
    grad_gain_one = jnp.sum(grad_hidden_one * normed_one, axis=0)
    grad_shift_one = jnp.sum(grad_hidden_one, axis=0)
    grad_one = layer_norm_back(grad_hidden_one, normed_one, inverse_one, gain_rows[0])
    grad_bias_out = jnp.sum(grad_one, axis=0)
    grad_one_low = grad_one.astype(jnp.bfloat16)
    grad_out_w = matmul_left_t(attended, grad_one_low)
    grad_attended = matmul_right_t(grad_one_low, back_out).astype(jnp.bfloat16)
    grad_attended = grad_attended.reshape(blocks_here, BLOCK, head_count, HEAD_DIM)
    scores = score_parts()
    attention = jnp.exp(scores - top_score) / exp_total
    grad_attention = jnp.einsum(
        "bqhd,bkhd->bhqk", grad_attended, value_heads, preferred_element_type=jnp.float32
    )
    grad_values = jnp.einsum(
        "bhqk,bqhd->bkhd",
        attention.astype(jnp.bfloat16),
        grad_attended,
        preferred_element_type=jnp.float32,
    )
    row_inner = jnp.sum(attention * grad_attention, axis=-1, keepdims=True)
    grad_scores = (attention * (grad_attention - row_inner) * 0.125).astype(jnp.bfloat16)
    grad_queries = jnp.einsum(
        "bhqk,bkhd->bqhd", grad_scores, key_heads, preferred_element_type=jnp.float32
    ).reshape(tokens_here, width)
    grad_keys = jnp.einsum(
        "bhqk,bqhd->bkhd", grad_scores, query_heads, preferred_element_type=jnp.float32
    )
    slot_grads = jnp.concatenate(
        [
            grad_keys.reshape(blocks_here, link_count, BLOCK, width),
            grad_values.reshape(blocks_here, link_count, BLOCK, width),
        ],
        axis=-1,
    )
    grad_keyvals = lax.psum_scatter(
        scatter_rows(linked_ids, slot_grads, tokens_here * lax.axis_size("ctx"), 2 * width),
        "ctx",
        scatter_dimension=0,
        tiled=True,
    )
    grad_mixed = jnp.concatenate([grad_queries, grad_keyvals], axis=1)
    grad_bias_query = jnp.sum(grad_queries, axis=0)
    grad_bias_value = jnp.sum(grad_keyvals[:, width:], axis=0)
    grad_mixed_low = grad_mixed.astype(jnp.bfloat16)
    grad_qkv_w = matmul_left_t(inputs, grad_mixed_low)
    grad_inputs = grad_one + matmul_right_t(grad_mixed_low, back_qkv)
    grad_vectors = jnp.stack(
        [
            grad_bias_query,
            grad_bias_value,
            grad_bias_out,
            grad_shift_one,
            grad_bias_back,
            grad_shift_two,
        ]
    )
    grad_gain_rows = jnp.stack([grad_gain_one, grad_gain_two])
    grad_inner_row = grad_inner_bias[None, :]
    reduced = over_cols(
        grad_qkv_w,
        grad_out_w,
        grad_expand_w,
        grad_shrink_w,
        grad_vectors,
        grad_gain_rows,
        grad_inner_row,
    )
    sum_qkv, sum_out, sum_expand, sum_shrink = over_rows(
        reduced[0], reduced[1], reduced[2], reduced[3]
    )
    final_vectors, final_gains, final_inner = lax.psum((reduced[4], reduced[5], reduced[6]), "fsdp")
    return (
        result.astype(jnp.bfloat16)[None],
        grad_inputs.astype(jnp.bfloat16)[None],
        sum_qkv,
        sum_out,
        sum_expand,
        sum_shrink,
        final_vectors,
        final_gains,
        final_inner.reshape(-1),
    )


def solution(mesh):
    return jax.shard_map(
        shards,
        mesh=mesh,
        in_specs=(
            P("fsdp", "ctx", None),
            P("fsdp", "ctx"),
            P("fsdp", "ctx"),
            P("fsdp", "ctx"),
            P("fsdp", "ctx"),
            P(None, "ctx"),
            P(None, "ctx"),
            P("ctx"),
            P("fsdp", "ctx", None),
            P("fsdp", None),
            P("fsdp", None),
            P("fsdp", "ctx", None),
        ),
        out_specs=(
            P("fsdp", "ctx", None),
            P("fsdp", "ctx", None),
            P("fsdp", "ctx"),
            P("fsdp", "ctx"),
            P("fsdp", "ctx"),
            P("fsdp", "ctx"),
            P(None, "ctx"),
            P(None, "ctx"),
            P("ctx"),
        ),
        check_vma=False,
    )
```

```python
import jax
import jax.numpy as jnp
from jax import lax
from jax.experimental import pallas as pl
from jax.experimental.pallas import tpu as pltpu
from jax.sharding import PartitionSpec as P

HEAD_DIM = 64
BLOCK = 64


def segment_of(positions, bounds):
    return jnp.sum((positions[..., None] >= bounds).astype(jnp.int32), axis=-1)


def layer_norm_parts(values, gain_row, shift_row):
    centre = values - jnp.mean(values, axis=-1, keepdims=True)
    inverse = lax.rsqrt(jnp.mean(centre * centre, axis=-1, keepdims=True) + 1e-05)
    normed = centre * inverse
    return (normed * gain_row + shift_row, normed, inverse)


def layer_norm_back(upstream, normed, inverse, gain_row):
    scaled = upstream * gain_row
    return inverse * (
        scaled
        - jnp.mean(scaled, axis=-1, keepdims=True)
        - normed * jnp.mean(scaled * normed, axis=-1, keepdims=True)
    )


def matmul(left_side, right_side):
    return jnp.dot(left_side, right_side, preferred_element_type=jnp.float32)


def matmul_left_t(left_side, right_side):
    return lax.dot_general(
        left_side, right_side, (((0,), (0,)), ((), ())), preferred_element_type=jnp.float32
    )


def matmul_right_t(left_side, right_side):
    return lax.dot_general(
        left_side, right_side, (((1,), (1,)), ((), ())), preferred_element_type=jnp.float32
    )


def over_cols(qkv_grad, out_grad, expand_grad, shrink_grad, vector_grad, gain_grad, inner_grad):
    return (
        lax.psum_scatter(qkv_grad, "ctx", scatter_dimension=1, tiled=True),
        lax.psum_scatter(out_grad, "ctx", scatter_dimension=1, tiled=True),
        lax.psum_scatter(expand_grad, "ctx", scatter_dimension=1, tiled=True),
        lax.psum_scatter(shrink_grad, "ctx", scatter_dimension=1, tiled=True),
        lax.psum_scatter(vector_grad, "ctx", scatter_dimension=1, tiled=True),
        lax.psum_scatter(gain_grad, "ctx", scatter_dimension=1, tiled=True),
        lax.psum_scatter(inner_grad, "ctx", scatter_dimension=1, tiled=True),
    )


def over_rows(qkv_grad, out_grad, expand_grad, shrink_grad):
    return (
        lax.psum_scatter(
            qkv_grad.astype(jnp.bfloat16), "fsdp", scatter_dimension=0, tiled=True
        ).astype(jnp.float32),
        lax.psum_scatter(
            out_grad.astype(jnp.bfloat16), "fsdp", scatter_dimension=0, tiled=True
        ).astype(jnp.float32),
        lax.psum_scatter(
            expand_grad.astype(jnp.bfloat16), "fsdp", scatter_dimension=0, tiled=True
        ).astype(jnp.float32),
        lax.psum_scatter(
            shrink_grad.astype(jnp.bfloat16), "fsdp", scatter_dimension=0, tiled=True
        ).astype(jnp.float32),
    )


def scatter_rows(link_ids, link_grads, row_count, feature_width):
    block_count = row_count // BLOCK
    inside = (link_ids >= 0) & (link_ids < block_count)
    target = jnp.where(inside, link_ids, block_count).reshape(-1)
    partial_value = jnp.zeros((block_count, BLOCK, feature_width), jnp.float32)
    partial_value = partial_value.at[target].add(
        link_grads.reshape(-1, BLOCK, feature_width), mode="drop"
    )
    return partial_value.reshape(row_count, feature_width)


def shards(
    hidden,
    project_in,
    project_out,
    expand_weight,
    shrink_weight,
    biases,
    gains,
    expand_bias,
    random_blocks,
    global_blocks,
    document_lengths,
    cotangent,
):
    inputs = hidden[0]
    tokens_here = inputs.shape[0]
    width = inputs.shape[1]
    head_count = width // HEAD_DIM
    blocks_here = tokens_here // BLOCK
    rand_count = random_blocks.shape[2]
    link_count = 3 + rand_count + global_blocks.shape[1]
    ctx_rank = lax.axis_index("ctx")
    last_block = tokens_here * lax.axis_size("ctx") // BLOCK - 1
    col_full = (
        lax.all_gather(project_in, "ctx", axis=1, tiled=True),
        lax.all_gather(project_out, "ctx", axis=1, tiled=True),
        lax.all_gather(expand_weight, "ctx", axis=1, tiled=True),
        lax.all_gather(shrink_weight, "ctx", axis=1, tiled=True),
        lax.all_gather(biases, "ctx", axis=1, tiled=True),
        lax.all_gather(gains, "ctx", axis=1, tiled=True),
        lax.all_gather(expand_bias.reshape(1, -1), "ctx", axis=1, tiled=True),
    )
    full_qkv, full_out, full_expand, full_shrink = (
        lax.all_gather(col_full[0], "fsdp", axis=0, tiled=True),
        lax.all_gather(col_full[1], "fsdp", axis=0, tiled=True),
        lax.all_gather(col_full[2], "fsdp", axis=0, tiled=True),
        lax.all_gather(col_full[3], "fsdp", axis=0, tiled=True),
    )
    vectors = col_full[4].astype(jnp.float32)
    gain_rows = col_full[5].astype(jnp.float32)
    inner_bias = col_full[6][0].astype(jnp.float32)
    block_ids = ctx_rank * blocks_here + jnp.arange(blocks_here, dtype=jnp.int32)
    window = jnp.stack(
        [jnp.maximum(block_ids - 1, 0), block_ids, jnp.minimum(block_ids + 1, last_block)], axis=1
    )
    global_links = jnp.broadcast_to(
        global_blocks[0][None, :], (blocks_here, global_blocks.shape[1])
    )
    linked_ids = jnp.concatenate([window, random_blocks[0], global_links], axis=1)
    lengths = document_lengths[0]
    doc_order = jnp.arange(lengths.shape[0], dtype=jnp.int32)
    bounds = jnp.sum(
        jnp.where(doc_order[None, :] <= doc_order[:-1, None], lengths[None, :], 0), axis=1
    )
    query_pos = (ctx_rank * tokens_here + jnp.arange(tokens_here, dtype=jnp.int32)).reshape(
        blocks_here, BLOCK
    )
    query_seg = segment_of(query_pos, bounds)
    key_pos = linked_ids[:, :, None] * BLOCK + jnp.arange(BLOCK, dtype=jnp.int32)[None, None, :]
    key_seg = segment_of(key_pos, bounds).reshape(blocks_here, -1)
    allowed = query_seg[:, None, :, None] == key_seg[:, None, None, :]
    zero_row = jnp.zeros((width,), jnp.float32)
    mixed_qkv = (
        matmul(inputs, full_qkv) + jnp.concatenate([vectors[0], zero_row, vectors[1]])
    ).astype(jnp.bfloat16)
    queries = mixed_qkv[:, :width]
    keyvals = mixed_qkv[:, width:]
    shard_piece = lax.all_gather(keyvals, "ctx", axis=0, tiled=True)
    block_count = shard_piece.shape[0] // BLOCK
    stacked = shard_piece.reshape(block_count, BLOCK, shard_piece.shape[1])
    picks = (
        linked_ids.reshape(-1)[:, None] == jnp.arange(block_count, dtype=jnp.int32)[None, :]
    ).astype(jnp.bfloat16)
    linked = jnp.einsum("lb,bkd->lkd", picks, stacked).reshape(
        blocks_here, link_count, BLOCK, 2 * width
    )
    query_heads = queries.reshape(blocks_here, BLOCK, head_count, HEAD_DIM)
    key_heads = linked[..., :width].reshape(blocks_here, link_count * BLOCK, head_count, HEAD_DIM)
    value_heads = linked[..., width:].reshape(blocks_here, link_count * BLOCK, head_count, HEAD_DIM)

    def score_parts():
        raw_scores = (
            jnp.einsum(
                "bqhd,bkhd->bhqk", query_heads, key_heads, preferred_element_type=jnp.float32
            )
            * 0.125
        )
        return jnp.where(allowed, raw_scores, -1e30)

    scores = score_parts()
    top_score = jnp.max(scores, axis=-1, keepdims=True)
    exp_total = jnp.sum(jnp.exp(scores - top_score), axis=-1, keepdims=True)
    attention = jnp.exp(scores - top_score) / exp_total
    attended = jnp.einsum(
        "bhqk,bkhd->bqhd",
        attention.astype(jnp.bfloat16),
        value_heads,
        preferred_element_type=jnp.float32,
    )
    attended = attended.reshape(tokens_here, width).astype(jnp.bfloat16)
    residual_one = inputs.astype(jnp.float32) + matmul(attended, full_out) + vectors[2]
    hidden_one, normed_one, inverse_one = layer_norm_parts(residual_one, gain_rows[0], vectors[3])
    hidden_low = hidden_one.astype(jnp.bfloat16)
    inner_pre = matmul(hidden_low, full_expand) + inner_bias
    activated, gelu_pull = jax.vjp(
        lambda argument: jax.nn.gelu(argument, approximate=False), inner_pre
    )
    active_low = activated.astype(jnp.bfloat16)
    residual_two = hidden_one + matmul(active_low, full_shrink) + vectors[4]
    result, normed_two, inverse_two = layer_norm_parts(residual_two, gain_rows[1], vectors[5])
    upstream = cotangent[0].astype(jnp.float32)
    grad_gain_two = jnp.sum(upstream * normed_two, axis=0)
    grad_shift_two = jnp.sum(upstream, axis=0)
    grad_two = layer_norm_back(upstream, normed_two, inverse_two, gain_rows[1])
    grad_bias_back = jnp.sum(grad_two, axis=0)
    grad_two_low = grad_two.astype(jnp.bfloat16)
    again_cols = (
        lax.all_gather(project_in, "ctx", axis=1, tiled=True),
        lax.all_gather(project_out, "ctx", axis=1, tiled=True),
        lax.all_gather(expand_weight, "ctx", axis=1, tiled=True),
        lax.all_gather(shrink_weight, "ctx", axis=1, tiled=True),
    )
    back_weights = (
        lax.all_gather(again_cols[0], "fsdp", axis=0, tiled=True),
        lax.all_gather(again_cols[1], "fsdp", axis=0, tiled=True),
        lax.all_gather(again_cols[2], "fsdp", axis=0, tiled=True),
        lax.all_gather(again_cols[3], "fsdp", axis=0, tiled=True),
    )
    back_qkv, back_out, back_expand, back_shrink = back_weights
    grad_shrink_w = matmul_left_t(active_low, grad_two_low)
    grad_active = matmul_right_t(grad_two_low, back_shrink)
    grad_inner = gelu_pull(grad_active)[0]
    grad_inner_bias = jnp.sum(grad_inner, axis=0)
    grad_inner_low = grad_inner.astype(jnp.bfloat16)
    grad_expand_w = matmul_left_t(hidden_low, grad_inner_low)
    grad_hidden_one = grad_two + matmul_right_t(grad_inner_low, back_expand)
    grad_gain_one = jnp.sum(grad_hidden_one * normed_one, axis=0)
    grad_shift_one = jnp.sum(grad_hidden_one, axis=0)
    grad_one = layer_norm_back(grad_hidden_one, normed_one, inverse_one, gain_rows[0])
    grad_bias_out = jnp.sum(grad_one, axis=0)
    grad_one_low = grad_one.astype(jnp.bfloat16)
    grad_out_w = matmul_left_t(attended, grad_one_low)
    grad_attended = matmul_right_t(grad_one_low, back_out).astype(jnp.bfloat16)
    grad_attended = grad_attended.reshape(blocks_here, BLOCK, head_count, HEAD_DIM)
    scores = score_parts()
    attention = jnp.exp(scores - top_score) / exp_total
    grad_attention = jnp.einsum(
        "bqhd,bkhd->bhqk", grad_attended, value_heads, preferred_element_type=jnp.float32
    )
    grad_values = jnp.einsum(
        "bhqk,bqhd->bkhd",
        attention.astype(jnp.bfloat16),
        grad_attended,
        preferred_element_type=jnp.float32,
    )
    row_inner = jnp.sum(attention * grad_attention, axis=-1, keepdims=True)
    grad_scores = (attention * (grad_attention - row_inner) * 0.125).astype(jnp.bfloat16)
    grad_queries = jnp.einsum(
        "bhqk,bkhd->bqhd", grad_scores, key_heads, preferred_element_type=jnp.float32
    ).reshape(tokens_here, width)
    grad_keys = jnp.einsum(
        "bhqk,bqhd->bkhd", grad_scores, query_heads, preferred_element_type=jnp.float32
    )
    slot_grads = jnp.concatenate(
        [
            grad_keys.reshape(blocks_here, link_count, BLOCK, width),
            grad_values.reshape(blocks_here, link_count, BLOCK, width),
        ],
        axis=-1,
    )
    grad_keyvals = lax.psum_scatter(
        scatter_rows(linked_ids, slot_grads, tokens_here * lax.axis_size("ctx"), 2 * width),
        "ctx",
        scatter_dimension=0,
        tiled=True,
    )
    grad_mixed = jnp.concatenate([grad_queries, grad_keyvals], axis=1)
    grad_bias_query = jnp.sum(grad_queries, axis=0)
    grad_bias_value = jnp.sum(grad_keyvals[:, width:], axis=0)
    grad_mixed_low = grad_mixed.astype(jnp.bfloat16)
    grad_qkv_w = matmul_left_t(inputs, grad_mixed_low)
    grad_inputs = grad_one + matmul_right_t(grad_mixed_low, back_qkv)
    grad_vectors = jnp.stack(
        [
            grad_bias_query,
            grad_bias_value,
            grad_bias_out,
            grad_shift_one,
            grad_bias_back,
            grad_shift_two,
        ]
    )
    grad_gain_rows = jnp.stack([grad_gain_one, grad_gain_two])
    grad_inner_row = grad_inner_bias[None, :]
    reduced = over_cols(
        grad_qkv_w,
        grad_out_w,
        grad_expand_w,
        grad_shrink_w,
        grad_vectors,
        grad_gain_rows,
        grad_inner_row,
    )
    sum_qkv, sum_out, sum_expand, sum_shrink = over_rows(
        reduced[0], reduced[1], reduced[2], reduced[3]
    )
    final_vectors, final_gains, final_inner = lax.psum((reduced[4], reduced[5], reduced[6]), "fsdp")
    return (
        result.astype(jnp.bfloat16)[None],
        grad_inputs.astype(jnp.bfloat16)[None],
        sum_qkv,
        sum_out,
        sum_expand,
        sum_shrink,
        final_vectors,
        final_gains,
        final_inner.reshape(-1),
    )


MESH = pl.DeviceIdType.MESH
BF = jnp.bfloat16
F32 = jnp.float32
SENDS = 128
RECVS = 128
NEG = -1e30


def dot_nn(a, b):
    return jnp.dot(a, b, preferred_element_type=F32)


def dot_nt(a, b):
    return lax.dot_general(a, b, (((1,), (1,)), ((), ())), preferred_element_type=F32)


def dot_tn(a, b):
    return lax.dot_general(a, b, (((0,), (0,)), ((), ())), preferred_element_type=F32)


def row_sum(values):
    return jnp.sum(values, axis=0, keepdims=True)


def layer_kernel(
    rand_ref, glob_ref, doc_ref, hid, cot, win, wout, wexp, wshr, bia, gai, ebi,
    o_out, o_gh, o_win, o_wout, o_wexp, o_wshr, o_gb, o_gg, o_ge,
    win3, xg, eo, ms, mg, ps, par, win_p, wout_p, wexp_f, wshr_p, w_in, w_out, w_shr, prm,
    q_s, kv, kh, vh, bias_s, p_s, a_f, a_b, a_all, hg, h1_s, n1_s, r1_s, dge, g_s, ysum, yb,
    rs1, d2_s, dg, du_s, dh_b, rs2, beg, d1_s, d1g, dab, da, ds_s, dkv, dkb, dkr, dz, dx_b, rs3,
    gs, rs_c, t_shr, rs_y, fsb, fs, ge, re_c, t_exp, re_y, te_f, te_b, re_z,
    go, ro_c, tob, ro_y, tob2, fo, gi, ri_c, tib, ri_y, ti2, fi,
    vg, vr, vs1, vc, vs2, vy, qb_s, vb_s, ob, ohr, ghb, ghr,
    ssem, rsem,
):
    ctx = lax.axis_index("ctx")
    seq = lax.axis_index("fsdp")
    z, x = ctx // 2, ctx % 2
    y, c = seq // 2, seq % 2
    zh, zl = z // 2, z % 2
    r = 2 * zl + x
    f = seq

    def dev(px, py, pz, pc):
        return (2 * pz + px, 2 * py + pc)

    def flip(v, on):
        return v + on - 2 * v * on

    def peer(j):
        return dev(flip(x, j % 2), y, 2 * zh + flip(zl, j // 2), c)

    def peer_rank(j):
        return 2 * flip(zl, j // 2) + flip(x, j % 2)

    core_mate = dev(x, y, z, 1 - c)
    y_mate = dev(x, 1 - y, z, c)
    z_mate = dev(x, y, 2 * (1 - zh) + zl, c)
    home = dev(x, y, 2 * c + zl, zh)

    pending = []
    counts = {"s": 0, "r": 0}

    def recvs(n):
        first = counts["r"]
        counts["r"] = first + n
        assert counts["r"] <= RECVS
        return first

    def sends(n):
        first = counts["s"]
        counts["s"] = first + n
        assert counts["s"] <= SENDS
        return first

    def copy_to(src, dst, si, ri, to):
        return pltpu.make_async_remote_copy(
            src_ref=src, dst_ref=dst, send_sem=ssem.at[si], recv_sem=rsem.at[ri],
            device_id=to, device_id_type=MESH,
        )

    def send(src, dst, ri, to):
        cp = copy_to(src, dst, sends(1), ri, to)
        cp.start()
        pending.append(cp.wait_send)

    def send_or_keep(src, dst, ri, to):
        si = sends(1)
        away = jnp.logical_or(to[0] != ctx, to[1] != seq)

        @pl.when(away)
        def _():
            copy_to(src, dst, si, ri, to).start()

        @pl.when(jnp.logical_not(away))
        def _():
            pltpu.make_async_copy(src, dst, rsem.at[ri]).start()

        def finish():
            @pl.when(away)
            def _():
                copy_to(src, dst, si, ri, to).wait_send()

        pending.append(finish)

    def arrived(dst, ri):
        pltpu.make_async_copy(dst, dst, rsem.at[ri]).wait()

    barrier = pltpu.get_barrier_semaphore()
    place = 2 * ctx + c
    for d in range(1, 16):
        other = (place + d) % 16
        pl.semaphore_signal(
            barrier, inc=1, device_id=(other // 2, 2 * y + other % 2), device_id_type=MESH
        )
    pl.semaphore_signal(barrier, inc=1, device_id=y_mate, device_id_type=MESH)

    lane = lax.broadcasted_iota(jnp.int32, (1, 128), 1)
    for i in range(2):
        block = 2 * ctx + i
        links = [jnp.maximum(block - 1, 0), block, jnp.minimum(block + 1, 15)]
        links += [rand_ref[i, k] for k in range(3)] + [glob_ref[0, k] for k in range(2)]
        count = jnp.zeros((1, 128), F32)
        for link in links:
            count += jnp.where(lane == link, 1.0, 0.0)
        ms[i : i + 1, :] = count
    edge = doc_ref[0, 0]
    edges = jnp.zeros((1, 128), F32)
    for k in range(7):
        edges += jnp.where(lane == k, edge.astype(F32), 0.0)
        edge = edge + doc_ref[0, k + 1]
    ms[2:3, :] = edges
    ms[3:8, :] = jnp.zeros((5, 128), F32)
    for j in range(3):
        win3[j] = win[:, 96 * j : 96 * j + 96]
    ps[...] = jnp.zeros((16, 128), F32)
    ps[0:6, 0:96] = bia[...].astype(F32)
    ps[6:8, 0:96] = gai[...].astype(F32)
    ps[8:11, :] = ebi[...].astype(F32)

    pl.semaphore_wait(barrier, 16)

    k_x, k_m, k_e = recvs(4), recvs(4), recvs(1)
    send_or_keep(hid, xg.at[r], k_x, home)
    send_or_keep(ms, mg.at[r], k_m, home)
    k_par = recvs(8)
    k_win = recvs(6)
    for j in range(3):
        unit = 3 * ctx + j
        rank = (unit % 8) // 2
        slot = 2 * (unit // 8) + unit % 2
        for half in range(2):
            send_or_keep(
                win3.at[j], win_p.at[f, slot], k_win + slot, dev(rank % 2, y, 2 * half + rank // 2, c)
            )
    for d in range(1, 8):
        other = (ctx + d) % 8
        send(ps, par.at[ctx], k_par + d, (other, seq))
    par[ctx] = ps[...]

    arrived(xg.at[r], k_x)
    arrived(mg.at[r], k_m)
    for j in range(1, 4):
        send(mg.at[r], mg.at[r], k_m + j, peer(j))
        send(xg.at[r], xg.at[r], k_x + j, peer(j))
    send_or_keep(cot, eo, k_e, home)

    k_wout = recvs(8)
    for d in range(8):
        other = (ctx + d) % 8
        if d == 0:
            pltpu.make_async_copy(wout, wout_p.at[f, ctx], rsem.at[k_wout]).start()
        else:
            send(wout, wout_p.at[f, ctx], k_wout + d, (other, seq))
    k_wexp = recvs(2)
    mine_exp = wexp_f.at[f, :, pl.ds(pl.multiple_of(384 * zh, 128), 384)]
    pltpu.make_async_copy(wexp, mine_exp, rsem.at[k_wexp]).start()
    send(wexp, mine_exp, k_wexp + 1, z_mate)
    k_wshr = recvs(4)
    for sub in range(2):
        for half in range(2):
            send_or_keep(
                wshr.at[sub], wshr_p.at[y, x, 2 * zh + zl], k_wshr + 2 * zh + zl,
                dev(sub, y, 2 * half + c, x),
            )

    k_win_y, k_win_c = recvs(1), recvs(2)
    for slot in range(6):
        arrived(win_p.at[f, slot], k_win + slot)
    send(win_p.at[f], win_p.at[f], k_win_y, y_mate)
    send(win_p.at[f], win_p.at[f], k_win_c, core_mate)
    f_y = 2 * (1 - y) + c
    arrived(win_p.at[f_y], k_win_y)
    send(win_p.at[f_y], win_p.at[f_y], k_win_c + 1, core_mate)

    for j in range(1, 4):
        arrived(mg.at[peer_rank(j)], k_m + j)
    counted = jnp.concatenate([mg[k, 0:2, :] for k in range(4)], axis=0)
    spread = (
        lax.broadcasted_iota(jnp.int32, (128, 1024), 1) // 64
        == lax.broadcasted_iota(jnp.int32, (128, 1024), 0)
    ).astype(BF)
    counted = dot_nn(counted.astype(BF), spread)
    logs = jnp.where(counted > 0.5, jnp.log(jnp.maximum(counted, 1.0)), NEG)
    key_pos = lax.broadcasted_iota(jnp.int32, (1, 1024), 1).astype(F32)
    row_pos = (lax.broadcasted_iota(jnp.int32, (512, 1), 0) + 512 * c).astype(F32)
    key_seg = jnp.zeros((1, 1024), F32)
    row_seg = jnp.zeros((512, 1), F32)
    for k in range(7):
        at = mg[0, 2:3, k : k + 1]
        key_seg += jnp.where(key_pos >= at, 1.0, 0.0)
        row_seg += jnp.where(row_pos >= at, 1.0, 0.0)
    for i in range(8):
        bias_s[i // 2, 64 * (i % 2) : 64 * (i % 2) + 64, :] = jnp.where(
            row_seg[64 * i : 64 * i + 64] == key_seg, logs[i : i + 1, :], NEG
        )

    for d in range(1, 8):
        arrived(par.at[(ctx + 8 - d) % 8], k_par + d)
    prm[...] = jnp.concatenate([par[b, 0:8, 0:96] for b in range(8)], axis=1)
    be = jnp.concatenate(
        [par[r, 8 + i : 9 + i, :] for i in range(3)] + [par[4 + r, 8 + i : 9 + i, :] for i in range(3)],
        axis=1,
    )
    zrow = jnp.zeros((1, 192), F32)
    z_bias = jnp.concatenate(
        [par[2 * r, 0:1, 0:96], par[2 * r + 1, 0:1, 0:96], zrow, par[2 * r, 1:2, 0:96], par[2 * r + 1, 1:2, 0:96]],
        axis=1,
    )


    arrived(win_p.at[2 * y + 1 - c], k_win_c)
    arrived(win_p.at[2 * (1 - y) + 1 - c], k_win_c + 1)
    for k in range(4):
        w_in[192 * k : 192 * k + 192, :] = jnp.concatenate([win_p[k, i] for i in range(6)], axis=1)

    def project(k):
        mixed = dot_nn(xg[k], w_in[...]) + z_bias
        q_s[k] = (mixed[:, 0:192].astype(BF).astype(F32) * 0.125).astype(BF)
        kv[c, pl.ds(pl.multiple_of(128 * k, 128), 128), :] = mixed[:, 192:576].astype(BF)

    project(r)

    def project_step(j, carry):
        rank = peer_rank(j)
        arrived(xg.at[rank], k_x + j)
        project(rank)
        return carry

    lax.fori_loop(1, 4, project_step, 0)
    k_kv = recvs(1)
    send(kv.at[c], kv.at[c], k_kv, core_mate)

    k_wout_y, k_wout_c = recvs(1), recvs(2)
    k_wexp_y, k_wexp_c = recvs(1), recvs(2)
    k_wshr_y, k_wshr_c = recvs(1), recvs(2)
    for d in range(8):
        arrived(wout_p.at[f, (ctx + 8 - d) % 8], k_wout + d)
    send(wout_p.at[f], wout_p.at[f], k_wout_y, y_mate)
    send(wout_p.at[f], wout_p.at[f], k_wout_c, core_mate)

    arrived(kv.at[1 - c], k_kv)
    for h in range(3):
        for half in range(2):
            kh[h, 512 * half : 512 * half + 512, :] = kv[half, :, 64 * h : 64 * h + 64]
            vh[h, 512 * half : 512 * half + 512, :] = kv[half, :, 192 + 64 * h : 256 + 64 * h]

    def attend(k, carry):
        outs = []
        for h in range(3):
            scores = dot_nt(q_s[k, :, 64 * h : 64 * h + 64], kh[h]) + bias_s[k]
            top = jnp.max(scores, axis=1, keepdims=True)
            exps = jnp.exp(scores - top)
            total = jnp.sum(exps, axis=1, keepdims=True)
            weights = (exps * (1.0 / total)).astype(BF)
            p_s[h, k] = weights
            outs.append(dot_nn(weights, vh[h]))
        both = jnp.concatenate(outs, axis=1)
        a_f[k] = both
        a_b[k] = both.astype(BF)
        return carry

    lax.fori_loop(0, 2, attend, 0)
    for half in range(2):
        at = pl.ds(pl.multiple_of(384 * half, 128), 384)
        piece = wexp_f.at[f, :, at]
        own = half == zh

        @pl.when(own)
        def _():
            arrived(piece, k_wexp)

        @pl.when(jnp.logical_not(own))
        def _():
            arrived(piece, k_wexp + 1)

    send(wexp_f.at[f], wexp_f.at[f], k_wexp_y, y_mate)
    send(wexp_f.at[f], wexp_f.at[f], k_wexp_c, core_mate)
    for k in range(4):
        arrived(wshr_p.at[y, c, k], k_wshr + k)
    send(wshr_p.at[y, c], wshr_p.at[y, c], k_wshr_y, y_mate)
    send(wshr_p.at[y, c], wshr_p.at[y, c], k_wshr_c, core_mate)
    arrived(wout_p.at[f_y], k_wout_y)
    send(wout_p.at[f_y], wout_p.at[f_y], k_wout_c + 1, core_mate)
    lax.fori_loop(2, 4, attend, 0)

    k_a = recvs(4)
    for j in range(1, 4):
        send(a_b.at[peer_rank(j)], a_all.at[r], k_a + j, peer(j))
    a_all[r] = a_b[r]

    arrived(wexp_f.at[f_y], k_wexp_y)
    send(wexp_f.at[f_y], wexp_f.at[f_y], k_wexp_c + 1, core_mate)
    arrived(wshr_p.at[1 - y, c], k_wshr_y)
    send(wshr_p.at[1 - y, c], wshr_p.at[1 - y, c], k_wshr_c + 1, core_mate)
    arrived(wout_p.at[2 * y + 1 - c], k_wout_c)
    arrived(wout_p.at[2 * (1 - y) + 1 - c], k_wout_c + 1)
    for k in range(4):
        w_out[192 * k : 192 * k + 192, :] = jnp.concatenate([wout_p[k, b] for b in range(8)], axis=1)

    for j in range(1, 4):
        arrived(a_all.at[peer_rank(j)], k_a + j)
    first = xg[r].astype(F32) + prm[2:3, :]
    for k in range(4):
        first += dot_nn(a_all[k], w_out[192 * k : 192 * k + 192, :])
    centre = first - jnp.mean(first, axis=1, keepdims=True)
    inverse = lax.rsqrt(jnp.mean(centre * centre, axis=1, keepdims=True) + 1e-05)
    normed = centre * inverse
    hidden_one = normed * prm[6:7, :] + prm[3:4, :]
    n1_s[...] = normed
    r1_s[...] = inverse
    h1_s[...] = hidden_one
    hg[r] = hidden_one.astype(BF)
    k_h = recvs(4)
    for j in range(1, 4):
        send(hg.at[r], hg.at[r], k_h + j, peer(j))

    arrived(wexp_f.at[2 * y + 1 - c], k_wexp_c)
    arrived(wexp_f.at[2 * (1 - y) + 1 - c], k_wexp_c + 1)
    arrived(wshr_p.at[y, 1 - c], k_wshr_c)
    arrived(wshr_p.at[1 - y, 1 - c], k_wshr_c + 1)
    for half in range(2):
        w_shr[384 * half : 384 * half + 384, :] = jnp.concatenate(
            [wshr_p[half, b % 2, b // 2] for b in range(8)], axis=1
        )

    def expand(k):
        inner = dot_nn(hg[k], wexp_f[...].reshape(768, 768)) + be
        below = 0.5 * (1.0 + lax.erf(inner * 0.7071067811865476))
        dge[k] = below + inner * jnp.exp(-0.5 * inner * inner) * 0.3989422804014327
        active = (inner * below).astype(BF)
        g_s[k] = active
        return dot_nn(active, w_shr[...])

    ysum[...] = expand(r)
    k_r1, s_r1 = recvs(4), sends(4)

    def expand_step(j, carry):
        rank = peer_rank(j)
        arrived(hg.at[rank], k_h + j)
        yb[j] = expand(rank).astype(BF)
        copy_to(yb.at[j], rs1.at[j], s_r1 + j, k_r1 + j, peer(j)).start()
        return carry

    lax.fori_loop(1, 4, expand_step, 0)
    for j in range(1, 4):
        pending.append(copy_to(yb.at[j], rs1.at[j], s_r1 + j, k_r1 + j, peer(j)).wait_send)

    arrived(eo, k_e)
    upstream = eo[...].astype(F32)
    second = h1_s[...] + prm[4:5, :] + ysum[...]
    for j in range(1, 4):
        arrived(rs1.at[j], k_r1 + j)
        second += rs1[j].astype(F32)
    centre = second - jnp.mean(second, axis=1, keepdims=True)
    inverse = lax.rsqrt(jnp.mean(centre * centre, axis=1, keepdims=True) + 1e-05)
    normed = centre * inverse
    scaled = upstream * prm[7:8, :]
    grad_two = inverse * (
        scaled
        - jnp.mean(scaled, axis=1, keepdims=True)
        - normed * jnp.mean(scaled * normed, axis=1, keepdims=True)
    )
    d2_s[...] = grad_two
    dg[r] = grad_two.astype(BF)
    k_d = recvs(4)
    for j in range(1, 4):
        send(dg.at[r], dg.at[r], k_d + j, peer(j))
    ob[...] = (normed * prm[7:8, :] + prm[5:6, :]).astype(BF)
    k_o = recvs(1)
    send_or_keep(ob, ohr, k_o, home)
    row_gain_two = row_sum(upstream * normed)
    row_shift_two = row_sum(upstream)
    row_back = row_sum(grad_two)

    def contract(k):
        inner = dge[k] * dot_nt(dg[k], w_shr[...])
        low = inner.astype(BF)
        du_s[k] = low
        beg[k] = row_sum(inner)
        return dot_nt(low, wexp_f[...].reshape(768, 768))

    ysum[...] = contract(r)
    k_r2, s_r2 = recvs(4), sends(4)

    def contract_step(j, carry):
        rank = peer_rank(j)
        arrived(dg.at[rank], k_d + j)
        dh_b[j] = contract(rank).astype(BF)
        copy_to(dh_b.at[j], rs2.at[j], s_r2 + j, k_r2 + j, peer(j)).start()
        return carry

    lax.fori_loop(1, 4, contract_step, 0)
    for j in range(1, 4):
        pending.append(copy_to(dh_b.at[j], rs2.at[j], s_r2 + j, k_r2 + j, peer(j)).wait_send)

    def shrink_grad(half):
        def step(i, carry):
            at = pl.multiple_of(384 * half + 128 * i, 128)
            rows = g_s[:, :, pl.ds(at, 128)].reshape(512, 128)
            part = dot_tn(rows, dg[...].reshape(512, 768))
            for b in range(8):
                gs[half, b % 2, b // 2, pl.ds(pl.multiple_of(128 * i, 128), 128), :] = part[
                    :, 96 * b : 96 * b + 96
                ].astype(BF)
            return carry

        lax.fori_loop(0, 3, step, 0)

    shrink_grad(0)
    shrink_grad(1)
    k_gs = recvs(2)
    for half in range(2):
        send(gs.at[half, 1 - c], rs_c.at[half], k_gs + half, core_mate)

    def expand_grad(i, carry):
        at = pl.ds(pl.multiple_of(128 * i, 128), 128)
        rows = hg[:, :, at].reshape(512, 128)
        ge[at, :] = dot_tn(rows, du_s[...].reshape(512, 768)).astype(BF)
        return carry

    lax.fori_loop(0, 6, expand_grad, 0)
    k_ge = recvs(2)
    for half in range(2):
        at = pl.ds(pl.multiple_of(192 * (2 * half + 1 - c), 64), 192)
        send(ge.at[at, :], re_c.at[half], k_ge + half, core_mate)

    grad_hidden = d2_s[...] + ysum[...]
    for j in range(1, 4):
        arrived(rs2.at[j], k_r2 + j)
        grad_hidden += rs2[j].astype(F32)
    normed = n1_s[...]
    scaled = grad_hidden * prm[6:7, :]
    grad_one = r1_s[...] * (
        scaled
        - jnp.mean(scaled, axis=1, keepdims=True)
        - normed * jnp.mean(scaled * normed, axis=1, keepdims=True)
    )
    d1_s[...] = grad_one
    low_one = grad_one.astype(BF)
    d1g[r] = low_one
    for k in range(4):
        dab[k] = dot_nt(low_one, w_out[192 * k : 192 * k + 192, :]).astype(BF)
    k_da, k_d1 = recvs(4), recvs(4)
    for j in range(1, 4):
        send(dab.at[peer_rank(j)], da.at[r], k_da + j, peer(j))
    da[r] = dab[r]
    for j in range(1, 4):
        send(d1g.at[r], d1g.at[r], k_d1 + j, peer(j))
    row_gain_one = row_sum(grad_hidden * normed)
    row_shift_one = row_sum(grad_hidden)
    row_out = row_sum(grad_one)

    k_gs_y, k_ge_y = recvs(1), recvs(1)
    for half in range(2):
        arrived(rs_c.at[half], k_gs + half)
        arrived(re_c.at[half], k_ge + half)
    t_shr[...] = (gs[1 - y, c].astype(F32) + rs_c[1 - y].astype(F32)).astype(BF)
    send(t_shr, rs_y, k_gs_y, y_mate)
    at_y = pl.ds(pl.multiple_of(192 * f_y, 64), 192)
    at_own = pl.ds(pl.multiple_of(192 * f, 64), 192)
    t_exp[...] = (ge[at_y, :].astype(F32) + re_c[1 - y].astype(F32)).astype(BF)
    send(t_exp, re_y, k_ge_y, y_mate)

    for j in range(1, 4):
        arrived(da.at[peer_rank(j)], k_da + j)

    def attend_back(k, carry):
        outs = []
        dots = da[k].astype(F32) * a_f[k]
        for h in range(3):
            at = slice(64 * h, 64 * h + 64)
            delta = jnp.sum(dots[:, at], axis=1, keepdims=True)
            slots = dot_nt(da[k, :, at], vh[h])
            low = (p_s[h, k].astype(F32) * (slots - delta)).astype(BF)
            ds_s[h, k] = low
            outs.append(dot_nn(low, kh[h]) * 0.125)
        queries = jnp.concatenate(outs, axis=1)
        qb_s[k] = row_sum(queries)
        dz[k, :, 0:192] = queries.astype(BF)
        return carry

    lax.fori_loop(0, 4, attend_back, 0)
    sums = []
    for h in range(3):
        at = slice(64 * h, 64 * h + 64)
        sums.append(dot_tn(q_s[...].reshape(512, 192)[:, at], ds_s[h].reshape(512, 1024)))
    for h in range(3):
        at = slice(64 * h, 64 * h + 64)
        sums.append(dot_tn(da[...].reshape(512, 192)[:, at], p_s[h].reshape(512, 1024)))
    sums = jnp.concatenate(sums, axis=0)
    dkv[0] = sums[:, 0:512].T
    dkv[1] = sums[:, 512:1024].T
    dkb[...] = dkv[1 - c].astype(BF)
    k_dk = recvs(1)
    send(dkb, dkr, k_dk, core_mate)

    for j in range(1, 4):
        arrived(d1g.at[peer_rank(j)], k_d1 + j)
    part = dot_tn(a_b[...].reshape(512, 192), d1g[...].reshape(512, 768))
    for b in range(8):
        go[b % 2, b // 2] = part[:, 96 * b : 96 * b + 96].astype(BF)
    k_go = recvs(1)
    send(go.at[1 - c], ro_c, k_go, core_mate)

    arrived(dkr, k_dk)
    keyvals = dkv[c] + dkr[...].astype(F32)
    vb_s[...] = row_sum(keyvals[:, 192:384])
    dz[:, :, 192:576] = keyvals.astype(BF).reshape(4, 128, 384)

    def input_part(k):
        return dot_nt(dz[k], w_in[...])

    k_r3, s_r3 = recvs(4), sends(4)

    def input_step(j, carry):
        dx_b[j] = input_part(peer_rank(j)).astype(BF)
        copy_to(dx_b.at[j], rs3.at[j], s_r3 + j, k_r3 + j, peer(j)).start()
        return carry

    lax.fori_loop(1, 4, input_step, 0)
    for j in range(1, 4):
        pending.append(copy_to(dx_b.at[j], rs3.at[j], s_r3 + j, k_r3 + j, peer(j)).wait_send)

    def project_grad(i, carry):
        at = pl.ds(pl.multiple_of(128 * i, 128), 128)
        rows = xg[:, :, at].reshape(512, 128)
        part = dot_tn(rows, dz[...].reshape(512, 576))
        for slot in range(6):
            gi[slot, at, :] = part[:, 96 * slot : 96 * slot + 96].astype(BF)
        return carry

    lax.fori_loop(0, 6, project_grad, 0)
    k_gi = recvs(2)
    for half in range(2):
        at = pl.ds(pl.multiple_of(192 * (2 * half + 1 - c), 64), 192)
        send(gi.at[:, at, :], ri_c.at[half], k_gi + half, core_mate)

    vg[...] = jnp.zeros((8, 16, 128), F32)
    rows = jnp.concatenate(
        [row_out, row_shift_one, row_back, row_shift_two, row_gain_one, row_gain_two], axis=0
    )
    for b in range(8):
        vg[b, 2:8, 0:96] = rows[:, 96 * b : 96 * b + 96]
    q_row = row_sum(qb_s[:, 0, :])
    v_row = vb_s[...]
    for i in range(2):
        vg[2 * r + i, 0:1, 0:96] = q_row[:, 96 * i : 96 * i + 96]
        vg[2 * r + i, 1:2, 0:96] = v_row[:, 96 * i : 96 * i + 96]
    inner_row = row_sum(beg[:, 0, :])
    for i in range(3):
        vg[r, 8 + i : 9 + i, :] = inner_row[:, 128 * i : 128 * i + 128]
        vg[4 + r, 8 + i : 9 + i, :] = inner_row[:, 384 + 128 * i : 512 + 128 * i]
    k_v = recvs(8)
    for d in range(1, 8):
        other = (ctx + d) % 8
        send(vg.at[other], vr.at[d], k_v + d, (other, seq))

    k_fs, k_re = recvs(4), recvs(1)
    arrived(rs_y, k_gs_y)
    fsb[...] = (gs[y, c].astype(F32) + rs_c[y].astype(F32) + rs_y[...].astype(F32)).astype(BF)
    for k in range(4):
        send_or_keep(fsb.at[k], fs.at[zh, x], k_fs + 2 * zh + x, dev(c, y, k, zl))
    arrived(re_y, k_ge_y)
    te_f[...] = ge[at_own, :].astype(F32) + re_c[y].astype(F32) + re_y[...].astype(F32)
    te_b[...] = te_f[:, pl.ds(pl.multiple_of(384 * (1 - zh), 128), 384)].astype(BF)
    send(te_b, re_z, k_re, z_mate)

    k_gi_y = recvs(1)
    for half in range(2):
        arrived(ri_c.at[half], k_gi + half)
    tib[...] = (gi[:, at_y, :].astype(F32) + ri_c[1 - y].astype(F32)).astype(BF)
    send(tib, ri_y, k_gi_y, y_mate)

    arrived(ro_c, k_go)
    tob[...] = (go[c].astype(F32) + ro_c[...].astype(F32)).astype(BF)
    k_go_y, k_fo = recvs(1), recvs(2)
    s_go, s_fo = sends(1), sends(4)
    stays = y == zl

    @pl.when(jnp.logical_not(stays))
    def _():
        copy_to(tob, ro_y, s_go, k_go_y, y_mate).start()

    @pl.when(stays)
    def _():
        arrived(ro_y, k_go_y)
        tob2[...] = (tob[...].astype(F32) + ro_y[...].astype(F32)).astype(BF)
        for k in range(4):
            to = dev(c, y, k, x)
            away = jnp.logical_or(to[0] != ctx, to[1] != seq)

            @pl.when(away)
            def _():
                copy_to(tob2.at[k], fo.at[zh], s_fo + k, k_fo + zh, to).start()

            @pl.when(jnp.logical_not(away))
            def _():
                pltpu.make_async_copy(tob2.at[k], fo.at[zh], rsem.at[k_fo + zh]).start()

    def finish_out():
        @pl.when(jnp.logical_not(stays))
        def _():
            copy_to(tob, ro_y, s_go, k_go_y, y_mate).wait_send()

        @pl.when(stays)
        def _():
            for k in range(4):
                to = dev(c, y, k, x)

                @pl.when(jnp.logical_or(to[0] != ctx, to[1] != seq))
                def _():
                    copy_to(tob2.at[k], fo.at[zh], s_fo + k, k_fo + zh, to).wait_send()

    pending.append(finish_out)

    grad_in = d1_s[...] + input_part(r)
    for j in range(1, 4):
        arrived(rs3.at[j], k_r3 + j)
        grad_in += rs3[j].astype(F32)
    ghb[...] = grad_in.astype(BF)
    k_gh = recvs(1)
    send_or_keep(ghb, ghr, k_gh, home)

    arrived(ri_y, k_gi_y)
    ti2[...] = (gi[:, at_own, :].astype(F32) + ri_c[y].astype(F32) + ri_y[...].astype(F32)).astype(BF)
    k_fi = recvs(6)
    for slot in range(6):
        unit = 8 * (slot // 2) + 2 * r + slot % 2
        send_or_keep(
            ti2.at[slot], fi.at[zh, unit % 3], k_fi + 3 * zh + unit % 3, (unit // 3, seq)
        )

    total = vg[ctx]
    for d in range(1, 8):
        arrived(vr.at[d], k_v + d)
        total += vr[d]
    vs1[...] = total
    k_vc = recvs(2)
    send(vs1, vc, k_vc, core_mate)
    arrived(vc, k_vc)
    vs2[...] = vs1[...] + vc[...]
    send(vs2, vy, k_vc + 1, y_mate)

    arrived(ohr, k_o)
    o_out[...] = ohr[...]
    for half in range(2):
        for sub in range(2):
            arrived(fs.at[half, sub], k_fs + 2 * half + sub)
    for sub in range(2):
        o_wshr[384 * sub : 384 * sub + 384, :] = fs[0, sub].astype(F32) + fs[1, sub].astype(F32)
    arrived(re_z, k_re)
    o_wexp[...] = te_f[:, pl.ds(pl.multiple_of(384 * zh, 128), 384)] + re_z[...].astype(F32)
    for half in range(2):
        arrived(fo.at[half], k_fo + half)
    o_wout[...] = fo[0].astype(F32) + fo[1].astype(F32)
    arrived(vy, k_vc + 1)
    total = vs2[...] + vy[...]
    o_gb[...] = total[0:6, 0:96]
    o_gg[...] = total[6:8, 0:96]
    o_ge[...] = total[8:11, :]
    for half in range(2):
        for j in range(3):
            arrived(fi.at[half, j], k_fi + 3 * half + j)
    o_win[...] = jnp.concatenate(
        [fi[0, j].astype(F32) + fi[1, j].astype(F32) for j in range(3)], axis=1
    )
    arrived(ghr, k_gh)
    o_gh[...] = ghr[...]
    for finish in pending:
        finish()


def fast_shards(
    hidden, project_in, project_out, expand_weight, shrink_weight, biases, gains, expand_bias,
    random_blocks, global_blocks, document_lengths, cotangent,
):
    vm = lambda *dims: pltpu.VMEM(dims, BF)
    vf = lambda *dims: pltpu.VMEM(dims, F32)
    scratch = [
        vm(3, 192, 96), vm(4, 128, 768), vm(128, 768), vf(8, 128), vf(4, 8, 128), vf(16, 128),
        vf(8, 16, 128), vm(4, 6, 192, 96), vm(4, 8, 192, 96), vm(4, 192, 768), vm(2, 2, 4, 384, 96),
        vm(768, 576), vm(768, 768), vm(768, 768), vf(8, 768),
        vm(4, 128, 192), vm(2, 512, 384), vm(3, 1024, 64), vm(3, 1024, 64), vf(4, 128, 1024),
        vm(3, 4, 128, 1024), vf(4, 128, 192), vm(4, 128, 192), vm(4, 128, 192), vm(4, 128, 768),
        vf(128, 768), vf(128, 768), vf(128, 1), vf(4, 128, 768), vm(4, 128, 768), vf(128, 768),
        vm(4, 128, 768),
        vm(4, 128, 768), vf(128, 768), vm(4, 128, 768), vm(4, 128, 768), vm(4, 128, 768),
        vm(4, 128, 768), vf(4, 1, 768), vf(128, 768), vm(4, 128, 768), vm(4, 128, 192),
        vm(4, 128, 192), vm(3, 4, 128, 1024), vf(2, 512, 384), vm(512, 384), vm(512, 384),
        vm(4, 128, 576), vm(4, 128, 768), vm(4, 128, 768),
        vm(2, 2, 4, 384, 96), vm(2, 4, 384, 96), vm(4, 384, 96), vm(4, 384, 96), vm(4, 384, 96),
        vm(2, 2, 384, 96), vm(768, 768), vm(2, 192, 768), vm(192, 768), vm(192, 768), vf(192, 768),
        vm(192, 384), vm(192, 384),
        vm(2, 4, 192, 96), vm(4, 192, 96), vm(4, 192, 96), vm(4, 192, 96), vm(4, 192, 96),
        vm(2, 192, 96), vm(6, 768, 96), vm(2, 6, 192, 96), vm(6, 192, 96), vm(6, 192, 96),
        vm(6, 192, 96), vm(2, 3, 192, 96),
        vf(8, 16, 128), vf(8, 16, 128), vf(16, 128), vf(16, 128), vf(16, 128), vf(16, 128),
        vf(4, 1, 192), vf(1, 192), vm(128, 768), vm(128, 768), vm(128, 768), vm(128, 768),
        pltpu.SemaphoreType.DMA((SENDS,)), pltpu.SemaphoreType.DMA((RECVS,)),
    ]
    out = lambda kind, *dims: jax.ShapeDtypeStruct(dims, kind)
    results = pl.pallas_call(
        layer_kernel,
        out_shape=(
            out(BF, 128, 768), out(BF, 128, 768), out(F32, 192, 288), out(F32, 192, 96),
            out(F32, 192, 384), out(F32, 768, 96), out(F32, 6, 96), out(F32, 2, 96), out(F32, 3, 128),
        ),
        in_specs=[pl.BlockSpec(memory_space=pltpu.SMEM)] * 3
        + [pl.BlockSpec(memory_space=pltpu.VMEM)] * 9,
        out_specs=tuple([pl.BlockSpec(memory_space=pltpu.VMEM)] * 9),
        scratch_shapes=scratch,
        compiler_params=pltpu.CompilerParams(
            collective_id=0, has_side_effects=True, vmem_limit_bytes=62 * 1024 * 1024
        ),
    )(
        random_blocks[0], global_blocks, document_lengths, hidden[0], cotangent[0], project_in,
        project_out, expand_weight, shrink_weight.reshape(2, 384, 96), biases, gains,
        expand_bias.reshape(3, 128),
    )
    return (
        results[0][None], results[1][None], results[2], results[3], results[4], results[5],
        results[6], results[7], results[8].reshape(-1),
    )


def solution(mesh):
    small = tuple(mesh.shape[name] for name in ("ctx", "fsdp")) == (8, 4)
    return jax.shard_map(
        fast_shards if small else shards,
        mesh=mesh,
        in_specs=(
            P("fsdp", "ctx", None),
            P("fsdp", "ctx"),
            P("fsdp", "ctx"),
            P("fsdp", "ctx"),
            P("fsdp", "ctx"),
            P(None, "ctx"),
            P(None, "ctx"),
            P("ctx"),
            P("fsdp", "ctx", None),
            P("fsdp", None),
            P("fsdp", None),
            P("fsdp", "ctx", None),
        ),
        out_specs=(
            P("fsdp", "ctx", None),
            P("fsdp", "ctx", None),
            P("fsdp", "ctx"),
            P("fsdp", "ctx"),
            P("fsdp", "ctx"),
            P("fsdp", "ctx"),
            P(None, "ctx"),
            P(None, "ctx"),
            P("ctx"),
        ),
        check_vma=False,
    )
```

```python
import jax
import jax.numpy as jnp
from jax import lax
from jax.experimental import pallas as pl
from jax.experimental.pallas import tpu as pltpu
from jax.sharding import PartitionSpec as P

HEAD_DIM = 64
BLOCK = 64


def segment_of(positions, bounds):
    return jnp.sum((positions[..., None] >= bounds).astype(jnp.int32), axis=-1)


def layer_norm_parts(values, gain_row, shift_row):
    centre = values - jnp.mean(values, axis=-1, keepdims=True)
    inverse = lax.rsqrt(jnp.mean(centre * centre, axis=-1, keepdims=True) + 1e-05)
    normed = centre * inverse
    return (normed * gain_row + shift_row, normed, inverse)


def layer_norm_back(upstream, normed, inverse, gain_row):
    scaled = upstream * gain_row
    return inverse * (
        scaled
        - jnp.mean(scaled, axis=-1, keepdims=True)
        - normed * jnp.mean(scaled * normed, axis=-1, keepdims=True)
    )


def matmul(left_side, right_side):
    return jnp.dot(left_side, right_side, preferred_element_type=jnp.float32)


def matmul_left_t(left_side, right_side):
    return lax.dot_general(
        left_side, right_side, (((0,), (0,)), ((), ())), preferred_element_type=jnp.float32
    )


def matmul_right_t(left_side, right_side):
    return lax.dot_general(
        left_side, right_side, (((1,), (1,)), ((), ())), preferred_element_type=jnp.float32
    )


def over_cols(qkv_grad, out_grad, expand_grad, shrink_grad, vector_grad, gain_grad, inner_grad):
    return (
        lax.psum_scatter(qkv_grad, "ctx", scatter_dimension=1, tiled=True),
        lax.psum_scatter(out_grad, "ctx", scatter_dimension=1, tiled=True),
        lax.psum_scatter(expand_grad, "ctx", scatter_dimension=1, tiled=True),
        lax.psum_scatter(shrink_grad, "ctx", scatter_dimension=1, tiled=True),
        lax.psum_scatter(vector_grad, "ctx", scatter_dimension=1, tiled=True),
        lax.psum_scatter(gain_grad, "ctx", scatter_dimension=1, tiled=True),
        lax.psum_scatter(inner_grad, "ctx", scatter_dimension=1, tiled=True),
    )


def over_rows(qkv_grad, out_grad, expand_grad, shrink_grad):
    return (
        lax.psum_scatter(
            qkv_grad.astype(jnp.bfloat16), "fsdp", scatter_dimension=0, tiled=True
        ).astype(jnp.float32),
        lax.psum_scatter(
            out_grad.astype(jnp.bfloat16), "fsdp", scatter_dimension=0, tiled=True
        ).astype(jnp.float32),
        lax.psum_scatter(
            expand_grad.astype(jnp.bfloat16), "fsdp", scatter_dimension=0, tiled=True
        ).astype(jnp.float32),
        lax.psum_scatter(
            shrink_grad.astype(jnp.bfloat16), "fsdp", scatter_dimension=0, tiled=True
        ).astype(jnp.float32),
    )


def scatter_rows(link_ids, link_grads, row_count, feature_width):
    block_count = row_count // BLOCK
    inside = (link_ids >= 0) & (link_ids < block_count)
    target = jnp.where(inside, link_ids, block_count).reshape(-1)
    partial_value = jnp.zeros((block_count, BLOCK, feature_width), jnp.float32)
    partial_value = partial_value.at[target].add(
        link_grads.reshape(-1, BLOCK, feature_width), mode="drop"
    )
    return partial_value.reshape(row_count, feature_width)


def shards(
    hidden,
    project_in,
    project_out,
    expand_weight,
    shrink_weight,
    biases,
    gains,
    expand_bias,
    random_blocks,
    global_blocks,
    document_lengths,
    cotangent,
):
    inputs = hidden[0]
    tokens_here = inputs.shape[0]
    width = inputs.shape[1]
    head_count = width // HEAD_DIM
    blocks_here = tokens_here // BLOCK
    rand_count = random_blocks.shape[2]
    link_count = 3 + rand_count + global_blocks.shape[1]
    ctx_rank = lax.axis_index("ctx")
    last_block = tokens_here * lax.axis_size("ctx") // BLOCK - 1
    col_full = (
        lax.all_gather(project_in, "ctx", axis=1, tiled=True),
        lax.all_gather(project_out, "ctx", axis=1, tiled=True),
        lax.all_gather(expand_weight, "ctx", axis=1, tiled=True),
        lax.all_gather(shrink_weight, "ctx", axis=1, tiled=True),
        lax.all_gather(biases, "ctx", axis=1, tiled=True),
        lax.all_gather(gains, "ctx", axis=1, tiled=True),
        lax.all_gather(expand_bias.reshape(1, -1), "ctx", axis=1, tiled=True),
    )
    full_qkv, full_out, full_expand, full_shrink = (
        lax.all_gather(col_full[0], "fsdp", axis=0, tiled=True),
        lax.all_gather(col_full[1], "fsdp", axis=0, tiled=True),
        lax.all_gather(col_full[2], "fsdp", axis=0, tiled=True),
        lax.all_gather(col_full[3], "fsdp", axis=0, tiled=True),
    )
    vectors = col_full[4].astype(jnp.float32)
    gain_rows = col_full[5].astype(jnp.float32)
    inner_bias = col_full[6][0].astype(jnp.float32)
    block_ids = ctx_rank * blocks_here + jnp.arange(blocks_here, dtype=jnp.int32)
    window = jnp.stack(
        [jnp.maximum(block_ids - 1, 0), block_ids, jnp.minimum(block_ids + 1, last_block)], axis=1
    )
    global_links = jnp.broadcast_to(
        global_blocks[0][None, :], (blocks_here, global_blocks.shape[1])
    )
    linked_ids = jnp.concatenate([window, random_blocks[0], global_links], axis=1)
    lengths = document_lengths[0]
    doc_order = jnp.arange(lengths.shape[0], dtype=jnp.int32)
    bounds = jnp.sum(
        jnp.where(doc_order[None, :] <= doc_order[:-1, None], lengths[None, :], 0), axis=1
    )
    query_pos = (ctx_rank * tokens_here + jnp.arange(tokens_here, dtype=jnp.int32)).reshape(
        blocks_here, BLOCK
    )
    query_seg = segment_of(query_pos, bounds)
    key_pos = linked_ids[:, :, None] * BLOCK + jnp.arange(BLOCK, dtype=jnp.int32)[None, None, :]
    key_seg = segment_of(key_pos, bounds).reshape(blocks_here, -1)
    allowed = query_seg[:, None, :, None] == key_seg[:, None, None, :]
    zero_row = jnp.zeros((width,), jnp.float32)
    mixed_qkv = (
        matmul(inputs, full_qkv) + jnp.concatenate([vectors[0], zero_row, vectors[1]])
    ).astype(jnp.bfloat16)
    queries = mixed_qkv[:, :width]
    keyvals = mixed_qkv[:, width:]
    shard_piece = lax.all_gather(keyvals, "ctx", axis=0, tiled=True)
    block_count = shard_piece.shape[0] // BLOCK
    stacked = shard_piece.reshape(block_count, BLOCK, shard_piece.shape[1])
    picks = (
        linked_ids.reshape(-1)[:, None] == jnp.arange(block_count, dtype=jnp.int32)[None, :]
    ).astype(jnp.bfloat16)
    linked = jnp.einsum("lb,bkd->lkd", picks, stacked).reshape(
        blocks_here, link_count, BLOCK, 2 * width
    )
    query_heads = queries.reshape(blocks_here, BLOCK, head_count, HEAD_DIM)
    key_heads = linked[..., :width].reshape(blocks_here, link_count * BLOCK, head_count, HEAD_DIM)
    value_heads = linked[..., width:].reshape(blocks_here, link_count * BLOCK, head_count, HEAD_DIM)

    def score_parts():
        raw_scores = (
            jnp.einsum(
                "bqhd,bkhd->bhqk", query_heads, key_heads, preferred_element_type=jnp.float32
            )
            * 0.125
        )
        return jnp.where(allowed, raw_scores, -1e30)

    scores = score_parts()
    top_score = jnp.max(scores, axis=-1, keepdims=True)
    exp_total = jnp.sum(jnp.exp(scores - top_score), axis=-1, keepdims=True)
    attention = jnp.exp(scores - top_score) / exp_total
    attended = jnp.einsum(
        "bhqk,bkhd->bqhd",
        attention.astype(jnp.bfloat16),
        value_heads,
        preferred_element_type=jnp.float32,
    )
    attended = attended.reshape(tokens_here, width).astype(jnp.bfloat16)
    residual_one = inputs.astype(jnp.float32) + matmul(attended, full_out) + vectors[2]
    hidden_one, normed_one, inverse_one = layer_norm_parts(residual_one, gain_rows[0], vectors[3])
    hidden_low = hidden_one.astype(jnp.bfloat16)
    inner_pre = matmul(hidden_low, full_expand) + inner_bias
    activated, gelu_pull = jax.vjp(
        lambda argument: jax.nn.gelu(argument, approximate=False), inner_pre
    )
    active_low = activated.astype(jnp.bfloat16)
    residual_two = hidden_one + matmul(active_low, full_shrink) + vectors[4]
    result, normed_two, inverse_two = layer_norm_parts(residual_two, gain_rows[1], vectors[5])
    upstream = cotangent[0].astype(jnp.float32)
    grad_gain_two = jnp.sum(upstream * normed_two, axis=0)
    grad_shift_two = jnp.sum(upstream, axis=0)
    grad_two = layer_norm_back(upstream, normed_two, inverse_two, gain_rows[1])
    grad_bias_back = jnp.sum(grad_two, axis=0)
    grad_two_low = grad_two.astype(jnp.bfloat16)
    again_cols = (
        lax.all_gather(project_in, "ctx", axis=1, tiled=True),
        lax.all_gather(project_out, "ctx", axis=1, tiled=True),
        lax.all_gather(expand_weight, "ctx", axis=1, tiled=True),
        lax.all_gather(shrink_weight, "ctx", axis=1, tiled=True),
    )
    back_weights = (
        lax.all_gather(again_cols[0], "fsdp", axis=0, tiled=True),
        lax.all_gather(again_cols[1], "fsdp", axis=0, tiled=True),
        lax.all_gather(again_cols[2], "fsdp", axis=0, tiled=True),
        lax.all_gather(again_cols[3], "fsdp", axis=0, tiled=True),
    )
    back_qkv, back_out, back_expand, back_shrink = back_weights
    grad_shrink_w = matmul_left_t(active_low, grad_two_low)
    grad_active = matmul_right_t(grad_two_low, back_shrink)
    grad_inner = gelu_pull(grad_active)[0]
    grad_inner_bias = jnp.sum(grad_inner, axis=0)
    grad_inner_low = grad_inner.astype(jnp.bfloat16)
    grad_expand_w = matmul_left_t(hidden_low, grad_inner_low)
    grad_hidden_one = grad_two + matmul_right_t(grad_inner_low, back_expand)
    grad_gain_one = jnp.sum(grad_hidden_one * normed_one, axis=0)
    grad_shift_one = jnp.sum(grad_hidden_one, axis=0)
    grad_one = layer_norm_back(grad_hidden_one, normed_one, inverse_one, gain_rows[0])
    grad_bias_out = jnp.sum(grad_one, axis=0)
    grad_one_low = grad_one.astype(jnp.bfloat16)
    grad_out_w = matmul_left_t(attended, grad_one_low)
    grad_attended = matmul_right_t(grad_one_low, back_out).astype(jnp.bfloat16)
    grad_attended = grad_attended.reshape(blocks_here, BLOCK, head_count, HEAD_DIM)
    scores = score_parts()
    attention = jnp.exp(scores - top_score) / exp_total
    grad_attention = jnp.einsum(
        "bqhd,bkhd->bhqk", grad_attended, value_heads, preferred_element_type=jnp.float32
    )
    grad_values = jnp.einsum(
        "bhqk,bqhd->bkhd",
        attention.astype(jnp.bfloat16),
        grad_attended,
        preferred_element_type=jnp.float32,
    )
    row_inner = jnp.sum(attention * grad_attention, axis=-1, keepdims=True)
    grad_scores = (attention * (grad_attention - row_inner) * 0.125).astype(jnp.bfloat16)
    grad_queries = jnp.einsum(
        "bhqk,bkhd->bqhd", grad_scores, key_heads, preferred_element_type=jnp.float32
    ).reshape(tokens_here, width)
    grad_keys = jnp.einsum(
        "bhqk,bqhd->bkhd", grad_scores, query_heads, preferred_element_type=jnp.float32
    )
    slot_grads = jnp.concatenate(
        [
            grad_keys.reshape(blocks_here, link_count, BLOCK, width),
            grad_values.reshape(blocks_here, link_count, BLOCK, width),
        ],
        axis=-1,
    )
    grad_keyvals = lax.psum_scatter(
        scatter_rows(linked_ids, slot_grads, tokens_here * lax.axis_size("ctx"), 2 * width),
        "ctx",
        scatter_dimension=0,
        tiled=True,
    )
    grad_mixed = jnp.concatenate([grad_queries, grad_keyvals], axis=1)
    grad_bias_query = jnp.sum(grad_queries, axis=0)
    grad_bias_value = jnp.sum(grad_keyvals[:, width:], axis=0)
    grad_mixed_low = grad_mixed.astype(jnp.bfloat16)
    grad_qkv_w = matmul_left_t(inputs, grad_mixed_low)
    grad_inputs = grad_one + matmul_right_t(grad_mixed_low, back_qkv)
    grad_vectors = jnp.stack(
        [
            grad_bias_query,
            grad_bias_value,
            grad_bias_out,
            grad_shift_one,
            grad_bias_back,
            grad_shift_two,
        ]
    )
    grad_gain_rows = jnp.stack([grad_gain_one, grad_gain_two])
    grad_inner_row = grad_inner_bias[None, :]
    reduced = over_cols(
        grad_qkv_w,
        grad_out_w,
        grad_expand_w,
        grad_shrink_w,
        grad_vectors,
        grad_gain_rows,
        grad_inner_row,
    )
    sum_qkv, sum_out, sum_expand, sum_shrink = over_rows(
        reduced[0], reduced[1], reduced[2], reduced[3]
    )
    final_vectors, final_gains, final_inner = lax.psum((reduced[4], reduced[5], reduced[6]), "fsdp")
    return (
        result.astype(jnp.bfloat16)[None],
        grad_inputs.astype(jnp.bfloat16)[None],
        sum_qkv,
        sum_out,
        sum_expand,
        sum_shrink,
        final_vectors,
        final_gains,
        final_inner.reshape(-1),
    )


MESH = pl.DeviceIdType.MESH
BF = jnp.bfloat16
F32 = jnp.float32
SENDS = 128
RECVS = 128
LOCALS = 16
NEG = -1e30


def dot_nn(a, b):
    return jnp.dot(a, b, preferred_element_type=F32)


def dot_nt(a, b):
    return lax.dot_general(a, b, (((1,), (1,)), ((), ())), preferred_element_type=F32)


def dot_tn(a, b):
    return lax.dot_general(a, b, (((0,), (0,)), ((), ())), preferred_element_type=F32)


def row_sum(values):
    return jnp.sum(values, axis=0, keepdims=True)


def pack(piece):
    return jnp.concatenate([piece[48 * q : 48 * q + 48] for q in range(4)], axis=1)


def layer_kernel(
    rand_ref, glob_ref, doc_ref, bia, gai, ebi, hid, cot, win, wout, wexp, wshr,
    o_out, o_gh, o_win, o_wout, o_wexp, o_wshr, o_gb, o_gg, o_ge,
    winv, woutv, win3, wout1, xg, eo, ms, mg, ps, par, win_p, wout_p, wexp_f, ws, w_in, w_out, prm,
    mq, q_s, kv, kh, vh, e_s, l_s, a_f, a_b, a_all, hg, h1_s, n1_s, r1_s, dge, g_s, ysum, yb,
    rs1, d2_s, dg, du_s, dh_b, rs2, beg, d1_s, d1g, dab, da, de, ds_s, dkv, dkb, dkr, dz, dx_b, rs3,
    gs, rs_c, t_shr, rs_y, fsb, fs, ge, re_c, t_exp, re_y, te_f, te_b, re_z,
    go, ro_c, tob, ro_y, tob2, fo, gi, ri_c, tib, ri_y, ti2, fi,
    vg, vr, vs1, vc, vs2, vy, qb_s, vb_s, ob, ohr, ghb, ghr,
    f_win, f_wout, f_wexp, f_wshr, f_gb, f_gg, f_ge,
    ssem, rsem, lsem,
):
    ctx = lax.axis_index("ctx")
    seq = lax.axis_index("fsdp")
    z, x = ctx // 2, ctx % 2
    y, c = seq // 2, seq % 2
    zh, zl = z // 2, z % 2
    r = 2 * zl + x
    f = seq

    def dev(px, py, pz, pc):
        return (2 * pz + px, 2 * py + pc)

    def flip(v, on):
        return v + on - 2 * v * on

    def peer(j):
        return dev(flip(x, j % 2), y, 2 * zh + flip(zl, j // 2), c)

    def peer_rank(j):
        return 2 * flip(zl, j // 2) + flip(x, j % 2)

    core_mate = dev(x, y, z, 1 - c)
    y_mate = dev(x, 1 - y, z, c)
    z_mate = dev(x, y, 2 * (1 - zh) + zl, c)
    home = dev(x, y, 2 * c + zl, zh)

    pending = []
    counts = {"s": 0, "r": 0, "l": 0}

    def take(kind, n, most):
        first = counts[kind]
        counts[kind] = first + n
        assert counts[kind] <= most
        return first

    def recvs(n):
        return take("r", n, RECVS)

    def sends(n):
        return take("s", n, SENDS)

    def local(src, dst):
        cp = pltpu.make_async_copy(src, dst, lsem.at[take("l", 1, LOCALS)])
        cp.start()
        return cp

    def copy_to(src, dst, si, ri, to):
        return pltpu.make_async_remote_copy(
            src_ref=src, dst_ref=dst, send_sem=ssem.at[si], recv_sem=rsem.at[ri],
            device_id=to, device_id_type=MESH,
        )

    def send(src, dst, ri, to):
        cp = copy_to(src, dst, sends(1), ri, to)
        cp.start()
        pending.append(cp.wait_send)

    def send_or_keep(src, dst, ri, to):
        si = sends(1)
        away = jnp.logical_or(to[0] != ctx, to[1] != seq)

        @pl.when(away)
        def _():
            copy_to(src, dst, si, ri, to).start()

        @pl.when(jnp.logical_not(away))
        def _():
            pltpu.make_async_copy(src, dst, rsem.at[ri]).start()

        def finish():
            @pl.when(away)
            def _():
                copy_to(src, dst, si, ri, to).wait_send()

        pending.append(finish)

    def arrived(dst, ri):
        pltpu.make_async_copy(dst, dst, rsem.at[ri]).wait()

    barrier = pltpu.get_barrier_semaphore()
    place = 2 * ctx + c
    for d in range(1, 16):
        other = (place + d) % 16
        pl.semaphore_signal(
            barrier, inc=1, device_id=(other // 2, 2 * y + other % 2), device_id_type=MESH
        )
    pl.semaphore_signal(barrier, inc=1, device_id=y_mate, device_id_type=MESH)
    in_win, in_wout = local(win, winv), local(wout, woutv)

    lane = lax.broadcasted_iota(jnp.int32, (1, 128), 1)
    for i in range(2):
        block = 2 * ctx + i
        links = [jnp.maximum(block - 1, 0), block, jnp.minimum(block + 1, 15)]
        links += [rand_ref[i, k] for k in range(3)] + [glob_ref[0, k] for k in range(2)]
        count = jnp.zeros((1, 128), F32)
        for link in links:
            count += jnp.where(jnp.logical_or(lane == link + 72, lane == link + 88), 1.0, 0.0)
        ms[i : i + 1, :] = count
    edge = doc_ref[0, 0]
    edges = jnp.zeros((1, 128), F32)
    for k in range(7):
        edges += jnp.where(lane == k, edge.astype(F32), 0.0)
        edge = edge + doc_ref[0, k + 1]
    ms[2:3, :] = edges
    ms[3:8, :] = jnp.zeros((5, 128), F32)
    ps[...] = jnp.zeros((16, 128), F32)
    ps[0:6, 0:96] = bia[...].astype(F32)
    ps[6:8, 0:96] = gai[...].astype(F32)
    ps[8:11, :] = ebi[...].astype(F32)
    in_win.wait()
    for j in range(3):
        win3[j] = pack(winv[:, 96 * j : 96 * j + 96])

    pl.semaphore_wait(barrier, 16)

    k_x, k_m, k_e = recvs(4), recvs(4), recvs(1)
    send_or_keep(hid, xg.at[r], k_x, home)
    send_or_keep(ms, mg.at[r], k_m, home)
    k_win = recvs(6)
    for j in range(3):
        unit = 3 * ctx + j
        rank = (unit % 8) // 2
        slot = 2 * (unit // 8) + unit % 2
        for half in range(2):
            send_or_keep(
                win3.at[j], win_p.at[f, slot], k_win + slot, dev(rank % 2, y, 2 * half + rank // 2, c)
            )
    k_par = recvs(8)
    for d in range(1, 8):
        other = (ctx + d) % 8
        send(ps, par.at[ctx], k_par + d, (other, seq))
    par[ctx] = ps[...]
    in_wout.wait()
    wout1[...] = pack(woutv[...])

    arrived(xg.at[r], k_x)
    arrived(mg.at[r], k_m)
    for j in range(1, 4):
        send(xg.at[r], xg.at[r], k_x + j, peer(j))
        send(mg.at[r], mg.at[r], k_m + j, peer(j))

    k_win_y, k_win_c = recvs(1), recvs(2)
    for slot in range(6):
        arrived(win_p.at[f, slot], k_win + slot)
    send(win_p.at[f], win_p.at[f], k_win_y, y_mate)
    send(win_p.at[f], win_p.at[f], k_win_c, core_mate)
    k_wout = recvs(8)
    for d in range(8):
        other = (ctx + d) % 8
        if d == 0:
            pltpu.make_async_copy(wout1, wout_p.at[f, ctx], rsem.at[k_wout]).start()
        else:
            send(wout1, wout_p.at[f, ctx], k_wout + d, (other, seq))

    for d in range(1, 8):
        arrived(par.at[(ctx + 8 - d) % 8], k_par + d)
    prm[...] = jnp.concatenate([par[b, 0:8, 0:96] for b in range(8)], axis=1)
    be = jnp.concatenate(
        [par[r, 8 + i : 9 + i, :] for i in range(3)] + [par[4 + r, 8 + i : 9 + i, :] for i in range(3)],
        axis=1,
    )
    zrow = jnp.zeros((1, 192), F32)
    z_bias = jnp.concatenate(
        [par[2 * r, 0:1, 0:96], par[2 * r + 1, 0:1, 0:96], zrow, par[2 * r, 1:2, 0:96], par[2 * r + 1, 1:2, 0:96]],
        axis=1,
    )

    def sided(positions, rows):
        segs = jnp.zeros((rows, 1), F32)
        for k in range(7):
            segs += jnp.where(positions >= mg[r, 2:3, k : k + 1], 1.0, 0.0)
        return segs

    wide = lax.broadcasted_iota(jnp.int32, (1024, 128), 1)
    key_row = lax.broadcasted_iota(jnp.int32, (1024, 1), 0)
    key_segs = sided(key_row.astype(F32), 1024).astype(jnp.int32) + 64
    hot = jnp.logical_or(
        jnp.logical_and(wide < 72, wide == key_segs),
        jnp.logical_and(
            wide >= 72,
            jnp.logical_or(wide == key_row // 64 + 72, wide == key_row // 64 + 88),
        ),
    )
    hot = jnp.where(hot, 1.0, 0.0).astype(BF)
    ones = jnp.where(jnp.logical_or(wide == 64, wide == 65), 1.0, 0.0).astype(BF)
    for h in range(3):
        kh[h, :, 64:128] = hot[:, 64:128]
        vh[h, :, 64:128] = ones[:, 64:128]
    row_pos = lax.broadcasted_iota(jnp.int32, (512, 1), 0) + 512 * c
    row_segs = sided(row_pos.astype(F32), 512).astype(jnp.int32) + 64
    for j in range(1, 4):
        arrived(mg.at[peer_rank(j)], k_m + j)
    for i in range(8):
        count = mg[i // 2, i % 2 : i % 2 + 1, :]
        logs = jnp.log(jnp.maximum(count, 1.0))
        high = logs.astype(BF).astype(F32)
        line = jnp.where(lane < 88, jnp.where(count > 0.5, high, NEG), logs - high)
        line = jnp.where(lane < 104, line, 0.0)
        same = row_segs[64 * i : 64 * i + 64] == wide[0:64]
        block = jnp.where(wide[0:64] < 72, jnp.where(same, 0.0, NEG), line)
        mq[i // 2, 64 * (i % 2) : 64 * (i % 2) + 64, :] = block.astype(BF)
    for h in range(3):
        q_s[:, h, :, 64:128] = mq[:, :, 64:128]

    f_y = 2 * (1 - y) + c
    arrived(win_p.at[f_y], k_win_y)
    send(win_p.at[f_y], win_p.at[f_y], k_win_c + 1, core_mate)

    def place_in(k):
        for q in range(4):
            w_in[pl.ds(pl.multiple_of(192 * k + 48 * q, 16), 48), :] = jnp.concatenate(
                [win_p[k, i, :, 96 * q : 96 * q + 96] for i in range(6)], axis=1
            )

    place_in(f)
    place_in(f_y)
    arrived(win_p.at[2 * y + 1 - c], k_win_c)
    place_in(2 * y + 1 - c)
    arrived(win_p.at[2 * (1 - y) + 1 - c], k_win_c + 1)
    place_in(2 * (1 - y) + 1 - c)

    def project(k):
        mixed = dot_nn(xg[k], w_in[...]) + z_bias
        queries = (mixed[:, 0:192].astype(BF).astype(F32) * 0.125).astype(BF)
        for h in range(3):
            q_s[k, h, :, 0:64] = queries[:, 64 * h : 64 * h + 64]
        kv[c, pl.ds(pl.multiple_of(128 * k, 128), 128), :] = mixed[:, 192:576].astype(BF)

    project(r)

    def project_step(j, carry):
        rank = peer_rank(j)
        arrived(xg.at[rank], k_x + j)
        project(rank)
        return carry

    lax.fori_loop(1, 4, project_step, 0)
    k_kv = recvs(1)
    send(kv.at[c], kv.at[c], k_kv, core_mate)

    k_wexp = recvs(2)
    mine_exp = wexp_f.at[f, :, pl.ds(pl.multiple_of(384 * zh, 128), 384)]
    pltpu.make_async_copy(wexp, mine_exp, rsem.at[k_wexp]).start()
    send(wexp, mine_exp, k_wexp + 1, z_mate)
    k_wshr = recvs(4)
    at_half = pl.ds(pl.multiple_of(384 * y, 128), 384)
    for sub in range(2):
        for half in range(2):
            send_or_keep(
                wshr.at[:, 384 * sub : 384 * sub + 384], ws.at[2 * zh + zl, x, :, at_half],
                k_wshr + 2 * zh + zl, dev(sub, y, 2 * half + c, x),
            )
    k_wout_y, k_wout_c = recvs(1), recvs(2)
    k_wexp_y, k_wexp_c = recvs(1), recvs(2)
    k_wshr_y, k_wshr_c = recvs(1), recvs(2)
    for d in range(8):
        arrived(wout_p.at[f, (ctx + 8 - d) % 8], k_wout + d)
    send(wout_p.at[f], wout_p.at[f], k_wout_y, y_mate)
    send(wout_p.at[f], wout_p.at[f], k_wout_c, core_mate)

    def split_heads(half):
        at = pl.ds(pl.multiple_of(512 * half, 512), 512)
        for h in range(3):
            kh[h, at, 0:64] = kv[half, :, 64 * h : 64 * h + 64]
            vh[h, at, 0:64] = kv[half, :, 192 + 64 * h : 256 + 64 * h]

    split_heads(c)
    arrived(kv.at[1 - c], k_kv)
    split_heads(1 - c)

    def attend(k, carry):
        outs = []
        for h in range(3):
            scores = dot_nt(q_s[k, h], kh[h])
            top = jnp.max(scores, axis=1, keepdims=True)
            exps = jnp.exp(scores - top).astype(BF)
            e_s[h, k] = exps
            sums = dot_nn(exps, vh[h])
            scale = 1.0 / sums[:, 64:65]
            l_s[h, k] = scale
            outs.append(sums[:, 0:64] * scale)
        both = jnp.concatenate(outs, axis=1)
        a_f[k] = both
        a_b[k] = both.astype(BF)
        return carry

    lax.fori_loop(0, 1, attend, 0)
    arrived(wout_p.at[f_y], k_wout_y)
    send(wout_p.at[f_y], wout_p.at[f_y], k_wout_c + 1, core_mate)
    lax.fori_loop(1, 2, attend, 0)
    arrived(mine_exp, k_wexp)
    arrived(wexp_f.at[f, :, pl.ds(pl.multiple_of(384 * (1 - zh), 128), 384)], k_wexp + 1)
    send(wexp_f.at[f], wexp_f.at[f], k_wexp_y, y_mate)
    send(wexp_f.at[f], wexp_f.at[f], k_wexp_c, core_mate)
    lax.fori_loop(2, 3, attend, 0)
    for k in range(4):
        arrived(ws.at[k, c, :, at_half], k_wshr + k)
    send(ws.at[:, c, :, at_half], ws.at[:, c, :, at_half], k_wshr_y, y_mate)
    send(ws.at[:, c, :, at_half], ws.at[:, c, :, at_half], k_wshr_c, core_mate)
    lax.fori_loop(3, 4, attend, 0)

    k_a = recvs(4)
    for j in range(1, 4):
        send(a_b.at[peer_rank(j)], a_all.at[r], k_a + j, peer(j))
    a_all[r] = a_b[r]
    send_or_keep(cot, eo, k_e, home)

    def place_out(k):
        for q in range(4):
            w_out[pl.ds(pl.multiple_of(192 * k + 48 * q, 16), 48), :] = jnp.concatenate(
                [wout_p[k, b, :, 96 * q : 96 * q + 96] for b in range(8)], axis=1
            )

    place_out(f)
    place_out(f_y)
    arrived(wout_p.at[2 * y + 1 - c], k_wout_c)
    place_out(2 * y + 1 - c)
    arrived(wout_p.at[2 * (1 - y) + 1 - c], k_wout_c + 1)
    place_out(2 * (1 - y) + 1 - c)
    arrived(wexp_f.at[f_y], k_wexp_y)
    send(wexp_f.at[f_y], wexp_f.at[f_y], k_wexp_c + 1, core_mate)

    for j in range(1, 4):
        arrived(a_all.at[peer_rank(j)], k_a + j)
    first = xg[r].astype(F32) + prm[2:3, :]
    for k in range(4):
        first += dot_nn(a_all[k], w_out[192 * k : 192 * k + 192, :])
    centre = first - jnp.mean(first, axis=1, keepdims=True)
    inverse = lax.rsqrt(jnp.mean(centre * centre, axis=1, keepdims=True) + 1e-05)
    normed = centre * inverse
    hidden_one = normed * prm[6:7, :] + prm[3:4, :]
    hg[r] = hidden_one.astype(BF)
    k_h = recvs(4)
    for j in range(1, 4):
        send(hg.at[r], hg.at[r], k_h + j, peer(j))
    n1_s[...] = normed
    r1_s[...] = inverse
    h1_s[...] = hidden_one

    other_half = pl.ds(pl.multiple_of(384 * (1 - y), 128), 384)
    arrived(ws.at[:, c, :, other_half], k_wshr_y)
    send(ws.at[:, c, :, other_half], ws.at[:, c, :, other_half], k_wshr_c + 1, core_mate)
    arrived(wexp_f.at[2 * y + 1 - c], k_wexp_c)
    arrived(wexp_f.at[2 * (1 - y) + 1 - c], k_wexp_c + 1)
    arrived(ws.at[:, 1 - c, :, at_half], k_wshr_c)
    arrived(ws.at[:, 1 - c, :, other_half], k_wshr_c + 1)

    def expand(k):
        inner = dot_nn(hg[k], wexp_f[...].reshape(768, 768)) + be
        below = 0.5 * (1.0 + lax.erf(inner * 0.7071067811865476))
        dge[k] = below + inner * jnp.exp(-0.5 * inner * inner) * 0.3989422804014327
        active = (inner * below).astype(BF)
        g_s[k] = active
        return dot_nt(active, ws[...].reshape(768, 768))

    ysum[...] = expand(r)
    k_r1, s_r1 = recvs(4), sends(4)

    def expand_step(j, carry):
        rank = peer_rank(j)
        arrived(hg.at[rank], k_h + j)
        yb[j] = expand(rank).astype(BF)
        copy_to(yb.at[j], rs1.at[j], s_r1 + j, k_r1 + j, peer(j)).start()
        return carry

    lax.fori_loop(1, 4, expand_step, 0)
    for j in range(1, 4):
        pending.append(copy_to(yb.at[j], rs1.at[j], s_r1 + j, k_r1 + j, peer(j)).wait_send)

    arrived(eo, k_e)
    upstream = eo[...].astype(F32)
    scaled = upstream * prm[7:8, :]
    scaled_mean = jnp.mean(scaled, axis=1, keepdims=True)
    row_shift_two = row_sum(upstream)
    second = h1_s[...] + prm[4:5, :] + ysum[...]
    for j in range(1, 4):
        arrived(rs1.at[j], k_r1 + j)
        second += rs1[j].astype(F32)
    centre = second - jnp.mean(second, axis=1, keepdims=True)
    inverse = lax.rsqrt(jnp.mean(centre * centre, axis=1, keepdims=True) + 1e-05)
    normed = centre * inverse
    grad_two = inverse * (
        scaled - scaled_mean - normed * jnp.mean(scaled * normed, axis=1, keepdims=True)
    )
    dg[r] = grad_two.astype(BF)
    k_d = recvs(4)
    for j in range(1, 4):
        send(dg.at[r], dg.at[r], k_d + j, peer(j))
    d2_s[...] = grad_two
    ob[...] = (normed * prm[7:8, :] + prm[5:6, :]).astype(BF)
    k_o = recvs(1)
    send_or_keep(ob, ohr, k_o, home)
    row_gain_two = row_sum(upstream * normed)
    row_back = row_sum(grad_two)

    def contract(k):
        inner = dge[k] * dot_nn(dg[k], ws[...].reshape(768, 768))
        low = inner.astype(BF)
        du_s[k] = low
        beg[k] = row_sum(inner)
        return dot_nt(low, wexp_f[...].reshape(768, 768))

    ysum[...] = contract(r)
    k_r2, s_r2 = recvs(4), sends(4)

    def contract_step(j, carry):
        rank = peer_rank(j)
        arrived(dg.at[rank], k_d + j)
        dh_b[j] = contract(rank).astype(BF)
        copy_to(dh_b.at[j], rs2.at[j], s_r2 + j, k_r2 + j, peer(j)).start()
        return carry

    lax.fori_loop(1, 4, contract_step, 0)
    for j in range(1, 4):
        pending.append(copy_to(dh_b.at[j], rs2.at[j], s_r2 + j, k_r2 + j, peer(j)).wait_send)

    for k in range(4):
        rows = dg[:, :, 192 * k : 192 * k + 192].reshape(512, 192)
        gs[k] = dot_tn(rows, g_s[...].reshape(512, 768)).astype(BF).reshape(2, 96, 768)
    k_gs = recvs(1)
    send(gs.at[:, 1 - c], rs_c, k_gs, core_mate)

    def expand_grad(i, carry):
        at = pl.ds(pl.multiple_of(128 * i, 128), 128)
        rows = hg[:, :, at].reshape(512, 128)
        ge[at, :] = dot_tn(rows, du_s[...].reshape(512, 768)).astype(BF)
        return carry

    lax.fori_loop(0, 6, expand_grad, 0)
    k_ge = recvs(2)
    for half in range(2):
        at = pl.ds(pl.multiple_of(192 * (2 * half + 1 - c), 64), 192)
        send(ge.at[at, :], re_c.at[half], k_ge + half, core_mate)
    k_gs_y, k_ge_y = recvs(1), recvs(1)
    arrived(rs_c, k_gs)
    t_shr[...] = (
        gs[:, c, :, other_half].astype(F32) + rs_c[:, :, other_half].astype(F32)
    ).astype(BF)
    send(t_shr, rs_y, k_gs_y, y_mate)

    grad_hidden = d2_s[...] + ysum[...]
    for j in range(1, 4):
        arrived(rs2.at[j], k_r2 + j)
        grad_hidden += rs2[j].astype(F32)
    normed = n1_s[...]
    scaled = grad_hidden * prm[6:7, :]
    grad_one = r1_s[...] * (
        scaled
        - jnp.mean(scaled, axis=1, keepdims=True)
        - normed * jnp.mean(scaled * normed, axis=1, keepdims=True)
    )
    low_one = grad_one.astype(BF)
    d1g[r] = low_one
    for k in range(4):
        dab[k] = dot_nt(low_one, w_out[192 * k : 192 * k + 192, :]).astype(BF)
    k_da, k_d1 = recvs(4), recvs(4)
    for j in range(1, 4):
        send(dab.at[peer_rank(j)], da.at[r], k_da + j, peer(j))
    da[r] = dab[r]
    d1_s[...] = grad_one
    row_gain_one = row_sum(grad_hidden * normed)
    row_shift_one = row_sum(grad_hidden)
    row_out = row_sum(grad_one)

    for half in range(2):
        arrived(re_c.at[half], k_ge + half)
    at_y = pl.ds(pl.multiple_of(192 * f_y, 64), 192)
    at_own = pl.ds(pl.multiple_of(192 * f, 64), 192)
    t_exp[...] = (ge[at_y, :].astype(F32) + re_c[1 - y].astype(F32)).astype(BF)
    send(t_exp, re_y, k_ge_y, y_mate)

    for j in range(1, 4):
        arrived(da.at[peer_rank(j)], k_da + j)
        send(d1g.at[r], d1g.at[r], k_d1 + j, peer(j))

    def attend_back(k, carry):
        outs = []
        grads = da[k].astype(F32)
        dots = grads * a_f[k]
        for h in range(3):
            at = slice(64 * h, 64 * h + 64)
            scale = l_s[h, k]
            delta = jnp.sum(dots[:, at], axis=1, keepdims=True) * scale
            high = delta.astype(BF).astype(F32)
            side = jnp.where(wide[0:128, 0:64] == 0, -high, 0.0)
            side = jnp.where(wide[0:128, 0:64] == 1, high - delta, side)
            both = jnp.concatenate([grads[:, at] * scale, side], axis=1).astype(BF)
            de[k, h] = both
            low = (e_s[h, k].astype(F32) * dot_nt(both, vh[h])).astype(BF)
            ds_s[h, k] = low
            outs.append(dot_nn(low, kh[h])[:, 0:64] * 0.125)
        queries = jnp.concatenate(outs, axis=1)
        qb_s[k] = row_sum(queries)
        dz[k, :, 0:192] = queries.astype(BF)
        return carry

    lax.fori_loop(0, 1, attend_back, 0)
    k_fs, k_re = recvs(4), recvs(1)
    arrived(rs_y, k_gs_y)
    fsb[...] = (
        gs[:, c, :, at_half].astype(F32) + rs_c[:, :, at_half].astype(F32) + rs_y[...].astype(F32)
    ).astype(BF)
    for k in range(4):
        send_or_keep(fsb.at[k], fs.at[zh, x], k_fs + 2 * zh + x, dev(c, y, k, zl))
    lax.fori_loop(1, 2, attend_back, 0)
    arrived(re_y, k_ge_y)
    te_f[...] = ge[at_own, :].astype(F32) + re_c[y].astype(F32) + re_y[...].astype(F32)
    te_b[...] = te_f[:, pl.ds(pl.multiple_of(384 * (1 - zh), 128), 384)].astype(BF)
    send(te_b, re_z, k_re, z_mate)
    lax.fori_loop(2, 4, attend_back, 0)
    sums = []
    for h in range(3):
        rows = q_s[:, h, :, 0:64].reshape(512, 64)
        sums.append(dot_tn(rows, ds_s[h].reshape(512, 1024)))
    for h in range(3):
        rows = de[:, h, :, 0:64].reshape(512, 64)
        sums.append(dot_tn(rows, e_s[h].reshape(512, 1024)))
    sums = jnp.concatenate(sums, axis=0)
    dkv[0] = sums[:, 0:512].T
    dkv[1] = sums[:, 512:1024].T
    dkb[...] = dkv[1 - c].astype(BF)
    k_dk = recvs(1)
    send(dkb, dkr, k_dk, core_mate)

    for j in range(1, 4):
        arrived(d1g.at[peer_rank(j)], k_d1 + j)
    part = dot_tn(a_b[...].reshape(512, 192), d1g[...].reshape(512, 768))
    for b in range(8):
        go[b % 2, b // 2] = pack(part[:, 96 * b : 96 * b + 96].astype(BF))
    k_go = recvs(1)
    send(go.at[1 - c], ro_c, k_go, core_mate)

    arrived(dkr, k_dk)
    keyvals = dkv[c] + dkr[...].astype(F32)
    vb_s[...] = row_sum(keyvals[:, 192:384])
    dz[:, :, 192:576] = keyvals.astype(BF).reshape(4, 128, 384)

    def input_part(k):
        return dot_nt(dz[k], w_in[...])

    k_r3, s_r3 = recvs(4), sends(4)

    def input_step(j, carry):
        dx_b[j] = input_part(peer_rank(j)).astype(BF)
        copy_to(dx_b.at[j], rs3.at[j], s_r3 + j, k_r3 + j, peer(j)).start()
        return carry

    lax.fori_loop(1, 4, input_step, 0)
    for j in range(1, 4):
        pending.append(copy_to(dx_b.at[j], rs3.at[j], s_r3 + j, k_r3 + j, peer(j)).wait_send)

    for k in range(4):
        rows = xg[:, :, 192 * k : 192 * k + 192].reshape(512, 192)
        part = dot_tn(rows, dz[...].reshape(512, 576)).astype(BF)
        for slot in range(6):
            gi[k, slot] = pack(part[:, 96 * slot : 96 * slot + 96])
    k_gi = recvs(2)
    for half in range(2):
        send(gi.at[2 * half + 1 - c], ri_c.at[half], k_gi + half, core_mate)

    vg[...] = jnp.zeros((8, 16, 128), F32)
    rows = jnp.concatenate(
        [row_out, row_shift_one, row_back, row_shift_two, row_gain_one, row_gain_two], axis=0
    )
    for b in range(8):
        vg[b, 2:8, 0:96] = rows[:, 96 * b : 96 * b + 96]
    q_row = row_sum(qb_s[:, 0, :])
    v_row = vb_s[...]
    for i in range(2):
        vg[2 * r + i, 0:1, 0:96] = q_row[:, 96 * i : 96 * i + 96]
        vg[2 * r + i, 1:2, 0:96] = v_row[:, 96 * i : 96 * i + 96]
    inner_row = row_sum(beg[:, 0, :])
    for i in range(3):
        vg[r, 8 + i : 9 + i, :] = inner_row[:, 128 * i : 128 * i + 128]
        vg[4 + r, 8 + i : 9 + i, :] = inner_row[:, 384 + 128 * i : 512 + 128 * i]
    k_v = recvs(8)
    for d in range(1, 8):
        other = (ctx + d) % 8
        send(vg.at[other], vr.at[d], k_v + d, (other, seq))

    k_gi_y = recvs(1)
    for half in range(2):
        arrived(ri_c.at[half], k_gi + half)
    tib[...] = (gi[f_y].astype(F32) + ri_c[1 - y].astype(F32)).astype(BF)
    send(tib, ri_y, k_gi_y, y_mate)

    arrived(ro_c, k_go)
    tob[...] = (go[c].astype(F32) + ro_c[...].astype(F32)).astype(BF)
    k_go_y, k_fo = recvs(1), recvs(2)
    s_go, s_fo = sends(1), sends(4)
    stays = y == zl

    @pl.when(jnp.logical_not(stays))
    def _():
        copy_to(tob, ro_y, s_go, k_go_y, y_mate).start()

    done = []

    for half in range(2):
        for sub in range(2):
            arrived(fs.at[half, sub], k_fs + 2 * half + sub)
    for sub in range(2):
        f_wshr[:, 384 * sub : 384 * sub + 384] = fs[0, sub].astype(F32) + fs[1, sub].astype(F32)
    done.append(local(f_wshr, o_wshr))
    arrived(re_z, k_re)
    f_wexp[...] = te_f[:, pl.ds(pl.multiple_of(384 * zh, 128), 384)] + re_z[...].astype(F32)
    done.append(local(f_wexp, o_wexp))

    grad_in = d1_s[...] + input_part(r)
    for j in range(1, 4):
        arrived(rs3.at[j], k_r3 + j)
        grad_in += rs3[j].astype(F32)
    ghb[...] = grad_in.astype(BF)
    k_gh = recvs(1)
    send_or_keep(ghb, ghr, k_gh, home)

    arrived(ri_y, k_gi_y)
    ti2[...] = (gi[f].astype(F32) + ri_c[y].astype(F32) + ri_y[...].astype(F32)).astype(BF)
    k_fi = recvs(6)
    for slot in range(6):
        unit = 8 * (slot // 2) + 2 * r + slot % 2
        send_or_keep(
            ti2.at[slot], fi.at[zh, unit % 3], k_fi + 3 * zh + unit % 3, (unit // 3, seq)
        )

    @pl.when(stays)
    def _():
        arrived(ro_y, k_go_y)
        tob2[...] = (tob[...].astype(F32) + ro_y[...].astype(F32)).astype(BF)
        for k in range(4):
            to = dev(c, y, k, x)
            away = jnp.logical_or(to[0] != ctx, to[1] != seq)

            @pl.when(away)
            def _():
                copy_to(tob2.at[k], fo.at[zh], s_fo + k, k_fo + zh, to).start()

            @pl.when(jnp.logical_not(away))
            def _():
                pltpu.make_async_copy(tob2.at[k], fo.at[zh], rsem.at[k_fo + zh]).start()

    def finish_out():
        @pl.when(jnp.logical_not(stays))
        def _():
            copy_to(tob, ro_y, s_go, k_go_y, y_mate).wait_send()

        @pl.when(stays)
        def _():
            for k in range(4):
                to = dev(c, y, k, x)

                @pl.when(jnp.logical_or(to[0] != ctx, to[1] != seq))
                def _():
                    copy_to(tob2.at[k], fo.at[zh], s_fo + k, k_fo + zh, to).wait_send()

    pending.append(finish_out)

    total = vg[ctx]
    for d in range(1, 8):
        arrived(vr.at[d], k_v + d)
        total += vr[d]
    vs1[...] = total
    k_vc = recvs(2)
    send(vs1, vc, k_vc, core_mate)
    arrived(vc, k_vc)
    vs2[...] = vs1[...] + vc[...]
    send(vs2, vy, k_vc + 1, y_mate)

    arrived(ohr, k_o)
    done.append(local(ohr, o_out))
    arrived(vy, k_vc + 1)
    total = vs2[...] + vy[...]
    f_gb[...] = total[0:6, 0:96]
    f_gg[...] = total[6:8, 0:96]
    f_ge[...] = total[8:11, :]
    done += [local(f_gb, o_gb), local(f_gg, o_gg), local(f_ge, o_ge)]
    for half in range(2):
        arrived(fo.at[half], k_fo + half)
    part = fo[0].astype(F32) + fo[1].astype(F32)
    for q in range(4):
        f_wout[48 * q : 48 * q + 48, :] = part[:, 96 * q : 96 * q + 96]
    done.append(local(f_wout, o_wout))
    for half in range(2):
        for j in range(3):
            arrived(fi.at[half, j], k_fi + 3 * half + j)
    parts = [fi[0, j].astype(F32) + fi[1, j].astype(F32) for j in range(3)]
    for q in range(4):
        f_win[48 * q : 48 * q + 48, :] = jnp.concatenate(
            [part[:, 96 * q : 96 * q + 96] for part in parts], axis=1
        )
    done.append(local(f_win, o_win))
    arrived(ghr, k_gh)
    done.append(local(ghr, o_gh))
    for finish in pending:
        finish()
    for copy in done:
        copy.wait()


def hand_over(*refs):
    ins, outs, held, into, out_of = refs[0:9], refs[9:18], refs[18:27], refs[27], refs[28]
    loads = [pltpu.make_async_copy(ins[i], held[i], into.at[i]) for i in range(9)]
    stores = [pltpu.make_async_copy(held[i], outs[i], out_of.at[i]) for i in range(9)]
    for load in loads:
        load.start()
    for load, store in zip(loads, stores):
        load.wait()
        store.start()
    for store in stores:
        store.wait()


def fast_shards(
    hidden, project_in, project_out, expand_weight, shrink_weight, biases, gains, expand_bias,
    random_blocks, global_blocks, document_lengths, cotangent,
):
    vm = lambda *dims: pltpu.VMEM(dims, BF)
    vf = lambda *dims: pltpu.VMEM(dims, F32)
    scratch = [
        vm(192, 288), vm(192, 96), vm(3, 48, 384), vm(48, 384), vm(4, 128, 768), vm(128, 768),
        vf(8, 128), vf(4, 8, 128), vf(16, 128), vf(8, 16, 128), vm(4, 6, 48, 384), vm(4, 8, 48, 384),
        vm(4, 192, 768), vm(4, 2, 96, 768), vm(768, 576), vm(768, 768), vf(8, 768),
        vm(4, 128, 128), vm(4, 3, 128, 128), vm(2, 512, 384), vm(3, 1024, 128), vm(3, 1024, 128),
        vm(3, 4, 128, 1024), vf(3, 4, 128, 1), vf(4, 128, 192), vm(4, 128, 192), vm(4, 128, 192),
        vm(4, 128, 768), vf(128, 768), vf(128, 768), vf(128, 1), vf(4, 128, 768), vm(4, 128, 768),
        vf(128, 768), vm(4, 128, 768),
        vm(4, 128, 768), vf(128, 768), vm(4, 128, 768), vm(4, 128, 768), vm(4, 128, 768),
        vm(4, 128, 768), vf(4, 1, 768), vf(128, 768), vm(4, 128, 768), vm(4, 128, 192),
        vm(4, 128, 192), vm(4, 3, 128, 128), vm(3, 4, 128, 1024), vf(2, 512, 384), vm(512, 384),
        vm(512, 384), vm(4, 128, 576), vm(4, 128, 768), vm(4, 128, 768),
        vm(4, 2, 96, 768), vm(4, 96, 768), vm(4, 96, 384), vm(4, 96, 384), vm(4, 96, 384),
        vm(2, 2, 96, 384), vm(768, 768), vm(2, 192, 768), vm(192, 768), vm(192, 768), vf(192, 768),
        vm(192, 384), vm(192, 384),
        vm(2, 4, 48, 384), vm(4, 48, 384), vm(4, 48, 384), vm(4, 48, 384), vm(4, 48, 384),
        vm(2, 48, 384), vm(4, 6, 48, 384), vm(2, 6, 48, 384), vm(6, 48, 384), vm(6, 48, 384),
        vm(6, 48, 384), vm(2, 3, 48, 384),
        vf(8, 16, 128), vf(8, 16, 128), vf(16, 128), vf(16, 128), vf(16, 128), vf(16, 128),
        vf(4, 1, 192), vf(1, 192), vm(128, 768), vm(128, 768), vm(128, 768), vm(128, 768),
        vf(192, 288), vf(192, 96), vf(192, 384), vf(96, 768), vf(6, 96), vf(2, 96), vf(3, 128),
        pltpu.SemaphoreType.DMA((SENDS,)), pltpu.SemaphoreType.DMA((RECVS,)),
        pltpu.SemaphoreType.DMA((LOCALS,)),
    ]
    out = lambda kind, *dims: jax.ShapeDtypeStruct(dims, kind)
    shapes = (
        out(BF, 128, 768), out(BF, 128, 768), out(F32, 192, 288), out(F32, 192, 96),
        out(F32, 192, 384), out(F32, 96, 768), out(F32, 6, 96), out(F32, 2, 96), out(F32, 3, 128),
    )
    anywhere = pl.BlockSpec(memory_space=pl.ANY)
    results = pl.pallas_call(
        layer_kernel,
        out_shape=shapes,
        in_specs=[pl.BlockSpec(memory_space=pltpu.SMEM)] * 3
        + [pl.BlockSpec(memory_space=pltpu.VMEM)] * 3
        + [anywhere] * 6,
        out_specs=(anywhere,) * 9,
        scratch_shapes=scratch,
        compiler_params=pltpu.CompilerParams(
            collective_id=0, has_side_effects=True, vmem_limit_bytes=58 * 1024 * 1024
        ),
    )(
        random_blocks[0], global_blocks, document_lengths, biases, gains,
        expand_bias.reshape(3, 128), hidden[0], cotangent[0], project_in, project_out,
        expand_weight, shrink_weight.T,
    )
    results = pl.pallas_call(
        hand_over,
        out_shape=shapes,
        in_specs=[anywhere] * 9,
        out_specs=(anywhere,) * 9,
        scratch_shapes=[pltpu.VMEM(one.shape, one.dtype) for one in shapes]
        + [pltpu.SemaphoreType.DMA((9,))] * 2,
    )(*results)
    return (
        results[0][None], results[1][None], results[2], results[3], results[4], results[5].T,
        results[6], results[7], results[8].reshape(-1),
    )


def solution(mesh):
    small = tuple(mesh.shape[name] for name in ("ctx", "fsdp")) == (8, 4)
    return jax.shard_map(
        fast_shards if small else shards,
        mesh=mesh,
        in_specs=(
            P("fsdp", "ctx", None),
            P("fsdp", "ctx"),
            P("fsdp", "ctx"),
            P("fsdp", "ctx"),
            P("fsdp", "ctx"),
            P(None, "ctx"),
            P(None, "ctx"),
            P("ctx"),
            P("fsdp", "ctx", None),
            P("fsdp", None),
            P("fsdp", None),
            P("fsdp", "ctx", None),
        ),
        out_specs=(
            P("fsdp", "ctx", None),
            P("fsdp", "ctx", None),
            P("fsdp", "ctx"),
            P("fsdp", "ctx"),
            P("fsdp", "ctx"),
            P("fsdp", "ctx"),
            P(None, "ctx"),
            P(None, "ctx"),
            P("ctx"),
        ),
        check_vma=False,
    )
```

```python
import jax
import jax.numpy as jnp
from jax import lax
from jax.experimental import pallas as pl
from jax.experimental.pallas import tpu as pltpu
from jax.sharding import PartitionSpec as P

HEAD_DIM = 64
BLOCK = 64


def segment_of(positions, bounds):
    return jnp.sum((positions[..., None] >= bounds).astype(jnp.int32), axis=-1)


def layer_norm_parts(values, gain_row, shift_row):
    centre = values - jnp.mean(values, axis=-1, keepdims=True)
    inverse = lax.rsqrt(jnp.mean(centre * centre, axis=-1, keepdims=True) + 1e-05)
    normed = centre * inverse
    return (normed * gain_row + shift_row, normed, inverse)


def layer_norm_back(upstream, normed, inverse, gain_row):
    scaled = upstream * gain_row
    return inverse * (
        scaled
        - jnp.mean(scaled, axis=-1, keepdims=True)
        - normed * jnp.mean(scaled * normed, axis=-1, keepdims=True)
    )


def matmul(left_side, right_side):
    return jnp.dot(left_side, right_side, preferred_element_type=jnp.float32)


def matmul_left_t(left_side, right_side):
    return lax.dot_general(
        left_side, right_side, (((0,), (0,)), ((), ())), preferred_element_type=jnp.float32
    )


def matmul_right_t(left_side, right_side):
    return lax.dot_general(
        left_side, right_side, (((1,), (1,)), ((), ())), preferred_element_type=jnp.float32
    )


def over_cols(qkv_grad, out_grad, expand_grad, shrink_grad, vector_grad, gain_grad, inner_grad):
    return (
        lax.psum_scatter(qkv_grad, "ctx", scatter_dimension=1, tiled=True),
        lax.psum_scatter(out_grad, "ctx", scatter_dimension=1, tiled=True),
        lax.psum_scatter(expand_grad, "ctx", scatter_dimension=1, tiled=True),
        lax.psum_scatter(shrink_grad, "ctx", scatter_dimension=1, tiled=True),
        lax.psum_scatter(vector_grad, "ctx", scatter_dimension=1, tiled=True),
        lax.psum_scatter(gain_grad, "ctx", scatter_dimension=1, tiled=True),
        lax.psum_scatter(inner_grad, "ctx", scatter_dimension=1, tiled=True),
    )


def over_rows(qkv_grad, out_grad, expand_grad, shrink_grad):
    return (
        lax.psum_scatter(
            qkv_grad.astype(jnp.bfloat16), "fsdp", scatter_dimension=0, tiled=True
        ).astype(jnp.float32),
        lax.psum_scatter(
            out_grad.astype(jnp.bfloat16), "fsdp", scatter_dimension=0, tiled=True
        ).astype(jnp.float32),
        lax.psum_scatter(
            expand_grad.astype(jnp.bfloat16), "fsdp", scatter_dimension=0, tiled=True
        ).astype(jnp.float32),
        lax.psum_scatter(
            shrink_grad.astype(jnp.bfloat16), "fsdp", scatter_dimension=0, tiled=True
        ).astype(jnp.float32),
    )


def scatter_rows(link_ids, link_grads, row_count, feature_width):
    block_count = row_count // BLOCK
    inside = (link_ids >= 0) & (link_ids < block_count)
    target = jnp.where(inside, link_ids, block_count).reshape(-1)
    partial_value = jnp.zeros((block_count, BLOCK, feature_width), jnp.float32)
    partial_value = partial_value.at[target].add(
        link_grads.reshape(-1, BLOCK, feature_width), mode="drop"
    )
    return partial_value.reshape(row_count, feature_width)


def shards(
    hidden,
    project_in,
    project_out,
    expand_weight,
    shrink_weight,
    biases,
    gains,
    expand_bias,
    random_blocks,
    global_blocks,
    document_lengths,
    cotangent,
):
    inputs = hidden[0]
    tokens_here = inputs.shape[0]
    width = inputs.shape[1]
    head_count = width // HEAD_DIM
    blocks_here = tokens_here // BLOCK
    rand_count = random_blocks.shape[2]
    link_count = 3 + rand_count + global_blocks.shape[1]
    ctx_rank = lax.axis_index("ctx")
    last_block = tokens_here * lax.axis_size("ctx") // BLOCK - 1
    col_full = (
        lax.all_gather(project_in, "ctx", axis=1, tiled=True),
        lax.all_gather(project_out, "ctx", axis=1, tiled=True),
        lax.all_gather(expand_weight, "ctx", axis=1, tiled=True),
        lax.all_gather(shrink_weight, "ctx", axis=1, tiled=True),
        lax.all_gather(biases, "ctx", axis=1, tiled=True),
        lax.all_gather(gains, "ctx", axis=1, tiled=True),
        lax.all_gather(expand_bias.reshape(1, -1), "ctx", axis=1, tiled=True),
    )
    full_qkv, full_out, full_expand, full_shrink = (
        lax.all_gather(col_full[0], "fsdp", axis=0, tiled=True),
        lax.all_gather(col_full[1], "fsdp", axis=0, tiled=True),
        lax.all_gather(col_full[2], "fsdp", axis=0, tiled=True),
        lax.all_gather(col_full[3], "fsdp", axis=0, tiled=True),
    )
    vectors = col_full[4].astype(jnp.float32)
    gain_rows = col_full[5].astype(jnp.float32)
    inner_bias = col_full[6][0].astype(jnp.float32)
    block_ids = ctx_rank * blocks_here + jnp.arange(blocks_here, dtype=jnp.int32)
    window = jnp.stack(
        [jnp.maximum(block_ids - 1, 0), block_ids, jnp.minimum(block_ids + 1, last_block)], axis=1
    )
    global_links = jnp.broadcast_to(
        global_blocks[0][None, :], (blocks_here, global_blocks.shape[1])
    )
    linked_ids = jnp.concatenate([window, random_blocks[0], global_links], axis=1)
    lengths = document_lengths[0]
    doc_order = jnp.arange(lengths.shape[0], dtype=jnp.int32)
    bounds = jnp.sum(
        jnp.where(doc_order[None, :] <= doc_order[:-1, None], lengths[None, :], 0), axis=1
    )
    query_pos = (ctx_rank * tokens_here + jnp.arange(tokens_here, dtype=jnp.int32)).reshape(
        blocks_here, BLOCK
    )
    query_seg = segment_of(query_pos, bounds)
    key_pos = linked_ids[:, :, None] * BLOCK + jnp.arange(BLOCK, dtype=jnp.int32)[None, None, :]
    key_seg = segment_of(key_pos, bounds).reshape(blocks_here, -1)
    allowed = query_seg[:, None, :, None] == key_seg[:, None, None, :]
    zero_row = jnp.zeros((width,), jnp.float32)
    mixed_qkv = (
        matmul(inputs, full_qkv) + jnp.concatenate([vectors[0], zero_row, vectors[1]])
    ).astype(jnp.bfloat16)
    queries = mixed_qkv[:, :width]
    keyvals = mixed_qkv[:, width:]
    shard_piece = lax.all_gather(keyvals, "ctx", axis=0, tiled=True)
    block_count = shard_piece.shape[0] // BLOCK
    stacked = shard_piece.reshape(block_count, BLOCK, shard_piece.shape[1])
    picks = (
        linked_ids.reshape(-1)[:, None] == jnp.arange(block_count, dtype=jnp.int32)[None, :]
    ).astype(jnp.bfloat16)
    linked = jnp.einsum("lb,bkd->lkd", picks, stacked).reshape(
        blocks_here, link_count, BLOCK, 2 * width
    )
    query_heads = queries.reshape(blocks_here, BLOCK, head_count, HEAD_DIM)
    key_heads = linked[..., :width].reshape(blocks_here, link_count * BLOCK, head_count, HEAD_DIM)
    value_heads = linked[..., width:].reshape(blocks_here, link_count * BLOCK, head_count, HEAD_DIM)

    def score_parts():
        raw_scores = (
            jnp.einsum(
                "bqhd,bkhd->bhqk", query_heads, key_heads, preferred_element_type=jnp.float32
            )
            * 0.125
        )
        return jnp.where(allowed, raw_scores, -1e30)

    scores = score_parts()
    top_score = jnp.max(scores, axis=-1, keepdims=True)
    exp_total = jnp.sum(jnp.exp(scores - top_score), axis=-1, keepdims=True)
    attention = jnp.exp(scores - top_score) / exp_total
    attended = jnp.einsum(
        "bhqk,bkhd->bqhd",
        attention.astype(jnp.bfloat16),
        value_heads,
        preferred_element_type=jnp.float32,
    )
    attended = attended.reshape(tokens_here, width).astype(jnp.bfloat16)
    residual_one = inputs.astype(jnp.float32) + matmul(attended, full_out) + vectors[2]
    hidden_one, normed_one, inverse_one = layer_norm_parts(residual_one, gain_rows[0], vectors[3])
    hidden_low = hidden_one.astype(jnp.bfloat16)
    inner_pre = matmul(hidden_low, full_expand) + inner_bias
    activated, gelu_pull = jax.vjp(
        lambda argument: jax.nn.gelu(argument, approximate=False), inner_pre
    )
    active_low = activated.astype(jnp.bfloat16)
    residual_two = hidden_one + matmul(active_low, full_shrink) + vectors[4]
    result, normed_two, inverse_two = layer_norm_parts(residual_two, gain_rows[1], vectors[5])
    upstream = cotangent[0].astype(jnp.float32)
    grad_gain_two = jnp.sum(upstream * normed_two, axis=0)
    grad_shift_two = jnp.sum(upstream, axis=0)
    grad_two = layer_norm_back(upstream, normed_two, inverse_two, gain_rows[1])
    grad_bias_back = jnp.sum(grad_two, axis=0)
    grad_two_low = grad_two.astype(jnp.bfloat16)
    again_cols = (
        lax.all_gather(project_in, "ctx", axis=1, tiled=True),
        lax.all_gather(project_out, "ctx", axis=1, tiled=True),
        lax.all_gather(expand_weight, "ctx", axis=1, tiled=True),
        lax.all_gather(shrink_weight, "ctx", axis=1, tiled=True),
    )
    back_weights = (
        lax.all_gather(again_cols[0], "fsdp", axis=0, tiled=True),
        lax.all_gather(again_cols[1], "fsdp", axis=0, tiled=True),
        lax.all_gather(again_cols[2], "fsdp", axis=0, tiled=True),
        lax.all_gather(again_cols[3], "fsdp", axis=0, tiled=True),
    )
    back_qkv, back_out, back_expand, back_shrink = back_weights
    grad_shrink_w = matmul_left_t(active_low, grad_two_low)
    grad_active = matmul_right_t(grad_two_low, back_shrink)
    grad_inner = gelu_pull(grad_active)[0]
    grad_inner_bias = jnp.sum(grad_inner, axis=0)
    grad_inner_low = grad_inner.astype(jnp.bfloat16)
    grad_expand_w = matmul_left_t(hidden_low, grad_inner_low)
    grad_hidden_one = grad_two + matmul_right_t(grad_inner_low, back_expand)
    grad_gain_one = jnp.sum(grad_hidden_one * normed_one, axis=0)
    grad_shift_one = jnp.sum(grad_hidden_one, axis=0)
    grad_one = layer_norm_back(grad_hidden_one, normed_one, inverse_one, gain_rows[0])
    grad_bias_out = jnp.sum(grad_one, axis=0)
    grad_one_low = grad_one.astype(jnp.bfloat16)
    grad_out_w = matmul_left_t(attended, grad_one_low)
    grad_attended = matmul_right_t(grad_one_low, back_out).astype(jnp.bfloat16)
    grad_attended = grad_attended.reshape(blocks_here, BLOCK, head_count, HEAD_DIM)
    scores = score_parts()
    attention = jnp.exp(scores - top_score) / exp_total
    grad_attention = jnp.einsum(
        "bqhd,bkhd->bhqk", grad_attended, value_heads, preferred_element_type=jnp.float32
    )
    grad_values = jnp.einsum(
        "bhqk,bqhd->bkhd",
        attention.astype(jnp.bfloat16),
        grad_attended,
        preferred_element_type=jnp.float32,
    )
    row_inner = jnp.sum(attention * grad_attention, axis=-1, keepdims=True)
    grad_scores = (attention * (grad_attention - row_inner) * 0.125).astype(jnp.bfloat16)
    grad_queries = jnp.einsum(
        "bhqk,bkhd->bqhd", grad_scores, key_heads, preferred_element_type=jnp.float32
    ).reshape(tokens_here, width)
    grad_keys = jnp.einsum(
        "bhqk,bqhd->bkhd", grad_scores, query_heads, preferred_element_type=jnp.float32
    )
    slot_grads = jnp.concatenate(
        [
            grad_keys.reshape(blocks_here, link_count, BLOCK, width),
            grad_values.reshape(blocks_here, link_count, BLOCK, width),
        ],
        axis=-1,
    )
    grad_keyvals = lax.psum_scatter(
        scatter_rows(linked_ids, slot_grads, tokens_here * lax.axis_size("ctx"), 2 * width),
        "ctx",
        scatter_dimension=0,
        tiled=True,
    )
    grad_mixed = jnp.concatenate([grad_queries, grad_keyvals], axis=1)
    grad_bias_query = jnp.sum(grad_queries, axis=0)
    grad_bias_value = jnp.sum(grad_keyvals[:, width:], axis=0)
    grad_mixed_low = grad_mixed.astype(jnp.bfloat16)
    grad_qkv_w = matmul_left_t(inputs, grad_mixed_low)
    grad_inputs = grad_one + matmul_right_t(grad_mixed_low, back_qkv)
    grad_vectors = jnp.stack(
        [
            grad_bias_query,
            grad_bias_value,
            grad_bias_out,
            grad_shift_one,
            grad_bias_back,
            grad_shift_two,
        ]
    )
    grad_gain_rows = jnp.stack([grad_gain_one, grad_gain_two])
    grad_inner_row = grad_inner_bias[None, :]
    reduced = over_cols(
        grad_qkv_w,
        grad_out_w,
        grad_expand_w,
        grad_shrink_w,
        grad_vectors,
        grad_gain_rows,
        grad_inner_row,
    )
    sum_qkv, sum_out, sum_expand, sum_shrink = over_rows(
        reduced[0], reduced[1], reduced[2], reduced[3]
    )
    final_vectors, final_gains, final_inner = lax.psum((reduced[4], reduced[5], reduced[6]), "fsdp")
    return (
        result.astype(jnp.bfloat16)[None],
        grad_inputs.astype(jnp.bfloat16)[None],
        sum_qkv,
        sum_out,
        sum_expand,
        sum_shrink,
        final_vectors,
        final_gains,
        final_inner.reshape(-1),
    )


MESH = pl.DeviceIdType.MESH
BF = jnp.bfloat16
F32 = jnp.float32
SENDS = 160
RECVS = 160
LOCALS = 16
NEG = -1e30


def dot_nn(a, b):
    return jnp.dot(a, b, preferred_element_type=F32)


def dot_nt(a, b):
    return lax.dot_general(a, b, (((1,), (1,)), ((), ())), preferred_element_type=F32)


def dot_tn(a, b):
    return lax.dot_general(a, b, (((0,), (0,)), ((), ())), preferred_element_type=F32)


def row_sum(values):
    return jnp.sum(values, axis=0, keepdims=True)


def pack(piece):
    return jnp.concatenate([piece[48 * q : 48 * q + 48] for q in range(4)], axis=1)


def layer_kernel(
    rand_ref, glob_ref, doc_ref, bia, gai, ebi, hid, cot, win, wout, wexp, wshr,
    o_out, o_gh, o_win, o_wout, o_wexp, o_wshr, o_gb, o_gg, o_ge,
    winv, woutv, win3, wout1, xg, eo, ms, mg, ps, par, win_p, wout_p, wexp_f, ws, w_in, w_out, prm,
    mq, q_s, kv, kh, vh, e_s, l_s, a_f, a_b, a_all, hg, h1_s, n1_s, r1_s, u_s, dge, g_s, ysum, yb,
    rs1, d2_s, dg, du_s, dh_b, rs2, beg, d1_s, d1g, dab, da, de, ds_s, dkv, dkb, dkr, dz, dx_b, rs3,
    gs, rs_c, t_shr, rs_y, fsb, fs, ge, re_c, t_exp, re_y, te_f, te_b, re_z,
    go, ro_c, tob, ro_y, tob2, fo, gi, ri_c, tib, ri_y, ti2, fi,
    vg, vr, vs1, vc, vs2, vy, qb_s, vb_s, ob, ohr, ghb, ghr,
    f_win, f_wout, f_wexp, f_wshr, f_gb, f_gg, f_ge,
    ssem, rsem, lsem,
):
    ctx = lax.axis_index("ctx")
    seq = lax.axis_index("fsdp")
    z, x = ctx // 2, ctx % 2
    y, c = seq // 2, seq % 2
    zh, zl = z // 2, z % 2
    r = 2 * zl + x
    f = seq

    def dev(px, py, pz, pc):
        return (2 * pz + px, 2 * py + pc)

    def flip(v, on):
        return v + on - 2 * v * on

    def peer(j):
        return dev(flip(x, j % 2), y, 2 * zh + flip(zl, j // 2), c)

    def peer_rank(j):
        return 2 * flip(zl, j // 2) + flip(x, j % 2)

    core_mate = dev(x, y, z, 1 - c)
    y_mate = dev(x, 1 - y, z, c)
    z_mate = dev(x, y, 2 * (1 - zh) + zl, c)
    home = dev(x, y, 2 * c + zl, zh)

    pending = []
    counts = {"s": 0, "r": 0, "l": 0}

    def take(kind, n, most):
        first = counts[kind]
        counts[kind] = first + n
        assert counts[kind] <= most
        return first

    def recvs(n):
        return take("r", n, RECVS)

    def sends(n):
        return take("s", n, SENDS)

    def local(src, dst):
        cp = pltpu.make_async_copy(src, dst, lsem.at[take("l", 1, LOCALS)])
        cp.start()
        return cp

    def copy_to(src, dst, si, ri, to):
        return pltpu.make_async_remote_copy(
            src_ref=src, dst_ref=dst, send_sem=ssem.at[si], recv_sem=rsem.at[ri],
            device_id=to, device_id_type=MESH,
        )

    def send(src, dst, ri, to):
        cp = copy_to(src, dst, sends(1), ri, to)
        cp.start()
        pending.append(cp.wait_send)

    def send_or_keep(src, dst, ri, to):
        si = sends(1)
        away = jnp.logical_or(to[0] != ctx, to[1] != seq)

        @pl.when(away)
        def _():
            copy_to(src, dst, si, ri, to).start()

        @pl.when(jnp.logical_not(away))
        def _():
            pltpu.make_async_copy(src, dst, rsem.at[ri]).start()

        def finish():
            @pl.when(away)
            def _():
                copy_to(src, dst, si, ri, to).wait_send()

        pending.append(finish)

    def arrived(dst, ri):
        pltpu.make_async_copy(dst, dst, rsem.at[ri]).wait()

    def pass_on(buf, first):
        for j, at in ((1, pl.ds(0, 64)), (2, pl.ds(64, 64))):
            rank = peer_rank(j)
            arrived(buf.at[rank], first + j)
            send(buf.at[rank, at], buf.at[rank, at], first + 3 * (2 - j), peer(3 - j))

    def far_arrived(buf, first):
        rank = peer_rank(3)
        arrived(buf.at[rank, pl.ds(0, 64)], first + 3)
        arrived(buf.at[rank, pl.ds(64, 64)], first)

    barrier = pltpu.get_barrier_semaphore()
    place = 2 * ctx + c
    for d in range(1, 16):
        other = (place + d) % 16
        pl.semaphore_signal(
            barrier, inc=1, device_id=(other // 2, 2 * y + other % 2), device_id_type=MESH
        )
    pl.semaphore_signal(barrier, inc=1, device_id=y_mate, device_id_type=MESH)
    in_win, in_wout = local(win, winv), local(wout, woutv)

    lane = lax.broadcasted_iota(jnp.int32, (1, 128), 1)
    for i in range(2):
        block = 2 * ctx + i
        links = [jnp.maximum(block - 1, 0), block, jnp.minimum(block + 1, 15)]
        links += [rand_ref[i, k] for k in range(3)] + [glob_ref[0, k] for k in range(2)]
        count = jnp.zeros((1, 128), F32)
        for link in links:
            count += jnp.where(jnp.logical_or(lane == link + 72, lane == link + 88), 1.0, 0.0)
        ms[i : i + 1, :] = count
    edge = doc_ref[0, 0]
    edges = jnp.zeros((1, 128), F32)
    for k in range(7):
        edges += jnp.where(lane == k, edge.astype(F32), 0.0)
        edge = edge + doc_ref[0, k + 1]
    ms[2:3, :] = edges
    ms[3:8, :] = jnp.zeros((5, 128), F32)
    ps[...] = jnp.zeros((16, 128), F32)
    ps[0:6, 0:96] = bia[...].astype(F32)
    ps[6:8, 0:96] = gai[...].astype(F32)
    ps[8:11, :] = ebi[...].astype(F32)
    in_win.wait()
    for j in range(3):
        win3[j] = pack(winv[:, 96 * j : 96 * j + 96])

    pl.semaphore_wait(barrier, 16)

    k_h, k_x, k_m, k_e = recvs(1), recvs(4), recvs(4), recvs(1)
    send_or_keep(hid, xg.at[r], k_h, home)
    send_or_keep(ms, mg.at[r], k_m, home)
    k_win = recvs(6)
    for j in range(3):
        unit = 3 * ctx + j
        rank = (unit % 8) // 2
        slot = 2 * (unit // 8) + unit % 2
        for half in range(2):
            send_or_keep(
                win3.at[j], win_p.at[f, slot], k_win + slot, dev(rank % 2, y, 2 * half + rank // 2, c)
            )
    k_par = recvs(8)
    for d in range(1, 8):
        other = (ctx + d) % 8
        send(ps, par.at[ctx], k_par + d, (other, seq))
    par[ctx] = ps[...]
    in_wout.wait()
    wout1[...] = pack(woutv[...])

    arrived(xg.at[r], k_h)
    arrived(mg.at[r], k_m)
    for j in range(1, 4):
        if j < 3:
            send(xg.at[r], xg.at[r], k_x + j, peer(j))
        send(mg.at[r], mg.at[r], k_m + j, peer(j))
    k_wout_y, k_wout_c = recvs(1), recvs(2)
    k_wexp_y, k_wexp_c = recvs(1), recvs(2)
    k_wshr_y, k_wshr_c = recvs(1), recvs(2)
    k_wout = recvs(8)
    for d in range(8):
        other = (ctx + d) % 8
        if d == 0:
            pltpu.make_async_copy(wout1, wout_p.at[f, ctx], rsem.at[k_wout]).start()
        else:
            send(wout1, wout_p.at[f, ctx], k_wout + d, (other, seq))


    def sided(positions, rows):
        segs = jnp.zeros((rows, 1), F32)
        for k in range(7):
            segs += jnp.where(positions >= mg[r, 2:3, k : k + 1], 1.0, 0.0)
        return segs

    wide = lax.broadcasted_iota(jnp.int32, (1024, 128), 1)
    key_row = lax.broadcasted_iota(jnp.int32, (1024, 1), 0)
    key_segs = sided(key_row.astype(F32), 1024).astype(jnp.int32) + 64
    hot = jnp.logical_or(
        jnp.logical_and(wide < 72, wide == key_segs),
        jnp.logical_and(
            wide >= 72,
            jnp.logical_or(wide == key_row // 64 + 72, wide == key_row // 64 + 88),
        ),
    )
    hot = jnp.where(hot, 1.0, 0.0).astype(BF)
    ones = jnp.where(jnp.logical_or(wide == 64, wide == 65), 1.0, 0.0).astype(BF)
    for h in range(3):
        kh[h, :, 64:128] = hot[:, 64:128]
        vh[h, :, 64:128] = ones[:, 64:128]

    k_win_y, k_win_c = recvs(1), recvs(2)
    for slot in range(6):
        arrived(win_p.at[f, slot], k_win + slot)
    send(win_p.at[f], win_p.at[f], k_win_y, y_mate)
    send(win_p.at[f], win_p.at[f], k_win_c, core_mate)
    pass_on(xg, k_x)
    k_wexp = recvs(2)
    mine_exp = wexp_f.at[f, :, pl.ds(pl.multiple_of(384 * zh, 128), 384)]
    pltpu.make_async_copy(wexp, mine_exp, rsem.at[k_wexp]).start()
    send(wexp, mine_exp, k_wexp + 1, z_mate)

    for d in range(1, 8):
        arrived(par.at[(ctx + 8 - d) % 8], k_par + d)
    prm[...] = jnp.concatenate([par[b, 0:8, 0:96] for b in range(8)], axis=1)
    be = jnp.concatenate(
        [par[r, 8 + i : 9 + i, :] for i in range(3)] + [par[4 + r, 8 + i : 9 + i, :] for i in range(3)],
        axis=1,
    )
    zrow = jnp.zeros((1, 192), F32)
    z_bias = jnp.concatenate(
        [par[2 * r, 0:1, 0:96], par[2 * r + 1, 0:1, 0:96], zrow, par[2 * r, 1:2, 0:96], par[2 * r + 1, 1:2, 0:96]],
        axis=1,
    )

    row_pos = lax.broadcasted_iota(jnp.int32, (512, 1), 0) + 512 * c
    row_segs = sided(row_pos.astype(F32), 512).astype(jnp.int32) + 64
    for j in range(1, 4):
        arrived(mg.at[peer_rank(j)], k_m + j)
    for i in range(8):
        count = mg[i // 2, i % 2 : i % 2 + 1, :]
        logs = jnp.log(jnp.maximum(count, 1.0))
        high = logs.astype(BF).astype(F32)
        line = jnp.where(lane < 88, jnp.where(count > 0.5, high, NEG), logs - high)
        line = jnp.where(lane < 104, line, 0.0)
        same = row_segs[64 * i : 64 * i + 64] == wide[0:64]
        block = jnp.where(wide[0:64] < 72, jnp.where(same, 0.0, NEG), line)
        mq[i // 2, 64 * (i % 2) : 64 * (i % 2) + 64, :] = block.astype(BF)
    for h in range(3):
        q_s[:, h, :, 64:128] = mq[:, :, 64:128]

    f_y = 2 * (1 - y) + c
    arrived(win_p.at[f_y], k_win_y)
    send(win_p.at[f_y], win_p.at[f_y], k_win_c + 1, core_mate)
    for d in range(8):
        arrived(wout_p.at[f, (ctx + 8 - d) % 8], k_wout + d)
    send(wout_p.at[f], wout_p.at[f], k_wout_y, y_mate)
    send(wout_p.at[f], wout_p.at[f], k_wout_c, core_mate)
    k_wshr = recvs(4)
    at_half = pl.ds(pl.multiple_of(384 * y, 128), 384)
    for sub in range(2):
        for half in range(2):
            send_or_keep(
                wshr.at[:, 384 * sub : 384 * sub + 384], ws.at[2 * zh + zl, x, :, at_half],
                k_wshr + 2 * zh + zl, dev(sub, y, 2 * half + c, x),
            )


    def place_in(k):
        for q in range(4):
            w_in[pl.ds(pl.multiple_of(192 * k + 48 * q, 16), 48), :] = jnp.concatenate(
                [win_p[k, i, :, 96 * q : 96 * q + 96] for i in range(6)], axis=1
            )

    place_in(f)
    place_in(f_y)
    arrived(win_p.at[2 * y + 1 - c], k_win_c)
    place_in(2 * y + 1 - c)
    arrived(win_p.at[2 * (1 - y) + 1 - c], k_win_c + 1)
    place_in(2 * (1 - y) + 1 - c)

    def project(k):
        mixed = dot_nn(xg[k], w_in[...]) + z_bias
        queries = (mixed[:, 0:192].astype(BF).astype(F32) * 0.125).astype(BF)
        for h in range(3):
            q_s[k, h, :, 0:64] = queries[:, 64 * h : 64 * h + 64]
        kv[c, pl.ds(pl.multiple_of(128 * k, 128), 128), :] = mixed[:, 192:576].astype(BF)

    project(r)

    def project_step(j, carry):
        rank = peer_rank(j)
        project(rank)
        return carry

    lax.fori_loop(1, 3, project_step, 0)
    far_arrived(xg, k_x)
    lax.fori_loop(3, 4, project_step, 0)
    k_kv = recvs(1)
    send(kv.at[c], kv.at[c], k_kv, core_mate)

    def split_heads(half):
        at = pl.ds(pl.multiple_of(512 * half, 512), 512)
        for h in range(3):
            kh[h, at, 0:64] = kv[half, :, 64 * h : 64 * h + 64]
            vh[h, at, 0:64] = kv[half, :, 192 + 64 * h : 256 + 64 * h]

    split_heads(c)
    arrived(mine_exp, k_wexp)
    arrived(wexp_f.at[f, :, pl.ds(pl.multiple_of(384 * (1 - zh), 128), 384)], k_wexp + 1)
    send(wexp_f.at[f], wexp_f.at[f], k_wexp_y, y_mate)
    send(wexp_f.at[f], wexp_f.at[f], k_wexp_c, core_mate)
    arrived(kv.at[1 - c], k_kv)
    split_heads(1 - c)

    k_a, s_a = recvs(16), sends(16)

    def attend(k, carry):
        outs = []
        for h in range(3):
            scores = dot_nt(q_s[k, h], kh[h])
            top = jnp.max(scores, axis=1, keepdims=True)
            exps = jnp.exp(scores - top).astype(BF)
            e_s[h, k] = exps
            sums = dot_nn(exps, vh[h])
            scale = 1.0 / sums[:, 64:65]
            l_s[h, k] = scale
            outs.append(sums[:, 0:64] * scale)
        both = jnp.concatenate(outs, axis=1)
        a_f[k] = both
        low = both.astype(BF)
        a_b[k] = low
        a_all[r, k] = jnp.concatenate([low[0:64], low[64:128]], axis=1)
        for j in range(1, 4):
            at = 4 * j + k
            copy_to(a_all.at[r, k], a_all.at[r, k], s_a + at, k_a + at, peer(j)).start()
        return carry

    lax.fori_loop(0, 1, attend, 0)
    arrived(wout_p.at[f_y], k_wout_y)
    send(wout_p.at[f_y], wout_p.at[f_y], k_wout_c + 1, core_mate)
    lax.fori_loop(1, 2, attend, 0)
    for k in range(4):
        arrived(ws.at[k, c, :, at_half], k_wshr + k)
    send(ws.at[:, c, :, at_half], ws.at[:, c, :, at_half], k_wshr_y, y_mate)
    send(ws.at[:, c, :, at_half], ws.at[:, c, :, at_half], k_wshr_c, core_mate)
    lax.fori_loop(2, 3, attend, 0)
    arrived(wexp_f.at[f_y], k_wexp_y)
    send(wexp_f.at[f_y], wexp_f.at[f_y], k_wexp_c + 1, core_mate)
    lax.fori_loop(3, 4, attend, 0)
    for j in range(1, 4):
        for k in range(4):
            at = 4 * j + k
            pending.append(
                copy_to(a_all.at[r, k], a_all.at[r, k], s_a + at, k_a + at, peer(j)).wait_send
            )
    send_or_keep(cot, eo, k_e, home)
    def place_out(k):
        for q in range(4):
            w_out[pl.ds(pl.multiple_of(192 * k + 48 * q, 16), 48), :] = jnp.concatenate(
                [wout_p[k, b, :, 96 * q : 96 * q + 96] for b in range(8)], axis=1
            )

    place_out(f)
    place_out(f_y)
    arrived(wout_p.at[2 * y + 1 - c], k_wout_c)
    place_out(2 * y + 1 - c)
    arrived(wout_p.at[2 * (1 - y) + 1 - c], k_wout_c + 1)
    place_out(2 * (1 - y) + 1 - c)
    other_half = pl.ds(pl.multiple_of(384 * (1 - y), 128), 384)
    arrived(ws.at[:, c, :, other_half], k_wshr_y)
    send(ws.at[:, c, :, other_half], ws.at[:, c, :, other_half], k_wshr_c + 1, core_mate)
    for j in range(1, 4):
        for k in range(4):
            arrived(a_all.at[peer_rank(j), k], k_a + 4 * j + k)
    arrived(wexp_f.at[2 * y + 1 - c], k_wexp_c)
    arrived(wexp_f.at[2 * (1 - y) + 1 - c], k_wexp_c + 1)
    arrived(ws.at[:, 1 - c, :, at_half], k_wshr_c)
    arrived(ws.at[:, 1 - c, :, other_half], k_wshr_c + 1)

    def first_norm(k):
        rows = jnp.concatenate(
            [
                jnp.concatenate([a_all[src, k, :, 192 * i : 192 * i + 192] for src in range(4)], axis=1)
                for i in range(2)
            ],
            axis=0,
        )
        first = xg[k].astype(F32) + prm[2:3, :] + dot_nn(rows, w_out[...])
        centre = first - jnp.mean(first, axis=1, keepdims=True)
        inverse = lax.rsqrt(jnp.mean(centre * centre, axis=1, keepdims=True) + 1e-05)
        normed = centre * inverse
        hidden_one = normed * prm[6:7, :] + prm[3:4, :]
        hg[k] = hidden_one.astype(BF)
        return normed, inverse, hidden_one

    def expand(k):
        inner = dot_nn(hg[k], wexp_f[...].reshape(768, 768)) + be
        below = 0.5 * (1.0 + lax.erf(inner * 0.7071067811865476))
        u_s[k] = inner
        dge[k] = below
        active = (inner * below).astype(BF)
        g_s[k] = active
        return dot_nt(active, ws[...].reshape(768, 768))

    k_r1, s_r1 = recvs(4), sends(4)

    def expand_step(i, carry):
        j = 3 - i
        rank = peer_rank(j)
        first_norm(rank)
        yb[j] = expand(rank).astype(BF)
        copy_to(yb.at[j], rs1.at[j], s_r1 + j, k_r1 + j, peer(j)).start()
        return carry

    lax.fori_loop(0, 3, expand_step, 0)
    for j in range(1, 4):
        pending.append(copy_to(yb.at[j], rs1.at[j], s_r1 + j, k_r1 + j, peer(j)).wait_send)
    normed, inverse, hidden_one = first_norm(r)
    n1_s[...] = normed
    r1_s[...] = inverse
    h1_s[...] = hidden_one
    ysum[...] = expand(r)

    def slope(k, carry):
        inner = u_s[k]
        dge[k] = dge[k] + inner * jnp.exp(-0.5 * inner * inner) * 0.3989422804014327
        return carry

    lax.fori_loop(0, 4, slope, 0)

    arrived(eo, k_e)
    upstream = eo[...].astype(F32)
    scaled = upstream * prm[7:8, :]
    scaled_mean = jnp.mean(scaled, axis=1, keepdims=True)
    row_shift_two = row_sum(upstream)
    second = h1_s[...] + prm[4:5, :] + ysum[...]
    for j in range(1, 4):
        arrived(rs1.at[j], k_r1 + j)
        second += rs1[j].astype(F32)
    centre = second - jnp.mean(second, axis=1, keepdims=True)
    inverse = lax.rsqrt(jnp.mean(centre * centre, axis=1, keepdims=True) + 1e-05)
    normed = centre * inverse
    grad_two = inverse * (
        scaled - scaled_mean - normed * jnp.mean(scaled * normed, axis=1, keepdims=True)
    )
    dg[r] = grad_two.astype(BF)
    k_d = recvs(4)
    for j in range(1, 3):
        send(dg.at[r], dg.at[r], k_d + j, peer(j))
    d2_s[...] = grad_two
    ob[...] = (normed * prm[7:8, :] + prm[5:6, :]).astype(BF)
    k_o = recvs(1)
    send_or_keep(ob, ohr, k_o, home)
    row_gain_two = row_sum(upstream * normed)
    row_back = row_sum(grad_two)

    def contract(k):
        inner = dge[k] * dot_nn(dg[k], ws[...].reshape(768, 768))
        low = inner.astype(BF)
        du_s[k] = low
        beg[k] = row_sum(inner)
        return dot_nt(low, wexp_f[...].reshape(768, 768))

    ysum[...] = contract(r)
    k_r2, s_r2 = recvs(4), sends(4)

    def contract_step(j, carry):
        rank = peer_rank(j)
        dh_b[j] = contract(rank).astype(BF)
        copy_to(dh_b.at[j], rs2.at[j], s_r2 + j, k_r2 + j, peer(j)).start()
        return carry

    pass_on(dg, k_d)
    lax.fori_loop(1, 3, contract_step, 0)
    far_arrived(dg, k_d)
    lax.fori_loop(3, 4, contract_step, 0)
    for j in range(1, 4):
        pending.append(copy_to(dh_b.at[j], rs2.at[j], s_r2 + j, k_r2 + j, peer(j)).wait_send)

    for k in range(4):
        rows = dg[:, :, 192 * k : 192 * k + 192].reshape(512, 192)
        gs[k] = dot_tn(rows, g_s[...].reshape(512, 768)).astype(BF).reshape(2, 96, 768)
    k_gs = recvs(1)
    send(gs.at[:, 1 - c], rs_c, k_gs, core_mate)

    def expand_grad(i, carry):
        at = pl.ds(pl.multiple_of(128 * i, 128), 128)
        rows = hg[:, :, at].reshape(512, 128)
        ge[at, :] = dot_tn(rows, du_s[...].reshape(512, 768)).astype(BF)
        return carry

    lax.fori_loop(0, 6, expand_grad, 0)
    k_ge = recvs(2)
    for half in range(2):
        at = pl.ds(pl.multiple_of(192 * (2 * half + 1 - c), 64), 192)
        send(ge.at[at, :], re_c.at[half], k_ge + half, core_mate)
    k_gs_y, k_ge_y = recvs(1), recvs(1)
    arrived(rs_c, k_gs)
    t_shr[...] = (
        gs[:, c, :, other_half].astype(F32) + rs_c[:, :, other_half].astype(F32)
    ).astype(BF)
    send(t_shr, rs_y, k_gs_y, y_mate)

    grad_hidden = d2_s[...] + ysum[...]
    for j in range(1, 4):
        arrived(rs2.at[j], k_r2 + j)
        grad_hidden += rs2[j].astype(F32)
    normed = n1_s[...]
    scaled = grad_hidden * prm[6:7, :]
    grad_one = r1_s[...] * (
        scaled
        - jnp.mean(scaled, axis=1, keepdims=True)
        - normed * jnp.mean(scaled * normed, axis=1, keepdims=True)
    )
    low_one = grad_one.astype(BF)
    d1g[r] = low_one
    for k in range(4):
        dab[k] = dot_nt(low_one, w_out[192 * k : 192 * k + 192, :]).astype(BF)
    k_da, k_d1 = recvs(4), recvs(4)
    for j in range(1, 4):
        send(dab.at[peer_rank(j)], da.at[r], k_da + j, peer(j))
    da[r] = dab[r]
    d1_s[...] = grad_one
    row_gain_one = row_sum(grad_hidden * normed)
    row_shift_one = row_sum(grad_hidden)
    row_out = row_sum(grad_one)

    for half in range(2):
        arrived(re_c.at[half], k_ge + half)
    at_y = pl.ds(pl.multiple_of(192 * f_y, 64), 192)
    at_own = pl.ds(pl.multiple_of(192 * f, 64), 192)
    t_exp[...] = (ge[at_y, :].astype(F32) + re_c[1 - y].astype(F32)).astype(BF)
    send(t_exp, re_y, k_ge_y, y_mate)

    for j in range(1, 4):
        arrived(da.at[peer_rank(j)], k_da + j)
    for j in range(1, 3):
        send(d1g.at[r], d1g.at[r], k_d1 + j, peer(j))

    def attend_back(k, carry):
        outs = []
        grads = da[k].astype(F32)
        dots = grads * a_f[k]
        for h in range(3):
            at = slice(64 * h, 64 * h + 64)
            scale = l_s[h, k]
            delta = jnp.sum(dots[:, at], axis=1, keepdims=True) * scale
            high = delta.astype(BF).astype(F32)
            side = jnp.where(wide[0:128, 0:64] == 0, -high, 0.0)
            side = jnp.where(wide[0:128, 0:64] == 1, high - delta, side)
            both = jnp.concatenate([grads[:, at] * scale, side], axis=1).astype(BF)
            de[k, h] = both
            low = (e_s[h, k].astype(F32) * dot_nt(both, vh[h])).astype(BF)
            ds_s[h, k] = low
            outs.append(dot_nn(low, kh[h])[:, 0:64] * 0.125)
        queries = jnp.concatenate(outs, axis=1)
        qb_s[k] = row_sum(queries)
        dz[k, :, 0:192] = queries.astype(BF)
        return carry

    lax.fori_loop(0, 1, attend_back, 0)
    k_fs, k_re = recvs(4), recvs(1)
    arrived(rs_y, k_gs_y)
    fsb[...] = (
        gs[:, c, :, at_half].astype(F32) + rs_c[:, :, at_half].astype(F32) + rs_y[...].astype(F32)
    ).astype(BF)
    for k in range(4):
        send_or_keep(fsb.at[k], fs.at[zh, x], k_fs + 2 * zh + x, dev(c, y, k, zl))
    lax.fori_loop(1, 2, attend_back, 0)
    arrived(re_y, k_ge_y)
    te_f[...] = ge[at_own, :].astype(F32) + re_c[y].astype(F32) + re_y[...].astype(F32)
    te_b[...] = te_f[:, pl.ds(pl.multiple_of(384 * (1 - zh), 128), 384)].astype(BF)
    send(te_b, re_z, k_re, z_mate)
    lax.fori_loop(2, 3, attend_back, 0)
    pass_on(d1g, k_d1)
    lax.fori_loop(3, 4, attend_back, 0)
    sums = []
    for h in range(3):
        rows = q_s[:, h, :, 0:64].reshape(512, 64)
        sums.append(dot_tn(rows, ds_s[h].reshape(512, 1024)))
    for h in range(3):
        rows = de[:, h, :, 0:64].reshape(512, 64)
        sums.append(dot_tn(rows, e_s[h].reshape(512, 1024)))
    sums = jnp.concatenate(sums, axis=0)
    dkv[0] = sums[:, 0:512].T
    dkv[1] = sums[:, 512:1024].T
    dkb[...] = dkv[1 - c].astype(BF)
    k_dk = recvs(1)
    send(dkb, dkr, k_dk, core_mate)

    def project_grad(first, count):
        for k in range(4):
            rows = xg[:, :, 192 * k : 192 * k + 192].reshape(512, 192)
            cols = dz[:, :, 96 * first : 96 * first + 96 * count].reshape(512, 96 * count)
            part = dot_tn(rows, cols).astype(BF)
            for slot in range(count):
                gi[k, first + slot] = pack(part[:, 96 * slot : 96 * slot + 96])

    some = {"q": pl.ds(0, 2), "kv": pl.ds(2, 4)}
    k_gi = {"q": recvs(2), "kv": recvs(2)}
    k_gi_y = {"q": recvs(1), "kv": recvs(1)}

    def over_cores(which):
        at = some[which]
        for half in range(2):
            send(gi.at[2 * half + 1 - c, at], ri_c.at[half, at], k_gi[which] + half, core_mate)

    def over_y(which):
        at = some[which]
        for half in range(2):
            arrived(ri_c.at[half, at], k_gi[which] + half)
        tib[at] = (gi[f_y, at].astype(F32) + ri_c[1 - y, at].astype(F32)).astype(BF)
        send(tib.at[at], ri_y.at[at], k_gi_y[which], y_mate)

    k_fi = recvs(6)

    def to_owners(which):
        at = some[which]
        arrived(ri_y.at[at], k_gi_y[which])
        ti2[at] = (
            gi[f, at].astype(F32) + ri_c[y, at].astype(F32) + ri_y[at].astype(F32)
        ).astype(BF)
        for slot in range(2) if which == "q" else range(2, 6):
            unit = 8 * (slot // 2) + 2 * r + slot % 2
            send_or_keep(
                ti2.at[slot], fi.at[zh, unit % 3], k_fi + 3 * zh + unit % 3, (unit // 3, seq)
            )

    project_grad(0, 2)
    over_cores("q")

    far_arrived(d1g, k_d1)
    part = dot_tn(a_b[...].reshape(512, 192), d1g[...].reshape(512, 768))
    for b in range(8):
        go[b % 2, b // 2] = pack(part[:, 96 * b : 96 * b + 96].astype(BF))
    k_go = recvs(1)
    send(go.at[1 - c], ro_c, k_go, core_mate)

    arrived(dkr, k_dk)
    keyvals = dkv[c] + dkr[...].astype(F32)
    vb_s[...] = row_sum(keyvals[:, 192:384])
    dz[:, :, 192:576] = keyvals.astype(BF).reshape(4, 128, 384)

    def input_part(k):
        return dot_nt(dz[k], w_in[...])

    k_r3, s_r3 = recvs(8), sends(8)

    def near(buf, j, i):
        return buf.at[j, pl.ds(64 * i, 64)]

    def input_copy(j, i):
        at = 2 * j + i
        return copy_to(near(dx_b, j, i), near(rs3, j, i), s_r3 + at, k_r3 + at, peer(j))

    def input_step(i, carry):
        j = 3 - i
        dx_b[j] = input_part(peer_rank(j)).astype(BF)
        input_copy(j, 0).start()
        return carry

    lax.fori_loop(0, 3, input_step, 0)
    for j in (3, 2, 1):
        input_copy(j, 1).start()
    for j in range(1, 4):
        for i in range(2):
            pending.append(input_copy(j, i).wait_send)
    over_y("q")
    project_grad(2, 4)
    over_cores("kv")

    vg[...] = jnp.zeros((8, 16, 128), F32)
    rows = jnp.concatenate(
        [row_out, row_shift_one, row_back, row_shift_two, row_gain_one, row_gain_two], axis=0
    )
    for b in range(8):
        vg[b, 2:8, 0:96] = rows[:, 96 * b : 96 * b + 96]
    q_row = row_sum(qb_s[:, 0, :])
    v_row = vb_s[...]
    for i in range(2):
        vg[2 * r + i, 0:1, 0:96] = q_row[:, 96 * i : 96 * i + 96]
        vg[2 * r + i, 1:2, 0:96] = v_row[:, 96 * i : 96 * i + 96]
    inner_row = row_sum(beg[:, 0, :])
    for i in range(3):
        vg[r, 8 + i : 9 + i, :] = inner_row[:, 128 * i : 128 * i + 128]
        vg[4 + r, 8 + i : 9 + i, :] = inner_row[:, 384 + 128 * i : 512 + 128 * i]
    k_v = recvs(8)
    for d in range(1, 8):
        other = (ctx + d) % 8
        send(vg.at[other], vr.at[d], k_v + d, (other, seq))

    over_y("kv")
    arrived(ro_c, k_go)
    tob[...] = (go[c].astype(F32) + ro_c[...].astype(F32)).astype(BF)
    k_go_y, k_fo = recvs(1), recvs(2)
    s_go, s_fo = sends(1), sends(4)
    stays = y == zl

    @pl.when(jnp.logical_not(stays))
    def _():
        copy_to(tob, ro_y, s_go, k_go_y, y_mate).start()

    k_gh = recvs(2)
    ysum[...] = d1_s[...] + input_part(r)

    def finish_input(i):
        at = pl.ds(64 * i, 64)
        grad_in = ysum[at, :]
        for j in range(1, 4):
            arrived(near(rs3, j, i), k_r3 + 2 * j + i)
            grad_in += rs3[j, at, :].astype(F32)
        ghb[at, :] = grad_in.astype(BF)
        send_or_keep(ghb.at[at, :], ghr.at[at, :], k_gh + i, home)

    to_owners("q")
    finish_input(0)

    done = []

    for half in range(2):
        for sub in range(2):
            arrived(fs.at[half, sub], k_fs + 2 * half + sub)
    for sub in range(2):
        f_wshr[:, 384 * sub : 384 * sub + 384] = fs[0, sub].astype(F32) + fs[1, sub].astype(F32)
    done.append(local(f_wshr, o_wshr))
    arrived(re_z, k_re)
    f_wexp[...] = te_f[:, pl.ds(pl.multiple_of(384 * zh, 128), 384)] + re_z[...].astype(F32)
    done.append(local(f_wexp, o_wexp))

    finish_input(1)
    to_owners("kv")

    @pl.when(stays)
    def _():
        arrived(ro_y, k_go_y)
        tob2[...] = (tob[...].astype(F32) + ro_y[...].astype(F32)).astype(BF)
        for k in range(4):
            to = dev(c, y, k, x)
            away = jnp.logical_or(to[0] != ctx, to[1] != seq)

            @pl.when(away)
            def _():
                copy_to(tob2.at[k], fo.at[zh], s_fo + k, k_fo + zh, to).start()

            @pl.when(jnp.logical_not(away))
            def _():
                pltpu.make_async_copy(tob2.at[k], fo.at[zh], rsem.at[k_fo + zh]).start()

    def finish_out():
        @pl.when(jnp.logical_not(stays))
        def _():
            copy_to(tob, ro_y, s_go, k_go_y, y_mate).wait_send()

        @pl.when(stays)
        def _():
            for k in range(4):
                to = dev(c, y, k, x)

                @pl.when(jnp.logical_or(to[0] != ctx, to[1] != seq))
                def _():
                    copy_to(tob2.at[k], fo.at[zh], s_fo + k, k_fo + zh, to).wait_send()

    pending.append(finish_out)

    total = vg[ctx]
    for d in range(1, 8):
        arrived(vr.at[d], k_v + d)
        total += vr[d]
    vs1[...] = total
    k_vc = recvs(2)
    send(vs1, vc, k_vc, core_mate)
    arrived(vc, k_vc)
    vs2[...] = vs1[...] + vc[...]
    send(vs2, vy, k_vc + 1, y_mate)

    arrived(ohr, k_o)
    done.append(local(ohr, o_out))
    arrived(vy, k_vc + 1)
    total = vs2[...] + vy[...]
    f_gb[...] = total[0:6, 0:96]
    f_gg[...] = total[6:8, 0:96]
    f_ge[...] = total[8:11, :]
    done += [local(f_gb, o_gb), local(f_gg, o_gg), local(f_ge, o_ge)]
    for half in range(2):
        arrived(fo.at[half], k_fo + half)
    part = fo[0].astype(F32) + fo[1].astype(F32)
    for q in range(4):
        f_wout[48 * q : 48 * q + 48, :] = part[:, 96 * q : 96 * q + 96]
    done.append(local(f_wout, o_wout))
    for half in range(2):
        for j in range(3):
            arrived(fi.at[half, j], k_fi + 3 * half + j)
    parts = [fi[0, j].astype(F32) + fi[1, j].astype(F32) for j in range(3)]
    for q in range(4):
        f_win[48 * q : 48 * q + 48, :] = jnp.concatenate(
            [part[:, 96 * q : 96 * q + 96] for part in parts], axis=1
        )
    done.append(local(f_win, o_win))
    for i in range(2):
        arrived(ghr.at[pl.ds(64 * i, 64), :], k_gh + i)
    done.append(local(ghr, o_gh))
    for finish in pending:
        finish()
    for copy in done:
        copy.wait()


def hand_over(*refs):
    ins, outs, held, into, out_of = refs[0:9], refs[9:18], refs[18:27], refs[27], refs[28]
    loads = [pltpu.make_async_copy(ins[i], held[i], into.at[i]) for i in range(9)]
    stores = [pltpu.make_async_copy(held[i], outs[i], out_of.at[i]) for i in range(9)]
    for load in loads:
        load.start()
    for load, store in zip(loads, stores):
        load.wait()
        store.start()
    for store in stores:
        store.wait()


def fast_shards(
    hidden, project_in, project_out, expand_weight, shrink_weight, biases, gains, expand_bias,
    random_blocks, global_blocks, document_lengths, cotangent,
):
    vm = lambda *dims: pltpu.VMEM(dims, BF)
    vf = lambda *dims: pltpu.VMEM(dims, F32)
    scratch = [
        vm(192, 288), vm(192, 96), vm(3, 48, 384), vm(48, 384), vm(4, 128, 768), vm(128, 768),
        vf(8, 128), vf(4, 8, 128), vf(16, 128), vf(8, 16, 128), vm(4, 6, 48, 384), vm(4, 8, 48, 384),
        vm(4, 192, 768), vm(4, 2, 96, 768), vm(768, 576), vm(768, 768), vf(8, 768),
        vm(4, 128, 128), vm(4, 3, 128, 128), vm(2, 512, 384), vm(3, 1024, 128), vm(3, 1024, 128),
        vm(3, 4, 128, 1024), vf(3, 4, 128, 1), vf(4, 128, 192), vm(4, 128, 192), vm(4, 4, 64, 384),
        vm(4, 128, 768), vf(128, 768), vf(128, 768), vf(128, 1), vf(4, 128, 768), vf(4, 128, 768), vm(4, 128, 768),
        vf(128, 768), vm(4, 128, 768),
        vm(4, 128, 768), vf(128, 768), vm(4, 128, 768), vm(4, 128, 768), vm(4, 128, 768),
        vm(4, 128, 768), vf(4, 1, 768), vf(128, 768), vm(4, 128, 768), vm(4, 128, 192),
        vm(4, 128, 192), vm(4, 3, 128, 128), vm(3, 4, 128, 1024), vf(2, 512, 384), vm(512, 384),
        vm(512, 384), vm(4, 128, 576), vm(4, 128, 768), vm(4, 128, 768),
        vm(4, 2, 96, 768), vm(4, 96, 768), vm(4, 96, 384), vm(4, 96, 384), vm(4, 96, 384),
        vm(2, 2, 96, 384), vm(768, 768), vm(2, 192, 768), vm(192, 768), vm(192, 768), vf(192, 768),
        vm(192, 384), vm(192, 384),
        vm(2, 4, 48, 384), vm(4, 48, 384), vm(4, 48, 384), vm(4, 48, 384), vm(4, 48, 384),
        vm(2, 48, 384), vm(4, 6, 48, 384), vm(2, 6, 48, 384), vm(6, 48, 384), vm(6, 48, 384),
        vm(6, 48, 384), vm(2, 3, 48, 384),
        vf(8, 16, 128), vf(8, 16, 128), vf(16, 128), vf(16, 128), vf(16, 128), vf(16, 128),
        vf(4, 1, 192), vf(1, 192), vm(128, 768), vm(128, 768), vm(128, 768), vm(128, 768),
        vf(192, 288), vf(192, 96), vf(192, 384), vf(96, 768), vf(6, 96), vf(2, 96), vf(3, 128),
        pltpu.SemaphoreType.DMA((SENDS,)), pltpu.SemaphoreType.DMA((RECVS,)),
        pltpu.SemaphoreType.DMA((LOCALS,)),
    ]
    out = lambda kind, *dims: jax.ShapeDtypeStruct(dims, kind)
    shapes = (
        out(BF, 128, 768), out(BF, 128, 768), out(F32, 192, 288), out(F32, 192, 96),
        out(F32, 192, 384), out(F32, 96, 768), out(F32, 6, 96), out(F32, 2, 96), out(F32, 3, 128),
    )
    anywhere = pl.BlockSpec(memory_space=pl.ANY)
    results = pl.pallas_call(
        layer_kernel,
        out_shape=shapes,
        in_specs=[pl.BlockSpec(memory_space=pltpu.SMEM)] * 3
        + [pl.BlockSpec(memory_space=pltpu.VMEM)] * 3
        + [anywhere] * 6,
        out_specs=(anywhere,) * 9,
        scratch_shapes=scratch,
        compiler_params=pltpu.CompilerParams(
            collective_id=0, has_side_effects=True, vmem_limit_bytes=58 * 1024 * 1024
        ),
    )(
        random_blocks[0], global_blocks, document_lengths, biases, gains,
        expand_bias.reshape(3, 128), hidden[0], cotangent[0], project_in, project_out,
        expand_weight, shrink_weight.T,
    )
    results = pl.pallas_call(
        hand_over,
        out_shape=shapes,
        in_specs=[anywhere] * 9,
        out_specs=(anywhere,) * 9,
        scratch_shapes=[pltpu.VMEM(one.shape, one.dtype) for one in shapes]
        + [pltpu.SemaphoreType.DMA((9,))] * 2,
    )(*results)
    return (
        results[0][None], results[1][None], results[2], results[3], results[4], results[5].T,
        results[6], results[7], results[8].reshape(-1),
    )


def solution(mesh):
    small = tuple(mesh.shape[name] for name in ("ctx", "fsdp")) == (8, 4)
    return jax.shard_map(
        fast_shards if small else shards,
        mesh=mesh,
        in_specs=(
            P("fsdp", "ctx", None),
            P("fsdp", "ctx"),
            P("fsdp", "ctx"),
            P("fsdp", "ctx"),
            P("fsdp", "ctx"),
            P(None, "ctx"),
            P(None, "ctx"),
            P("ctx"),
            P("fsdp", "ctx", None),
            P("fsdp", None),
            P("fsdp", None),
            P("fsdp", "ctx", None),
        ),
        out_specs=(
            P("fsdp", "ctx", None),
            P("fsdp", "ctx", None),
            P("fsdp", "ctx"),
            P("fsdp", "ctx"),
            P("fsdp", "ctx"),
            P("fsdp", "ctx"),
            P(None, "ctx"),
            P(None, "ctx"),
            P("ctx"),
        ),
        check_vma=False,
    )
```

```python
import jax
import jax.numpy as jnp
from jax import lax
from jax.experimental import pallas as pl
from jax.experimental.pallas import tpu as pltpu
from jax.sharding import PartitionSpec as P

HEAD_DIM = 64
BLOCK = 64


def segment_of(positions, bounds):
    return jnp.sum((positions[..., None] >= bounds).astype(jnp.int32), axis=-1)


def layer_norm_parts(values, gain_row, shift_row):
    centre = values - jnp.mean(values, axis=-1, keepdims=True)
    inverse = lax.rsqrt(jnp.mean(centre * centre, axis=-1, keepdims=True) + 1e-05)
    normed = centre * inverse
    return (normed * gain_row + shift_row, normed, inverse)


def layer_norm_back(upstream, normed, inverse, gain_row):
    scaled = upstream * gain_row
    return inverse * (
        scaled
        - jnp.mean(scaled, axis=-1, keepdims=True)
        - normed * jnp.mean(scaled * normed, axis=-1, keepdims=True)
    )


def matmul(left_side, right_side):
    return jnp.dot(left_side, right_side, preferred_element_type=jnp.float32)


def matmul_left_t(left_side, right_side):
    return lax.dot_general(
        left_side, right_side, (((0,), (0,)), ((), ())), preferred_element_type=jnp.float32
    )


def matmul_right_t(left_side, right_side):
    return lax.dot_general(
        left_side, right_side, (((1,), (1,)), ((), ())), preferred_element_type=jnp.float32
    )


def over_cols(qkv_grad, out_grad, expand_grad, shrink_grad, vector_grad, gain_grad, inner_grad):
    return (
        lax.psum_scatter(qkv_grad, "ctx", scatter_dimension=1, tiled=True),
        lax.psum_scatter(out_grad, "ctx", scatter_dimension=1, tiled=True),
        lax.psum_scatter(expand_grad, "ctx", scatter_dimension=1, tiled=True),
        lax.psum_scatter(shrink_grad, "ctx", scatter_dimension=1, tiled=True),
        lax.psum_scatter(vector_grad, "ctx", scatter_dimension=1, tiled=True),
        lax.psum_scatter(gain_grad, "ctx", scatter_dimension=1, tiled=True),
        lax.psum_scatter(inner_grad, "ctx", scatter_dimension=1, tiled=True),
    )


def over_rows(qkv_grad, out_grad, expand_grad, shrink_grad):
    return (
        lax.psum_scatter(
            qkv_grad.astype(jnp.bfloat16), "fsdp", scatter_dimension=0, tiled=True
        ).astype(jnp.float32),
        lax.psum_scatter(
            out_grad.astype(jnp.bfloat16), "fsdp", scatter_dimension=0, tiled=True
        ).astype(jnp.float32),
        lax.psum_scatter(
            expand_grad.astype(jnp.bfloat16), "fsdp", scatter_dimension=0, tiled=True
        ).astype(jnp.float32),
        lax.psum_scatter(
            shrink_grad.astype(jnp.bfloat16), "fsdp", scatter_dimension=0, tiled=True
        ).astype(jnp.float32),
    )


def scatter_rows(link_ids, link_grads, row_count, feature_width):
    block_count = row_count // BLOCK
    inside = (link_ids >= 0) & (link_ids < block_count)
    target = jnp.where(inside, link_ids, block_count).reshape(-1)
    partial_value = jnp.zeros((block_count, BLOCK, feature_width), jnp.float32)
    partial_value = partial_value.at[target].add(
        link_grads.reshape(-1, BLOCK, feature_width), mode="drop"
    )
    return partial_value.reshape(row_count, feature_width)


def shards(
    hidden,
    project_in,
    project_out,
    expand_weight,
    shrink_weight,
    biases,
    gains,
    expand_bias,
    random_blocks,
    global_blocks,
    document_lengths,
    cotangent,
):
    inputs = hidden[0]
    tokens_here = inputs.shape[0]
    width = inputs.shape[1]
    head_count = width // HEAD_DIM
    blocks_here = tokens_here // BLOCK
    rand_count = random_blocks.shape[2]
    link_count = 3 + rand_count + global_blocks.shape[1]
    ctx_rank = lax.axis_index("ctx")
    last_block = tokens_here * lax.axis_size("ctx") // BLOCK - 1
    col_full = (
        lax.all_gather(project_in, "ctx", axis=1, tiled=True),
        lax.all_gather(project_out, "ctx", axis=1, tiled=True),
        lax.all_gather(expand_weight, "ctx", axis=1, tiled=True),
        lax.all_gather(shrink_weight, "ctx", axis=1, tiled=True),
        lax.all_gather(biases, "ctx", axis=1, tiled=True),
        lax.all_gather(gains, "ctx", axis=1, tiled=True),
        lax.all_gather(expand_bias.reshape(1, -1), "ctx", axis=1, tiled=True),
    )
    full_qkv, full_out, full_expand, full_shrink = (
        lax.all_gather(col_full[0], "fsdp", axis=0, tiled=True),
        lax.all_gather(col_full[1], "fsdp", axis=0, tiled=True),
        lax.all_gather(col_full[2], "fsdp", axis=0, tiled=True),
        lax.all_gather(col_full[3], "fsdp", axis=0, tiled=True),
    )
    vectors = col_full[4].astype(jnp.float32)
    gain_rows = col_full[5].astype(jnp.float32)
    inner_bias = col_full[6][0].astype(jnp.float32)
    block_ids = ctx_rank * blocks_here + jnp.arange(blocks_here, dtype=jnp.int32)
    window = jnp.stack(
        [jnp.maximum(block_ids - 1, 0), block_ids, jnp.minimum(block_ids + 1, last_block)], axis=1
    )
    global_links = jnp.broadcast_to(
        global_blocks[0][None, :], (blocks_here, global_blocks.shape[1])
    )
    linked_ids = jnp.concatenate([window, random_blocks[0], global_links], axis=1)
    lengths = document_lengths[0]
    doc_order = jnp.arange(lengths.shape[0], dtype=jnp.int32)
    bounds = jnp.sum(
        jnp.where(doc_order[None, :] <= doc_order[:-1, None], lengths[None, :], 0), axis=1
    )
    query_pos = (ctx_rank * tokens_here + jnp.arange(tokens_here, dtype=jnp.int32)).reshape(
        blocks_here, BLOCK
    )
    query_seg = segment_of(query_pos, bounds)
    key_pos = linked_ids[:, :, None] * BLOCK + jnp.arange(BLOCK, dtype=jnp.int32)[None, None, :]
    key_seg = segment_of(key_pos, bounds).reshape(blocks_here, -1)
    allowed = query_seg[:, None, :, None] == key_seg[:, None, None, :]
    zero_row = jnp.zeros((width,), jnp.float32)
    mixed_qkv = (
        matmul(inputs, full_qkv) + jnp.concatenate([vectors[0], zero_row, vectors[1]])
    ).astype(jnp.bfloat16)
    queries = mixed_qkv[:, :width]
    keyvals = mixed_qkv[:, width:]
    shard_piece = lax.all_gather(keyvals, "ctx", axis=0, tiled=True)
    block_count = shard_piece.shape[0] // BLOCK
    stacked = shard_piece.reshape(block_count, BLOCK, shard_piece.shape[1])
    picks = (
        linked_ids.reshape(-1)[:, None] == jnp.arange(block_count, dtype=jnp.int32)[None, :]
    ).astype(jnp.bfloat16)
    linked = jnp.einsum("lb,bkd->lkd", picks, stacked).reshape(
        blocks_here, link_count, BLOCK, 2 * width
    )
    query_heads = queries.reshape(blocks_here, BLOCK, head_count, HEAD_DIM)
    key_heads = linked[..., :width].reshape(blocks_here, link_count * BLOCK, head_count, HEAD_DIM)
    value_heads = linked[..., width:].reshape(blocks_here, link_count * BLOCK, head_count, HEAD_DIM)

    def score_parts():
        raw_scores = (
            jnp.einsum(
                "bqhd,bkhd->bhqk", query_heads, key_heads, preferred_element_type=jnp.float32
            )
            * 0.125
        )
        return jnp.where(allowed, raw_scores, -1e30)

    scores = score_parts()
    top_score = jnp.max(scores, axis=-1, keepdims=True)
    exp_total = jnp.sum(jnp.exp(scores - top_score), axis=-1, keepdims=True)
    attention = jnp.exp(scores - top_score) / exp_total
    attended = jnp.einsum(
        "bhqk,bkhd->bqhd",
        attention.astype(jnp.bfloat16),
        value_heads,
        preferred_element_type=jnp.float32,
    )
    attended = attended.reshape(tokens_here, width).astype(jnp.bfloat16)
    residual_one = inputs.astype(jnp.float32) + matmul(attended, full_out) + vectors[2]
    hidden_one, normed_one, inverse_one = layer_norm_parts(residual_one, gain_rows[0], vectors[3])
    hidden_low = hidden_one.astype(jnp.bfloat16)
    inner_pre = matmul(hidden_low, full_expand) + inner_bias
    activated, gelu_pull = jax.vjp(
        lambda argument: jax.nn.gelu(argument, approximate=False), inner_pre
    )
    active_low = activated.astype(jnp.bfloat16)
    residual_two = hidden_one + matmul(active_low, full_shrink) + vectors[4]
    result, normed_two, inverse_two = layer_norm_parts(residual_two, gain_rows[1], vectors[5])
    upstream = cotangent[0].astype(jnp.float32)
    grad_gain_two = jnp.sum(upstream * normed_two, axis=0)
    grad_shift_two = jnp.sum(upstream, axis=0)
    grad_two = layer_norm_back(upstream, normed_two, inverse_two, gain_rows[1])
    grad_bias_back = jnp.sum(grad_two, axis=0)
    grad_two_low = grad_two.astype(jnp.bfloat16)
    again_cols = (
        lax.all_gather(project_in, "ctx", axis=1, tiled=True),
        lax.all_gather(project_out, "ctx", axis=1, tiled=True),
        lax.all_gather(expand_weight, "ctx", axis=1, tiled=True),
        lax.all_gather(shrink_weight, "ctx", axis=1, tiled=True),
    )
    back_weights = (
        lax.all_gather(again_cols[0], "fsdp", axis=0, tiled=True),
        lax.all_gather(again_cols[1], "fsdp", axis=0, tiled=True),
        lax.all_gather(again_cols[2], "fsdp", axis=0, tiled=True),
        lax.all_gather(again_cols[3], "fsdp", axis=0, tiled=True),
    )
    back_qkv, back_out, back_expand, back_shrink = back_weights
    grad_shrink_w = matmul_left_t(active_low, grad_two_low)
    grad_active = matmul_right_t(grad_two_low, back_shrink)
    grad_inner = gelu_pull(grad_active)[0]
    grad_inner_bias = jnp.sum(grad_inner, axis=0)
    grad_inner_low = grad_inner.astype(jnp.bfloat16)
    grad_expand_w = matmul_left_t(hidden_low, grad_inner_low)
    grad_hidden_one = grad_two + matmul_right_t(grad_inner_low, back_expand)
    grad_gain_one = jnp.sum(grad_hidden_one * normed_one, axis=0)
    grad_shift_one = jnp.sum(grad_hidden_one, axis=0)
    grad_one = layer_norm_back(grad_hidden_one, normed_one, inverse_one, gain_rows[0])
    grad_bias_out = jnp.sum(grad_one, axis=0)
    grad_one_low = grad_one.astype(jnp.bfloat16)
    grad_out_w = matmul_left_t(attended, grad_one_low)
    grad_attended = matmul_right_t(grad_one_low, back_out).astype(jnp.bfloat16)
    grad_attended = grad_attended.reshape(blocks_here, BLOCK, head_count, HEAD_DIM)
    scores = score_parts()
    attention = jnp.exp(scores - top_score) / exp_total
    grad_attention = jnp.einsum(
        "bqhd,bkhd->bhqk", grad_attended, value_heads, preferred_element_type=jnp.float32
    )
    grad_values = jnp.einsum(
        "bhqk,bqhd->bkhd",
        attention.astype(jnp.bfloat16),
        grad_attended,
        preferred_element_type=jnp.float32,
    )
    row_inner = jnp.sum(attention * grad_attention, axis=-1, keepdims=True)
    grad_scores = (attention * (grad_attention - row_inner) * 0.125).astype(jnp.bfloat16)
    grad_queries = jnp.einsum(
        "bhqk,bkhd->bqhd", grad_scores, key_heads, preferred_element_type=jnp.float32
    ).reshape(tokens_here, width)
    grad_keys = jnp.einsum(
        "bhqk,bqhd->bkhd", grad_scores, query_heads, preferred_element_type=jnp.float32
    )
    slot_grads = jnp.concatenate(
        [
            grad_keys.reshape(blocks_here, link_count, BLOCK, width),
            grad_values.reshape(blocks_here, link_count, BLOCK, width),
        ],
        axis=-1,
    )
    grad_keyvals = lax.psum_scatter(
        scatter_rows(linked_ids, slot_grads, tokens_here * lax.axis_size("ctx"), 2 * width),
        "ctx",
        scatter_dimension=0,
        tiled=True,
    )
    grad_mixed = jnp.concatenate([grad_queries, grad_keyvals], axis=1)
    grad_bias_query = jnp.sum(grad_queries, axis=0)
    grad_bias_value = jnp.sum(grad_keyvals[:, width:], axis=0)
    grad_mixed_low = grad_mixed.astype(jnp.bfloat16)
    grad_qkv_w = matmul_left_t(inputs, grad_mixed_low)
    grad_inputs = grad_one + matmul_right_t(grad_mixed_low, back_qkv)
    grad_vectors = jnp.stack(
        [
            grad_bias_query,
            grad_bias_value,
            grad_bias_out,
            grad_shift_one,
            grad_bias_back,
            grad_shift_two,
        ]
    )
    grad_gain_rows = jnp.stack([grad_gain_one, grad_gain_two])
    grad_inner_row = grad_inner_bias[None, :]
    reduced = over_cols(
        grad_qkv_w,
        grad_out_w,
        grad_expand_w,
        grad_shrink_w,
        grad_vectors,
        grad_gain_rows,
        grad_inner_row,
    )
    sum_qkv, sum_out, sum_expand, sum_shrink = over_rows(
        reduced[0], reduced[1], reduced[2], reduced[3]
    )
    final_vectors, final_gains, final_inner = lax.psum((reduced[4], reduced[5], reduced[6]), "fsdp")
    return (
        result.astype(jnp.bfloat16)[None],
        grad_inputs.astype(jnp.bfloat16)[None],
        sum_qkv,
        sum_out,
        sum_expand,
        sum_shrink,
        final_vectors,
        final_gains,
        final_inner.reshape(-1),
    )


MESH = pl.DeviceIdType.MESH
BF = jnp.bfloat16
F32 = jnp.float32
SENDS = 176
RECVS = 176
LOCALS = 24
NEG = -1e30


def dot_nn(a, b):
    return jnp.dot(a, b, preferred_element_type=F32)


def dot_nt(a, b):
    return lax.dot_general(a, b, (((1,), (1,)), ((), ())), preferred_element_type=F32)


def dot_tn(a, b):
    return lax.dot_general(a, b, (((0,), (0,)), ((), ())), preferred_element_type=F32)


def row_sum(values):
    return jnp.sum(values, axis=0, keepdims=True)


def pack(piece):
    return jnp.concatenate([piece[48 * q : 48 * q + 48] for q in range(4)], axis=1)


def layer_kernel(
    rand_hbm, glob_hbm, doc_hbm, bia_hbm, gai_hbm, ebi_hbm, hid, cot, win, wout, wexp, wshr,
    o_out, o_gh, o_win, o_wout, o_wexp, o_wshr, o_gb, o_gg, o_ge,
    winv, woutv, win3, wout1, xg, eo, ms, mg, ps, par, win_p, wout_p, wexp_f, ws, w_in, w_out, prm,
    mq, q_s, kv, kh, vh, e_s, l_s, a_f, a_b, a_all, hg, h1_s, n1_s, r1_s, u_s, dge, g_s, ysum, yb,
    rs1, d2_s, dg, du_s, dh_b, rs2, beg, d1_s, d1g, dab, da, de, ds_s, dkv, dkb, dkr, dz, dx_b, rs3,
    gs, rs_c, t_shr, rs_y, fsb, fs, ge, re_c, t_exp, re_y, te_f, te_b, re_z,
    go, ro_c, tob, ro_y, tob2, fo, gi, ri_c, tib, ri_y, ti2, fi,
    vg, vr, vs1, vc, vs2, vy, qb_s, vb_s, ob, ohr, ghb, ghr,
    f_win, f_wout, f_wexp, f_wshr, f_gb, f_gg, f_ge,
    rand_ref, glob_ref, doc_ref, bia, gai, ebi,
    ssem, rsem, lsem,
):
    ctx = lax.axis_index("ctx")
    seq = lax.axis_index("fsdp")
    z, x = ctx // 2, ctx % 2
    y, c = seq // 2, seq % 2
    zh, zl = z // 2, z % 2
    r = 2 * zl + x
    f = seq

    def dev(px, py, pz, pc):
        return (2 * pz + px, 2 * py + pc)

    def flip(v, on):
        return v + on - 2 * v * on

    def peer(j):
        return dev(flip(x, j % 2), y, 2 * zh + flip(zl, j // 2), c)

    def peer_rank(j):
        return 2 * flip(zl, j // 2) + flip(x, j % 2)

    peers = [peer(j) for j in range(4)]
    ranks = [peer_rank(j) for j in range(4)]
    core_mate = dev(x, y, z, 1 - c)
    y_mate = dev(x, 1 - y, z, c)
    z_mate = dev(x, y, 2 * (1 - zh) + zl, c)
    home = dev(x, y, 2 * c + zl, zh)

    pending = []
    counts = {"s": 0, "r": 0, "l": 0}

    def take(kind, n, most):
        first = counts[kind]
        counts[kind] = first + n
        assert counts[kind] <= most
        return first

    def recvs(n):
        return take("r", n, RECVS)

    def sends(n):
        return take("s", n, SENDS)

    def local(src, dst):
        cp = pltpu.make_async_copy(src, dst, lsem.at[take("l", 1, LOCALS)])
        cp.start()
        return cp

    def copy_to(src, dst, si, ri, to):
        return pltpu.make_async_remote_copy(
            src_ref=src, dst_ref=dst, send_sem=ssem.at[si], recv_sem=rsem.at[ri],
            device_id=to, device_id_type=MESH,
        )

    def send(src, dst, ri, to):
        si = sends(1)
        copy_to(src, dst, si, ri, to).start()
        pending.append(lambda: copy_to(src, dst, si, ri, to).wait_send())

    def send_or_keep(src, dst, ri, to):
        si = sends(1)
        away = jnp.logical_or(to[0] != ctx, to[1] != seq)

        @pl.when(away)
        def _():
            copy_to(src, dst, si, ri, to).start()

        @pl.when(jnp.logical_not(away))
        def _():
            pltpu.make_async_copy(src, dst, rsem.at[ri]).start()

        def finish():
            @pl.when(jnp.logical_or(to[0] != ctx, to[1] != seq))
            def _():
                copy_to(src, dst, si, ri, to).wait_send()

        pending.append(finish)

    def arrived(dst, ri):
        pltpu.make_async_copy(dst, dst, rsem.at[ri]).wait()

    def split(rows):
        return [(1, 0, rows), (2, rows, 128 - rows)]

    def near_parts(buf, rows):
        return [
            (j, buf.at[ranks[j]], buf.at[ranks[j], pl.ds(at, size)] if size else None)
            for j, at, size in split(rows)
        ]

    def pass_on(parts, first):
        for j, block, part in parts:
            arrived(block, first + j)
            if part is not None:
                send(part, part, first + 3 * (2 - j), peers[3 - j])

    def far_arrived(buf, first, rows):
        for j, at, size in split(rows):
            if size:
                arrived(buf.at[ranks[3], pl.ds(at, size)], first + 3 * (2 - j))

    def served(step, services):
        def run(k, carry):
            for at, before, serve in services:
                if before:
                    pl.when(k == at)(serve)
            step(k)
            for at, before, serve in services:
                if not before:
                    pl.when(k == at)(serve)
            return carry

        return run

    barrier = pltpu.get_barrier_semaphore()
    place = 2 * ctx + c
    for d in range(1, 16):
        other = (place + d) % 16
        pl.semaphore_signal(
            barrier, inc=1, device_id=(other // 2, 2 * y + other % 2), device_id_type=MESH
        )
    pl.semaphore_signal(barrier, inc=1, device_id=y_mate, device_id_type=MESH)
    small = [
        local(*pair)
        for pair in ((rand_hbm, rand_ref), (glob_hbm, glob_ref), (doc_hbm, doc_ref), (bia_hbm, bia), (gai_hbm, gai), (ebi_hbm, ebi))
    ]
    in_win, in_wout = local(win, winv), local(wout, woutv)

    for copy in small:
        copy.wait()

    lane = lax.broadcasted_iota(jnp.int32, (1, 128), 1)
    for i in range(2):
        block = 2 * ctx + i
        links = [jnp.maximum(block - 1, 0), block, jnp.minimum(block + 1, 15)]
        links += [rand_ref[i, k] for k in range(3)] + [glob_ref[0, k] for k in range(2)]
        count = jnp.zeros((1, 128), F32)
        for link in links:
            count += jnp.where(jnp.logical_or(lane == link + 72, lane == link + 88), 1.0, 0.0)
        ms[i : i + 1, :] = count
    edge = doc_ref[0, 0]
    edges = jnp.zeros((1, 128), F32)
    for k in range(7):
        edges += jnp.where(lane == k, edge.astype(F32), 0.0)
        edge = edge + doc_ref[0, k + 1]
    ms[2:3, :] = edges
    ms[3:8, :] = jnp.zeros((5, 128), F32)
    ps[...] = jnp.zeros((16, 128), F32)
    ps[0:6, 0:96] = bia[...].astype(F32)
    ps[6:8, 0:96] = gai[...].astype(F32)
    ps[8:11, :] = ebi[...].astype(F32)
    in_win.wait()
    for j in range(3):
        win3[j] = pack(winv[:, 96 * j : 96 * j + 96])

    pl.semaphore_wait(barrier, 16)

    k_h, k_x, k_m, k_e = recvs(1), recvs(4), recvs(4), recvs(1)
    send_or_keep(hid, xg.at[r], k_h, home)
    send_or_keep(ms, mg.at[r], k_m, home)
    k_win = recvs(6)
    for j in range(3):
        unit = 3 * ctx + j
        rank = (unit % 8) // 2
        slot = 2 * (unit // 8) + unit % 2
        for half in range(2):
            send_or_keep(
                win3.at[j], win_p.at[f, slot], k_win + slot, dev(rank % 2, y, 2 * half + rank // 2, c)
            )
    k_par = recvs(8)
    for d in range(1, 8):
        other = (ctx + d) % 8
        send(ps, par.at[ctx], k_par + d, (other, seq))
    par[ctx] = ps[...]
    in_wout.wait()
    wout1[...] = pack(woutv[...])

    arrived(xg.at[r], k_h)
    arrived(mg.at[r], k_m)
    for j in range(1, 4):
        if j < 3:
            send(xg.at[r], xg.at[r], k_x + j, peer(j))
        send(mg.at[r], mg.at[r], k_m + j, peer(j))
    k_wout_y, k_wout_c = recvs(1), recvs(2)
    k_wexp_y, k_wexp_c = recvs(1), recvs(2)
    k_wshr_y, k_wshr_c = recvs(1), recvs(2)
    k_wout = recvs(8)
    for d in range(8):
        other = (ctx + d) % 8
        if d == 0:
            pltpu.make_async_copy(wout1, wout_p.at[f, ctx], rsem.at[k_wout]).start()
        else:
            send(wout1, wout_p.at[f, ctx], k_wout + d, (other, seq))


    def sided(positions, rows):
        segs = jnp.zeros((rows, 1), F32)
        for k in range(7):
            segs += jnp.where(positions >= mg[r, 2:3, k : k + 1], 1.0, 0.0)
        return segs

    wide = lax.broadcasted_iota(jnp.int32, (1024, 128), 1)
    key_row = lax.broadcasted_iota(jnp.int32, (1024, 1), 0)
    key_segs = sided(key_row.astype(F32), 1024).astype(jnp.int32) + 64
    hot = jnp.logical_or(
        jnp.logical_and(wide < 72, wide == key_segs),
        jnp.logical_and(
            wide >= 72,
            jnp.logical_or(wide == key_row // 64 + 72, wide == key_row // 64 + 88),
        ),
    )
    hot = jnp.where(hot, 1.0, 0.0).astype(BF)
    ones = jnp.where(jnp.logical_or(wide == 64, wide == 65), 1.0, 0.0).astype(BF)
    for h in range(3):
        kh[h, :, 64:128] = hot[:, 64:128]
        vh[h, :, 64:128] = ones[:, 64:128]

    k_win_y, k_win_c = recvs(1), recvs(2)
    for slot in range(6):
        arrived(win_p.at[f, slot], k_win + slot)
    send(win_p.at[f], win_p.at[f], k_win_y, y_mate)
    send(win_p.at[f], win_p.at[f], k_win_c, core_mate)
    pass_on(near_parts(xg, 64), k_x)
    k_wexp = recvs(2)
    mine_exp = wexp_f.at[f, :, pl.ds(pl.multiple_of(384 * zh, 128), 384)]
    pltpu.make_async_copy(wexp, mine_exp, rsem.at[k_wexp]).start()
    send(wexp, mine_exp, k_wexp + 1, z_mate)

    for d in range(1, 8):
        arrived(par.at[(ctx + 8 - d) % 8], k_par + d)
    prm[...] = jnp.concatenate([par[b, 0:8, 0:96] for b in range(8)], axis=1)
    be = jnp.concatenate(
        [par[r, 8 + i : 9 + i, :] for i in range(3)] + [par[4 + r, 8 + i : 9 + i, :] for i in range(3)],
        axis=1,
    )
    zrow = jnp.zeros((1, 192), F32)
    z_bias = jnp.concatenate(
        [par[2 * r, 0:1, 0:96], par[2 * r + 1, 0:1, 0:96], zrow, par[2 * r, 1:2, 0:96], par[2 * r + 1, 1:2, 0:96]],
        axis=1,
    )

    row_pos = lax.broadcasted_iota(jnp.int32, (512, 1), 0) + 512 * c
    row_segs = sided(row_pos.astype(F32), 512).astype(jnp.int32) + 64
    for j in range(1, 4):
        arrived(mg.at[peer_rank(j)], k_m + j)
    for i in range(8):
        count = mg[i // 2, i % 2 : i % 2 + 1, :]
        logs = jnp.log(jnp.maximum(count, 1.0))
        high = logs.astype(BF).astype(F32)
        line = jnp.where(lane < 88, jnp.where(count > 0.5, high, NEG), logs - high)
        line = jnp.where(lane < 104, line, 0.0)
        same = row_segs[64 * i : 64 * i + 64] == wide[0:64]
        block = jnp.where(wide[0:64] < 72, jnp.where(same, 0.0, NEG), line)
        mq[i // 2, 64 * (i % 2) : 64 * (i % 2) + 64, :] = block.astype(BF)
    for h in range(3):
        q_s[:, h, :, 64:128] = mq[:, :, 64:128]

    f_y = 2 * (1 - y) + c
    arrived(win_p.at[f_y], k_win_y)
    send(win_p.at[f_y], win_p.at[f_y], k_win_c + 1, core_mate)
    for d in range(8):
        arrived(wout_p.at[f, (ctx + 8 - d) % 8], k_wout + d)
    send(wout_p.at[f], wout_p.at[f], k_wout_y, y_mate)
    send(wout_p.at[f], wout_p.at[f], k_wout_c, core_mate)
    k_wshr = recvs(4)
    at_half = pl.ds(pl.multiple_of(384 * y, 128), 384)
    for sub in range(2):
        for half in range(2):
            send_or_keep(
                wshr.at[:, 384 * sub : 384 * sub + 384], ws.at[2 * zh + zl, x, :, at_half],
                k_wshr + 2 * zh + zl, dev(sub, y, 2 * half + c, x),
            )


    def place_in(k):
        for q in range(4):
            w_in[pl.ds(pl.multiple_of(192 * k + 48 * q, 16), 48), :] = jnp.concatenate(
                [win_p[k, i, :, 96 * q : 96 * q + 96] for i in range(6)], axis=1
            )

    place_in(f)
    place_in(f_y)
    arrived(win_p.at[2 * y + 1 - c], k_win_c)
    place_in(2 * y + 1 - c)
    arrived(win_p.at[2 * (1 - y) + 1 - c], k_win_c + 1)
    place_in(2 * (1 - y) + 1 - c)

    def project(k):
        mixed = dot_nn(xg[k], w_in[...]) + z_bias
        queries = (mixed[:, 0:192].astype(BF).astype(F32) * 0.125).astype(BF)
        for h in range(3):
            q_s[k, h, :, 0:64] = queries[:, 64 * h : 64 * h + 64]
        kv[c, pl.ds(pl.multiple_of(128 * k, 128), 128), :] = mixed[:, 192:576].astype(BF)

    lax.fori_loop(
        0, 4,
        served(lambda j: project(peer_rank(j)), [(3, True, lambda: far_arrived(xg, k_x, 64))]), 0,
    )
    k_kv = recvs(1)
    send(kv.at[c], kv.at[c], k_kv, core_mate)

    def split_heads(half):
        at = pl.ds(pl.multiple_of(512 * half, 512), 512)
        for h in range(3):
            kh[h, at, 0:64] = kv[half, :, 64 * h : 64 * h + 64]
            vh[h, at, 0:64] = kv[half, :, 192 + 64 * h : 256 + 64 * h]

    split_heads(c)
    arrived(mine_exp, k_wexp)
    arrived(wexp_f.at[f, :, pl.ds(pl.multiple_of(384 * (1 - zh), 128), 384)], k_wexp + 1)
    send(wexp_f.at[f], wexp_f.at[f], k_wexp_y, y_mate)
    send(wexp_f.at[f], wexp_f.at[f], k_wexp_c, core_mate)
    arrived(kv.at[1 - c], k_kv)
    split_heads(1 - c)

    k_a, s_a = recvs(16), sends(16)

    def attend(k):
        outs = []
        for h in range(3):
            scores = dot_nt(q_s[k, h], kh[h])
            top = jnp.max(scores, axis=1, keepdims=True)
            exps = jnp.exp(scores - top).astype(BF)
            e_s[h, k] = exps
            sums = dot_nn(exps, vh[h])
            scale = 1.0 / sums[:, 64:65]
            l_s[h, k] = scale
            outs.append(sums[:, 0:64] * scale)
        both = jnp.concatenate(outs, axis=1)
        a_f[k] = both
        low = both.astype(BF)
        a_b[k] = low
        a_all[r, k] = jnp.concatenate([low[0:64], low[64:128]], axis=1)
        for j in range(1, 4):
            at = 4 * j + k
            copy_to(a_all.at[r, k], a_all.at[r, k], s_a + at, k_a + at, peers[j]).start()

    wout_there, wexp_there = wout_p.at[f_y], wexp_f.at[f_y]
    ws_mine = ws.at[:, c, :, at_half]

    def relay_0():
        arrived(wout_there, k_wout_y)
        send(wout_there, wout_there, k_wout_c + 1, core_mate)

    def relay_1():
        for k in range(4):
            arrived(ws.at[k, c, :, at_half], k_wshr + k)
        send(ws_mine, ws_mine, k_wshr_y, y_mate)
        send(ws_mine, ws_mine, k_wshr_c, core_mate)

    def relay_2():
        arrived(wexp_there, k_wexp_y)
        send(wexp_there, wexp_there, k_wexp_c + 1, core_mate)

    lax.fori_loop(0, 4, served(attend, [(0, False, relay_0), (1, False, relay_1), (2, False, relay_2)]), 0)
    for j in range(1, 4):
        for k in range(4):
            at = 4 * j + k
            pending.append(
                copy_to(a_all.at[r, k], a_all.at[r, k], s_a + at, k_a + at, peer(j)).wait_send
            )
    send_or_keep(cot, eo, k_e, home)
    def place_out(k):
        for q in range(4):
            w_out[pl.ds(pl.multiple_of(192 * k + 48 * q, 16), 48), :] = jnp.concatenate(
                [wout_p[k, b, :, 96 * q : 96 * q + 96] for b in range(8)], axis=1
            )

    place_out(f)
    place_out(f_y)
    arrived(wout_p.at[2 * y + 1 - c], k_wout_c)
    place_out(2 * y + 1 - c)
    arrived(wout_p.at[2 * (1 - y) + 1 - c], k_wout_c + 1)
    place_out(2 * (1 - y) + 1 - c)
    other_half = pl.ds(pl.multiple_of(384 * (1 - y), 128), 384)
    arrived(ws.at[:, c, :, other_half], k_wshr_y)
    send(ws.at[:, c, :, other_half], ws.at[:, c, :, other_half], k_wshr_c + 1, core_mate)
    for j in range(1, 4):
        for k in range(4):
            arrived(a_all.at[peer_rank(j), k], k_a + 4 * j + k)
    arrived(wexp_f.at[2 * y + 1 - c], k_wexp_c)
    arrived(wexp_f.at[2 * (1 - y) + 1 - c], k_wexp_c + 1)

    def first_norm(k):
        rows = jnp.concatenate(
            [
                jnp.concatenate([a_all[src, k, :, 192 * i : 192 * i + 192] for src in range(4)], axis=1)
                for i in range(2)
            ],
            axis=0,
        )
        first = xg[k].astype(F32) + prm[2:3, :] + dot_nn(rows, w_out[...])
        centre = first - jnp.mean(first, axis=1, keepdims=True)
        inverse = lax.rsqrt(jnp.mean(centre * centre, axis=1, keepdims=True) + 1e-05)
        normed = centre * inverse
        hidden_one = normed * prm[6:7, :] + prm[3:4, :]
        hg[k] = hidden_one.astype(BF)
        return normed, inverse, hidden_one

    def expand(k):
        inner = dot_nn(hg[k], wexp_f[...].reshape(768, 768)) + be
        below = 0.5 * (1.0 + lax.erf(inner * 0.7071067811865476))
        u_s[k] = inner
        dge[k] = below
        active = (inner * below).astype(BF)
        g_s[k] = active

    def widen(k):
        normed, inverse, hidden_one = first_norm(k)
        n1_s[...] = normed
        r1_s[...] = inverse
        h1_s[...] = hidden_one
        expand(k)

    widen(ranks[3])
    arrived(ws.at[:, 1 - c, :, at_half], k_wshr_c)
    arrived(ws.at[:, 1 - c, :, other_half], k_wshr_c + 1)
    k_r1, s_r1 = recvs(4), sends(4)

    def expand_step(i, carry):
        j = 3 - i
        rank = peer_rank(j)

        @pl.when(i > 0)
        def _():
            widen(rank)

        value = dot_nt(g_s[rank], ws[...].reshape(768, 768))

        @pl.when(i < 3)
        def _():
            yb[j] = value.astype(BF)
            copy_to(yb.at[j], rs1.at[j], s_r1 + j, k_r1 + j, peer(j)).start()

        @pl.when(i == 3)
        def _():
            ysum[...] = value

        return carry

    lax.fori_loop(0, 4, expand_step, 0)
    for j in range(1, 4):
        pending.append(copy_to(yb.at[j], rs1.at[j], s_r1 + j, k_r1 + j, peer(j)).wait_send)

    def slope(k, carry):
        inner = u_s[k]
        dge[k] = dge[k] + inner * jnp.exp(-0.5 * inner * inner) * 0.3989422804014327
        return carry

    lax.fori_loop(0, 4, slope, 0)

    arrived(eo, k_e)
    upstream = eo[...].astype(F32)
    scaled = upstream * prm[7:8, :]
    scaled_mean = jnp.mean(scaled, axis=1, keepdims=True)
    row_shift_two = row_sum(upstream)
    second = h1_s[...] + prm[4:5, :] + ysum[...]
    for j in range(1, 4):
        arrived(rs1.at[j], k_r1 + j)
        second += rs1[j].astype(F32)
    centre = second - jnp.mean(second, axis=1, keepdims=True)
    inverse = lax.rsqrt(jnp.mean(centre * centre, axis=1, keepdims=True) + 1e-05)
    normed = centre * inverse
    grad_two = inverse * (
        scaled - scaled_mean - normed * jnp.mean(scaled * normed, axis=1, keepdims=True)
    )
    dg[r] = grad_two.astype(BF)
    k_d = recvs(4)
    for j in range(1, 3):
        send(dg.at[r], dg.at[r], k_d + j, peer(j))
    d2_s[...] = grad_two
    ob[...] = (normed * prm[7:8, :] + prm[5:6, :]).astype(BF)
    k_o = recvs(1)
    send_or_keep(ob, ohr, k_o, home)
    row_gain_two = row_sum(upstream * normed)
    row_back = row_sum(grad_two)

    def contract(k):
        inner = dge[k] * dot_nn(dg[k], ws[...].reshape(768, 768))
        low = inner.astype(BF)
        du_s[k] = low
        beg[k] = row_sum(inner)
        return dot_nt(low, wexp_f[...].reshape(768, 768))

    k_r2, s_r2 = recvs(4), sends(4)

    def contract_step(j):
        value = contract(peer_rank(j))

        @pl.when(j == 0)
        def _():
            ysum[...] = value

        @pl.when(j > 0)
        def _():
            dh_b[j] = value.astype(BF)
            copy_to(dh_b.at[j], rs2.at[j], s_r2 + j, k_r2 + j, peer(j)).start()

    dg_parts = near_parts(dg, 64)
    gathered = [
        (1, True, lambda: pass_on(dg_parts, k_d)),
        (3, True, lambda: far_arrived(dg, k_d, 64)),
    ]
    lax.fori_loop(0, 4, served(contract_step, gathered), 0)
    for j in range(1, 4):
        pending.append(copy_to(dh_b.at[j], rs2.at[j], s_r2 + j, k_r2 + j, peer(j)).wait_send)

    for k in range(4):
        rows = dg[:, :, 192 * k : 192 * k + 192].reshape(512, 192)
        gs[k] = dot_tn(rows, g_s[...].reshape(512, 768)).astype(BF).reshape(2, 96, 768)
    k_gs = recvs(1)
    send(gs.at[:, 1 - c], rs_c, k_gs, core_mate)

    def expand_grad(i, carry):
        at = pl.ds(pl.multiple_of(128 * i, 128), 128)
        rows = hg[:, :, at].reshape(512, 128)
        ge[at, :] = dot_tn(rows, du_s[...].reshape(512, 768)).astype(BF)
        return carry

    lax.fori_loop(0, 6, expand_grad, 0)
    k_ge = recvs(2)
    for half in range(2):
        at = pl.ds(pl.multiple_of(192 * (2 * half + 1 - c), 64), 192)
        send(ge.at[at, :], re_c.at[half], k_ge + half, core_mate)
    k_gs_y, k_ge_y = recvs(1), recvs(1)
    arrived(rs_c, k_gs)
    t_shr[...] = (
        gs[:, c, :, other_half].astype(F32) + rs_c[:, :, other_half].astype(F32)
    ).astype(BF)
    send(t_shr, rs_y, k_gs_y, y_mate)

    grad_hidden = d2_s[...] + ysum[...]
    for j in range(1, 4):
        arrived(rs2.at[j], k_r2 + j)
        grad_hidden += rs2[j].astype(F32)
    normed = n1_s[...]
    scaled = grad_hidden * prm[6:7, :]
    grad_one = r1_s[...] * (
        scaled
        - jnp.mean(scaled, axis=1, keepdims=True)
        - normed * jnp.mean(scaled * normed, axis=1, keepdims=True)
    )
    low_one = grad_one.astype(BF)
    d1g[r] = low_one
    for k in range(4):
        dab[k] = dot_nt(low_one, w_out[192 * k : 192 * k + 192, :]).astype(BF)
    k_da, k_d1 = recvs(4), recvs(4)
    for j in range(1, 4):
        send(dab.at[peer_rank(j)], da.at[r], k_da + j, peer(j))
    da[r] = dab[r]
    d1_s[...] = grad_one
    row_gain_one = row_sum(grad_hidden * normed)
    row_shift_one = row_sum(grad_hidden)
    row_out = row_sum(grad_one)

    for half in range(2):
        arrived(re_c.at[half], k_ge + half)
    at_y = pl.ds(pl.multiple_of(192 * f_y, 64), 192)
    at_own = pl.ds(pl.multiple_of(192 * f, 64), 192)
    t_exp[...] = (ge[at_y, :].astype(F32) + re_c[1 - y].astype(F32)).astype(BF)
    send(t_exp, re_y, k_ge_y, y_mate)

    for j in range(1, 4):
        arrived(da.at[peer_rank(j)], k_da + j)
    for j in range(1, 3):
        send(d1g.at[r], d1g.at[r], k_d1 + j, peer(j))

    def attend_back(k):
        outs = []
        grads = da[k].astype(F32)
        dots = grads * a_f[k]
        for h in range(3):
            at = slice(64 * h, 64 * h + 64)
            scale = l_s[h, k]
            delta = jnp.sum(dots[:, at], axis=1, keepdims=True) * scale
            high = delta.astype(BF).astype(F32)
            side = jnp.where(wide[0:128, 0:64] == 0, -high, 0.0)
            side = jnp.where(wide[0:128, 0:64] == 1, high - delta, side)
            both = jnp.concatenate([grads[:, at] * scale, side], axis=1).astype(BF)
            de[k, h] = both
            low = (e_s[h, k].astype(F32) * dot_nt(both, vh[h])).astype(BF)
            ds_s[h, k] = low
            outs.append(dot_nn(low, kh[h])[:, 0:64] * 0.125)
        queries = jnp.concatenate(outs, axis=1)
        qb_s[k] = row_sum(queries)
        dz[k, :, 0:192] = queries.astype(BF)

    k_fs, k_re = recvs(4), recvs(1)
    shrink_owners = [dev(c, y, k, zl) for k in range(4)]
    fs_at = fs.at[zh, x]
    fsb_at = [fsb.at[k] for k in range(4)]
    k_own = k_fs + 2 * zh + x

    def pass_0():
        arrived(rs_y, k_gs_y)
        fsb[...] = (
            gs[:, c, :, at_half].astype(F32) + rs_c[:, :, at_half].astype(F32) + rs_y[...].astype(F32)
        ).astype(BF)
        for k in range(4):
            send_or_keep(fsb_at[k], fs_at, k_own, shrink_owners[k])

    def pass_1():
        arrived(re_y, k_ge_y)
        te_f[...] = ge[at_own, :].astype(F32) + re_c[y].astype(F32) + re_y[...].astype(F32)
        te_b[...] = te_f[:, pl.ds(pl.multiple_of(384 * (1 - zh), 128), 384)].astype(BF)
        send(te_b, re_z, k_re, z_mate)

    d1g_parts = near_parts(d1g, 0)

    def pass_2():
        pass_on(d1g_parts, k_d1)

    lax.fori_loop(0, 4, served(attend_back, [(0, False, pass_0), (1, False, pass_1), (2, False, pass_2)]), 0)
    sums = []
    for h in range(3):
        rows = q_s[:, h, :, 0:64].reshape(512, 64)
        sums.append(dot_tn(rows, ds_s[h].reshape(512, 1024)))
    for h in range(3):
        rows = de[:, h, :, 0:64].reshape(512, 64)
        sums.append(dot_tn(rows, e_s[h].reshape(512, 1024)))
    sums = jnp.concatenate(sums, axis=0)
    dkv[0] = sums[:, 0:512].T
    dkv[1] = sums[:, 512:1024].T
    dkb[...] = dkv[1 - c].astype(BF)
    k_dk = recvs(1)
    send(dkb, dkr, k_dk, core_mate)

    def project_grad(first, count):
        for k in range(4):
            rows = xg[:, :, 192 * k : 192 * k + 192].reshape(512, 192)
            cols = dz[:, :, 96 * first : 96 * first + 96 * count].reshape(512, 96 * count)
            part = dot_tn(rows, cols).astype(BF)
            for slot in range(count):
                gi[k, first + slot] = pack(part[:, 96 * slot : 96 * slot + 96])

    some = {"q": pl.ds(0, 2), "kv": pl.ds(2, 4)}
    k_gi = {"q": recvs(2), "kv": recvs(2)}
    k_gi_y = {"q": recvs(1), "kv": recvs(1)}

    def over_cores(which):
        at = some[which]
        for half in range(2):
            send(gi.at[2 * half + 1 - c, at], ri_c.at[half, at], k_gi[which] + half, core_mate)

    def over_y(which):
        at = some[which]
        for half in range(2):
            arrived(ri_c.at[half, at], k_gi[which] + half)
        tib[at] = (gi[f_y, at].astype(F32) + ri_c[1 - y, at].astype(F32)).astype(BF)
        send(tib.at[at], ri_y.at[at], k_gi_y[which], y_mate)

    k_fi = recvs(6)

    def to_owners(which):
        at = some[which]
        arrived(ri_y.at[at], k_gi_y[which])
        ti2[at] = (
            gi[f, at].astype(F32) + ri_c[y, at].astype(F32) + ri_y[at].astype(F32)
        ).astype(BF)
        for slot in range(2) if which == "q" else range(2, 6):
            unit = 8 * (slot // 2) + 2 * r + slot % 2
            send_or_keep(
                ti2.at[slot], fi.at[zh, unit % 3], k_fi + 3 * zh + unit % 3, (unit // 3, seq)
            )

    project_grad(0, 2)
    over_cores("q")

    arrived(dkr, k_dk)
    keyvals = dkv[c] + dkr[...].astype(F32)
    vb_s[...] = row_sum(keyvals[:, 192:384])
    dz[:, :, 192:576] = keyvals.astype(BF).reshape(4, 128, 384)

    def input_part(k):
        return dot_nt(dz[k], w_in[...])

    k_r3, s_r3 = recvs(8), sends(8)

    def near(buf, j, i):
        return buf.at[j, pl.ds(64 * i, 64)]

    def input_copy(j, i):
        at = 2 * j + i
        return copy_to(near(dx_b, j, i), near(rs3, j, i), s_r3 + at, k_r3 + at, peer(j))

    def input_step(i, carry):
        j = 3 - i
        dx_b[j] = input_part(peer_rank(j)).astype(BF)
        input_copy(j, 0).start()
        return carry

    lax.fori_loop(0, 3, input_step, 0)
    for j in (3, 2, 1):
        input_copy(j, 1).start()
    for j in range(1, 4):
        for i in range(2):
            pending.append(input_copy(j, i).wait_send)
    over_y("q")
    project_grad(2, 4)
    over_cores("kv")

    far_arrived(d1g, k_d1, 0)
    part = dot_tn(a_b[...].reshape(512, 192), d1g[...].reshape(512, 768))
    for b in range(8):
        go[b % 2, b // 2] = pack(part[:, 96 * b : 96 * b + 96].astype(BF))
    k_go = recvs(1)
    send(go.at[1 - c], ro_c, k_go, core_mate)

    vg[...] = jnp.zeros((8, 16, 128), F32)
    rows = jnp.concatenate(
        [row_out, row_shift_one, row_back, row_shift_two, row_gain_one, row_gain_two], axis=0
    )
    for b in range(8):
        vg[b, 2:8, 0:96] = rows[:, 96 * b : 96 * b + 96]
    q_row = row_sum(qb_s[:, 0, :])
    v_row = vb_s[...]
    for i in range(2):
        vg[2 * r + i, 0:1, 0:96] = q_row[:, 96 * i : 96 * i + 96]
        vg[2 * r + i, 1:2, 0:96] = v_row[:, 96 * i : 96 * i + 96]
    inner_row = row_sum(beg[:, 0, :])
    for i in range(3):
        vg[r, 8 + i : 9 + i, :] = inner_row[:, 128 * i : 128 * i + 128]
        vg[4 + r, 8 + i : 9 + i, :] = inner_row[:, 384 + 128 * i : 512 + 128 * i]
    k_v = recvs(8)
    for d in range(1, 8):
        other = (ctx + d) % 8
        send(vg.at[other], vr.at[d], k_v + d, (other, seq))

    over_y("kv")
    arrived(ro_c, k_go)
    tob[...] = (go[c].astype(F32) + ro_c[...].astype(F32)).astype(BF)
    k_go_y, k_fo = recvs(1), recvs(2)
    s_go, s_fo = sends(1), sends(4)
    stays = y == zl

    @pl.when(jnp.logical_not(stays))
    def _():
        copy_to(tob, ro_y, s_go, k_go_y, y_mate).start()

    k_gh = recvs(2)
    ysum[...] = d1_s[...] + input_part(r)

    def finish_input(i):
        at = pl.ds(64 * i, 64)
        grad_in = ysum[at, :]
        for j in range(1, 4):
            arrived(near(rs3, j, i), k_r3 + 2 * j + i)
            grad_in += rs3[j, at, :].astype(F32)
        ghb[at, :] = grad_in.astype(BF)
        send_or_keep(ghb.at[at, :], ghr.at[at, :], k_gh + i, home)

    to_owners("q")
    finish_input(0)

    done = []

    for half in range(2):
        for sub in range(2):
            arrived(fs.at[half, sub], k_fs + 2 * half + sub)
    for sub in range(2):
        f_wshr[:, 384 * sub : 384 * sub + 384] = fs[0, sub].astype(F32) + fs[1, sub].astype(F32)
    done.append(local(f_wshr, o_wshr))
    arrived(re_z, k_re)
    f_wexp[...] = te_f[:, pl.ds(pl.multiple_of(384 * zh, 128), 384)] + re_z[...].astype(F32)
    done.append(local(f_wexp, o_wexp))

    finish_input(1)
    to_owners("kv")

    @pl.when(stays)
    def _():
        arrived(ro_y, k_go_y)
        tob2[...] = (tob[...].astype(F32) + ro_y[...].astype(F32)).astype(BF)
        for k in range(4):
            to = dev(c, y, k, x)
            away = jnp.logical_or(to[0] != ctx, to[1] != seq)

            @pl.when(away)
            def _():
                copy_to(tob2.at[k], fo.at[zh], s_fo + k, k_fo + zh, to).start()

            @pl.when(jnp.logical_not(away))
            def _():
                pltpu.make_async_copy(tob2.at[k], fo.at[zh], rsem.at[k_fo + zh]).start()

    def finish_out():
        @pl.when(jnp.logical_not(stays))
        def _():
            copy_to(tob, ro_y, s_go, k_go_y, y_mate).wait_send()

        @pl.when(stays)
        def _():
            for k in range(4):
                to = dev(c, y, k, x)

                @pl.when(jnp.logical_or(to[0] != ctx, to[1] != seq))
                def _():
                    copy_to(tob2.at[k], fo.at[zh], s_fo + k, k_fo + zh, to).wait_send()

    pending.append(finish_out)

    total = vg[ctx]
    for d in range(1, 8):
        arrived(vr.at[d], k_v + d)
        total += vr[d]
    vs1[...] = total
    k_vc = recvs(2)
    send(vs1, vc, k_vc, core_mate)
    arrived(vc, k_vc)
    vs2[...] = vs1[...] + vc[...]
    send(vs2, vy, k_vc + 1, y_mate)

    arrived(ohr, k_o)
    done.append(local(ohr, o_out))
    arrived(vy, k_vc + 1)
    total = vs2[...] + vy[...]
    f_gb[...] = total[0:6, 0:96]
    f_gg[...] = total[6:8, 0:96]
    f_ge[...] = total[8:11, :]
    done += [local(f_gb, o_gb), local(f_gg, o_gg), local(f_ge, o_ge)]
    for half in range(2):
        arrived(fo.at[half], k_fo + half)
    part = fo[0].astype(F32) + fo[1].astype(F32)
    for q in range(4):
        f_wout[48 * q : 48 * q + 48, :] = part[:, 96 * q : 96 * q + 96]
    done.append(local(f_wout, o_wout))
    for half in range(2):
        for j in range(3):
            arrived(fi.at[half, j], k_fi + 3 * half + j)
    parts = [fi[0, j].astype(F32) + fi[1, j].astype(F32) for j in range(3)]
    for q in range(4):
        f_win[48 * q : 48 * q + 48, :] = jnp.concatenate(
            [part[:, 96 * q : 96 * q + 96] for part in parts], axis=1
        )
    done.append(local(f_win, o_win))
    for i in range(2):
        arrived(ghr.at[pl.ds(64 * i, 64), :], k_gh + i)
    done.append(local(ghr, o_gh))
    for finish in pending:
        finish()
    for copy in done:
        copy.wait()


def hand_over(*refs):
    ins, outs, held, into, out_of = refs[0:9], refs[9:18], refs[18:27], refs[27], refs[28]
    loads = [pltpu.make_async_copy(ins[i], held[i], into.at[i]) for i in range(9)]
    stores = [pltpu.make_async_copy(held[i], outs[i], out_of.at[i]) for i in range(9)]
    for load in loads:
        load.start()
    for load, store in zip(loads, stores):
        load.wait()
        store.start()
    for store in stores:
        store.wait()


def fast_shards(
    hidden, project_in, project_out, expand_weight, shrink_weight, biases, gains, expand_bias,
    random_blocks, global_blocks, document_lengths, cotangent,
):
    vm = lambda *dims: pltpu.VMEM(dims, BF)
    vf = lambda *dims: pltpu.VMEM(dims, F32)
    scratch = [
        vm(192, 288), vm(192, 96), vm(3, 48, 384), vm(48, 384), vm(4, 128, 768), vm(128, 768),
        vf(8, 128), vf(4, 8, 128), vf(16, 128), vf(8, 16, 128), vm(4, 6, 48, 384), vm(4, 8, 48, 384),
        vm(4, 192, 768), vm(4, 2, 96, 768), vm(768, 576), vm(768, 768), vf(8, 768),
        vm(4, 128, 128), vm(4, 3, 128, 128), vm(2, 512, 384), vm(3, 1024, 128), vm(3, 1024, 128),
        vm(3, 4, 128, 1024), vf(3, 4, 128, 1), vf(4, 128, 192), vm(4, 128, 192), vm(4, 4, 64, 384),
        vm(4, 128, 768), vf(128, 768), vf(128, 768), vf(128, 1), vf(4, 128, 768), vf(4, 128, 768), vm(4, 128, 768),
        vf(128, 768), vm(4, 128, 768),
        vm(4, 128, 768), vf(128, 768), vm(4, 128, 768), vm(4, 128, 768), vm(4, 128, 768),
        vm(4, 128, 768), vf(4, 1, 768), vf(128, 768), vm(4, 128, 768), vm(4, 128, 192),
        vm(4, 128, 192), vm(4, 3, 128, 128), vm(3, 4, 128, 1024), vf(2, 512, 384), vm(512, 384),
        vm(512, 384), vm(4, 128, 576), vm(4, 128, 768), vm(4, 128, 768),
        vm(4, 2, 96, 768), vm(4, 96, 768), vm(4, 96, 384), vm(4, 96, 384), vm(4, 96, 384),
        vm(2, 2, 96, 384), vm(768, 768), vm(2, 192, 768), vm(192, 768), vm(192, 768), vf(192, 768),
        vm(192, 384), vm(192, 384),
        vm(2, 4, 48, 384), vm(4, 48, 384), vm(4, 48, 384), vm(4, 48, 384), vm(4, 48, 384),
        vm(2, 48, 384), vm(4, 6, 48, 384), vm(2, 6, 48, 384), vm(6, 48, 384), vm(6, 48, 384),
        vm(6, 48, 384), vm(2, 3, 48, 384),
        vf(8, 16, 128), vf(8, 16, 128), vf(16, 128), vf(16, 128), vf(16, 128), vf(16, 128),
        vf(4, 1, 192), vf(1, 192), vm(128, 768), vm(128, 768), vm(128, 768), vm(128, 768),
        vf(192, 288), vf(192, 96), vf(192, 384), vf(96, 768), vf(6, 96), vf(2, 96), vf(3, 128),
        pltpu.SMEM((2, 3), jnp.int32), pltpu.SMEM((1, 2), jnp.int32), pltpu.SMEM((1, 8), jnp.int32),
        vm(6, 96), vm(2, 96), vm(3, 128),
        pltpu.SemaphoreType.DMA((SENDS,)), pltpu.SemaphoreType.DMA((RECVS,)),
        pltpu.SemaphoreType.DMA((LOCALS,)),
    ]
    out = lambda kind, *dims: jax.ShapeDtypeStruct(dims, kind)
    shapes = (
        out(BF, 128, 768), out(BF, 128, 768), out(F32, 192, 288), out(F32, 192, 96),
        out(F32, 192, 384), out(F32, 96, 768), out(F32, 6, 96), out(F32, 2, 96), out(F32, 3, 128),
    )
    anywhere = pl.BlockSpec(memory_space=pl.ANY)
    results = pl.pallas_call(
        layer_kernel,
        out_shape=shapes,
        in_specs=[anywhere] * 12,
        out_specs=(anywhere,) * 9,
        scratch_shapes=scratch,
        compiler_params=pltpu.CompilerParams(
            collective_id=0, has_side_effects=True, vmem_limit_bytes=58 * 1024 * 1024
        ),
    )(
        random_blocks[0], global_blocks, document_lengths, biases, gains,
        expand_bias.reshape(3, 128), hidden[0], cotangent[0], project_in, project_out,
        expand_weight, shrink_weight.T,
    )
    results = pl.pallas_call(
        hand_over,
        out_shape=shapes,
        in_specs=[anywhere] * 9,
        out_specs=(anywhere,) * 9,
        scratch_shapes=[pltpu.VMEM(one.shape, one.dtype) for one in shapes]
        + [pltpu.SemaphoreType.DMA((9,))] * 2,
    )(*results)
    return (
        results[0][None], results[1][None], results[2], results[3], results[4], results[5].T,
        results[6], results[7], results[8].reshape(-1),
    )


def solution(mesh):
    small = tuple(mesh.shape[name] for name in ("ctx", "fsdp")) == (8, 4)
    return jax.shard_map(
        fast_shards if small else shards,
        mesh=mesh,
        in_specs=(
            P("fsdp", "ctx", None),
            P("fsdp", "ctx"),
            P("fsdp", "ctx"),
            P("fsdp", "ctx"),
            P("fsdp", "ctx"),
            P(None, "ctx"),
            P(None, "ctx"),
            P("ctx"),
            P("fsdp", "ctx", None),
            P("fsdp", None),
            P("fsdp", None),
            P("fsdp", "ctx", None),
        ),
        out_specs=(
            P("fsdp", "ctx", None),
            P("fsdp", "ctx", None),
            P("fsdp", "ctx"),
            P("fsdp", "ctx"),
            P("fsdp", "ctx"),
            P("fsdp", "ctx"),
            P(None, "ctx"),
            P(None, "ctx"),
            P("ctx"),
        ),
        check_vma=False,
    )
```

```python
import jax
import jax.numpy as jnp
from jax import lax
from jax.experimental import pallas as pl
from jax.experimental.pallas import tpu as pltpu
from jax.sharding import PartitionSpec as P

HEAD_DIM = 64
BLOCK = 64


def segment_of(positions, bounds):
    return jnp.sum((positions[..., None] >= bounds).astype(jnp.int32), axis=-1)


def layer_norm_parts(values, gain_row, shift_row):
    centre = values - jnp.mean(values, axis=-1, keepdims=True)
    inverse = lax.rsqrt(jnp.mean(centre * centre, axis=-1, keepdims=True) + 1e-05)
    normed = centre * inverse
    return (normed * gain_row + shift_row, normed, inverse)


def layer_norm_back(upstream, normed, inverse, gain_row):
    scaled = upstream * gain_row
    return inverse * (
        scaled
        - jnp.mean(scaled, axis=-1, keepdims=True)
        - normed * jnp.mean(scaled * normed, axis=-1, keepdims=True)
    )


def matmul(left_side, right_side):
    return jnp.dot(left_side, right_side, preferred_element_type=jnp.float32)


def matmul_left_t(left_side, right_side):
    return lax.dot_general(
        left_side, right_side, (((0,), (0,)), ((), ())), preferred_element_type=jnp.float32
    )


def matmul_right_t(left_side, right_side):
    return lax.dot_general(
        left_side, right_side, (((1,), (1,)), ((), ())), preferred_element_type=jnp.float32
    )


def over_cols(qkv_grad, out_grad, expand_grad, shrink_grad, vector_grad, gain_grad, inner_grad):
    return (
        lax.psum_scatter(qkv_grad, "ctx", scatter_dimension=1, tiled=True),
        lax.psum_scatter(out_grad, "ctx", scatter_dimension=1, tiled=True),
        lax.psum_scatter(expand_grad, "ctx", scatter_dimension=1, tiled=True),
        lax.psum_scatter(shrink_grad, "ctx", scatter_dimension=1, tiled=True),
        lax.psum_scatter(vector_grad, "ctx", scatter_dimension=1, tiled=True),
        lax.psum_scatter(gain_grad, "ctx", scatter_dimension=1, tiled=True),
        lax.psum_scatter(inner_grad, "ctx", scatter_dimension=1, tiled=True),
    )


def over_rows(qkv_grad, out_grad, expand_grad, shrink_grad):
    return (
        lax.psum_scatter(
            qkv_grad.astype(jnp.bfloat16), "fsdp", scatter_dimension=0, tiled=True
        ).astype(jnp.float32),
        lax.psum_scatter(
            out_grad.astype(jnp.bfloat16), "fsdp", scatter_dimension=0, tiled=True
        ).astype(jnp.float32),
        lax.psum_scatter(
            expand_grad.astype(jnp.bfloat16), "fsdp", scatter_dimension=0, tiled=True
        ).astype(jnp.float32),
        lax.psum_scatter(
            shrink_grad.astype(jnp.bfloat16), "fsdp", scatter_dimension=0, tiled=True
        ).astype(jnp.float32),
    )


def scatter_rows(link_ids, link_grads, row_count, feature_width):
    block_count = row_count // BLOCK
    inside = (link_ids >= 0) & (link_ids < block_count)
    target = jnp.where(inside, link_ids, block_count).reshape(-1)
    partial_value = jnp.zeros((block_count, BLOCK, feature_width), jnp.float32)
    partial_value = partial_value.at[target].add(
        link_grads.reshape(-1, BLOCK, feature_width), mode="drop"
    )
    return partial_value.reshape(row_count, feature_width)


def shards(
    hidden,
    project_in,
    project_out,
    expand_weight,
    shrink_weight,
    biases,
    gains,
    expand_bias,
    random_blocks,
    global_blocks,
    document_lengths,
    cotangent,
):
    inputs = hidden[0]
    tokens_here = inputs.shape[0]
    width = inputs.shape[1]
    head_count = width // HEAD_DIM
    blocks_here = tokens_here // BLOCK
    rand_count = random_blocks.shape[2]
    link_count = 3 + rand_count + global_blocks.shape[1]
    ctx_rank = lax.axis_index("ctx")
    last_block = tokens_here * lax.axis_size("ctx") // BLOCK - 1
    col_full = (
        lax.all_gather(project_in, "ctx", axis=1, tiled=True),
        lax.all_gather(project_out, "ctx", axis=1, tiled=True),
        lax.all_gather(expand_weight, "ctx", axis=1, tiled=True),
        lax.all_gather(shrink_weight, "ctx", axis=1, tiled=True),
        lax.all_gather(biases, "ctx", axis=1, tiled=True),
        lax.all_gather(gains, "ctx", axis=1, tiled=True),
        lax.all_gather(expand_bias.reshape(1, -1), "ctx", axis=1, tiled=True),
    )
    full_qkv, full_out, full_expand, full_shrink = (
        lax.all_gather(col_full[0], "fsdp", axis=0, tiled=True),
        lax.all_gather(col_full[1], "fsdp", axis=0, tiled=True),
        lax.all_gather(col_full[2], "fsdp", axis=0, tiled=True),
        lax.all_gather(col_full[3], "fsdp", axis=0, tiled=True),
    )
    vectors = col_full[4].astype(jnp.float32)
    gain_rows = col_full[5].astype(jnp.float32)
    inner_bias = col_full[6][0].astype(jnp.float32)
    block_ids = ctx_rank * blocks_here + jnp.arange(blocks_here, dtype=jnp.int32)
    window = jnp.stack(
        [jnp.maximum(block_ids - 1, 0), block_ids, jnp.minimum(block_ids + 1, last_block)], axis=1
    )
    global_links = jnp.broadcast_to(
        global_blocks[0][None, :], (blocks_here, global_blocks.shape[1])
    )
    linked_ids = jnp.concatenate([window, random_blocks[0], global_links], axis=1)
    lengths = document_lengths[0]
    doc_order = jnp.arange(lengths.shape[0], dtype=jnp.int32)
    bounds = jnp.sum(
        jnp.where(doc_order[None, :] <= doc_order[:-1, None], lengths[None, :], 0), axis=1
    )
    query_pos = (ctx_rank * tokens_here + jnp.arange(tokens_here, dtype=jnp.int32)).reshape(
        blocks_here, BLOCK
    )
    query_seg = segment_of(query_pos, bounds)
    key_pos = linked_ids[:, :, None] * BLOCK + jnp.arange(BLOCK, dtype=jnp.int32)[None, None, :]
    key_seg = segment_of(key_pos, bounds).reshape(blocks_here, -1)
    allowed = query_seg[:, None, :, None] == key_seg[:, None, None, :]
    zero_row = jnp.zeros((width,), jnp.float32)
    mixed_qkv = (
        matmul(inputs, full_qkv) + jnp.concatenate([vectors[0], zero_row, vectors[1]])
    ).astype(jnp.bfloat16)
    queries = mixed_qkv[:, :width]
    keyvals = mixed_qkv[:, width:]
    shard_piece = lax.all_gather(keyvals, "ctx", axis=0, tiled=True)
    block_count = shard_piece.shape[0] // BLOCK
    stacked = shard_piece.reshape(block_count, BLOCK, shard_piece.shape[1])
    picks = (
        linked_ids.reshape(-1)[:, None] == jnp.arange(block_count, dtype=jnp.int32)[None, :]
    ).astype(jnp.bfloat16)
    linked = jnp.einsum("lb,bkd->lkd", picks, stacked).reshape(
        blocks_here, link_count, BLOCK, 2 * width
    )
    query_heads = queries.reshape(blocks_here, BLOCK, head_count, HEAD_DIM)
    key_heads = linked[..., :width].reshape(blocks_here, link_count * BLOCK, head_count, HEAD_DIM)
    value_heads = linked[..., width:].reshape(blocks_here, link_count * BLOCK, head_count, HEAD_DIM)

    def score_parts():
        raw_scores = (
            jnp.einsum(
                "bqhd,bkhd->bhqk", query_heads, key_heads, preferred_element_type=jnp.float32
            )
            * 0.125
        )
        return jnp.where(allowed, raw_scores, -1e30)

    scores = score_parts()
    top_score = jnp.max(scores, axis=-1, keepdims=True)
    exp_total = jnp.sum(jnp.exp(scores - top_score), axis=-1, keepdims=True)
    attention = jnp.exp(scores - top_score) / exp_total
    attended = jnp.einsum(
        "bhqk,bkhd->bqhd",
        attention.astype(jnp.bfloat16),
        value_heads,
        preferred_element_type=jnp.float32,
    )
    attended = attended.reshape(tokens_here, width).astype(jnp.bfloat16)
    residual_one = inputs.astype(jnp.float32) + matmul(attended, full_out) + vectors[2]
    hidden_one, normed_one, inverse_one = layer_norm_parts(residual_one, gain_rows[0], vectors[3])
    hidden_low = hidden_one.astype(jnp.bfloat16)
    inner_pre = matmul(hidden_low, full_expand) + inner_bias
    activated, gelu_pull = jax.vjp(
        lambda argument: jax.nn.gelu(argument, approximate=False), inner_pre
    )
    active_low = activated.astype(jnp.bfloat16)
    residual_two = hidden_one + matmul(active_low, full_shrink) + vectors[4]
    result, normed_two, inverse_two = layer_norm_parts(residual_two, gain_rows[1], vectors[5])
    upstream = cotangent[0].astype(jnp.float32)
    grad_gain_two = jnp.sum(upstream * normed_two, axis=0)
    grad_shift_two = jnp.sum(upstream, axis=0)
    grad_two = layer_norm_back(upstream, normed_two, inverse_two, gain_rows[1])
    grad_bias_back = jnp.sum(grad_two, axis=0)
    grad_two_low = grad_two.astype(jnp.bfloat16)
    again_cols = (
        lax.all_gather(project_in, "ctx", axis=1, tiled=True),
        lax.all_gather(project_out, "ctx", axis=1, tiled=True),
        lax.all_gather(expand_weight, "ctx", axis=1, tiled=True),
        lax.all_gather(shrink_weight, "ctx", axis=1, tiled=True),
    )
    back_weights = (
        lax.all_gather(again_cols[0], "fsdp", axis=0, tiled=True),
        lax.all_gather(again_cols[1], "fsdp", axis=0, tiled=True),
        lax.all_gather(again_cols[2], "fsdp", axis=0, tiled=True),
        lax.all_gather(again_cols[3], "fsdp", axis=0, tiled=True),
    )
    back_qkv, back_out, back_expand, back_shrink = back_weights
    grad_shrink_w = matmul_left_t(active_low, grad_two_low)
    grad_active = matmul_right_t(grad_two_low, back_shrink)
    grad_inner = gelu_pull(grad_active)[0]
    grad_inner_bias = jnp.sum(grad_inner, axis=0)
    grad_inner_low = grad_inner.astype(jnp.bfloat16)
    grad_expand_w = matmul_left_t(hidden_low, grad_inner_low)
    grad_hidden_one = grad_two + matmul_right_t(grad_inner_low, back_expand)
    grad_gain_one = jnp.sum(grad_hidden_one * normed_one, axis=0)
    grad_shift_one = jnp.sum(grad_hidden_one, axis=0)
    grad_one = layer_norm_back(grad_hidden_one, normed_one, inverse_one, gain_rows[0])
    grad_bias_out = jnp.sum(grad_one, axis=0)
    grad_one_low = grad_one.astype(jnp.bfloat16)
    grad_out_w = matmul_left_t(attended, grad_one_low)
    grad_attended = matmul_right_t(grad_one_low, back_out).astype(jnp.bfloat16)
    grad_attended = grad_attended.reshape(blocks_here, BLOCK, head_count, HEAD_DIM)
    scores = score_parts()
    attention = jnp.exp(scores - top_score) / exp_total
    grad_attention = jnp.einsum(
        "bqhd,bkhd->bhqk", grad_attended, value_heads, preferred_element_type=jnp.float32
    )
    grad_values = jnp.einsum(
        "bhqk,bqhd->bkhd",
        attention.astype(jnp.bfloat16),
        grad_attended,
        preferred_element_type=jnp.float32,
    )
    row_inner = jnp.sum(attention * grad_attention, axis=-1, keepdims=True)
    grad_scores = (attention * (grad_attention - row_inner) * 0.125).astype(jnp.bfloat16)
    grad_queries = jnp.einsum(
        "bhqk,bkhd->bqhd", grad_scores, key_heads, preferred_element_type=jnp.float32
    ).reshape(tokens_here, width)
    grad_keys = jnp.einsum(
        "bhqk,bqhd->bkhd", grad_scores, query_heads, preferred_element_type=jnp.float32
    )
    slot_grads = jnp.concatenate(
        [
            grad_keys.reshape(blocks_here, link_count, BLOCK, width),
            grad_values.reshape(blocks_here, link_count, BLOCK, width),
        ],
        axis=-1,
    )
    grad_keyvals = lax.psum_scatter(
        scatter_rows(linked_ids, slot_grads, tokens_here * lax.axis_size("ctx"), 2 * width),
        "ctx",
        scatter_dimension=0,
        tiled=True,
    )
    grad_mixed = jnp.concatenate([grad_queries, grad_keyvals], axis=1)
    grad_bias_query = jnp.sum(grad_queries, axis=0)
    grad_bias_value = jnp.sum(grad_keyvals[:, width:], axis=0)
    grad_mixed_low = grad_mixed.astype(jnp.bfloat16)
    grad_qkv_w = matmul_left_t(inputs, grad_mixed_low)
    grad_inputs = grad_one + matmul_right_t(grad_mixed_low, back_qkv)
    grad_vectors = jnp.stack(
        [
            grad_bias_query,
            grad_bias_value,
            grad_bias_out,
            grad_shift_one,
            grad_bias_back,
            grad_shift_two,
        ]
    )
    grad_gain_rows = jnp.stack([grad_gain_one, grad_gain_two])
    grad_inner_row = grad_inner_bias[None, :]
    reduced = over_cols(
        grad_qkv_w,
        grad_out_w,
        grad_expand_w,
        grad_shrink_w,
        grad_vectors,
        grad_gain_rows,
        grad_inner_row,
    )
    sum_qkv, sum_out, sum_expand, sum_shrink = over_rows(
        reduced[0], reduced[1], reduced[2], reduced[3]
    )
    final_vectors, final_gains, final_inner = lax.psum((reduced[4], reduced[5], reduced[6]), "fsdp")
    return (
        result.astype(jnp.bfloat16)[None],
        grad_inputs.astype(jnp.bfloat16)[None],
        sum_qkv,
        sum_out,
        sum_expand,
        sum_shrink,
        final_vectors,
        final_gains,
        final_inner.reshape(-1),
    )


MESH = pl.DeviceIdType.MESH
BF = jnp.bfloat16
F32 = jnp.float32
SENDS = 192
RECVS = 192
LOCALS = 24
NEG = -1e30


def dot_nn(a, b):
    return jnp.dot(a, b, preferred_element_type=F32)


def dot_nt(a, b):
    return lax.dot_general(a, b, (((1,), (1,)), ((), ())), preferred_element_type=F32)


def dot_tn(a, b):
    return lax.dot_general(a, b, (((0,), (0,)), ((), ())), preferred_element_type=F32)


def row_sum(values):
    return jnp.sum(values, axis=0, keepdims=True)


def pack(piece):
    return jnp.concatenate([piece[48 * q : 48 * q + 48] for q in range(4)], axis=1)


def layer_kernel(
    rand_hbm, glob_hbm, doc_hbm, bia_hbm, gai_hbm, ebi_hbm, hid, cot, win, wout, wexp, wshr,
    o_out, o_gh, o_win, o_wout, o_wexp, o_wshr, o_gb, o_gg, o_ge,
    winv, woutv, win3, wout1, xg, eo, ms, mg, ps, par, win_p, wout_p, wexp_f, ws, w_in, w_out, prm,
    mq, q_s, kv, kh, vh, e_s, l_s, a_f, a_b, a_all, hg, h1_s, n1_s, r1_s, u_s, dge, g_s, ysum, yb,
    rd1, rd3, rs1, d2_s, dg, du_s, dh_b, rs2, beg, d1_s, d1g, dab, da, de, ds_s, dkv, dkb, dkr, dz, dx_b, rs3,
    gs, rs_c, t_shr, rs_y, fsb, fs, ge, re_c, t_exp, re_y, te_f, te_b, re_z,
    go, ro_c, tob, ro_y, tob2, fo, gi, ri_c, tib, ri_y, ti2, fi,
    vg, vr, vs1, vc, vs2, vy, qb_s, vb_s, ob, ohr, ghb, ghr,
    f_win, f_wout, f_wexp, f_wshr, f_gb, f_gg, f_ge,
    rand_ref, glob_ref, doc_ref, bia, gai, ebi,
    ssem, rsem, lsem,
):
    ctx = lax.axis_index("ctx")
    seq = lax.axis_index("fsdp")
    z, x = ctx // 2, ctx % 2
    y, c = seq // 2, seq % 2
    zh, zl = z // 2, z % 2
    r = 2 * zl + x
    f = seq

    def dev(px, py, pz, pc):
        return (2 * pz + px, 2 * py + pc)

    def flip(v, on):
        return v + on - 2 * v * on

    def peer(j):
        return dev(flip(x, j % 2), y, 2 * zh + flip(zl, j // 2), c)

    def peer_rank(j):
        return 2 * flip(zl, j // 2) + flip(x, j % 2)

    peers = [peer(j) for j in range(4)]
    ranks = [peer_rank(j) for j in range(4)]
    core_mate = dev(x, y, z, 1 - c)
    y_mate = dev(x, 1 - y, z, c)
    z_mate = dev(x, y, 2 * (1 - zh) + zl, c)
    home = dev(x, y, 2 * c + zl, zh)

    pending = []
    counts = {"s": 0, "r": 0, "l": 0}

    def take(kind, n, most):
        first = counts[kind]
        counts[kind] = first + n
        assert counts[kind] <= most
        return first

    def recvs(n):
        return take("r", n, RECVS)

    def sends(n):
        return take("s", n, SENDS)

    def local(src, dst):
        cp = pltpu.make_async_copy(src, dst, lsem.at[take("l", 1, LOCALS)])
        cp.start()
        return cp

    def copy_to(src, dst, si, ri, to):
        return pltpu.make_async_remote_copy(
            src_ref=src, dst_ref=dst, send_sem=ssem.at[si], recv_sem=rsem.at[ri],
            device_id=to, device_id_type=MESH,
        )

    def send(src, dst, ri, to):
        si = sends(1)
        copy_to(src, dst, si, ri, to).start()
        pending.append(lambda: copy_to(src, dst, si, ri, to).wait_send())

    def send_or_keep(src, dst, ri, to):
        si = sends(1)
        away = jnp.logical_or(to[0] != ctx, to[1] != seq)

        @pl.when(away)
        def _():
            copy_to(src, dst, si, ri, to).start()

        @pl.when(jnp.logical_not(away))
        def _():
            pltpu.make_async_copy(src, dst, rsem.at[ri]).start()

        def finish():
            @pl.when(jnp.logical_or(to[0] != ctx, to[1] != seq))
            def _():
                copy_to(src, dst, si, ri, to).wait_send()

        pending.append(finish)

    def arrived(dst, ri):
        pltpu.make_async_copy(dst, dst, rsem.at[ri]).wait()

    def split(rows):
        return [(1, 0, rows), (2, rows, 128 - rows)]

    def near_parts(buf, rows):
        return [
            (j, buf.at[ranks[j]], buf.at[ranks[j], pl.ds(at, size)] if size else None)
            for j, at, size in split(rows)
        ]

    def pass_on(parts, first):
        for j, block, part in parts:
            arrived(block, first + j)
            if part is not None:
                send(part, part, first + 3 * (2 - j), peers[3 - j])

    def far_arrived(buf, first, rows):
        for j, at, size in split(rows):
            if size:
                arrived(buf.at[ranks[3], pl.ds(at, size)], first + 3 * (2 - j))

    def merging(out, rs, rd):
        k_rs, s_rs, k_rd, s_rd = recvs(4), sends(4), recvs(2), sends(2)

        def to_near(i):
            return copy_to(
                out.at[3, pl.ds(64 * i, 64)], rd.at[i], s_rd + i, k_rd + i, peers[1 + i]
            )

        def to_peer(j, i):
            at = 2 * (j - 1) + i
            rows = pl.ds(64 * i, 64)
            return copy_to(out.at[j, rows], rs.at[j, rows], s_rs + at, k_rs + at, peers[j])

        def far_done():
            for i in range(2):
                to_near(i).start()

        def merge():
            for j, i in ((2, 0), (1, 1)):
                arrived(rd.at[i], k_rd + i)
                rows = pl.ds(64 * i, 64)
                out[j, rows] = (out[j, rows].astype(F32) + rd[i].astype(F32)).astype(BF)
                to_peer(j, i).start()

        def finish():
            for i in range(2):
                to_near(i).wait_send()
                for j in (1, 2):
                    to_peer(j, i).wait_send()

        def here(j, i):
            arrived(rs.at[j, pl.ds(64 * i, 64)], k_rs + 2 * (j - 1) + i)

        pending.append(finish)
        return far_done, lambda: to_peer(2, 1).start(), lambda: to_peer(1, 0).start(), merge, here

    def served(step, services):
        def run(k, carry):
            for at, before, serve in services:
                if before:
                    pl.when(k == at)(serve)
            step(k)
            for at, before, serve in services:
                if not before:
                    pl.when(k == at)(serve)
            return carry

        return run

    barrier = pltpu.get_barrier_semaphore()
    place = 2 * ctx + c
    for d in range(1, 16):
        other = (place + d) % 16
        pl.semaphore_signal(
            barrier, inc=1, device_id=(other // 2, 2 * y + other % 2), device_id_type=MESH
        )
    pl.semaphore_signal(barrier, inc=1, device_id=y_mate, device_id_type=MESH)
    small = [
        local(*pair)
        for pair in ((rand_hbm, rand_ref), (glob_hbm, glob_ref), (doc_hbm, doc_ref), (bia_hbm, bia), (gai_hbm, gai), (ebi_hbm, ebi))
    ]
    in_win, in_wout = local(win, winv), local(wout, woutv)

    for copy in small:
        copy.wait()

    lane = lax.broadcasted_iota(jnp.int32, (1, 128), 1)
    for i in range(2):
        block = 2 * ctx + i
        links = [jnp.maximum(block - 1, 0), block, jnp.minimum(block + 1, 15)]
        links += [rand_ref[i, k] for k in range(3)] + [glob_ref[0, k] for k in range(2)]
        count = jnp.zeros((1, 128), F32)
        for link in links:
            count += jnp.where(jnp.logical_or(lane == link + 72, lane == link + 88), 1.0, 0.0)
        ms[i : i + 1, :] = count
    edge = doc_ref[0, 0]
    edges = jnp.zeros((1, 128), F32)
    for k in range(7):
        edges += jnp.where(lane == k, edge.astype(F32), 0.0)
        edge = edge + doc_ref[0, k + 1]
    ms[2:3, :] = edges
    ms[3:8, :] = jnp.zeros((5, 128), F32)
    ps[...] = jnp.zeros((16, 128), F32)
    ps[0:6, 0:96] = bia[...].astype(F32)
    ps[6:8, 0:96] = gai[...].astype(F32)
    ps[8:11, :] = ebi[...].astype(F32)
    in_win.wait()
    for j in range(3):
        win3[j] = pack(winv[:, 96 * j : 96 * j + 96])

    pl.semaphore_wait(barrier, 16)

    k_h, k_x, k_m, k_e = recvs(1), recvs(4), recvs(4), recvs(1)
    send_or_keep(hid, xg.at[r], k_h, home)
    send_or_keep(ms, mg.at[r], k_m, home)
    k_win = recvs(6)
    for j in range(3):
        unit = 3 * ctx + j
        rank = (unit % 8) // 2
        slot = 2 * (unit // 8) + unit % 2
        for half in range(2):
            send_or_keep(
                win3.at[j], win_p.at[f, slot], k_win + slot, dev(rank % 2, y, 2 * half + rank // 2, c)
            )
    k_par = recvs(8)
    for d in range(1, 8):
        other = (ctx + d) % 8
        send(ps, par.at[ctx], k_par + d, (other, seq))
    par[ctx] = ps[...]
    in_wout.wait()
    wout1[...] = pack(woutv[...])

    arrived(xg.at[r], k_h)
    arrived(mg.at[r], k_m)
    for j in range(1, 4):
        if j < 3:
            send(xg.at[r], xg.at[r], k_x + j, peer(j))
        send(mg.at[r], mg.at[r], k_m + j, peer(j))
    k_wout_y, k_wout_c = recvs(1), recvs(2)
    k_wexp_y, k_wexp_c = recvs(1), recvs(2)
    k_wshr_y, k_wshr_c = recvs(1), recvs(2)
    k_wout = recvs(8)
    for d in range(8):
        other = (ctx + d) % 8
        if d == 0:
            pltpu.make_async_copy(wout1, wout_p.at[f, ctx], rsem.at[k_wout]).start()
        else:
            send(wout1, wout_p.at[f, ctx], k_wout + d, (other, seq))


    def sided(positions, rows):
        segs = jnp.zeros((rows, 1), F32)
        for k in range(7):
            segs += jnp.where(positions >= mg[r, 2:3, k : k + 1], 1.0, 0.0)
        return segs

    wide = lax.broadcasted_iota(jnp.int32, (1024, 128), 1)
    key_row = lax.broadcasted_iota(jnp.int32, (1024, 1), 0)
    key_segs = sided(key_row.astype(F32), 1024).astype(jnp.int32) + 64
    hot = jnp.logical_or(
        jnp.logical_and(wide < 72, wide == key_segs),
        jnp.logical_and(
            wide >= 72,
            jnp.logical_or(wide == key_row // 64 + 72, wide == key_row // 64 + 88),
        ),
    )
    hot = jnp.where(hot, 1.0, 0.0).astype(BF)
    ones = jnp.where(jnp.logical_or(wide == 64, wide == 65), 1.0, 0.0).astype(BF)
    for h in range(3):
        kh[h, :, 64:128] = hot[:, 64:128]
        vh[h, :, 64:128] = ones[:, 64:128]

    k_win_y, k_win_c = recvs(1), recvs(2)
    for slot in range(6):
        arrived(win_p.at[f, slot], k_win + slot)
    send(win_p.at[f], win_p.at[f], k_win_y, y_mate)
    send(win_p.at[f], win_p.at[f], k_win_c, core_mate)
    pass_on(near_parts(xg, 64), k_x)
    k_wexp = recvs(2)
    mine_exp = wexp_f.at[f, :, pl.ds(pl.multiple_of(384 * zh, 128), 384)]
    pltpu.make_async_copy(wexp, mine_exp, rsem.at[k_wexp]).start()
    send(wexp, mine_exp, k_wexp + 1, z_mate)

    for d in range(1, 8):
        arrived(par.at[(ctx + 8 - d) % 8], k_par + d)
    prm[...] = jnp.concatenate([par[b, 0:8, 0:96] for b in range(8)], axis=1)
    be = jnp.concatenate(
        [par[r, 8 + i : 9 + i, :] for i in range(3)] + [par[4 + r, 8 + i : 9 + i, :] for i in range(3)],
        axis=1,
    )
    zrow = jnp.zeros((1, 192), F32)
    z_bias = jnp.concatenate(
        [par[2 * r, 0:1, 0:96], par[2 * r + 1, 0:1, 0:96], zrow, par[2 * r, 1:2, 0:96], par[2 * r + 1, 1:2, 0:96]],
        axis=1,
    )

    row_pos = lax.broadcasted_iota(jnp.int32, (512, 1), 0) + 512 * c
    row_segs = sided(row_pos.astype(F32), 512).astype(jnp.int32) + 64
    for j in range(1, 4):
        arrived(mg.at[peer_rank(j)], k_m + j)
    for i in range(8):
        count = mg[i // 2, i % 2 : i % 2 + 1, :]
        logs = jnp.log(jnp.maximum(count, 1.0))
        high = logs.astype(BF).astype(F32)
        line = jnp.where(lane < 88, jnp.where(count > 0.5, high, NEG), logs - high)
        line = jnp.where(lane < 104, line, 0.0)
        same = row_segs[64 * i : 64 * i + 64] == wide[0:64]
        block = jnp.where(wide[0:64] < 72, jnp.where(same, 0.0, NEG), line)
        mq[i // 2, 64 * (i % 2) : 64 * (i % 2) + 64, :] = block.astype(BF)
    for h in range(3):
        q_s[:, h, :, 64:128] = mq[:, :, 64:128]

    f_y = 2 * (1 - y) + c
    arrived(win_p.at[f_y], k_win_y)
    send(win_p.at[f_y], win_p.at[f_y], k_win_c + 1, core_mate)
    for d in range(8):
        arrived(wout_p.at[f, (ctx + 8 - d) % 8], k_wout + d)
    send(wout_p.at[f], wout_p.at[f], k_wout_y, y_mate)
    send(wout_p.at[f], wout_p.at[f], k_wout_c, core_mate)
    k_wshr = recvs(4)
    at_half = pl.ds(pl.multiple_of(384 * y, 128), 384)
    for sub in range(2):
        for half in range(2):
            send_or_keep(
                wshr.at[:, 384 * sub : 384 * sub + 384], ws.at[2 * zh + zl, x, :, at_half],
                k_wshr + 2 * zh + zl, dev(sub, y, 2 * half + c, x),
            )


    def place_in(k):
        for q in range(4):
            w_in[pl.ds(pl.multiple_of(192 * k + 48 * q, 16), 48), :] = jnp.concatenate(
                [win_p[k, i, :, 96 * q : 96 * q + 96] for i in range(6)], axis=1
            )

    place_in(f)
    place_in(f_y)
    arrived(win_p.at[2 * y + 1 - c], k_win_c)
    place_in(2 * y + 1 - c)
    arrived(win_p.at[2 * (1 - y) + 1 - c], k_win_c + 1)
    place_in(2 * (1 - y) + 1 - c)

    def project(k):
        mixed = dot_nn(xg[k], w_in[...]) + z_bias
        queries = (mixed[:, 0:192].astype(BF).astype(F32) * 0.125).astype(BF)
        for h in range(3):
            q_s[k, h, :, 0:64] = queries[:, 64 * h : 64 * h + 64]
        kv[c, pl.ds(pl.multiple_of(128 * k, 128), 128), :] = mixed[:, 192:576].astype(BF)

    lax.fori_loop(
        0, 4,
        served(lambda j: project(peer_rank(j)), [(3, True, lambda: far_arrived(xg, k_x, 64))]), 0,
    )
    k_kv = recvs(1)
    send(kv.at[c], kv.at[c], k_kv, core_mate)

    def split_heads(half):
        at = pl.ds(pl.multiple_of(512 * half, 512), 512)
        for h in range(3):
            kh[h, at, 0:64] = kv[half, :, 64 * h : 64 * h + 64]
            vh[h, at, 0:64] = kv[half, :, 192 + 64 * h : 256 + 64 * h]

    split_heads(c)
    arrived(mine_exp, k_wexp)
    arrived(wexp_f.at[f, :, pl.ds(pl.multiple_of(384 * (1 - zh), 128), 384)], k_wexp + 1)
    send(wexp_f.at[f], wexp_f.at[f], k_wexp_y, y_mate)
    send(wexp_f.at[f], wexp_f.at[f], k_wexp_c, core_mate)
    arrived(kv.at[1 - c], k_kv)
    split_heads(1 - c)

    k_a, s_a = recvs(16), sends(16)

    def attend(k):
        outs = []
        for h in range(3):
            scores = dot_nt(q_s[k, h], kh[h])
            top = jnp.max(scores, axis=1, keepdims=True)
            exps = jnp.exp(scores - top).astype(BF)
            e_s[h, k] = exps
            sums = dot_nn(exps, vh[h])
            scale = 1.0 / sums[:, 64:65]
            l_s[h, k] = scale
            outs.append(sums[:, 0:64] * scale)
        both = jnp.concatenate(outs, axis=1)
        a_f[k] = both
        low = both.astype(BF)
        a_b[k] = low
        a_all[r, k] = jnp.concatenate([low[0:64], low[64:128]], axis=1)
        for j in range(1, 4):
            at = 4 * j + k
            copy_to(a_all.at[r, k], a_all.at[r, k], s_a + at, k_a + at, peers[j]).start()

    wout_there, wexp_there = wout_p.at[f_y], wexp_f.at[f_y]
    ws_mine = ws.at[:, c, :, at_half]

    def relay_0():
        arrived(wout_there, k_wout_y)
        send(wout_there, wout_there, k_wout_c + 1, core_mate)

    def relay_1():
        for k in range(4):
            arrived(ws.at[k, c, :, at_half], k_wshr + k)
        send(ws_mine, ws_mine, k_wshr_y, y_mate)
        send(ws_mine, ws_mine, k_wshr_c, core_mate)

    def relay_2():
        arrived(wexp_there, k_wexp_y)
        send(wexp_there, wexp_there, k_wexp_c + 1, core_mate)

    lax.fori_loop(0, 4, served(attend, [(0, False, relay_0), (1, False, relay_1), (2, False, relay_2)]), 0)
    for j in range(1, 4):
        for k in range(4):
            at = 4 * j + k
            pending.append(
                copy_to(a_all.at[r, k], a_all.at[r, k], s_a + at, k_a + at, peer(j)).wait_send
            )
    send_or_keep(cot, eo, k_e, home)
    def place_out(k):
        for q in range(4):
            w_out[pl.ds(pl.multiple_of(192 * k + 48 * q, 16), 48), :] = jnp.concatenate(
                [wout_p[k, b, :, 96 * q : 96 * q + 96] for b in range(8)], axis=1
            )

    place_out(f)
    place_out(f_y)
    arrived(wout_p.at[2 * y + 1 - c], k_wout_c)
    place_out(2 * y + 1 - c)
    arrived(wout_p.at[2 * (1 - y) + 1 - c], k_wout_c + 1)
    place_out(2 * (1 - y) + 1 - c)
    other_half = pl.ds(pl.multiple_of(384 * (1 - y), 128), 384)
    arrived(ws.at[:, c, :, other_half], k_wshr_y)
    send(ws.at[:, c, :, other_half], ws.at[:, c, :, other_half], k_wshr_c + 1, core_mate)
    for j in range(1, 4):
        for k in range(4):
            arrived(a_all.at[peer_rank(j), k], k_a + 4 * j + k)
    arrived(wexp_f.at[2 * y + 1 - c], k_wexp_c)
    arrived(wexp_f.at[2 * (1 - y) + 1 - c], k_wexp_c + 1)

    def first_norm(k):
        rows = jnp.concatenate(
            [
                jnp.concatenate([a_all[src, k, :, 192 * i : 192 * i + 192] for src in range(4)], axis=1)
                for i in range(2)
            ],
            axis=0,
        )
        first = xg[k].astype(F32) + prm[2:3, :] + dot_nn(rows, w_out[...])
        centre = first - jnp.mean(first, axis=1, keepdims=True)
        inverse = lax.rsqrt(jnp.mean(centre * centre, axis=1, keepdims=True) + 1e-05)
        normed = centre * inverse
        hidden_one = normed * prm[6:7, :] + prm[3:4, :]
        hg[k] = hidden_one.astype(BF)
        return normed, inverse, hidden_one

    def expand(k):
        inner = dot_nn(hg[k], wexp_f[...].reshape(768, 768)) + be
        below = 0.5 * (1.0 + lax.erf(inner * 0.7071067811865476))
        u_s[k] = inner
        dge[k] = below
        active = (inner * below).astype(BF)
        g_s[k] = active

    def widen(k):
        normed, inverse, hidden_one = first_norm(k)
        n1_s[...] = normed
        r1_s[...] = inverse
        h1_s[...] = hidden_one
        expand(k)

    widen(ranks[3])
    arrived(ws.at[:, 1 - c, :, at_half], k_wshr_c)
    arrived(ws.at[:, 1 - c, :, other_half], k_wshr_c + 1)
    far_1, second_1, third_1, merge_1, here_1 = merging(yb, rs1, rd1)

    def expand_step(i, carry):
        j = 3 - i
        rank = peer_rank(j)

        @pl.when(i > 0)
        def _():
            widen(rank)

        value = dot_nt(g_s[rank], ws[...].reshape(768, 768))

        @pl.when(i < 3)
        def _():
            yb[j] = value.astype(BF)

        pl.when(i == 0)(far_1)
        pl.when(i == 1)(second_1)

        @pl.when(i == 2)
        def _():
            third_1()
            merge_1()

        @pl.when(i == 3)
        def _():
            ysum[...] = value

        return carry

    lax.fori_loop(0, 4, expand_step, 0)
    def slope(k, carry):
        inner = u_s[k]
        dge[k] = dge[k] + inner * jnp.exp(-0.5 * inner * inner) * 0.3989422804014327
        return carry

    lax.fori_loop(0, 4, slope, 0)

    arrived(eo, k_e)
    upstream = eo[...].astype(F32)
    scaled = upstream * prm[7:8, :]
    scaled_mean = jnp.mean(scaled, axis=1, keepdims=True)
    row_shift_two = row_sum(upstream)
    second = h1_s[...] + prm[4:5, :] + ysum[...]
    for j in range(1, 3):
        for i in range(2):
            here_1(j, i)
        second += rs1[j].astype(F32)
    centre = second - jnp.mean(second, axis=1, keepdims=True)
    inverse = lax.rsqrt(jnp.mean(centre * centre, axis=1, keepdims=True) + 1e-05)
    normed = centre * inverse
    grad_two = inverse * (
        scaled - scaled_mean - normed * jnp.mean(scaled * normed, axis=1, keepdims=True)
    )
    dg[r] = grad_two.astype(BF)
    k_d = recvs(4)
    for j in range(1, 3):
        send(dg.at[r], dg.at[r], k_d + j, peer(j))
    d2_s[...] = grad_two
    ob[...] = (normed * prm[7:8, :] + prm[5:6, :]).astype(BF)
    k_o = recvs(1)
    send_or_keep(ob, ohr, k_o, home)
    row_gain_two = row_sum(upstream * normed)
    row_back = row_sum(grad_two)

    def contract(k):
        inner = dge[k] * dot_nn(dg[k], ws[...].reshape(768, 768))
        low = inner.astype(BF)
        du_s[k] = low
        beg[k] = row_sum(inner)
        return dot_nt(low, wexp_f[...].reshape(768, 768))

    k_r2, s_r2 = recvs(4), sends(4)

    def contract_step(j):
        value = contract(peer_rank(j))

        @pl.when(j == 0)
        def _():
            ysum[...] = value

        @pl.when(j > 0)
        def _():
            dh_b[j] = value.astype(BF)
            copy_to(dh_b.at[j], rs2.at[j], s_r2 + j, k_r2 + j, peer(j)).start()

    dg_parts = near_parts(dg, 64)
    gathered = [
        (1, True, lambda: pass_on(dg_parts, k_d)),
        (3, True, lambda: far_arrived(dg, k_d, 64)),
    ]
    lax.fori_loop(0, 4, served(contract_step, gathered), 0)
    for j in range(1, 4):
        pending.append(copy_to(dh_b.at[j], rs2.at[j], s_r2 + j, k_r2 + j, peer(j)).wait_send)

    for k in range(4):
        rows = dg[:, :, 192 * k : 192 * k + 192].reshape(512, 192)
        gs[k] = dot_tn(rows, g_s[...].reshape(512, 768)).astype(BF).reshape(2, 96, 768)
    k_gs = recvs(1)
    send(gs.at[:, 1 - c], rs_c, k_gs, core_mate)

    def expand_grad(i, carry):
        at = pl.ds(pl.multiple_of(128 * i, 128), 128)
        rows = hg[:, :, at].reshape(512, 128)
        ge[at, :] = dot_tn(rows, du_s[...].reshape(512, 768)).astype(BF)
        return carry

    lax.fori_loop(0, 6, expand_grad, 0)
    k_ge = recvs(2)
    for half in range(2):
        at = pl.ds(pl.multiple_of(192 * (2 * half + 1 - c), 64), 192)
        send(ge.at[at, :], re_c.at[half], k_ge + half, core_mate)
    k_gs_y, k_ge_y = recvs(1), recvs(1)
    arrived(rs_c, k_gs)
    t_shr[...] = (
        gs[:, c, :, other_half].astype(F32) + rs_c[:, :, other_half].astype(F32)
    ).astype(BF)
    send(t_shr, rs_y, k_gs_y, y_mate)

    grad_hidden = d2_s[...] + ysum[...]
    for j in range(1, 4):
        arrived(rs2.at[j], k_r2 + j)
        grad_hidden += rs2[j].astype(F32)
    normed = n1_s[...]
    scaled = grad_hidden * prm[6:7, :]
    grad_one = r1_s[...] * (
        scaled
        - jnp.mean(scaled, axis=1, keepdims=True)
        - normed * jnp.mean(scaled * normed, axis=1, keepdims=True)
    )
    low_one = grad_one.astype(BF)
    d1g[r] = low_one
    for k in range(4):
        dab[k] = dot_nt(low_one, w_out[192 * k : 192 * k + 192, :]).astype(BF)
    k_da, k_d1 = recvs(4), recvs(4)
    for j in range(1, 4):
        send(dab.at[peer_rank(j)], da.at[r], k_da + j, peer(j))
    da[r] = dab[r]
    d1_s[...] = grad_one
    row_gain_one = row_sum(grad_hidden * normed)
    row_shift_one = row_sum(grad_hidden)
    row_out = row_sum(grad_one)

    for half in range(2):
        arrived(re_c.at[half], k_ge + half)
    at_y = pl.ds(pl.multiple_of(192 * f_y, 64), 192)
    at_own = pl.ds(pl.multiple_of(192 * f, 64), 192)
    t_exp[...] = (ge[at_y, :].astype(F32) + re_c[1 - y].astype(F32)).astype(BF)
    send(t_exp, re_y, k_ge_y, y_mate)

    for j in range(1, 4):
        arrived(da.at[peer_rank(j)], k_da + j)
    for j in range(1, 3):
        send(d1g.at[r], d1g.at[r], k_d1 + j, peer(j))

    def attend_back(k):
        outs = []
        grads = da[k].astype(F32)
        dots = grads * a_f[k]
        for h in range(3):
            at = slice(64 * h, 64 * h + 64)
            scale = l_s[h, k]
            delta = jnp.sum(dots[:, at], axis=1, keepdims=True) * scale
            high = delta.astype(BF).astype(F32)
            side = jnp.where(wide[0:128, 0:64] == 0, -high, 0.0)
            side = jnp.where(wide[0:128, 0:64] == 1, high - delta, side)
            both = jnp.concatenate([grads[:, at] * scale, side], axis=1).astype(BF)
            de[k, h] = both
            low = (e_s[h, k].astype(F32) * dot_nt(both, vh[h])).astype(BF)
            ds_s[h, k] = low
            outs.append(dot_nn(low, kh[h])[:, 0:64] * 0.125)
        queries = jnp.concatenate(outs, axis=1)
        qb_s[k] = row_sum(queries)
        dz[k, :, 0:192] = queries.astype(BF)

    k_fs, k_re = recvs(4), recvs(1)
    shrink_owners = [dev(c, y, k, zl) for k in range(4)]
    fs_at = fs.at[zh, x]
    fsb_at = [fsb.at[k] for k in range(4)]
    k_own = k_fs + 2 * zh + x

    def pass_0():
        arrived(rs_y, k_gs_y)
        fsb[...] = (
            gs[:, c, :, at_half].astype(F32) + rs_c[:, :, at_half].astype(F32) + rs_y[...].astype(F32)
        ).astype(BF)
        for k in range(4):
            send_or_keep(fsb_at[k], fs_at, k_own, shrink_owners[k])

    def pass_1():
        arrived(re_y, k_ge_y)
        te_f[...] = ge[at_own, :].astype(F32) + re_c[y].astype(F32) + re_y[...].astype(F32)
        te_b[...] = te_f[:, pl.ds(pl.multiple_of(384 * (1 - zh), 128), 384)].astype(BF)
        send(te_b, re_z, k_re, z_mate)

    d1g_parts = near_parts(d1g, 0)

    def pass_2():
        pass_on(d1g_parts, k_d1)

    lax.fori_loop(0, 4, served(attend_back, [(0, False, pass_0), (1, False, pass_1), (2, False, pass_2)]), 0)
    sums = []
    for h in range(3):
        rows = q_s[:, h, :, 0:64].reshape(512, 64)
        sums.append(dot_tn(rows, ds_s[h].reshape(512, 1024)))
    for h in range(3):
        rows = de[:, h, :, 0:64].reshape(512, 64)
        sums.append(dot_tn(rows, e_s[h].reshape(512, 1024)))
    sums = jnp.concatenate(sums, axis=0)
    dkv[0] = sums[:, 0:512].T
    dkv[1] = sums[:, 512:1024].T
    dkb[...] = dkv[1 - c].astype(BF)
    k_dk = recvs(1)
    send(dkb, dkr, k_dk, core_mate)

    def project_grad(first, count):
        for k in range(4):
            rows = xg[:, :, 192 * k : 192 * k + 192].reshape(512, 192)
            cols = dz[:, :, 96 * first : 96 * first + 96 * count].reshape(512, 96 * count)
            part = dot_tn(rows, cols).astype(BF)
            for slot in range(count):
                gi[k, first + slot] = pack(part[:, 96 * slot : 96 * slot + 96])

    some = {"q": pl.ds(0, 2), "kv": pl.ds(2, 4)}
    k_gi = {"q": recvs(2), "kv": recvs(2)}
    k_gi_y = {"q": recvs(1), "kv": recvs(1)}

    def over_cores(which):
        at = some[which]
        for half in range(2):
            send(gi.at[2 * half + 1 - c, at], ri_c.at[half, at], k_gi[which] + half, core_mate)

    def over_y(which):
        at = some[which]
        for half in range(2):
            arrived(ri_c.at[half, at], k_gi[which] + half)
        tib[at] = (gi[f_y, at].astype(F32) + ri_c[1 - y, at].astype(F32)).astype(BF)
        send(tib.at[at], ri_y.at[at], k_gi_y[which], y_mate)

    k_fi = recvs(6)

    def to_owners(which):
        at = some[which]
        arrived(ri_y.at[at], k_gi_y[which])
        ti2[at] = (
            gi[f, at].astype(F32) + ri_c[y, at].astype(F32) + ri_y[at].astype(F32)
        ).astype(BF)
        for slot in range(2) if which == "q" else range(2, 6):
            unit = 8 * (slot // 2) + 2 * r + slot % 2
            send_or_keep(
                ti2.at[slot], fi.at[zh, unit % 3], k_fi + 3 * zh + unit % 3, (unit // 3, seq)
            )

    project_grad(0, 2)
    over_cores("q")

    arrived(dkr, k_dk)
    keyvals = dkv[c] + dkr[...].astype(F32)
    vb_s[...] = row_sum(keyvals[:, 192:384])
    dz[:, :, 192:576] = keyvals.astype(BF).reshape(4, 128, 384)

    def input_part(k):
        return dot_nt(dz[k], w_in[...])

    far_3, second_3, third_3, merge_3, here_3 = merging(dx_b, rs3, rd3)

    def input_step(i, carry):
        j = 3 - i
        dx_b[j] = input_part(peer_rank(j)).astype(BF)
        pl.when(i == 0)(far_3)
        pl.when(i == 1)(second_3)
        pl.when(i == 2)(third_3)
        return carry

    lax.fori_loop(0, 3, input_step, 0)
    over_y("q")
    project_grad(2, 4)
    over_cores("kv")
    merge_3()

    far_arrived(d1g, k_d1, 0)
    part = dot_tn(a_b[...].reshape(512, 192), d1g[...].reshape(512, 768))
    for b in range(8):
        go[b % 2, b // 2] = pack(part[:, 96 * b : 96 * b + 96].astype(BF))
    k_go = recvs(1)
    send(go.at[1 - c], ro_c, k_go, core_mate)

    over_y("kv")

    vg[...] = jnp.zeros((8, 16, 128), F32)
    rows = jnp.concatenate(
        [row_out, row_shift_one, row_back, row_shift_two, row_gain_one, row_gain_two], axis=0
    )
    for b in range(8):
        vg[b, 2:8, 0:96] = rows[:, 96 * b : 96 * b + 96]
    q_row = row_sum(qb_s[:, 0, :])
    v_row = vb_s[...]
    for i in range(2):
        vg[2 * r + i, 0:1, 0:96] = q_row[:, 96 * i : 96 * i + 96]
        vg[2 * r + i, 1:2, 0:96] = v_row[:, 96 * i : 96 * i + 96]
    inner_row = row_sum(beg[:, 0, :])
    for i in range(3):
        vg[r, 8 + i : 9 + i, :] = inner_row[:, 128 * i : 128 * i + 128]
        vg[4 + r, 8 + i : 9 + i, :] = inner_row[:, 384 + 128 * i : 512 + 128 * i]
    k_v = recvs(8)
    for d in range(1, 8):
        other = (ctx + d) % 8
        send(vg.at[other], vr.at[d], k_v + d, (other, seq))

    arrived(ro_c, k_go)
    tob[...] = (go[c].astype(F32) + ro_c[...].astype(F32)).astype(BF)
    k_go_y, k_fo = recvs(1), recvs(2)
    s_go, s_fo = sends(1), sends(4)
    stays = y == zl

    @pl.when(jnp.logical_not(stays))
    def _():
        copy_to(tob, ro_y, s_go, k_go_y, y_mate).start()

    k_gh = recvs(2)
    ysum[...] = d1_s[...] + input_part(r)

    def finish_input(i):
        at = pl.ds(64 * i, 64)
        grad_in = ysum[at, :]
        for j in range(1, 3):
            here_3(j, i)
            grad_in += rs3[j, at, :].astype(F32)
        ghb[at, :] = grad_in.astype(BF)
        send_or_keep(ghb.at[at, :], ghr.at[at, :], k_gh + i, home)

    to_owners("q")
    finish_input(0)

    done = []

    for half in range(2):
        for sub in range(2):
            arrived(fs.at[half, sub], k_fs + 2 * half + sub)
    for sub in range(2):
        f_wshr[:, 384 * sub : 384 * sub + 384] = fs[0, sub].astype(F32) + fs[1, sub].astype(F32)
    done.append(local(f_wshr, o_wshr))
    arrived(re_z, k_re)
    f_wexp[...] = te_f[:, pl.ds(pl.multiple_of(384 * zh, 128), 384)] + re_z[...].astype(F32)
    done.append(local(f_wexp, o_wexp))

    to_owners("kv")
    finish_input(1)

    @pl.when(stays)
    def _():
        arrived(ro_y, k_go_y)
        tob2[...] = (tob[...].astype(F32) + ro_y[...].astype(F32)).astype(BF)
        for k in range(4):
            to = dev(c, y, k, x)
            away = jnp.logical_or(to[0] != ctx, to[1] != seq)

            @pl.when(away)
            def _():
                copy_to(tob2.at[k], fo.at[zh], s_fo + k, k_fo + zh, to).start()

            @pl.when(jnp.logical_not(away))
            def _():
                pltpu.make_async_copy(tob2.at[k], fo.at[zh], rsem.at[k_fo + zh]).start()

    def finish_out():
        @pl.when(jnp.logical_not(stays))
        def _():
            copy_to(tob, ro_y, s_go, k_go_y, y_mate).wait_send()

        @pl.when(stays)
        def _():
            for k in range(4):
                to = dev(c, y, k, x)

                @pl.when(jnp.logical_or(to[0] != ctx, to[1] != seq))
                def _():
                    copy_to(tob2.at[k], fo.at[zh], s_fo + k, k_fo + zh, to).wait_send()

    pending.append(finish_out)

    total = vg[ctx]
    for d in range(1, 8):
        arrived(vr.at[d], k_v + d)
        total += vr[d]
    vs1[...] = total
    k_vc = recvs(2)
    send(vs1, vc, k_vc, core_mate)
    arrived(vc, k_vc)
    vs2[...] = vs1[...] + vc[...]
    send(vs2, vy, k_vc + 1, y_mate)

    arrived(ohr, k_o)
    done.append(local(ohr, o_out))
    arrived(vy, k_vc + 1)
    total = vs2[...] + vy[...]
    f_gb[...] = total[0:6, 0:96]
    f_gg[...] = total[6:8, 0:96]
    f_ge[...] = total[8:11, :]
    done += [local(f_gb, o_gb), local(f_gg, o_gg), local(f_ge, o_ge)]
    for half in range(2):
        arrived(fo.at[half], k_fo + half)
    part = fo[0].astype(F32) + fo[1].astype(F32)
    for q in range(4):
        f_wout[48 * q : 48 * q + 48, :] = part[:, 96 * q : 96 * q + 96]
    done.append(local(f_wout, o_wout))
    for half in range(2):
        for j in range(3):
            arrived(fi.at[half, j], k_fi + 3 * half + j)
    parts = [fi[0, j].astype(F32) + fi[1, j].astype(F32) for j in range(3)]
    for q in range(4):
        f_win[48 * q : 48 * q + 48, :] = jnp.concatenate(
            [part[:, 96 * q : 96 * q + 96] for part in parts], axis=1
        )
    done.append(local(f_win, o_win))
    for i in range(2):
        arrived(ghr.at[pl.ds(64 * i, 64), :], k_gh + i)
    done.append(local(ghr, o_gh))
    for finish in pending:
        finish()
    for copy in done:
        copy.wait()


def hand_over(*refs):
    ins, outs, held, into, out_of = refs[0:9], refs[9:18], refs[18:27], refs[27], refs[28]
    loads = [pltpu.make_async_copy(ins[i], held[i], into.at[i]) for i in range(9)]
    stores = [pltpu.make_async_copy(held[i], outs[i], out_of.at[i]) for i in range(9)]
    for load in loads:
        load.start()
    for load, store in zip(loads, stores):
        load.wait()
        store.start()
    for store in stores:
        store.wait()


def fast_shards(
    hidden, project_in, project_out, expand_weight, shrink_weight, biases, gains, expand_bias,
    random_blocks, global_blocks, document_lengths, cotangent,
):
    vm = lambda *dims: pltpu.VMEM(dims, BF)
    vf = lambda *dims: pltpu.VMEM(dims, F32)
    scratch = [
        vm(192, 288), vm(192, 96), vm(3, 48, 384), vm(48, 384), vm(4, 128, 768), vm(128, 768),
        vf(8, 128), vf(4, 8, 128), vf(16, 128), vf(8, 16, 128), vm(4, 6, 48, 384), vm(4, 8, 48, 384),
        vm(4, 192, 768), vm(4, 2, 96, 768), vm(768, 576), vm(768, 768), vf(8, 768),
        vm(4, 128, 128), vm(4, 3, 128, 128), vm(2, 512, 384), vm(3, 1024, 128), vm(3, 1024, 128),
        vm(3, 4, 128, 1024), vf(3, 4, 128, 1), vf(4, 128, 192), vm(4, 128, 192), vm(4, 4, 64, 384),
        vm(4, 128, 768), vf(128, 768), vf(128, 768), vf(128, 1), vf(4, 128, 768), vf(4, 128, 768), vm(4, 128, 768),
        vf(128, 768), vm(4, 128, 768),
        vm(2, 64, 768), vm(2, 64, 768), vm(4, 128, 768), vf(128, 768), vm(4, 128, 768),
        vm(4, 128, 768), vm(4, 128, 768),
        vm(4, 128, 768), vf(4, 1, 768), vf(128, 768), vm(4, 128, 768), vm(4, 128, 192),
        vm(4, 128, 192), vm(4, 3, 128, 128), vm(3, 4, 128, 1024), vf(2, 512, 384), vm(512, 384),
        vm(512, 384), vm(4, 128, 576), vm(4, 128, 768), vm(4, 128, 768),
        vm(4, 2, 96, 768), vm(4, 96, 768), vm(4, 96, 384), vm(4, 96, 384), vm(4, 96, 384),
        vm(2, 2, 96, 384), vm(768, 768), vm(2, 192, 768), vm(192, 768), vm(192, 768), vf(192, 768),
        vm(192, 384), vm(192, 384),
        vm(2, 4, 48, 384), vm(4, 48, 384), vm(4, 48, 384), vm(4, 48, 384), vm(4, 48, 384),
        vm(2, 48, 384), vm(4, 6, 48, 384), vm(2, 6, 48, 384), vm(6, 48, 384), vm(6, 48, 384),
        vm(6, 48, 384), vm(2, 3, 48, 384),
        vf(8, 16, 128), vf(8, 16, 128), vf(16, 128), vf(16, 128), vf(16, 128), vf(16, 128),
        vf(4, 1, 192), vf(1, 192), vm(128, 768), vm(128, 768), vm(128, 768), vm(128, 768),
        vf(192, 288), vf(192, 96), vf(192, 384), vf(96, 768), vf(6, 96), vf(2, 96), vf(3, 128),
        pltpu.SMEM((2, 3), jnp.int32), pltpu.SMEM((1, 2), jnp.int32), pltpu.SMEM((1, 8), jnp.int32),
        vm(6, 96), vm(2, 96), vm(3, 128),
        pltpu.SemaphoreType.DMA((SENDS,)), pltpu.SemaphoreType.DMA((RECVS,)),
        pltpu.SemaphoreType.DMA((LOCALS,)),
    ]
    out = lambda kind, *dims: jax.ShapeDtypeStruct(dims, kind)
    shapes = (
        out(BF, 128, 768), out(BF, 128, 768), out(F32, 192, 288), out(F32, 192, 96),
        out(F32, 192, 384), out(F32, 96, 768), out(F32, 6, 96), out(F32, 2, 96), out(F32, 3, 128),
    )
    anywhere = pl.BlockSpec(memory_space=pl.ANY)
    results = pl.pallas_call(
        layer_kernel,
        out_shape=shapes,
        in_specs=[anywhere] * 12,
        out_specs=(anywhere,) * 9,
        scratch_shapes=scratch,
        compiler_params=pltpu.CompilerParams(
            collective_id=0, has_side_effects=True, vmem_limit_bytes=58 * 1024 * 1024
        ),
    )(
        random_blocks[0], global_blocks, document_lengths, biases, gains,
        expand_bias.reshape(3, 128), hidden[0], cotangent[0], project_in, project_out,
        expand_weight, shrink_weight.T,
    )
    results = pl.pallas_call(
        hand_over,
        out_shape=shapes,
        in_specs=[anywhere] * 9,
        out_specs=(anywhere,) * 9,
        scratch_shapes=[pltpu.VMEM(one.shape, one.dtype) for one in shapes]
        + [pltpu.SemaphoreType.DMA((9,))] * 2,
    )(*results)
    return (
        results[0][None], results[1][None], results[2], results[3], results[4], results[5].T,
        results[6], results[7], results[8].reshape(-1),
    )


def solution(mesh):
    small = tuple(mesh.shape[name] for name in ("ctx", "fsdp")) == (8, 4)
    return jax.shard_map(
        fast_shards if small else shards,
        mesh=mesh,
        in_specs=(
            P("fsdp", "ctx", None),
            P("fsdp", "ctx"),
            P("fsdp", "ctx"),
            P("fsdp", "ctx"),
            P("fsdp", "ctx"),
            P(None, "ctx"),
            P(None, "ctx"),
            P("ctx"),
            P("fsdp", "ctx", None),
            P("fsdp", None),
            P("fsdp", None),
            P("fsdp", "ctx", None),
        ),
        out_specs=(
            P("fsdp", "ctx", None),
            P("fsdp", "ctx", None),
            P("fsdp", "ctx"),
            P("fsdp", "ctx"),
            P("fsdp", "ctx"),
            P("fsdp", "ctx"),
            P(None, "ctx"),
            P(None, "ctx"),
            P("ctx"),
        ),
        check_vma=False,
    )
```

```python
import jax
import jax.numpy as jnp
from jax import lax
from jax.experimental import pallas as pl
from jax.experimental.pallas import tpu as pltpu
from jax.sharding import PartitionSpec as P

HEAD_DIM = 64
BLOCK = 64


def segment_of(positions, bounds):
    return jnp.sum((positions[..., None] >= bounds).astype(jnp.int32), axis=-1)


def layer_norm_parts(values, gain_row, shift_row):
    centre = values - jnp.mean(values, axis=-1, keepdims=True)
    inverse = lax.rsqrt(jnp.mean(centre * centre, axis=-1, keepdims=True) + 1e-05)
    normed = centre * inverse
    return (normed * gain_row + shift_row, normed, inverse)


def layer_norm_back(upstream, normed, inverse, gain_row):
    scaled = upstream * gain_row
    return inverse * (
        scaled
        - jnp.mean(scaled, axis=-1, keepdims=True)
        - normed * jnp.mean(scaled * normed, axis=-1, keepdims=True)
    )


def matmul(left_side, right_side):
    return jnp.dot(left_side, right_side, preferred_element_type=jnp.float32)


def matmul_left_t(left_side, right_side):
    return lax.dot_general(
        left_side, right_side, (((0,), (0,)), ((), ())), preferred_element_type=jnp.float32
    )


def matmul_right_t(left_side, right_side):
    return lax.dot_general(
        left_side, right_side, (((1,), (1,)), ((), ())), preferred_element_type=jnp.float32
    )


def over_cols(qkv_grad, out_grad, expand_grad, shrink_grad, vector_grad, gain_grad, inner_grad):
    return (
        lax.psum_scatter(qkv_grad, "ctx", scatter_dimension=1, tiled=True),
        lax.psum_scatter(out_grad, "ctx", scatter_dimension=1, tiled=True),
        lax.psum_scatter(expand_grad, "ctx", scatter_dimension=1, tiled=True),
        lax.psum_scatter(shrink_grad, "ctx", scatter_dimension=1, tiled=True),
        lax.psum_scatter(vector_grad, "ctx", scatter_dimension=1, tiled=True),
        lax.psum_scatter(gain_grad, "ctx", scatter_dimension=1, tiled=True),
        lax.psum_scatter(inner_grad, "ctx", scatter_dimension=1, tiled=True),
    )


def over_rows(qkv_grad, out_grad, expand_grad, shrink_grad):
    return (
        lax.psum_scatter(
            qkv_grad.astype(jnp.bfloat16), "fsdp", scatter_dimension=0, tiled=True
        ).astype(jnp.float32),
        lax.psum_scatter(
            out_grad.astype(jnp.bfloat16), "fsdp", scatter_dimension=0, tiled=True
        ).astype(jnp.float32),
        lax.psum_scatter(
            expand_grad.astype(jnp.bfloat16), "fsdp", scatter_dimension=0, tiled=True
        ).astype(jnp.float32),
        lax.psum_scatter(
            shrink_grad.astype(jnp.bfloat16), "fsdp", scatter_dimension=0, tiled=True
        ).astype(jnp.float32),
    )


def scatter_rows(link_ids, link_grads, row_count, feature_width):
    block_count = row_count // BLOCK
    inside = (link_ids >= 0) & (link_ids < block_count)
    target = jnp.where(inside, link_ids, block_count).reshape(-1)
    partial_value = jnp.zeros((block_count, BLOCK, feature_width), jnp.float32)
    partial_value = partial_value.at[target].add(
        link_grads.reshape(-1, BLOCK, feature_width), mode="drop"
    )
    return partial_value.reshape(row_count, feature_width)


def shards(
    hidden,
    project_in,
    project_out,
    expand_weight,
    shrink_weight,
    biases,
    gains,
    expand_bias,
    random_blocks,
    global_blocks,
    document_lengths,
    cotangent,
):
    inputs = hidden[0]
    tokens_here = inputs.shape[0]
    width = inputs.shape[1]
    head_count = width // HEAD_DIM
    blocks_here = tokens_here // BLOCK
    rand_count = random_blocks.shape[2]
    link_count = 3 + rand_count + global_blocks.shape[1]
    ctx_rank = lax.axis_index("ctx")
    last_block = tokens_here * lax.axis_size("ctx") // BLOCK - 1
    col_full = (
        lax.all_gather(project_in, "ctx", axis=1, tiled=True),
        lax.all_gather(project_out, "ctx", axis=1, tiled=True),
        lax.all_gather(expand_weight, "ctx", axis=1, tiled=True),
        lax.all_gather(shrink_weight, "ctx", axis=1, tiled=True),
        lax.all_gather(biases, "ctx", axis=1, tiled=True),
        lax.all_gather(gains, "ctx", axis=1, tiled=True),
        lax.all_gather(expand_bias.reshape(1, -1), "ctx", axis=1, tiled=True),
    )
    full_qkv, full_out, full_expand, full_shrink = (
        lax.all_gather(col_full[0], "fsdp", axis=0, tiled=True),
        lax.all_gather(col_full[1], "fsdp", axis=0, tiled=True),
        lax.all_gather(col_full[2], "fsdp", axis=0, tiled=True),
        lax.all_gather(col_full[3], "fsdp", axis=0, tiled=True),
    )
    vectors = col_full[4].astype(jnp.float32)
    gain_rows = col_full[5].astype(jnp.float32)
    inner_bias = col_full[6][0].astype(jnp.float32)
    block_ids = ctx_rank * blocks_here + jnp.arange(blocks_here, dtype=jnp.int32)
    window = jnp.stack(
        [jnp.maximum(block_ids - 1, 0), block_ids, jnp.minimum(block_ids + 1, last_block)], axis=1
    )
    global_links = jnp.broadcast_to(
        global_blocks[0][None, :], (blocks_here, global_blocks.shape[1])
    )
    linked_ids = jnp.concatenate([window, random_blocks[0], global_links], axis=1)
    lengths = document_lengths[0]
    doc_order = jnp.arange(lengths.shape[0], dtype=jnp.int32)
    bounds = jnp.sum(
        jnp.where(doc_order[None, :] <= doc_order[:-1, None], lengths[None, :], 0), axis=1
    )
    query_pos = (ctx_rank * tokens_here + jnp.arange(tokens_here, dtype=jnp.int32)).reshape(
        blocks_here, BLOCK
    )
    query_seg = segment_of(query_pos, bounds)
    key_pos = linked_ids[:, :, None] * BLOCK + jnp.arange(BLOCK, dtype=jnp.int32)[None, None, :]
    key_seg = segment_of(key_pos, bounds).reshape(blocks_here, -1)
    allowed = query_seg[:, None, :, None] == key_seg[:, None, None, :]
    zero_row = jnp.zeros((width,), jnp.float32)
    mixed_qkv = (
        matmul(inputs, full_qkv) + jnp.concatenate([vectors[0], zero_row, vectors[1]])
    ).astype(jnp.bfloat16)
    queries = mixed_qkv[:, :width]
    keyvals = mixed_qkv[:, width:]
    shard_piece = lax.all_gather(keyvals, "ctx", axis=0, tiled=True)
    block_count = shard_piece.shape[0] // BLOCK
    stacked = shard_piece.reshape(block_count, BLOCK, shard_piece.shape[1])
    picks = (
        linked_ids.reshape(-1)[:, None] == jnp.arange(block_count, dtype=jnp.int32)[None, :]
    ).astype(jnp.bfloat16)
    linked = jnp.einsum("lb,bkd->lkd", picks, stacked).reshape(
        blocks_here, link_count, BLOCK, 2 * width
    )
    query_heads = queries.reshape(blocks_here, BLOCK, head_count, HEAD_DIM)
    key_heads = linked[..., :width].reshape(blocks_here, link_count * BLOCK, head_count, HEAD_DIM)
    value_heads = linked[..., width:].reshape(blocks_here, link_count * BLOCK, head_count, HEAD_DIM)

    def score_parts():
        raw_scores = (
            jnp.einsum(
                "bqhd,bkhd->bhqk", query_heads, key_heads, preferred_element_type=jnp.float32
            )
            * 0.125
        )
        return jnp.where(allowed, raw_scores, -1e30)

    scores = score_parts()
    top_score = jnp.max(scores, axis=-1, keepdims=True)
    exp_total = jnp.sum(jnp.exp(scores - top_score), axis=-1, keepdims=True)
    attention = jnp.exp(scores - top_score) / exp_total
    attended = jnp.einsum(
        "bhqk,bkhd->bqhd",
        attention.astype(jnp.bfloat16),
        value_heads,
        preferred_element_type=jnp.float32,
    )
    attended = attended.reshape(tokens_here, width).astype(jnp.bfloat16)
    residual_one = inputs.astype(jnp.float32) + matmul(attended, full_out) + vectors[2]
    hidden_one, normed_one, inverse_one = layer_norm_parts(residual_one, gain_rows[0], vectors[3])
    hidden_low = hidden_one.astype(jnp.bfloat16)
    inner_pre = matmul(hidden_low, full_expand) + inner_bias
    activated, gelu_pull = jax.vjp(
        lambda argument: jax.nn.gelu(argument, approximate=False), inner_pre
    )
    active_low = activated.astype(jnp.bfloat16)
    residual_two = hidden_one + matmul(active_low, full_shrink) + vectors[4]
    result, normed_two, inverse_two = layer_norm_parts(residual_two, gain_rows[1], vectors[5])
    upstream = cotangent[0].astype(jnp.float32)
    grad_gain_two = jnp.sum(upstream * normed_two, axis=0)
    grad_shift_two = jnp.sum(upstream, axis=0)
    grad_two = layer_norm_back(upstream, normed_two, inverse_two, gain_rows[1])
    grad_bias_back = jnp.sum(grad_two, axis=0)
    grad_two_low = grad_two.astype(jnp.bfloat16)
    again_cols = (
        lax.all_gather(project_in, "ctx", axis=1, tiled=True),
        lax.all_gather(project_out, "ctx", axis=1, tiled=True),
        lax.all_gather(expand_weight, "ctx", axis=1, tiled=True),
        lax.all_gather(shrink_weight, "ctx", axis=1, tiled=True),
    )
    back_weights = (
        lax.all_gather(again_cols[0], "fsdp", axis=0, tiled=True),
        lax.all_gather(again_cols[1], "fsdp", axis=0, tiled=True),
        lax.all_gather(again_cols[2], "fsdp", axis=0, tiled=True),
        lax.all_gather(again_cols[3], "fsdp", axis=0, tiled=True),
    )
    back_qkv, back_out, back_expand, back_shrink = back_weights
    grad_shrink_w = matmul_left_t(active_low, grad_two_low)
    grad_active = matmul_right_t(grad_two_low, back_shrink)
    grad_inner = gelu_pull(grad_active)[0]
    grad_inner_bias = jnp.sum(grad_inner, axis=0)
    grad_inner_low = grad_inner.astype(jnp.bfloat16)
    grad_expand_w = matmul_left_t(hidden_low, grad_inner_low)
    grad_hidden_one = grad_two + matmul_right_t(grad_inner_low, back_expand)
    grad_gain_one = jnp.sum(grad_hidden_one * normed_one, axis=0)
    grad_shift_one = jnp.sum(grad_hidden_one, axis=0)
    grad_one = layer_norm_back(grad_hidden_one, normed_one, inverse_one, gain_rows[0])
    grad_bias_out = jnp.sum(grad_one, axis=0)
    grad_one_low = grad_one.astype(jnp.bfloat16)
    grad_out_w = matmul_left_t(attended, grad_one_low)
    grad_attended = matmul_right_t(grad_one_low, back_out).astype(jnp.bfloat16)
    grad_attended = grad_attended.reshape(blocks_here, BLOCK, head_count, HEAD_DIM)
    scores = score_parts()
    attention = jnp.exp(scores - top_score) / exp_total
    grad_attention = jnp.einsum(
        "bqhd,bkhd->bhqk", grad_attended, value_heads, preferred_element_type=jnp.float32
    )
    grad_values = jnp.einsum(
        "bhqk,bqhd->bkhd",
        attention.astype(jnp.bfloat16),
        grad_attended,
        preferred_element_type=jnp.float32,
    )
    row_inner = jnp.sum(attention * grad_attention, axis=-1, keepdims=True)
    grad_scores = (attention * (grad_attention - row_inner) * 0.125).astype(jnp.bfloat16)
    grad_queries = jnp.einsum(
        "bhqk,bkhd->bqhd", grad_scores, key_heads, preferred_element_type=jnp.float32
    ).reshape(tokens_here, width)
    grad_keys = jnp.einsum(
        "bhqk,bqhd->bkhd", grad_scores, query_heads, preferred_element_type=jnp.float32
    )
    slot_grads = jnp.concatenate(
        [
            grad_keys.reshape(blocks_here, link_count, BLOCK, width),
            grad_values.reshape(blocks_here, link_count, BLOCK, width),
        ],
        axis=-1,
    )
    grad_keyvals = lax.psum_scatter(
        scatter_rows(linked_ids, slot_grads, tokens_here * lax.axis_size("ctx"), 2 * width),
        "ctx",
        scatter_dimension=0,
        tiled=True,
    )
    grad_mixed = jnp.concatenate([grad_queries, grad_keyvals], axis=1)
    grad_bias_query = jnp.sum(grad_queries, axis=0)
    grad_bias_value = jnp.sum(grad_keyvals[:, width:], axis=0)
    grad_mixed_low = grad_mixed.astype(jnp.bfloat16)
    grad_qkv_w = matmul_left_t(inputs, grad_mixed_low)
    grad_inputs = grad_one + matmul_right_t(grad_mixed_low, back_qkv)
    grad_vectors = jnp.stack(
        [
            grad_bias_query,
            grad_bias_value,
            grad_bias_out,
            grad_shift_one,
            grad_bias_back,
            grad_shift_two,
        ]
    )
    grad_gain_rows = jnp.stack([grad_gain_one, grad_gain_two])
    grad_inner_row = grad_inner_bias[None, :]
    reduced = over_cols(
        grad_qkv_w,
        grad_out_w,
        grad_expand_w,
        grad_shrink_w,
        grad_vectors,
        grad_gain_rows,
        grad_inner_row,
    )
    sum_qkv, sum_out, sum_expand, sum_shrink = over_rows(
        reduced[0], reduced[1], reduced[2], reduced[3]
    )
    final_vectors, final_gains, final_inner = lax.psum((reduced[4], reduced[5], reduced[6]), "fsdp")
    return (
        result.astype(jnp.bfloat16)[None],
        grad_inputs.astype(jnp.bfloat16)[None],
        sum_qkv,
        sum_out,
        sum_expand,
        sum_shrink,
        final_vectors,
        final_gains,
        final_inner.reshape(-1),
    )


MESH = pl.DeviceIdType.MESH
BF = jnp.bfloat16
F32 = jnp.float32
SENDS = 192
RECVS = 192
LOCALS = 24
NEG = -1e30


def dot_nn(a, b):
    return jnp.dot(a, b, preferred_element_type=F32)


def dot_nt(a, b):
    return lax.dot_general(a, b, (((1,), (1,)), ((), ())), preferred_element_type=F32)


def dot_tn(a, b):
    return lax.dot_general(a, b, (((0,), (0,)), ((), ())), preferred_element_type=F32)


def row_sum(values):
    return jnp.sum(values, axis=0, keepdims=True)


def pack(piece):
    return jnp.concatenate([piece[48 * q : 48 * q + 48] for q in range(4)], axis=1)


def layer_kernel(
    rand_hbm, glob_hbm, doc_hbm, bia_hbm, gai_hbm, ebi_hbm, hid, cot, win, wout, wexp, wshr,
    o_out, o_gh, o_win, o_wout, o_wexp, o_wshr, o_gb, o_gg, o_ge,
    winv, woutv, win3, wout1, xg, eo, ms, mg, ps, par, win_p, wout_p, wexp_f, ws, w_in, w_out, prm,
    mq, q_s, kv, kh, vh, e_s, l_s, a_f, a_b, a_all, hg, h1_s, n1_s, r1_s, u_s, dge, g_s, ysum, yb,
    rd1, rd3, rs1, d2_s, dg, du_s, dh_b, rs2, beg, d1_s, d1g, dab, da, de, ds_s, dkv, dkb, dkr, dz, dx_b, rs3,
    gs, rs_c, t_shr, rs_y, fsb, fs, ge, re_c, t_exp, re_y, te_f, te_b, re_z,
    go, ro_c, tob, ro_y, tob2, fo, gi, ri_c, tib, ri_y, ti2, fi,
    vg, vr, vs1, vc, vs2, vy, qb_s, vb_s, ob, ohr, ghb, ghr,
    f_win, f_wout, f_wexp, f_wshr, f_gb, f_gg, f_ge,
    rand_ref, glob_ref, doc_ref, bia, gai, ebi,
    ssem, rsem, lsem,
):
    ctx = lax.axis_index("ctx")
    seq = lax.axis_index("fsdp")
    z, x = ctx // 2, ctx % 2
    y, c = seq // 2, seq % 2
    zh, zl = z // 2, z % 2
    r = 2 * zl + x
    f = seq

    def dev(px, py, pz, pc):
        return (2 * pz + px, 2 * py + pc)

    def flip(v, on):
        return v + on - 2 * v * on

    def peer(j):
        return dev(flip(x, j % 2), y, 2 * zh + flip(zl, j // 2), c)

    def peer_rank(j):
        return 2 * flip(zl, j // 2) + flip(x, j % 2)

    peers = [peer(j) for j in range(4)]
    ranks = [peer_rank(j) for j in range(4)]
    core_mate = dev(x, y, z, 1 - c)
    y_mate = dev(x, 1 - y, z, c)
    z_mate = dev(x, y, 2 * (1 - zh) + zl, c)
    home = dev(x, y, 2 * c + zl, zh)

    pending = []
    counts = {"s": 0, "r": 0, "l": 0}

    def take(kind, n, most):
        first = counts[kind]
        counts[kind] = first + n
        assert counts[kind] <= most
        return first

    def recvs(n):
        return take("r", n, RECVS)

    def sends(n):
        return take("s", n, SENDS)

    def local(src, dst):
        cp = pltpu.make_async_copy(src, dst, lsem.at[take("l", 1, LOCALS)])
        cp.start()
        return cp

    def copy_to(src, dst, si, ri, to):
        return pltpu.make_async_remote_copy(
            src_ref=src, dst_ref=dst, send_sem=ssem.at[si], recv_sem=rsem.at[ri],
            device_id=to, device_id_type=MESH,
        )

    def send(src, dst, ri, to):
        si = sends(1)
        copy_to(src, dst, si, ri, to).start()
        pending.append(lambda: copy_to(src, dst, si, ri, to).wait_send())

    def send_or_keep(src, dst, ri, to):
        si = sends(1)
        away = jnp.logical_or(to[0] != ctx, to[1] != seq)

        @pl.when(away)
        def _():
            copy_to(src, dst, si, ri, to).start()

        @pl.when(jnp.logical_not(away))
        def _():
            pltpu.make_async_copy(src, dst, rsem.at[ri]).start()

        def finish():
            @pl.when(jnp.logical_or(to[0] != ctx, to[1] != seq))
            def _():
                copy_to(src, dst, si, ri, to).wait_send()

        pending.append(finish)

    def arrived(dst, ri):
        pltpu.make_async_copy(dst, dst, rsem.at[ri]).wait()

    def split(rows):
        return [(1, 0, rows), (2, rows, 128 - rows)]

    def near_parts(buf, rows):
        return [
            (j, buf.at[ranks[j]], buf.at[ranks[j], pl.ds(at, size)] if size else None)
            for j, at, size in split(rows)
        ]

    def pass_on(parts, first):
        for j, block, part in parts:
            arrived(block, first + j)
            if part is not None:
                send(part, part, first + 3 * (2 - j), peers[3 - j])

    def far_arrived(buf, first, rows):
        for j, at, size in split(rows):
            if size:
                arrived(buf.at[ranks[3], pl.ds(at, size)], first + 3 * (2 - j))

    def merging(out, rs, rd):
        k_rs, s_rs, k_rd, s_rd = recvs(4), sends(4), recvs(2), sends(2)

        def to_near(i):
            return copy_to(
                out.at[3, pl.ds(64 * i, 64)], rd.at[i], s_rd + i, k_rd + i, peers[1 + i]
            )

        def to_peer(j, i):
            at = 2 * (j - 1) + i
            rows = pl.ds(64 * i, 64)
            return copy_to(out.at[j, rows], rs.at[j, rows], s_rs + at, k_rs + at, peers[j])

        def far_done():
            for i in range(2):
                to_near(i).start()

        def merge():
            for j, i in ((2, 0), (1, 1)):
                arrived(rd.at[i], k_rd + i)
                rows = pl.ds(64 * i, 64)
                out[j, rows] = (out[j, rows].astype(F32) + rd[i].astype(F32)).astype(BF)
                to_peer(j, i).start()

        def finish():
            for i in range(2):
                to_near(i).wait_send()
                for j in (1, 2):
                    to_peer(j, i).wait_send()

        def here(j, i):
            arrived(rs.at[j, pl.ds(64 * i, 64)], k_rs + 2 * (j - 1) + i)

        pending.append(finish)
        return far_done, lambda: to_peer(2, 1).start(), lambda: to_peer(1, 0).start(), merge, here

    def served(step, services):
        def run(k, carry):
            for at, before, serve in services:
                if before:
                    pl.when(k == at)(serve)
            step(k)
            for at, before, serve in services:
                if not before:
                    pl.when(k == at)(serve)
            return carry

        return run

    barrier = pltpu.get_barrier_semaphore()
    place = 2 * ctx + c
    for d in range(1, 16):
        other = (place + d) % 16
        pl.semaphore_signal(
            barrier, inc=1, device_id=(other // 2, 2 * y + other % 2), device_id_type=MESH
        )
    pl.semaphore_signal(barrier, inc=1, device_id=y_mate, device_id_type=MESH)
    small = [
        local(*pair)
        for pair in ((rand_hbm, rand_ref), (glob_hbm, glob_ref), (doc_hbm, doc_ref), (bia_hbm, bia), (gai_hbm, gai), (ebi_hbm, ebi))
    ]
    in_win, in_wout = local(win, winv), local(wout, woutv)

    for copy in small:
        copy.wait()

    lane = lax.broadcasted_iota(jnp.int32, (1, 128), 1)
    for i in range(2):
        block = 2 * ctx + i
        links = [jnp.maximum(block - 1, 0), block, jnp.minimum(block + 1, 15)]
        links += [rand_ref[i, k] for k in range(3)] + [glob_ref[0, k] for k in range(2)]
        count = jnp.zeros((1, 128), F32)
        for link in links:
            count += jnp.where(jnp.logical_or(lane == link + 72, lane == link + 88), 1.0, 0.0)
        ms[i : i + 1, :] = count
    edge = doc_ref[0, 0]
    edges = jnp.zeros((1, 128), F32)
    for k in range(7):
        edges += jnp.where(lane == k, edge.astype(F32), 0.0)
        edge = edge + doc_ref[0, k + 1]
    ms[2:3, :] = edges
    ms[3:8, :] = jnp.zeros((5, 128), F32)
    ps[...] = jnp.zeros((16, 128), F32)
    ps[0:6, 0:96] = bia[...].astype(F32)
    ps[6:8, 0:96] = gai[...].astype(F32)
    ps[8:11, :] = ebi[...].astype(F32)
    in_win.wait()
    for j in range(3):
        win3[j] = pack(winv[:, 96 * j : 96 * j + 96])

    pl.semaphore_wait(barrier, 16)

    k_h, k_x, k_m, k_e = recvs(1), recvs(4), recvs(4), recvs(1)
    send_or_keep(hid, xg.at[r], k_h, home)
    send_or_keep(ms, mg.at[r], k_m, home)
    k_win = recvs(6)
    for j in range(3):
        unit = 3 * ctx + j
        rank = (unit % 8) // 2
        slot = 2 * (unit // 8) + unit % 2
        for half in range(2):
            send_or_keep(
                win3.at[j], win_p.at[f, slot], k_win + slot, dev(rank % 2, y, 2 * half + rank // 2, c)
            )
    k_par = recvs(8)
    for d in range(1, 8):
        other = (ctx + d) % 8
        send(ps, par.at[ctx], k_par + d, (other, seq))
    par[ctx] = ps[...]
    in_wout.wait()
    wout1[...] = pack(woutv[...])

    arrived(xg.at[r], k_h)
    arrived(mg.at[r], k_m)
    for j in range(1, 4):
        if j < 3:
            send(xg.at[r], xg.at[r], k_x + j, peer(j))
        send(mg.at[r], mg.at[r], k_m + j, peer(j))
    k_wout_y, k_wout_c = recvs(1), recvs(2)
    k_wexp_y, k_wexp_c = recvs(1), recvs(2)
    k_wshr_y, k_wshr_c = recvs(1), recvs(2)
    k_wout = recvs(8)
    for d in range(8):
        other = (ctx + d) % 8
        if d == 0:
            pltpu.make_async_copy(wout1, wout_p.at[f, ctx], rsem.at[k_wout]).start()
        else:
            send(wout1, wout_p.at[f, ctx], k_wout + d, (other, seq))


    def sided(positions, rows):
        segs = jnp.zeros((rows, 1), F32)
        for k in range(7):
            segs += jnp.where(positions >= mg[r, 2:3, k : k + 1], 1.0, 0.0)
        return segs

    wide = lax.broadcasted_iota(jnp.int32, (1024, 128), 1)
    key_row = lax.broadcasted_iota(jnp.int32, (1024, 1), 0)
    key_segs = sided(key_row.astype(F32), 1024).astype(jnp.int32) + 64
    hot = jnp.logical_or(
        jnp.logical_and(wide < 72, wide == key_segs),
        jnp.logical_and(
            wide >= 72,
            jnp.logical_or(wide == key_row // 64 + 72, wide == key_row // 64 + 88),
        ),
    )
    hot = jnp.where(hot, 1.0, 0.0).astype(BF)
    ones = jnp.where(jnp.logical_or(wide == 64, wide == 65), 1.0, 0.0).astype(BF)
    for h in range(3):
        kh[h, :, 64:128] = hot[:, 64:128]
        vh[h, :, 64:128] = ones[:, 64:128]

    k_win_y, k_win_c = recvs(1), recvs(2)
    for slot in range(6):
        arrived(win_p.at[f, slot], k_win + slot)
    send(win_p.at[f], win_p.at[f], k_win_y, y_mate)
    send(win_p.at[f], win_p.at[f], k_win_c, core_mate)
    pass_on(near_parts(xg, 64), k_x)
    k_wexp = recvs(2)
    mine_exp = wexp_f.at[f, :, pl.ds(pl.multiple_of(384 * zh, 128), 384)]
    pltpu.make_async_copy(wexp, mine_exp, rsem.at[k_wexp]).start()
    send(wexp, mine_exp, k_wexp + 1, z_mate)

    for d in range(1, 8):
        arrived(par.at[(ctx + 8 - d) % 8], k_par + d)
    prm[...] = jnp.concatenate([par[b, 0:8, 0:96] for b in range(8)], axis=1)
    be = jnp.concatenate(
        [par[r, 8 + i : 9 + i, :] for i in range(3)] + [par[4 + r, 8 + i : 9 + i, :] for i in range(3)],
        axis=1,
    )
    zrow = jnp.zeros((1, 192), F32)
    z_bias = jnp.concatenate(
        [par[2 * r, 0:1, 0:96], par[2 * r + 1, 0:1, 0:96], zrow, par[2 * r, 1:2, 0:96], par[2 * r + 1, 1:2, 0:96]],
        axis=1,
    )

    row_pos = lax.broadcasted_iota(jnp.int32, (512, 1), 0) + 512 * c
    row_segs = sided(row_pos.astype(F32), 512).astype(jnp.int32) + 64
    for j in range(1, 4):
        arrived(mg.at[peer_rank(j)], k_m + j)
    for i in range(8):
        count = mg[i // 2, i % 2 : i % 2 + 1, :]
        logs = jnp.log(jnp.maximum(count, 1.0))
        high = logs.astype(BF).astype(F32)
        line = jnp.where(lane < 88, jnp.where(count > 0.5, high, NEG), logs - high)
        line = jnp.where(lane < 104, line, 0.0)
        same = row_segs[64 * i : 64 * i + 64] == wide[0:64]
        block = jnp.where(wide[0:64] < 72, jnp.where(same, 0.0, NEG), line)
        mq[i // 2, 64 * (i % 2) : 64 * (i % 2) + 64, :] = block.astype(BF)
    for h in range(3):
        q_s[:, h, :, 64:128] = mq[:, :, 64:128]

    f_y = 2 * (1 - y) + c
    arrived(win_p.at[f_y], k_win_y)
    send(win_p.at[f_y], win_p.at[f_y], k_win_c + 1, core_mate)
    for d in range(8):
        arrived(wout_p.at[f, (ctx + 8 - d) % 8], k_wout + d)
    send(wout_p.at[f], wout_p.at[f], k_wout_y, y_mate)
    send(wout_p.at[f], wout_p.at[f], k_wout_c, core_mate)
    k_wshr = recvs(4)
    at_half = pl.ds(pl.multiple_of(384 * y, 128), 384)
    for sub in range(2):
        for half in range(2):
            send_or_keep(
                wshr.at[:, 384 * sub : 384 * sub + 384], ws.at[2 * zh + zl, x, :, at_half],
                k_wshr + 2 * zh + zl, dev(sub, y, 2 * half + c, x),
            )


    def place_in(k):
        for q in range(4):
            w_in[pl.ds(pl.multiple_of(192 * k + 48 * q, 16), 48), :] = jnp.concatenate(
                [win_p[k, i, :, 96 * q : 96 * q + 96] for i in range(6)], axis=1
            )

    place_in(f)
    place_in(f_y)
    arrived(win_p.at[2 * y + 1 - c], k_win_c)
    place_in(2 * y + 1 - c)
    arrived(win_p.at[2 * (1 - y) + 1 - c], k_win_c + 1)
    place_in(2 * (1 - y) + 1 - c)

    def project(k):
        mixed = dot_nn(xg[k], w_in[...]) + z_bias
        queries = (mixed[:, 0:192].astype(BF).astype(F32) * 0.125).astype(BF)
        for h in range(3):
            q_s[k, h, :, 0:64] = queries[:, 64 * h : 64 * h + 64]
        kv[c, pl.ds(pl.multiple_of(128 * k, 128), 128), :] = mixed[:, 192:576].astype(BF)

    lax.fori_loop(
        0, 4,
        served(lambda j: project(peer_rank(j)), [(3, True, lambda: far_arrived(xg, k_x, 64))]), 0,
    )
    k_kv = recvs(1)
    send(kv.at[c], kv.at[c], k_kv, core_mate)

    def split_heads(half):
        at = pl.ds(pl.multiple_of(512 * half, 512), 512)
        for h in range(3):
            kh[h, at, 0:64] = kv[half, :, 64 * h : 64 * h + 64]
            vh[h, at, 0:64] = kv[half, :, 192 + 64 * h : 256 + 64 * h]

    split_heads(c)
    arrived(mine_exp, k_wexp)
    arrived(wexp_f.at[f, :, pl.ds(pl.multiple_of(384 * (1 - zh), 128), 384)], k_wexp + 1)
    send(wexp_f.at[f], wexp_f.at[f], k_wexp_y, y_mate)
    send(wexp_f.at[f], wexp_f.at[f], k_wexp_c, core_mate)
    arrived(kv.at[1 - c], k_kv)
    split_heads(1 - c)

    k_a, s_a = recvs(16), sends(16)

    def attend(k):
        outs = []
        for h in range(3):
            scores = dot_nt(q_s[k, h], kh[h])
            top = jnp.max(scores, axis=1, keepdims=True)
            exps = jnp.exp(scores - top).astype(BF)
            e_s[h, k] = exps
            sums = dot_nn(exps, vh[h])
            scale = 1.0 / sums[:, 64:65]
            l_s[h, k] = scale
            outs.append(sums[:, 0:64] * scale)
        both = jnp.concatenate(outs, axis=1)
        a_f[k] = both
        low = both.astype(BF)
        a_b[k] = low
        a_all[r, k] = jnp.concatenate([low[0:64], low[64:128]], axis=1)
        for j in range(1, 4):
            at = 4 * j + k
            copy_to(a_all.at[r, k], a_all.at[r, k], s_a + at, k_a + at, peers[j]).start()

    wout_there, wexp_there = wout_p.at[f_y], wexp_f.at[f_y]
    ws_mine = ws.at[:, c, :, at_half]

    def relay_0():
        arrived(wout_there, k_wout_y)
        send(wout_there, wout_there, k_wout_c + 1, core_mate)

    def relay_1():
        for k in range(4):
            arrived(ws.at[k, c, :, at_half], k_wshr + k)
        send(ws_mine, ws_mine, k_wshr_y, y_mate)
        send(ws_mine, ws_mine, k_wshr_c, core_mate)

    def relay_2():
        arrived(wexp_there, k_wexp_y)
        send(wexp_there, wexp_there, k_wexp_c + 1, core_mate)

    lax.fori_loop(0, 4, served(attend, [(0, False, relay_0), (1, False, relay_1), (2, False, relay_2)]), 0)
    for j in range(1, 4):
        for k in range(4):
            at = 4 * j + k
            pending.append(
                copy_to(a_all.at[r, k], a_all.at[r, k], s_a + at, k_a + at, peer(j)).wait_send
            )
    send_or_keep(cot, eo, k_e, home)
    def place_out(k):
        for q in range(4):
            w_out[pl.ds(pl.multiple_of(192 * k + 48 * q, 16), 48), :] = jnp.concatenate(
                [wout_p[k, b, :, 96 * q : 96 * q + 96] for b in range(8)], axis=1
            )

    place_out(f)
    place_out(f_y)
    arrived(wout_p.at[2 * y + 1 - c], k_wout_c)
    place_out(2 * y + 1 - c)
    arrived(wout_p.at[2 * (1 - y) + 1 - c], k_wout_c + 1)
    place_out(2 * (1 - y) + 1 - c)
    other_half = pl.ds(pl.multiple_of(384 * (1 - y), 128), 384)
    arrived(ws.at[:, c, :, other_half], k_wshr_y)
    send(ws.at[:, c, :, other_half], ws.at[:, c, :, other_half], k_wshr_c + 1, core_mate)
    for j in range(1, 4):
        for k in range(4):
            arrived(a_all.at[peer_rank(j), k], k_a + 4 * j + k)
    arrived(wexp_f.at[2 * y + 1 - c], k_wexp_c)
    arrived(wexp_f.at[2 * (1 - y) + 1 - c], k_wexp_c + 1)

    def first_norm(k):
        rows = jnp.concatenate(
            [
                jnp.concatenate([a_all[src, k, :, 192 * i : 192 * i + 192] for src in range(4)], axis=1)
                for i in range(2)
            ],
            axis=0,
        )
        first = xg[k].astype(F32) + prm[2:3, :] + dot_nn(rows, w_out[...])
        centre = first - jnp.mean(first, axis=1, keepdims=True)
        inverse = lax.rsqrt(jnp.mean(centre * centre, axis=1, keepdims=True) + 1e-05)
        normed = centre * inverse
        hidden_one = normed * prm[6:7, :] + prm[3:4, :]
        hg[k] = hidden_one.astype(BF)
        return normed, inverse, hidden_one

    def expand(k):
        inner = dot_nn(hg[k], wexp_f[...].reshape(768, 768)) + be
        below = 0.5 * (1.0 + lax.erf(inner * 0.7071067811865476))
        u_s[k] = inner
        dge[k] = below
        active = (inner * below).astype(BF)
        g_s[k] = active

    def widen(k):
        normed, inverse, hidden_one = first_norm(k)
        n1_s[...] = normed
        r1_s[...] = inverse
        h1_s[...] = hidden_one
        expand(k)

    widen(ranks[3])
    arrived(ws.at[:, 1 - c, :, at_half], k_wshr_c)
    arrived(ws.at[:, 1 - c, :, other_half], k_wshr_c + 1)
    far_1, second_1, third_1, merge_1, here_1 = merging(yb, rs1, rd1)

    def expand_step(i, carry):
        j = 3 - i
        rank = peer_rank(j)

        @pl.when(i > 0)
        def _():
            widen(rank)

        value = dot_nt(g_s[rank], ws[...].reshape(768, 768))

        @pl.when(i < 3)
        def _():
            yb[j] = value.astype(BF)

        pl.when(i == 0)(far_1)
        pl.when(i == 1)(second_1)

        @pl.when(i == 2)
        def _():
            third_1()
            merge_1()

        @pl.when(i == 3)
        def _():
            ysum[...] = value

        return carry

    lax.fori_loop(0, 4, expand_step, 0)
    def slope(k, carry):
        inner = u_s[k]
        dge[k] = dge[k] + inner * jnp.exp(-0.5 * inner * inner) * 0.3989422804014327
        return carry

    lax.fori_loop(0, 4, slope, 0)

    arrived(eo, k_e)
    upstream = eo[...].astype(F32)
    scaled = upstream * prm[7:8, :]
    scaled_mean = jnp.mean(scaled, axis=1, keepdims=True)
    row_shift_two = row_sum(upstream)
    second = h1_s[...] + prm[4:5, :] + ysum[...]
    for j in range(1, 3):
        for i in range(2):
            here_1(j, i)
        second += rs1[j].astype(F32)
    centre = second - jnp.mean(second, axis=1, keepdims=True)
    inverse = lax.rsqrt(jnp.mean(centre * centre, axis=1, keepdims=True) + 1e-05)
    normed = centre * inverse
    grad_two = inverse * (
        scaled - scaled_mean - normed * jnp.mean(scaled * normed, axis=1, keepdims=True)
    )
    dg[r] = grad_two.astype(BF)
    k_d = recvs(4)
    for j in range(1, 3):
        send(dg.at[r], dg.at[r], k_d + j, peer(j))
    d2_s[...] = grad_two
    ob[...] = (normed * prm[7:8, :] + prm[5:6, :]).astype(BF)
    k_o = recvs(1)
    send_or_keep(ob, ohr, k_o, home)
    row_gain_two = row_sum(upstream * normed)
    row_back = row_sum(grad_two)

    def contract(k):
        inner = dge[k] * dot_nn(dg[k], ws[...].reshape(768, 768))
        low = inner.astype(BF)
        du_s[k] = low
        beg[k] = row_sum(inner)
        return dot_nt(low, wexp_f[...].reshape(768, 768))

    k_r2, s_r2 = recvs(4), sends(4)

    def contract_step(j):
        value = contract(peer_rank(j))

        @pl.when(j == 0)
        def _():
            ysum[...] = value

        @pl.when(j > 0)
        def _():
            dh_b[j] = value.astype(BF)
            copy_to(dh_b.at[j], rs2.at[j], s_r2 + j, k_r2 + j, peer(j)).start()

    dg_parts = near_parts(dg, 64)
    gathered = [
        (1, True, lambda: pass_on(dg_parts, k_d)),
        (3, True, lambda: far_arrived(dg, k_d, 64)),
    ]
    lax.fori_loop(0, 4, served(contract_step, gathered), 0)
    for j in range(1, 4):
        pending.append(copy_to(dh_b.at[j], rs2.at[j], s_r2 + j, k_r2 + j, peer(j)).wait_send)

    for k in range(4):
        rows = dg[:, :, 192 * k : 192 * k + 192].reshape(512, 192)
        gs[k] = dot_tn(rows, g_s[...].reshape(512, 768)).astype(BF).reshape(2, 96, 768)
    k_gs = recvs(1)
    send(gs.at[:, 1 - c], rs_c, k_gs, core_mate)

    def expand_grad(i, carry):
        at = pl.ds(pl.multiple_of(128 * i, 128), 128)
        rows = hg[:, :, at].reshape(512, 128)
        ge[at, :] = dot_tn(rows, du_s[...].reshape(512, 768)).astype(BF)
        return carry

    lax.fori_loop(0, 6, expand_grad, 0)
    k_ge = recvs(2)
    for half in range(2):
        at = pl.ds(pl.multiple_of(192 * (2 * half + 1 - c), 64), 192)
        send(ge.at[at, :], re_c.at[half], k_ge + half, core_mate)
    k_gs_y, k_ge_y = recvs(1), recvs(1)
    arrived(rs_c, k_gs)
    t_shr[...] = (
        gs[:, c, :, other_half].astype(F32) + rs_c[:, :, other_half].astype(F32)
    ).astype(BF)
    send(t_shr, rs_y, k_gs_y, y_mate)

    grad_hidden = d2_s[...] + ysum[...]
    for j in range(1, 4):
        arrived(rs2.at[j], k_r2 + j)
        grad_hidden += rs2[j].astype(F32)
    normed = n1_s[...]
    scaled = grad_hidden * prm[6:7, :]
    grad_one = r1_s[...] * (
        scaled
        - jnp.mean(scaled, axis=1, keepdims=True)
        - normed * jnp.mean(scaled * normed, axis=1, keepdims=True)
    )
    low_one = grad_one.astype(BF)
    d1g[r] = low_one
    for k in range(4):
        dab[k] = dot_nt(low_one, w_out[192 * k : 192 * k + 192, :]).astype(BF)
    k_da, k_d1 = recvs(4), recvs(4)
    for j in range(1, 4):
        send(dab.at[peer_rank(j)], da.at[r], k_da + j, peer(j))
    da[r] = dab[r]
    d1_s[...] = grad_one
    row_gain_one = row_sum(grad_hidden * normed)
    row_shift_one = row_sum(grad_hidden)
    row_out = row_sum(grad_one)

    for half in range(2):
        arrived(re_c.at[half], k_ge + half)
    at_y = pl.ds(pl.multiple_of(192 * f_y, 64), 192)
    at_own = pl.ds(pl.multiple_of(192 * f, 64), 192)
    t_exp[...] = (ge[at_y, :].astype(F32) + re_c[1 - y].astype(F32)).astype(BF)
    send(t_exp, re_y, k_ge_y, y_mate)


    d1g_mine = d1g.at[r]

    def send_d1():
        for j in range(1, 3):
            send(d1g_mine, d1g_mine, k_d1 + j, peers[j])

    def attend_back(j):
        k = peer_rank(j)

        @pl.when(j > 0)
        def _():
            arrived(da.at[k], k_da + j)

        outs = []
        grads = da[k].astype(F32)
        dots = grads * a_f[k]
        for h in range(3):
            at = slice(64 * h, 64 * h + 64)
            scale = l_s[h, k]
            delta = jnp.sum(dots[:, at], axis=1, keepdims=True) * scale
            high = delta.astype(BF).astype(F32)
            side = jnp.where(wide[0:128, 0:64] == 0, -high, 0.0)
            side = jnp.where(wide[0:128, 0:64] == 1, high - delta, side)
            both = jnp.concatenate([grads[:, at] * scale, side], axis=1).astype(BF)
            de[k, h] = both
            low = (e_s[h, k].astype(F32) * dot_nt(both, vh[h])).astype(BF)
            ds_s[h, k] = low
            outs.append(dot_nn(low, kh[h])[:, 0:64] * 0.125)
        queries = jnp.concatenate(outs, axis=1)
        qb_s[k] = row_sum(queries)
        dz[k, :, 0:192] = queries.astype(BF)

    k_fs, k_re = recvs(4), recvs(1)
    shrink_owners = [dev(c, y, k, zl) for k in range(4)]
    fs_at = fs.at[zh, x]
    fsb_at = [fsb.at[k] for k in range(4)]
    k_own = k_fs + 2 * zh + x

    def pass_0():
        arrived(rs_y, k_gs_y)
        fsb[...] = (
            gs[:, c, :, at_half].astype(F32) + rs_c[:, :, at_half].astype(F32) + rs_y[...].astype(F32)
        ).astype(BF)
        for k in range(4):
            send_or_keep(fsb_at[k], fs_at, k_own, shrink_owners[k])

    def pass_1():
        arrived(re_y, k_ge_y)
        te_f[...] = ge[at_own, :].astype(F32) + re_c[y].astype(F32) + re_y[...].astype(F32)
        te_b[...] = te_f[:, pl.ds(pl.multiple_of(384 * (1 - zh), 128), 384)].astype(BF)
        send(te_b, re_z, k_re, z_mate)

    d1g_parts = near_parts(d1g, 0)

    def pass_2():
        pass_on(d1g_parts, k_d1)

    lax.fori_loop(0, 4, served(attend_back, [(0, False, send_d1), (1, False, pass_0), (2, False, pass_1), (3, False, pass_2)]), 0)
    sums = []
    for h in range(3):
        rows = q_s[:, h, :, 0:64].reshape(512, 64)
        sums.append(dot_tn(rows, ds_s[h].reshape(512, 1024)))
    for h in range(3):
        rows = de[:, h, :, 0:64].reshape(512, 64)
        sums.append(dot_tn(rows, e_s[h].reshape(512, 1024)))
    sums = jnp.concatenate(sums, axis=0)
    dkv[0] = sums[:, 0:512].T
    dkv[1] = sums[:, 512:1024].T
    dkb[...] = dkv[1 - c].astype(BF)
    k_dk = recvs(1)
    send(dkb, dkr, k_dk, core_mate)

    def project_grad(first, count):
        for k in range(4):
            rows = xg[:, :, 192 * k : 192 * k + 192].reshape(512, 192)
            cols = dz[:, :, 96 * first : 96 * first + 96 * count].reshape(512, 96 * count)
            part = dot_tn(rows, cols).astype(BF)
            for slot in range(count):
                gi[k, first + slot] = pack(part[:, 96 * slot : 96 * slot + 96])

    some = {"q": pl.ds(0, 2), "kv": pl.ds(2, 4)}
    k_gi = {"q": recvs(2), "kv": recvs(2)}
    k_gi_y = {"q": recvs(1), "kv": recvs(1)}

    def over_cores(which):
        at = some[which]
        for half in range(2):
            send(gi.at[2 * half + 1 - c, at], ri_c.at[half, at], k_gi[which] + half, core_mate)

    def over_y(which):
        at = some[which]
        for half in range(2):
            arrived(ri_c.at[half, at], k_gi[which] + half)
        tib[at] = (gi[f_y, at].astype(F32) + ri_c[1 - y, at].astype(F32)).astype(BF)
        send(tib.at[at], ri_y.at[at], k_gi_y[which], y_mate)

    k_fi = recvs(6)

    def to_owners(which):
        at = some[which]
        arrived(ri_y.at[at], k_gi_y[which])
        ti2[at] = (
            gi[f, at].astype(F32) + ri_c[y, at].astype(F32) + ri_y[at].astype(F32)
        ).astype(BF)
        for slot in range(2) if which == "q" else range(2, 6):
            unit = 8 * (slot // 2) + 2 * r + slot % 2
            send_or_keep(
                ti2.at[slot], fi.at[zh, unit % 3], k_fi + 3 * zh + unit % 3, (unit // 3, seq)
            )

    project_grad(0, 2)
    over_cores("q")

    arrived(dkr, k_dk)
    keyvals = dkv[c] + dkr[...].astype(F32)
    vb_s[...] = row_sum(keyvals[:, 192:384])
    dz[:, :, 192:576] = keyvals.astype(BF).reshape(4, 128, 384)

    def input_part(k):
        return dot_nt(dz[k], w_in[...])

    far_3, second_3, third_3, merge_3, here_3 = merging(dx_b, rs3, rd3)

    def input_step(i, carry):
        j = 3 - i
        dx_b[j] = input_part(peer_rank(j)).astype(BF)
        pl.when(i == 0)(far_3)
        pl.when(i == 1)(second_3)
        pl.when(i == 2)(third_3)
        return carry

    lax.fori_loop(0, 3, input_step, 0)
    over_y("q")
    project_grad(2, 4)
    over_cores("kv")
    merge_3()

    far_arrived(d1g, k_d1, 0)
    part = dot_tn(a_b[...].reshape(512, 192), d1g[...].reshape(512, 768))
    for b in range(8):
        go[b % 2, b // 2] = pack(part[:, 96 * b : 96 * b + 96].astype(BF))
    k_go = recvs(1)
    send(go.at[1 - c], ro_c, k_go, core_mate)

    over_y("kv")

    vg[...] = jnp.zeros((8, 16, 128), F32)
    rows = jnp.concatenate(
        [row_out, row_shift_one, row_back, row_shift_two, row_gain_one, row_gain_two], axis=0
    )
    for b in range(8):
        vg[b, 2:8, 0:96] = rows[:, 96 * b : 96 * b + 96]
    q_row = row_sum(qb_s[:, 0, :])
    v_row = vb_s[...]
    for i in range(2):
        vg[2 * r + i, 0:1, 0:96] = q_row[:, 96 * i : 96 * i + 96]
        vg[2 * r + i, 1:2, 0:96] = v_row[:, 96 * i : 96 * i + 96]
    inner_row = row_sum(beg[:, 0, :])
    for i in range(3):
        vg[r, 8 + i : 9 + i, :] = inner_row[:, 128 * i : 128 * i + 128]
        vg[4 + r, 8 + i : 9 + i, :] = inner_row[:, 384 + 128 * i : 512 + 128 * i]
    k_v = recvs(8)
    for d in range(1, 8):
        other = (ctx + d) % 8
        send(vg.at[other], vr.at[d], k_v + d, (other, seq))

    arrived(ro_c, k_go)
    tob[...] = (go[c].astype(F32) + ro_c[...].astype(F32)).astype(BF)
    k_go_y, k_fo = recvs(1), recvs(2)
    s_go, s_fo = sends(1), sends(4)
    stays = y == zl

    @pl.when(jnp.logical_not(stays))
    def _():
        copy_to(tob, ro_y, s_go, k_go_y, y_mate).start()

    k_gh = recvs(2)
    ysum[...] = d1_s[...] + input_part(r)

    def finish_input(i):
        at = pl.ds(64 * i, 64)
        grad_in = ysum[at, :]
        for j in range(1, 3):
            here_3(j, i)
            grad_in += rs3[j, at, :].astype(F32)
        ghb[at, :] = grad_in.astype(BF)
        send_or_keep(ghb.at[at, :], ghr.at[at, :], k_gh + i, home)

    to_owners("q")
    finish_input(0)

    done = []

    for half in range(2):
        for sub in range(2):
            arrived(fs.at[half, sub], k_fs + 2 * half + sub)
    for sub in range(2):
        f_wshr[:, 384 * sub : 384 * sub + 384] = fs[0, sub].astype(F32) + fs[1, sub].astype(F32)
    done.append(local(f_wshr, o_wshr))
    arrived(re_z, k_re)
    f_wexp[...] = te_f[:, pl.ds(pl.multiple_of(384 * zh, 128), 384)] + re_z[...].astype(F32)
    done.append(local(f_wexp, o_wexp))

    to_owners("kv")
    finish_input(1)

    @pl.when(stays)
    def _():
        arrived(ro_y, k_go_y)
        tob2[...] = (tob[...].astype(F32) + ro_y[...].astype(F32)).astype(BF)
        for k in range(4):
            to = dev(c, y, k, x)
            away = jnp.logical_or(to[0] != ctx, to[1] != seq)

            @pl.when(away)
            def _():
                copy_to(tob2.at[k], fo.at[zh], s_fo + k, k_fo + zh, to).start()

            @pl.when(jnp.logical_not(away))
            def _():
                pltpu.make_async_copy(tob2.at[k], fo.at[zh], rsem.at[k_fo + zh]).start()

    def finish_out():
        @pl.when(jnp.logical_not(stays))
        def _():
            copy_to(tob, ro_y, s_go, k_go_y, y_mate).wait_send()

        @pl.when(stays)
        def _():
            for k in range(4):
                to = dev(c, y, k, x)

                @pl.when(jnp.logical_or(to[0] != ctx, to[1] != seq))
                def _():
                    copy_to(tob2.at[k], fo.at[zh], s_fo + k, k_fo + zh, to).wait_send()

    pending.append(finish_out)

    total = vg[ctx]
    for d in range(1, 8):
        arrived(vr.at[d], k_v + d)
        total += vr[d]
    vs1[...] = total
    k_vc = recvs(2)
    send(vs1, vc, k_vc, core_mate)
    arrived(vc, k_vc)
    vs2[...] = vs1[...] + vc[...]
    send(vs2, vy, k_vc + 1, y_mate)

    arrived(ohr, k_o)
    done.append(local(ohr, o_out))
    arrived(vy, k_vc + 1)
    total = vs2[...] + vy[...]
    f_gb[...] = total[0:6, 0:96]
    f_gg[...] = total[6:8, 0:96]
    f_ge[...] = total[8:11, :]
    done += [local(f_gb, o_gb), local(f_gg, o_gg), local(f_ge, o_ge)]
    for half in range(2):
        arrived(fo.at[half], k_fo + half)
    part = fo[0].astype(F32) + fo[1].astype(F32)
    for q in range(4):
        f_wout[48 * q : 48 * q + 48, :] = part[:, 96 * q : 96 * q + 96]
    done.append(local(f_wout, o_wout))
    for half in range(2):
        for j in range(3):
            arrived(fi.at[half, j], k_fi + 3 * half + j)
    parts = [fi[0, j].astype(F32) + fi[1, j].astype(F32) for j in range(3)]
    for q in range(4):
        f_win[48 * q : 48 * q + 48, :] = jnp.concatenate(
            [part[:, 96 * q : 96 * q + 96] for part in parts], axis=1
        )
    done.append(local(f_win, o_win))
    for i in range(2):
        arrived(ghr.at[pl.ds(64 * i, 64), :], k_gh + i)
    done.append(local(ghr, o_gh))
    for finish in pending:
        finish()
    for copy in done:
        copy.wait()


def hand_over(*refs):
    ins, outs, held, into, out_of = refs[0:9], refs[9:18], refs[18:27], refs[27], refs[28]
    loads = [pltpu.make_async_copy(ins[i], held[i], into.at[i]) for i in range(9)]
    stores = [pltpu.make_async_copy(held[i], outs[i], out_of.at[i]) for i in range(9)]
    for load in loads:
        load.start()
    for load, store in zip(loads, stores):
        load.wait()
        store.start()
    for store in stores:
        store.wait()


def fast_shards(
    hidden, project_in, project_out, expand_weight, shrink_weight, biases, gains, expand_bias,
    random_blocks, global_blocks, document_lengths, cotangent,
):
    vm = lambda *dims: pltpu.VMEM(dims, BF)
    vf = lambda *dims: pltpu.VMEM(dims, F32)
    scratch = [
        vm(192, 288), vm(192, 96), vm(3, 48, 384), vm(48, 384), vm(4, 128, 768), vm(128, 768),
        vf(8, 128), vf(4, 8, 128), vf(16, 128), vf(8, 16, 128), vm(4, 6, 48, 384), vm(4, 8, 48, 384),
        vm(4, 192, 768), vm(4, 2, 96, 768), vm(768, 576), vm(768, 768), vf(8, 768),
        vm(4, 128, 128), vm(4, 3, 128, 128), vm(2, 512, 384), vm(3, 1024, 128), vm(3, 1024, 128),
        vm(3, 4, 128, 1024), vf(3, 4, 128, 1), vf(4, 128, 192), vm(4, 128, 192), vm(4, 4, 64, 384),
        vm(4, 128, 768), vf(128, 768), vf(128, 768), vf(128, 1), vf(4, 128, 768), vf(4, 128, 768), vm(4, 128, 768),
        vf(128, 768), vm(4, 128, 768),
        vm(2, 64, 768), vm(2, 64, 768), vm(4, 128, 768), vf(128, 768), vm(4, 128, 768),
        vm(4, 128, 768), vm(4, 128, 768),
        vm(4, 128, 768), vf(4, 1, 768), vf(128, 768), vm(4, 128, 768), vm(4, 128, 192),
        vm(4, 128, 192), vm(4, 3, 128, 128), vm(3, 4, 128, 1024), vf(2, 512, 384), vm(512, 384),
        vm(512, 384), vm(4, 128, 576), vm(4, 128, 768), vm(4, 128, 768),
        vm(4, 2, 96, 768), vm(4, 96, 768), vm(4, 96, 384), vm(4, 96, 384), vm(4, 96, 384),
        vm(2, 2, 96, 384), vm(768, 768), vm(2, 192, 768), vm(192, 768), vm(192, 768), vf(192, 768),
        vm(192, 384), vm(192, 384),
        vm(2, 4, 48, 384), vm(4, 48, 384), vm(4, 48, 384), vm(4, 48, 384), vm(4, 48, 384),
        vm(2, 48, 384), vm(4, 6, 48, 384), vm(2, 6, 48, 384), vm(6, 48, 384), vm(6, 48, 384),
        vm(6, 48, 384), vm(2, 3, 48, 384),
        vf(8, 16, 128), vf(8, 16, 128), vf(16, 128), vf(16, 128), vf(16, 128), vf(16, 128),
        vf(4, 1, 192), vf(1, 192), vm(128, 768), vm(128, 768), vm(128, 768), vm(128, 768),
        vf(192, 288), vf(192, 96), vf(192, 384), vf(96, 768), vf(6, 96), vf(2, 96), vf(3, 128),
        pltpu.SMEM((2, 3), jnp.int32), pltpu.SMEM((1, 2), jnp.int32), pltpu.SMEM((1, 8), jnp.int32),
        vm(6, 96), vm(2, 96), vm(3, 128),
        pltpu.SemaphoreType.DMA((SENDS,)), pltpu.SemaphoreType.DMA((RECVS,)),
        pltpu.SemaphoreType.DMA((LOCALS,)),
    ]
    out = lambda kind, *dims: jax.ShapeDtypeStruct(dims, kind)
    shapes = (
        out(BF, 128, 768), out(BF, 128, 768), out(F32, 192, 288), out(F32, 192, 96),
        out(F32, 192, 384), out(F32, 96, 768), out(F32, 6, 96), out(F32, 2, 96), out(F32, 3, 128),
    )
    anywhere = pl.BlockSpec(memory_space=pl.ANY)
    results = pl.pallas_call(
        layer_kernel,
        out_shape=shapes,
        in_specs=[anywhere] * 12,
        out_specs=(anywhere,) * 9,
        scratch_shapes=scratch,
        compiler_params=pltpu.CompilerParams(
            collective_id=0, has_side_effects=True, vmem_limit_bytes=58 * 1024 * 1024
        ),
    )(
        random_blocks[0], global_blocks, document_lengths, biases, gains,
        expand_bias.reshape(3, 128), hidden[0], cotangent[0], project_in, project_out,
        expand_weight, shrink_weight.T,
    )
    results = pl.pallas_call(
        hand_over,
        out_shape=shapes,
        in_specs=[anywhere] * 9,
        out_specs=(anywhere,) * 9,
        scratch_shapes=[pltpu.VMEM(one.shape, one.dtype) for one in shapes]
        + [pltpu.SemaphoreType.DMA((9,))] * 2,
    )(*results)
    return (
        results[0][None], results[1][None], results[2], results[3], results[4], results[5].T,
        results[6], results[7], results[8].reshape(-1),
    )


def solution(mesh):
    small = tuple(mesh.shape[name] for name in ("ctx", "fsdp")) == (8, 4)
    return jax.shard_map(
        fast_shards if small else shards,
        mesh=mesh,
        in_specs=(
            P("fsdp", "ctx", None),
            P("fsdp", "ctx"),
            P("fsdp", "ctx"),
            P("fsdp", "ctx"),
            P("fsdp", "ctx"),
            P(None, "ctx"),
            P(None, "ctx"),
            P("ctx"),
            P("fsdp", "ctx", None),
            P("fsdp", None),
            P("fsdp", None),
            P("fsdp", "ctx", None),
        ),
        out_specs=(
            P("fsdp", "ctx", None),
            P("fsdp", "ctx", None),
            P("fsdp", "ctx"),
            P("fsdp", "ctx"),
            P("fsdp", "ctx"),
            P("fsdp", "ctx"),
            P(None, "ctx"),
            P(None, "ctx"),
            P("ctx"),
        ),
        check_vma=False,
    )
```

```python
import jax
import jax.numpy as jnp
from jax import lax
from jax.experimental import pallas as pl
from jax.experimental.pallas import tpu as pltpu
from jax.sharding import PartitionSpec as P

HEAD_DIM = 64
BLOCK = 64


def segment_of(positions, bounds):
    return jnp.sum((positions[..., None] >= bounds).astype(jnp.int32), axis=-1)


def layer_norm_parts(values, gain_row, shift_row):
    centre = values - jnp.mean(values, axis=-1, keepdims=True)
    inverse = lax.rsqrt(jnp.mean(centre * centre, axis=-1, keepdims=True) + 1e-05)
    normed = centre * inverse
    return (normed * gain_row + shift_row, normed, inverse)


def layer_norm_back(upstream, normed, inverse, gain_row):
    scaled = upstream * gain_row
    return inverse * (
        scaled
        - jnp.mean(scaled, axis=-1, keepdims=True)
        - normed * jnp.mean(scaled * normed, axis=-1, keepdims=True)
    )


def matmul(left_side, right_side):
    return jnp.dot(left_side, right_side, preferred_element_type=jnp.float32)


def matmul_left_t(left_side, right_side):
    return lax.dot_general(
        left_side, right_side, (((0,), (0,)), ((), ())), preferred_element_type=jnp.float32
    )


def matmul_right_t(left_side, right_side):
    return lax.dot_general(
        left_side, right_side, (((1,), (1,)), ((), ())), preferred_element_type=jnp.float32
    )


def over_cols(qkv_grad, out_grad, expand_grad, shrink_grad, vector_grad, gain_grad, inner_grad):
    return (
        lax.psum_scatter(qkv_grad, "ctx", scatter_dimension=1, tiled=True),
        lax.psum_scatter(out_grad, "ctx", scatter_dimension=1, tiled=True),
        lax.psum_scatter(expand_grad, "ctx", scatter_dimension=1, tiled=True),
        lax.psum_scatter(shrink_grad, "ctx", scatter_dimension=1, tiled=True),
        lax.psum_scatter(vector_grad, "ctx", scatter_dimension=1, tiled=True),
        lax.psum_scatter(gain_grad, "ctx", scatter_dimension=1, tiled=True),
        lax.psum_scatter(inner_grad, "ctx", scatter_dimension=1, tiled=True),
    )


def over_rows(qkv_grad, out_grad, expand_grad, shrink_grad):
    return (
        lax.psum_scatter(
            qkv_grad.astype(jnp.bfloat16), "fsdp", scatter_dimension=0, tiled=True
        ).astype(jnp.float32),
        lax.psum_scatter(
            out_grad.astype(jnp.bfloat16), "fsdp", scatter_dimension=0, tiled=True
        ).astype(jnp.float32),
        lax.psum_scatter(
            expand_grad.astype(jnp.bfloat16), "fsdp", scatter_dimension=0, tiled=True
        ).astype(jnp.float32),
        lax.psum_scatter(
            shrink_grad.astype(jnp.bfloat16), "fsdp", scatter_dimension=0, tiled=True
        ).astype(jnp.float32),
    )


def scatter_rows(link_ids, link_grads, row_count, feature_width):
    block_count = row_count // BLOCK
    inside = (link_ids >= 0) & (link_ids < block_count)
    target = jnp.where(inside, link_ids, block_count).reshape(-1)
    partial_value = jnp.zeros((block_count, BLOCK, feature_width), jnp.float32)
    partial_value = partial_value.at[target].add(
        link_grads.reshape(-1, BLOCK, feature_width), mode="drop"
    )
    return partial_value.reshape(row_count, feature_width)


def shards(
    hidden,
    project_in,
    project_out,
    expand_weight,
    shrink_weight,
    biases,
    gains,
    expand_bias,
    random_blocks,
    global_blocks,
    document_lengths,
    cotangent,
):
    inputs = hidden[0]
    tokens_here = inputs.shape[0]
    width = inputs.shape[1]
    head_count = width // HEAD_DIM
    blocks_here = tokens_here // BLOCK
    rand_count = random_blocks.shape[2]
    link_count = 3 + rand_count + global_blocks.shape[1]
    ctx_rank = lax.axis_index("ctx")
    last_block = tokens_here * lax.axis_size("ctx") // BLOCK - 1
    col_full = (
        lax.all_gather(project_in, "ctx", axis=1, tiled=True),
        lax.all_gather(project_out, "ctx", axis=1, tiled=True),
        lax.all_gather(expand_weight, "ctx", axis=1, tiled=True),
        lax.all_gather(shrink_weight, "ctx", axis=1, tiled=True),
        lax.all_gather(biases, "ctx", axis=1, tiled=True),
        lax.all_gather(gains, "ctx", axis=1, tiled=True),
        lax.all_gather(expand_bias.reshape(1, -1), "ctx", axis=1, tiled=True),
    )
    full_qkv, full_out, full_expand, full_shrink = (
        lax.all_gather(col_full[0], "fsdp", axis=0, tiled=True),
        lax.all_gather(col_full[1], "fsdp", axis=0, tiled=True),
        lax.all_gather(col_full[2], "fsdp", axis=0, tiled=True),
        lax.all_gather(col_full[3], "fsdp", axis=0, tiled=True),
    )
    vectors = col_full[4].astype(jnp.float32)
    gain_rows = col_full[5].astype(jnp.float32)
    inner_bias = col_full[6][0].astype(jnp.float32)
    block_ids = ctx_rank * blocks_here + jnp.arange(blocks_here, dtype=jnp.int32)
    window = jnp.stack(
        [jnp.maximum(block_ids - 1, 0), block_ids, jnp.minimum(block_ids + 1, last_block)], axis=1
    )
    global_links = jnp.broadcast_to(
        global_blocks[0][None, :], (blocks_here, global_blocks.shape[1])
    )
    linked_ids = jnp.concatenate([window, random_blocks[0], global_links], axis=1)
    lengths = document_lengths[0]
    doc_order = jnp.arange(lengths.shape[0], dtype=jnp.int32)
    bounds = jnp.sum(
        jnp.where(doc_order[None, :] <= doc_order[:-1, None], lengths[None, :], 0), axis=1
    )
    query_pos = (ctx_rank * tokens_here + jnp.arange(tokens_here, dtype=jnp.int32)).reshape(
        blocks_here, BLOCK
    )
    query_seg = segment_of(query_pos, bounds)
    key_pos = linked_ids[:, :, None] * BLOCK + jnp.arange(BLOCK, dtype=jnp.int32)[None, None, :]
    key_seg = segment_of(key_pos, bounds).reshape(blocks_here, -1)
    allowed = query_seg[:, None, :, None] == key_seg[:, None, None, :]
    zero_row = jnp.zeros((width,), jnp.float32)
    mixed_qkv = (
        matmul(inputs, full_qkv) + jnp.concatenate([vectors[0], zero_row, vectors[1]])
    ).astype(jnp.bfloat16)
    queries = mixed_qkv[:, :width]
    keyvals = mixed_qkv[:, width:]
    shard_piece = lax.all_gather(keyvals, "ctx", axis=0, tiled=True)
    block_count = shard_piece.shape[0] // BLOCK
    stacked = shard_piece.reshape(block_count, BLOCK, shard_piece.shape[1])
    picks = (
        linked_ids.reshape(-1)[:, None] == jnp.arange(block_count, dtype=jnp.int32)[None, :]
    ).astype(jnp.bfloat16)
    linked = jnp.einsum("lb,bkd->lkd", picks, stacked).reshape(
        blocks_here, link_count, BLOCK, 2 * width
    )
    query_heads = queries.reshape(blocks_here, BLOCK, head_count, HEAD_DIM)
    key_heads = linked[..., :width].reshape(blocks_here, link_count * BLOCK, head_count, HEAD_DIM)
    value_heads = linked[..., width:].reshape(blocks_here, link_count * BLOCK, head_count, HEAD_DIM)

    def score_parts():
        raw_scores = (
            jnp.einsum(
                "bqhd,bkhd->bhqk", query_heads, key_heads, preferred_element_type=jnp.float32
            )
            * 0.125
        )
        return jnp.where(allowed, raw_scores, -1e30)

    scores = score_parts()
    top_score = jnp.max(scores, axis=-1, keepdims=True)
    exp_total = jnp.sum(jnp.exp(scores - top_score), axis=-1, keepdims=True)
    attention = jnp.exp(scores - top_score) / exp_total
    attended = jnp.einsum(
        "bhqk,bkhd->bqhd",
        attention.astype(jnp.bfloat16),
        value_heads,
        preferred_element_type=jnp.float32,
    )
    attended = attended.reshape(tokens_here, width).astype(jnp.bfloat16)
    residual_one = inputs.astype(jnp.float32) + matmul(attended, full_out) + vectors[2]
    hidden_one, normed_one, inverse_one = layer_norm_parts(residual_one, gain_rows[0], vectors[3])
    hidden_low = hidden_one.astype(jnp.bfloat16)
    inner_pre = matmul(hidden_low, full_expand) + inner_bias
    activated, gelu_pull = jax.vjp(
        lambda argument: jax.nn.gelu(argument, approximate=False), inner_pre
    )
    active_low = activated.astype(jnp.bfloat16)
    residual_two = hidden_one + matmul(active_low, full_shrink) + vectors[4]
    result, normed_two, inverse_two = layer_norm_parts(residual_two, gain_rows[1], vectors[5])
    upstream = cotangent[0].astype(jnp.float32)
    grad_gain_two = jnp.sum(upstream * normed_two, axis=0)
    grad_shift_two = jnp.sum(upstream, axis=0)
    grad_two = layer_norm_back(upstream, normed_two, inverse_two, gain_rows[1])
    grad_bias_back = jnp.sum(grad_two, axis=0)
    grad_two_low = grad_two.astype(jnp.bfloat16)
    again_cols = (
        lax.all_gather(project_in, "ctx", axis=1, tiled=True),
        lax.all_gather(project_out, "ctx", axis=1, tiled=True),
        lax.all_gather(expand_weight, "ctx", axis=1, tiled=True),
        lax.all_gather(shrink_weight, "ctx", axis=1, tiled=True),
    )
    back_weights = (
        lax.all_gather(again_cols[0], "fsdp", axis=0, tiled=True),
        lax.all_gather(again_cols[1], "fsdp", axis=0, tiled=True),
        lax.all_gather(again_cols[2], "fsdp", axis=0, tiled=True),
        lax.all_gather(again_cols[3], "fsdp", axis=0, tiled=True),
    )
    back_qkv, back_out, back_expand, back_shrink = back_weights
    grad_shrink_w = matmul_left_t(active_low, grad_two_low)
    grad_active = matmul_right_t(grad_two_low, back_shrink)
    grad_inner = gelu_pull(grad_active)[0]
    grad_inner_bias = jnp.sum(grad_inner, axis=0)
    grad_inner_low = grad_inner.astype(jnp.bfloat16)
    grad_expand_w = matmul_left_t(hidden_low, grad_inner_low)
    grad_hidden_one = grad_two + matmul_right_t(grad_inner_low, back_expand)
    grad_gain_one = jnp.sum(grad_hidden_one * normed_one, axis=0)
    grad_shift_one = jnp.sum(grad_hidden_one, axis=0)
    grad_one = layer_norm_back(grad_hidden_one, normed_one, inverse_one, gain_rows[0])
    grad_bias_out = jnp.sum(grad_one, axis=0)
    grad_one_low = grad_one.astype(jnp.bfloat16)
    grad_out_w = matmul_left_t(attended, grad_one_low)
    grad_attended = matmul_right_t(grad_one_low, back_out).astype(jnp.bfloat16)
    grad_attended = grad_attended.reshape(blocks_here, BLOCK, head_count, HEAD_DIM)
    scores = score_parts()
    attention = jnp.exp(scores - top_score) / exp_total
    grad_attention = jnp.einsum(
        "bqhd,bkhd->bhqk", grad_attended, value_heads, preferred_element_type=jnp.float32
    )
    grad_values = jnp.einsum(
        "bhqk,bqhd->bkhd",
        attention.astype(jnp.bfloat16),
        grad_attended,
        preferred_element_type=jnp.float32,
    )
    row_inner = jnp.sum(attention * grad_attention, axis=-1, keepdims=True)
    grad_scores = (attention * (grad_attention - row_inner) * 0.125).astype(jnp.bfloat16)
    grad_queries = jnp.einsum(
        "bhqk,bkhd->bqhd", grad_scores, key_heads, preferred_element_type=jnp.float32
    ).reshape(tokens_here, width)
    grad_keys = jnp.einsum(
        "bhqk,bqhd->bkhd", grad_scores, query_heads, preferred_element_type=jnp.float32
    )
    slot_grads = jnp.concatenate(
        [
            grad_keys.reshape(blocks_here, link_count, BLOCK, width),
            grad_values.reshape(blocks_here, link_count, BLOCK, width),
        ],
        axis=-1,
    )
    grad_keyvals = lax.psum_scatter(
        scatter_rows(linked_ids, slot_grads, tokens_here * lax.axis_size("ctx"), 2 * width),
        "ctx",
        scatter_dimension=0,
        tiled=True,
    )
    grad_mixed = jnp.concatenate([grad_queries, grad_keyvals], axis=1)
    grad_bias_query = jnp.sum(grad_queries, axis=0)
    grad_bias_value = jnp.sum(grad_keyvals[:, width:], axis=0)
    grad_mixed_low = grad_mixed.astype(jnp.bfloat16)
    grad_qkv_w = matmul_left_t(inputs, grad_mixed_low)
    grad_inputs = grad_one + matmul_right_t(grad_mixed_low, back_qkv)
    grad_vectors = jnp.stack(
        [
            grad_bias_query,
            grad_bias_value,
            grad_bias_out,
            grad_shift_one,
            grad_bias_back,
            grad_shift_two,
        ]
    )
    grad_gain_rows = jnp.stack([grad_gain_one, grad_gain_two])
    grad_inner_row = grad_inner_bias[None, :]
    reduced = over_cols(
        grad_qkv_w,
        grad_out_w,
        grad_expand_w,
        grad_shrink_w,
        grad_vectors,
        grad_gain_rows,
        grad_inner_row,
    )
    sum_qkv, sum_out, sum_expand, sum_shrink = over_rows(
        reduced[0], reduced[1], reduced[2], reduced[3]
    )
    final_vectors, final_gains, final_inner = lax.psum((reduced[4], reduced[5], reduced[6]), "fsdp")
    return (
        result.astype(jnp.bfloat16)[None],
        grad_inputs.astype(jnp.bfloat16)[None],
        sum_qkv,
        sum_out,
        sum_expand,
        sum_shrink,
        final_vectors,
        final_gains,
        final_inner.reshape(-1),
    )


MESH = pl.DeviceIdType.MESH
BF = jnp.bfloat16
F32 = jnp.float32
SENDS = 192
RECVS = 192
LOCALS = 24
NEG = -1e30


def dot_nn(a, b):
    return jnp.dot(a, b, preferred_element_type=F32)


def dot_nt(a, b):
    return lax.dot_general(a, b, (((1,), (1,)), ((), ())), preferred_element_type=F32)


def dot_tn(a, b):
    return lax.dot_general(a, b, (((0,), (0,)), ((), ())), preferred_element_type=F32)


def row_sum(values):
    return jnp.sum(values, axis=0, keepdims=True)


def pack(piece):
    return jnp.concatenate([piece[48 * q : 48 * q + 48] for q in range(4)], axis=1)


def layer_kernel(
    rand_hbm, glob_hbm, doc_hbm, bia_hbm, gai_hbm, ebi_hbm, hid, cot, win, wout, wexp, wshr,
    o_out, o_gh, o_win, o_wout, o_wexp, o_wshr, o_gb, o_gg, o_ge,
    winv, woutv, win3, wout1, xg, eo, ms, mg, ps, par, win_p, wout_p, wexp_f, ws, w_in, w_out, prm,
    mq, q_s, kv, kh, vh, e_s, l_s, a_f, a_b, a_all, hg, h1_s, n1_s, r1_s, u_s, dge, g_s, ysum, yb,
    rd1, rd3, rs1, d2_s, dg, du_s, dh_b, rs2, beg, d1_s, d1g, dab, da, de, ds_s, dkv, dkb, dkr, dz, dx_b, rs3,
    gs, rs_c, t_shr, rs_y, fsb, fs, ge, re_c, t_exp, re_y, te_f, te_b, re_z,
    go, ro_c, tob, ro_y, tob2, fo, gi, ri_c, tib, ri_y, ti2, fi,
    vg, vr, vs1, vc, vs2, vy, qb_s, vb_s, ob, ohr, ghb, ghr,
    f_win, f_wout, f_wexp, f_wshr, f_gb, f_gg, f_ge,
    rand_ref, glob_ref, doc_ref, bia, gai, ebi,
    ssem, rsem, lsem,
):
    ctx = lax.axis_index("ctx")
    seq = lax.axis_index("fsdp")
    z, x = ctx // 2, ctx % 2
    y, c = seq // 2, seq % 2
    zh, zl = z // 2, z % 2
    r = 2 * zl + x
    f = seq

    def dev(px, py, pz, pc):
        return (2 * pz + px, 2 * py + pc)

    def flip(v, on):
        return v + on - 2 * v * on

    def peer(j):
        return dev(flip(x, j % 2), y, 2 * zh + flip(zl, j // 2), c)

    def peer_rank(j):
        return 2 * flip(zl, j // 2) + flip(x, j % 2)

    peers = [peer(j) for j in range(4)]
    ranks = [peer_rank(j) for j in range(4)]
    core_mate = dev(x, y, z, 1 - c)
    y_mate = dev(x, 1 - y, z, c)
    z_mate = dev(x, y, 2 * (1 - zh) + zl, c)
    home = dev(x, y, 2 * c + zl, zh)

    pending = []
    counts = {"s": 0, "r": 0, "l": 0}

    def take(kind, n, most):
        first = counts[kind]
        counts[kind] = first + n
        assert counts[kind] <= most
        return first

    def recvs(n):
        return take("r", n, RECVS)

    def sends(n):
        return take("s", n, SENDS)

    def local(src, dst):
        cp = pltpu.make_async_copy(src, dst, lsem.at[take("l", 1, LOCALS)])
        cp.start()
        return cp

    def copy_to(src, dst, si, ri, to):
        return pltpu.make_async_remote_copy(
            src_ref=src, dst_ref=dst, send_sem=ssem.at[si], recv_sem=rsem.at[ri],
            device_id=to, device_id_type=MESH,
        )

    def send(src, dst, ri, to):
        si = sends(1)
        copy_to(src, dst, si, ri, to).start()
        pending.append(lambda: copy_to(src, dst, si, ri, to).wait_send())

    def send_or_keep(src, dst, ri, to):
        si = sends(1)
        away = jnp.logical_or(to[0] != ctx, to[1] != seq)

        @pl.when(away)
        def _():
            copy_to(src, dst, si, ri, to).start()

        @pl.when(jnp.logical_not(away))
        def _():
            pltpu.make_async_copy(src, dst, rsem.at[ri]).start()

        def finish():
            @pl.when(jnp.logical_or(to[0] != ctx, to[1] != seq))
            def _():
                copy_to(src, dst, si, ri, to).wait_send()

        pending.append(finish)

    def arrived(dst, ri):
        pltpu.make_async_copy(dst, dst, rsem.at[ri]).wait()

    def split(rows):
        return [(1, 0, rows), (2, rows, 128 - rows)]

    def near_parts(buf, rows):
        return [
            (j, buf.at[ranks[j]], buf.at[ranks[j], pl.ds(at, size)] if size else None)
            for j, at, size in split(rows)
        ]

    def pass_on(parts, first):
        for j, block, part in parts:
            arrived(block, first + j)
            if part is not None:
                send(part, part, first + 3 * (2 - j), peers[3 - j])

    def far_arrived(buf, first, rows):
        for j, at, size in split(rows):
            if size:
                arrived(buf.at[ranks[3], pl.ds(at, size)], first + 3 * (2 - j))

    def merging(out, rs, rd):
        k_rs, s_rs, k_rd, s_rd = recvs(4), sends(4), recvs(2), sends(2)

        def to_near(i):
            return copy_to(
                out.at[3, pl.ds(64 * i, 64)], rd.at[i], s_rd + i, k_rd + i, peers[1 + i]
            )

        def to_peer(j, i):
            at = 2 * (j - 1) + i
            rows = pl.ds(64 * i, 64)
            return copy_to(out.at[j, rows], rs.at[j, rows], s_rs + at, k_rs + at, peers[j])

        def far_done():
            for i in range(2):
                to_near(i).start()

        def merge():
            for j, i in ((2, 0), (1, 1)):
                arrived(rd.at[i], k_rd + i)
                rows = pl.ds(64 * i, 64)
                out[j, rows] = (out[j, rows].astype(F32) + rd[i].astype(F32)).astype(BF)
                to_peer(j, i).start()

        def finish():
            for i in range(2):
                to_near(i).wait_send()
                for j in (1, 2):
                    to_peer(j, i).wait_send()

        def here(j, i):
            arrived(rs.at[j, pl.ds(64 * i, 64)], k_rs + 2 * (j - 1) + i)

        pending.append(finish)
        return far_done, lambda: to_peer(2, 1).start(), lambda: to_peer(1, 0).start(), merge, here

    def served(step, services):
        def run(k, carry):
            for at, before, serve in services:
                if before:
                    pl.when(k == at)(serve)
            step(k)
            for at, before, serve in services:
                if not before:
                    pl.when(k == at)(serve)
            return carry

        return run

    barrier = pltpu.get_barrier_semaphore()
    place = 2 * ctx + c
    for d in range(1, 16):
        other = (place + d) % 16
        pl.semaphore_signal(
            barrier, inc=1, device_id=(other // 2, 2 * y + other % 2), device_id_type=MESH
        )
    pl.semaphore_signal(barrier, inc=1, device_id=y_mate, device_id_type=MESH)
    small = [
        local(*pair)
        for pair in ((rand_hbm, rand_ref), (glob_hbm, glob_ref), (doc_hbm, doc_ref), (bia_hbm, bia), (gai_hbm, gai), (ebi_hbm, ebi))
    ]
    in_win, in_wout = local(win, winv), local(wout, woutv)

    for copy in small:
        copy.wait()

    lane = lax.broadcasted_iota(jnp.int32, (1, 128), 1)
    for i in range(2):
        block = 2 * ctx + i
        links = [jnp.maximum(block - 1, 0), block, jnp.minimum(block + 1, 15)]
        links += [rand_ref[i, k] for k in range(3)] + [glob_ref[0, k] for k in range(2)]
        count = jnp.zeros((1, 128), F32)
        for link in links:
            count += jnp.where(jnp.logical_or(lane == link + 72, lane == link + 88), 1.0, 0.0)
        ms[i : i + 1, :] = count
    edge = doc_ref[0, 0]
    edges = jnp.zeros((1, 128), F32)
    for k in range(7):
        edges += jnp.where(lane == k, edge.astype(F32), 0.0)
        edge = edge + doc_ref[0, k + 1]
    ms[2:3, :] = edges
    ms[3:8, :] = jnp.zeros((5, 128), F32)
    ps[...] = jnp.zeros((16, 128), F32)
    ps[0:6, 0:96] = bia[...].astype(F32)
    ps[6:8, 0:96] = gai[...].astype(F32)
    ps[8:11, :] = ebi[...].astype(F32)
    in_win.wait()
    for j in range(3):
        win3[j] = pack(winv[:, 96 * j : 96 * j + 96])

    pl.semaphore_wait(barrier, 16)

    k_h, k_x, k_m, k_e = recvs(1), recvs(4), recvs(4), recvs(1)
    send_or_keep(hid, xg.at[r], k_h, home)
    send_or_keep(ms, mg.at[r], k_m, home)
    k_win = recvs(6)
    for j in range(3):
        unit = 3 * ctx + j
        rank = (unit % 8) // 2
        slot = 2 * (unit // 8) + unit % 2
        for half in range(2):
            send_or_keep(
                win3.at[j], win_p.at[f, slot], k_win + slot, dev(rank % 2, y, 2 * half + rank // 2, c)
            )
    k_par = recvs(8)
    for d in range(1, 8):
        other = (ctx + d) % 8
        send(ps, par.at[ctx], k_par + d, (other, seq))
    par[ctx] = ps[...]
    in_wout.wait()
    wout1[...] = pack(woutv[...])

    arrived(xg.at[r], k_h)
    arrived(mg.at[r], k_m)
    for j in range(1, 4):
        if j < 3:
            send(xg.at[r], xg.at[r], k_x + j, peer(j))
        send(mg.at[r], mg.at[r], k_m + j, peer(j))
    k_wout_y, k_wout_c = recvs(1), recvs(2)
    k_wexp_y, k_wexp_c = recvs(1), recvs(2)
    k_wshr_y, k_wshr_c = recvs(1), recvs(2)
    k_wout = recvs(8)
    for d in range(8):
        other = (ctx + d) % 8
        if d == 0:
            pltpu.make_async_copy(wout1, wout_p.at[f, ctx], rsem.at[k_wout]).start()
        else:
            send(wout1, wout_p.at[f, ctx], k_wout + d, (other, seq))


    def sided(positions, rows):
        segs = jnp.zeros((rows, 1), F32)
        for k in range(7):
            segs += jnp.where(positions >= mg[r, 2:3, k : k + 1], 1.0, 0.0)
        return segs

    wide = lax.broadcasted_iota(jnp.int32, (1024, 128), 1)
    key_row = lax.broadcasted_iota(jnp.int32, (1024, 1), 0)
    key_segs = sided(key_row.astype(F32), 1024).astype(jnp.int32) + 64
    hot = jnp.logical_or(
        jnp.logical_and(wide < 72, wide == key_segs),
        jnp.logical_and(
            wide >= 72,
            jnp.logical_or(wide == key_row // 64 + 72, wide == key_row // 64 + 88),
        ),
    )
    hot = jnp.where(hot, 1.0, 0.0).astype(BF)
    ones = jnp.where(jnp.logical_or(wide == 64, wide == 65), 1.0, 0.0).astype(BF)
    for h in range(3):
        kh[h, :, 64:128] = hot[:, 64:128]
        vh[h, :, 64:128] = ones[:, 64:128]

    k_win_y, k_win_c = recvs(1), recvs(2)
    for slot in range(6):
        arrived(win_p.at[f, slot], k_win + slot)
    send(win_p.at[f], win_p.at[f], k_win_y, y_mate)
    send(win_p.at[f], win_p.at[f], k_win_c, core_mate)
    k_wexp = recvs(2)
    mine_exp = wexp_f.at[f, :, pl.ds(pl.multiple_of(384 * zh, 128), 384)]
    pltpu.make_async_copy(wexp, mine_exp, rsem.at[k_wexp]).start()
    send(wexp, mine_exp, k_wexp + 1, z_mate)

    pass_on(near_parts(xg, 64), k_x)

    for d in range(1, 8):
        arrived(par.at[(ctx + 8 - d) % 8], k_par + d)
    prm[...] = jnp.concatenate([par[b, 0:8, 0:96] for b in range(8)], axis=1)
    be = jnp.concatenate(
        [par[r, 8 + i : 9 + i, :] for i in range(3)] + [par[4 + r, 8 + i : 9 + i, :] for i in range(3)],
        axis=1,
    )
    zrow = jnp.zeros((1, 192), F32)
    z_bias = jnp.concatenate(
        [par[2 * r, 0:1, 0:96], par[2 * r + 1, 0:1, 0:96], zrow, par[2 * r, 1:2, 0:96], par[2 * r + 1, 1:2, 0:96]],
        axis=1,
    )

    row_pos = lax.broadcasted_iota(jnp.int32, (512, 1), 0) + 512 * c
    row_segs = sided(row_pos.astype(F32), 512).astype(jnp.int32) + 64
    for j in range(1, 4):
        arrived(mg.at[peer_rank(j)], k_m + j)
    for i in range(8):
        count = mg[i // 2, i % 2 : i % 2 + 1, :]
        logs = jnp.log(jnp.maximum(count, 1.0))
        high = logs.astype(BF).astype(F32)
        line = jnp.where(lane < 88, jnp.where(count > 0.5, high, NEG), logs - high)
        line = jnp.where(lane < 104, line, 0.0)
        same = row_segs[64 * i : 64 * i + 64] == wide[0:64]
        block = jnp.where(wide[0:64] < 72, jnp.where(same, 0.0, NEG), line)
        mq[i // 2, 64 * (i % 2) : 64 * (i % 2) + 64, :] = block.astype(BF)
    for h in range(3):
        q_s[:, h, :, 64:128] = mq[:, :, 64:128]

    f_y = 2 * (1 - y) + c
    arrived(win_p.at[f_y], k_win_y)
    send(win_p.at[f_y], win_p.at[f_y], k_win_c + 1, core_mate)
    for d in range(8):
        arrived(wout_p.at[f, (ctx + 8 - d) % 8], k_wout + d)
    send(wout_p.at[f], wout_p.at[f], k_wout_y, y_mate)
    send(wout_p.at[f], wout_p.at[f], k_wout_c, core_mate)
    k_wshr = recvs(4)
    at_half = pl.ds(pl.multiple_of(384 * y, 128), 384)
    for sub in range(2):
        for half in range(2):
            send_or_keep(
                wshr.at[:, 384 * sub : 384 * sub + 384], ws.at[2 * zh + zl, x, :, at_half],
                k_wshr + 2 * zh + zl, dev(sub, y, 2 * half + c, x),
            )


    def place_in(k):
        for q in range(4):
            w_in[pl.ds(pl.multiple_of(192 * k + 48 * q, 16), 48), :] = jnp.concatenate(
                [win_p[k, i, :, 96 * q : 96 * q + 96] for i in range(6)], axis=1
            )

    place_in(f)
    place_in(f_y)
    arrived(win_p.at[2 * y + 1 - c], k_win_c)
    place_in(2 * y + 1 - c)
    arrived(win_p.at[2 * (1 - y) + 1 - c], k_win_c + 1)
    place_in(2 * (1 - y) + 1 - c)

    def project(k):
        mixed = dot_nn(xg[k], w_in[...]) + z_bias
        queries = (mixed[:, 0:192].astype(BF).astype(F32) * 0.125).astype(BF)
        for h in range(3):
            q_s[k, h, :, 0:64] = queries[:, 64 * h : 64 * h + 64]
        kv[c, pl.ds(pl.multiple_of(128 * k, 128), 128), :] = mixed[:, 192:576].astype(BF)

    lax.fori_loop(
        0, 4,
        served(lambda j: project(peer_rank(j)), [(3, True, lambda: far_arrived(xg, k_x, 64))]), 0,
    )
    k_kv = recvs(1)
    send(kv.at[c], kv.at[c], k_kv, core_mate)

    def split_heads(half):
        at = pl.ds(pl.multiple_of(512 * half, 512), 512)
        for h in range(3):
            kh[h, at, 0:64] = kv[half, :, 64 * h : 64 * h + 64]
            vh[h, at, 0:64] = kv[half, :, 192 + 64 * h : 256 + 64 * h]

    split_heads(c)
    arrived(mine_exp, k_wexp)
    arrived(wexp_f.at[f, :, pl.ds(pl.multiple_of(384 * (1 - zh), 128), 384)], k_wexp + 1)
    send(wexp_f.at[f], wexp_f.at[f], k_wexp_y, y_mate)
    send(wexp_f.at[f], wexp_f.at[f], k_wexp_c, core_mate)
    arrived(kv.at[1 - c], k_kv)
    split_heads(1 - c)

    k_a, s_a = recvs(16), sends(16)

    def attend(k):
        outs = []
        for h in range(3):
            scores = dot_nt(q_s[k, h], kh[h])
            top = jnp.max(scores, axis=1, keepdims=True)
            exps = jnp.exp(scores - top).astype(BF)
            e_s[h, k] = exps
            sums = dot_nn(exps, vh[h])
            scale = 1.0 / sums[:, 64:65]
            l_s[h, k] = scale
            outs.append(sums[:, 0:64] * scale)
        both = jnp.concatenate(outs, axis=1)
        a_f[k] = both
        low = both.astype(BF)
        a_b[k] = low
        a_all[r, k] = jnp.concatenate([low[0:64], low[64:128]], axis=1)
        for j in range(1, 4):
            at = 4 * j + k
            copy_to(a_all.at[r, k], a_all.at[r, k], s_a + at, k_a + at, peers[j]).start()

    wout_there, wexp_there = wout_p.at[f_y], wexp_f.at[f_y]
    ws_mine = ws.at[:, c, :, at_half]

    def relay_0():
        arrived(wout_there, k_wout_y)
        send(wout_there, wout_there, k_wout_c + 1, core_mate)

    def relay_1():
        for k in range(4):
            arrived(ws.at[k, c, :, at_half], k_wshr + k)
        send(ws_mine, ws_mine, k_wshr_y, y_mate)
        send(ws_mine, ws_mine, k_wshr_c, core_mate)

    def relay_2():
        arrived(wexp_there, k_wexp_y)
        send(wexp_there, wexp_there, k_wexp_c + 1, core_mate)

    lax.fori_loop(0, 4, served(attend, [(0, False, relay_0), (1, False, relay_1), (2, False, relay_2)]), 0)
    for j in range(1, 4):
        for k in range(4):
            at = 4 * j + k
            pending.append(
                copy_to(a_all.at[r, k], a_all.at[r, k], s_a + at, k_a + at, peer(j)).wait_send
            )
    send_or_keep(cot, eo, k_e, home)
    def place_out(k):
        for q in range(4):
            w_out[pl.ds(pl.multiple_of(192 * k + 48 * q, 16), 48), :] = jnp.concatenate(
                [wout_p[k, b, :, 96 * q : 96 * q + 96] for b in range(8)], axis=1
            )

    place_out(f)
    place_out(f_y)
    arrived(wout_p.at[2 * y + 1 - c], k_wout_c)
    place_out(2 * y + 1 - c)
    arrived(wout_p.at[2 * (1 - y) + 1 - c], k_wout_c + 1)
    place_out(2 * (1 - y) + 1 - c)
    other_half = pl.ds(pl.multiple_of(384 * (1 - y), 128), 384)
    arrived(ws.at[:, c, :, other_half], k_wshr_y)
    send(ws.at[:, c, :, other_half], ws.at[:, c, :, other_half], k_wshr_c + 1, core_mate)
    for j in range(1, 4):
        for k in range(4):
            arrived(a_all.at[peer_rank(j), k], k_a + 4 * j + k)
    arrived(wexp_f.at[2 * y + 1 - c], k_wexp_c)
    arrived(wexp_f.at[2 * (1 - y) + 1 - c], k_wexp_c + 1)

    def first_norm(k):
        rows = jnp.concatenate(
            [
                jnp.concatenate([a_all[src, k, :, 192 * i : 192 * i + 192] for src in range(4)], axis=1)
                for i in range(2)
            ],
            axis=0,
        )
        first = xg[k].astype(F32) + prm[2:3, :] + dot_nn(rows, w_out[...])
        centre = first - jnp.mean(first, axis=1, keepdims=True)
        inverse = lax.rsqrt(jnp.mean(centre * centre, axis=1, keepdims=True) + 1e-05)
        normed = centre * inverse
        hidden_one = normed * prm[6:7, :] + prm[3:4, :]
        hg[k] = hidden_one.astype(BF)
        return normed, inverse, hidden_one

    def expand(k):
        inner = dot_nn(hg[k], wexp_f[...].reshape(768, 768)) + be
        below = 0.5 * (1.0 + lax.erf(inner * 0.7071067811865476))
        u_s[k] = inner
        dge[k] = below
        active = (inner * below).astype(BF)
        g_s[k] = active

    def widen(k):
        normed, inverse, hidden_one = first_norm(k)
        n1_s[...] = normed
        r1_s[...] = inverse
        h1_s[...] = hidden_one
        expand(k)

    widen(ranks[3])
    arrived(ws.at[:, 1 - c, :, at_half], k_wshr_c)
    arrived(ws.at[:, 1 - c, :, other_half], k_wshr_c + 1)
    far_1, second_1, third_1, merge_1, here_1 = merging(yb, rs1, rd1)

    def expand_step(i, carry):
        j = 3 - i
        rank = peer_rank(j)

        @pl.when(i > 0)
        def _():
            widen(rank)

        value = dot_nt(g_s[rank], ws[...].reshape(768, 768))

        @pl.when(i < 3)
        def _():
            yb[j] = value.astype(BF)

        pl.when(i == 0)(far_1)
        pl.when(i == 1)(second_1)

        @pl.when(i == 2)
        def _():
            third_1()
            merge_1()

        @pl.when(i == 3)
        def _():
            ysum[...] = value

        return carry

    lax.fori_loop(0, 4, expand_step, 0)
    def slope(k, carry):
        inner = u_s[k]
        dge[k] = dge[k] + inner * jnp.exp(-0.5 * inner * inner) * 0.3989422804014327
        return carry

    lax.fori_loop(0, 4, slope, 0)

    arrived(eo, k_e)
    upstream = eo[...].astype(F32)
    scaled = upstream * prm[7:8, :]
    scaled_mean = jnp.mean(scaled, axis=1, keepdims=True)
    row_shift_two = row_sum(upstream)
    second = h1_s[...] + prm[4:5, :] + ysum[...]
    for j in range(1, 3):
        for i in range(2):
            here_1(j, i)
        second += rs1[j].astype(F32)
    centre = second - jnp.mean(second, axis=1, keepdims=True)
    inverse = lax.rsqrt(jnp.mean(centre * centre, axis=1, keepdims=True) + 1e-05)
    normed = centre * inverse
    grad_two = inverse * (
        scaled - scaled_mean - normed * jnp.mean(scaled * normed, axis=1, keepdims=True)
    )
    dg[r] = grad_two.astype(BF)
    k_d = recvs(4)
    for j in range(1, 3):
        send(dg.at[r], dg.at[r], k_d + j, peer(j))
    d2_s[...] = grad_two
    ob[...] = (normed * prm[7:8, :] + prm[5:6, :]).astype(BF)
    k_o = recvs(1)
    send_or_keep(ob, ohr, k_o, home)
    row_gain_two = row_sum(upstream * normed)
    row_back = row_sum(grad_two)

    def contract(k):
        inner = dge[k] * dot_nn(dg[k], ws[...].reshape(768, 768))
        low = inner.astype(BF)
        du_s[k] = low
        beg[k] = row_sum(inner)
        return dot_nt(low, wexp_f[...].reshape(768, 768))

    k_r2, s_r2 = recvs(4), sends(4)

    def contract_step(j):
        value = contract(peer_rank(j))

        @pl.when(j == 0)
        def _():
            ysum[...] = value

        @pl.when(j > 0)
        def _():
            dh_b[j] = value.astype(BF)
            copy_to(dh_b.at[j], rs2.at[j], s_r2 + j, k_r2 + j, peer(j)).start()

    dg_parts = near_parts(dg, 64)
    gathered = [
        (1, True, lambda: pass_on(dg_parts, k_d)),
        (3, True, lambda: far_arrived(dg, k_d, 64)),
    ]
    lax.fori_loop(0, 4, served(contract_step, gathered), 0)
    for j in range(1, 4):
        pending.append(copy_to(dh_b.at[j], rs2.at[j], s_r2 + j, k_r2 + j, peer(j)).wait_send)

    for k in range(4):
        rows = dg[:, :, 192 * k : 192 * k + 192].reshape(512, 192)
        gs[k] = dot_tn(rows, g_s[...].reshape(512, 768)).astype(BF).reshape(2, 96, 768)
    k_gs = recvs(1)
    send(gs.at[:, 1 - c], rs_c, k_gs, core_mate)

    def expand_grad(i, carry):
        at = pl.ds(pl.multiple_of(128 * i, 128), 128)
        rows = hg[:, :, at].reshape(512, 128)
        ge[at, :] = dot_tn(rows, du_s[...].reshape(512, 768)).astype(BF)
        return carry

    lax.fori_loop(0, 6, expand_grad, 0)
    k_ge = recvs(2)
    for half in range(2):
        at = pl.ds(pl.multiple_of(192 * (2 * half + 1 - c), 64), 192)
        send(ge.at[at, :], re_c.at[half], k_ge + half, core_mate)
    k_gs_y, k_ge_y = recvs(1), recvs(1)
    arrived(rs_c, k_gs)
    t_shr[...] = (
        gs[:, c, :, other_half].astype(F32) + rs_c[:, :, other_half].astype(F32)
    ).astype(BF)
    send(t_shr, rs_y, k_gs_y, y_mate)

    grad_hidden = d2_s[...] + ysum[...]
    for j in range(1, 4):
        arrived(rs2.at[j], k_r2 + j)
        grad_hidden += rs2[j].astype(F32)
    normed = n1_s[...]
    scaled = grad_hidden * prm[6:7, :]
    grad_one = r1_s[...] * (
        scaled
        - jnp.mean(scaled, axis=1, keepdims=True)
        - normed * jnp.mean(scaled * normed, axis=1, keepdims=True)
    )
    low_one = grad_one.astype(BF)
    d1g[r] = low_one
    for k in range(4):
        dab[k] = dot_nt(low_one, w_out[192 * k : 192 * k + 192, :]).astype(BF)
    k_da, k_d1 = recvs(4), recvs(4)
    for j in range(1, 4):
        send(dab.at[peer_rank(j)], da.at[r], k_da + j, peer(j))
    da[r] = dab[r]
    d1_s[...] = grad_one
    row_gain_one = row_sum(grad_hidden * normed)
    row_shift_one = row_sum(grad_hidden)
    row_out = row_sum(grad_one)

    for half in range(2):
        arrived(re_c.at[half], k_ge + half)
    at_y = pl.ds(pl.multiple_of(192 * f_y, 64), 192)
    at_own = pl.ds(pl.multiple_of(192 * f, 64), 192)
    t_exp[...] = (ge[at_y, :].astype(F32) + re_c[1 - y].astype(F32)).astype(BF)
    send(t_exp, re_y, k_ge_y, y_mate)


    d1g_mine = d1g.at[r]

    def send_d1():
        for j in range(1, 3):
            send(d1g_mine, d1g_mine, k_d1 + j, peers[j])

    def attend_back(j):
        k = peer_rank(j)

        @pl.when(j > 0)
        def _():
            arrived(da.at[k], k_da + j)

        outs = []
        grads = da[k].astype(F32)
        dots = grads * a_f[k]
        for h in range(3):
            at = slice(64 * h, 64 * h + 64)
            scale = l_s[h, k]
            delta = jnp.sum(dots[:, at], axis=1, keepdims=True) * scale
            high = delta.astype(BF).astype(F32)
            side = jnp.where(wide[0:128, 0:64] == 0, -high, 0.0)
            side = jnp.where(wide[0:128, 0:64] == 1, high - delta, side)
            both = jnp.concatenate([grads[:, at] * scale, side], axis=1).astype(BF)
            de[k, h] = both
            low = (e_s[h, k].astype(F32) * dot_nt(both, vh[h])).astype(BF)
            ds_s[h, k] = low
            outs.append(dot_nn(low, kh[h])[:, 0:64] * 0.125)
        queries = jnp.concatenate(outs, axis=1)
        qb_s[k] = row_sum(queries)
        dz[k, :, 0:192] = queries.astype(BF)

    k_fs, k_re = recvs(4), recvs(1)
    shrink_owners = [dev(c, y, k, zl) for k in range(4)]
    fs_at = fs.at[zh, x]
    fsb_at = [fsb.at[k] for k in range(4)]
    k_own = k_fs + 2 * zh + x

    def pass_0():
        arrived(rs_y, k_gs_y)
        fsb[...] = (
            gs[:, c, :, at_half].astype(F32) + rs_c[:, :, at_half].astype(F32) + rs_y[...].astype(F32)
        ).astype(BF)
        for k in range(4):
            send_or_keep(fsb_at[k], fs_at, k_own, shrink_owners[k])

    def pass_1():
        arrived(re_y, k_ge_y)
        te_f[...] = ge[at_own, :].astype(F32) + re_c[y].astype(F32) + re_y[...].astype(F32)
        te_b[...] = te_f[:, pl.ds(pl.multiple_of(384 * (1 - zh), 128), 384)].astype(BF)
        send(te_b, re_z, k_re, z_mate)

    d1g_parts = near_parts(d1g, 0)

    def pass_2():
        pass_on(d1g_parts, k_d1)

    lax.fori_loop(0, 4, served(attend_back, [(0, False, send_d1), (1, False, pass_0), (2, False, pass_1), (3, False, pass_2)]), 0)
    sums = []
    for h in range(3):
        rows = q_s[:, h, :, 0:64].reshape(512, 64)
        sums.append(dot_tn(rows, ds_s[h].reshape(512, 1024)))
    for h in range(3):
        rows = de[:, h, :, 0:64].reshape(512, 64)
        sums.append(dot_tn(rows, e_s[h].reshape(512, 1024)))
    sums = jnp.concatenate(sums, axis=0)
    dkv[0] = sums[:, 0:512].T
    dkv[1] = sums[:, 512:1024].T
    dkb[...] = dkv[1 - c].astype(BF)
    k_dk = recvs(1)
    send(dkb, dkr, k_dk, core_mate)

    def project_grad(first, count):
        for k in range(4):
            rows = xg[:, :, 192 * k : 192 * k + 192].reshape(512, 192)
            cols = dz[:, :, 96 * first : 96 * first + 96 * count].reshape(512, 96 * count)
            part = dot_tn(rows, cols).astype(BF)
            for slot in range(count):
                gi[k, first + slot] = pack(part[:, 96 * slot : 96 * slot + 96])

    some = {"q": pl.ds(0, 2), "kv": pl.ds(2, 4)}
    k_gi = {"q": recvs(2), "kv": recvs(2)}
    k_gi_y = {"q": recvs(1), "kv": recvs(1)}

    def over_cores(which):
        at = some[which]
        for half in range(2):
            send(gi.at[2 * half + 1 - c, at], ri_c.at[half, at], k_gi[which] + half, core_mate)

    def over_y(which):
        at = some[which]
        for half in range(2):
            arrived(ri_c.at[half, at], k_gi[which] + half)
        tib[at] = (gi[f_y, at].astype(F32) + ri_c[1 - y, at].astype(F32)).astype(BF)
        send(tib.at[at], ri_y.at[at], k_gi_y[which], y_mate)

    k_fi = recvs(6)

    def to_owners(which):
        at = some[which]
        arrived(ri_y.at[at], k_gi_y[which])
        ti2[at] = (
            gi[f, at].astype(F32) + ri_c[y, at].astype(F32) + ri_y[at].astype(F32)
        ).astype(BF)
        for slot in range(2) if which == "q" else range(2, 6):
            unit = 8 * (slot // 2) + 2 * r + slot % 2
            send_or_keep(
                ti2.at[slot], fi.at[zh, unit % 3], k_fi + 3 * zh + unit % 3, (unit // 3, seq)
            )

    project_grad(0, 2)
    over_cores("q")

    arrived(dkr, k_dk)
    keyvals = dkv[c] + dkr[...].astype(F32)
    vb_s[...] = row_sum(keyvals[:, 192:384])
    dz[:, :, 192:576] = keyvals.astype(BF).reshape(4, 128, 384)

    def input_part(k):
        return dot_nt(dz[k], w_in[...])

    far_3, second_3, third_3, merge_3, here_3 = merging(dx_b, rs3, rd3)

    def input_step(i, carry):
        j = 3 - i
        dx_b[j] = input_part(peer_rank(j)).astype(BF)
        pl.when(i == 0)(far_3)
        pl.when(i == 1)(second_3)
        pl.when(i == 2)(third_3)
        return carry

    lax.fori_loop(0, 3, input_step, 0)
    over_y("q")
    project_grad(2, 4)
    over_cores("kv")
    merge_3()

    far_arrived(d1g, k_d1, 0)
    part = dot_tn(a_b[...].reshape(512, 192), d1g[...].reshape(512, 768))
    for b in range(8):
        go[b % 2, b // 2] = pack(part[:, 96 * b : 96 * b + 96].astype(BF))
    k_go = recvs(1)
    send(go.at[1 - c], ro_c, k_go, core_mate)

    over_y("kv")

    vg[...] = jnp.zeros((8, 16, 128), F32)
    rows = jnp.concatenate(
        [row_out, row_shift_one, row_back, row_shift_two, row_gain_one, row_gain_two], axis=0
    )
    for b in range(8):
        vg[b, 2:8, 0:96] = rows[:, 96 * b : 96 * b + 96]
    q_row = row_sum(qb_s[:, 0, :])
    v_row = vb_s[...]
    for i in range(2):
        vg[2 * r + i, 0:1, 0:96] = q_row[:, 96 * i : 96 * i + 96]
        vg[2 * r + i, 1:2, 0:96] = v_row[:, 96 * i : 96 * i + 96]
    inner_row = row_sum(beg[:, 0, :])
    for i in range(3):
        vg[r, 8 + i : 9 + i, :] = inner_row[:, 128 * i : 128 * i + 128]
        vg[4 + r, 8 + i : 9 + i, :] = inner_row[:, 384 + 128 * i : 512 + 128 * i]
    k_v = recvs(8)
    for d in range(1, 8):
        other = (ctx + d) % 8
        send(vg.at[other], vr.at[d], k_v + d, (other, seq))

    arrived(ro_c, k_go)
    tob[...] = (go[c].astype(F32) + ro_c[...].astype(F32)).astype(BF)
    k_go_y, k_fo = recvs(1), recvs(2)
    s_go, s_fo = sends(1), sends(4)
    stays = y == zl

    @pl.when(jnp.logical_not(stays))
    def _():
        copy_to(tob, ro_y, s_go, k_go_y, y_mate).start()

    k_gh = recvs(2)
    ysum[...] = d1_s[...] + input_part(r)

    def finish_input(i):
        at = pl.ds(64 * i, 64)
        grad_in = ysum[at, :]
        for j in range(1, 3):
            here_3(j, i)
            grad_in += rs3[j, at, :].astype(F32)
        ghb[at, :] = grad_in.astype(BF)
        send_or_keep(ghb.at[at, :], ghr.at[at, :], k_gh + i, home)

    to_owners("q")
    finish_input(0)

    done = []

    for half in range(2):
        for sub in range(2):
            arrived(fs.at[half, sub], k_fs + 2 * half + sub)
    for sub in range(2):
        f_wshr[:, 384 * sub : 384 * sub + 384] = fs[0, sub].astype(F32) + fs[1, sub].astype(F32)
    done.append(local(f_wshr, o_wshr))
    arrived(re_z, k_re)
    f_wexp[...] = te_f[:, pl.ds(pl.multiple_of(384 * zh, 128), 384)] + re_z[...].astype(F32)
    done.append(local(f_wexp, o_wexp))

    to_owners("kv")
    finish_input(1)

    @pl.when(stays)
    def _():
        arrived(ro_y, k_go_y)
        tob2[...] = (tob[...].astype(F32) + ro_y[...].astype(F32)).astype(BF)
        for k in range(4):
            to = dev(c, y, k, x)
            away = jnp.logical_or(to[0] != ctx, to[1] != seq)

            @pl.when(away)
            def _():
                copy_to(tob2.at[k], fo.at[zh], s_fo + k, k_fo + zh, to).start()

            @pl.when(jnp.logical_not(away))
            def _():
                pltpu.make_async_copy(tob2.at[k], fo.at[zh], rsem.at[k_fo + zh]).start()

    def finish_out():
        @pl.when(jnp.logical_not(stays))
        def _():
            copy_to(tob, ro_y, s_go, k_go_y, y_mate).wait_send()

        @pl.when(stays)
        def _():
            for k in range(4):
                to = dev(c, y, k, x)

                @pl.when(jnp.logical_or(to[0] != ctx, to[1] != seq))
                def _():
                    copy_to(tob2.at[k], fo.at[zh], s_fo + k, k_fo + zh, to).wait_send()

    pending.append(finish_out)

    total = vg[ctx]
    for d in range(1, 8):
        arrived(vr.at[d], k_v + d)
        total += vr[d]
    vs1[...] = total
    k_vc = recvs(2)
    send(vs1, vc, k_vc, core_mate)
    arrived(vc, k_vc)
    vs2[...] = vs1[...] + vc[...]
    send(vs2, vy, k_vc + 1, y_mate)

    arrived(ohr, k_o)
    done.append(local(ohr, o_out))
    arrived(vy, k_vc + 1)
    total = vs2[...] + vy[...]
    f_gb[...] = total[0:6, 0:96]
    f_gg[...] = total[6:8, 0:96]
    f_ge[...] = total[8:11, :]
    done += [local(f_gb, o_gb), local(f_gg, o_gg), local(f_ge, o_ge)]
    for half in range(2):
        arrived(fo.at[half], k_fo + half)
    part = fo[0].astype(F32) + fo[1].astype(F32)
    for q in range(4):
        f_wout[48 * q : 48 * q + 48, :] = part[:, 96 * q : 96 * q + 96]
    done.append(local(f_wout, o_wout))
    for half in range(2):
        for j in range(3):
            arrived(fi.at[half, j], k_fi + 3 * half + j)
    parts = [fi[0, j].astype(F32) + fi[1, j].astype(F32) for j in range(3)]
    for q in range(4):
        f_win[48 * q : 48 * q + 48, :] = jnp.concatenate(
            [part[:, 96 * q : 96 * q + 96] for part in parts], axis=1
        )
    done.append(local(f_win, o_win))
    for i in range(2):
        arrived(ghr.at[pl.ds(64 * i, 64), :], k_gh + i)
    done.append(local(ghr, o_gh))
    for finish in pending:
        finish()
    for copy in done:
        copy.wait()


def hand_over(*refs):
    ins, outs, held, into, out_of = refs[0:9], refs[9:18], refs[18:27], refs[27], refs[28]
    loads = [pltpu.make_async_copy(ins[i], held[i], into.at[i]) for i in range(9)]
    stores = [pltpu.make_async_copy(held[i], outs[i], out_of.at[i]) for i in range(9)]
    for load in loads:
        load.start()
    for load, store in zip(loads, stores):
        load.wait()
        store.start()
    for store in stores:
        store.wait()


def fast_shards(
    hidden, project_in, project_out, expand_weight, shrink_weight, biases, gains, expand_bias,
    random_blocks, global_blocks, document_lengths, cotangent,
):
    vm = lambda *dims: pltpu.VMEM(dims, BF)
    vf = lambda *dims: pltpu.VMEM(dims, F32)
    scratch = [
        vm(192, 288), vm(192, 96), vm(3, 48, 384), vm(48, 384), vm(4, 128, 768), vm(128, 768),
        vf(8, 128), vf(4, 8, 128), vf(16, 128), vf(8, 16, 128), vm(4, 6, 48, 384), vm(4, 8, 48, 384),
        vm(4, 192, 768), vm(4, 2, 96, 768), vm(768, 576), vm(768, 768), vf(8, 768),
        vm(4, 128, 128), vm(4, 3, 128, 128), vm(2, 512, 384), vm(3, 1024, 128), vm(3, 1024, 128),
        vm(3, 4, 128, 1024), vf(3, 4, 128, 1), vf(4, 128, 192), vm(4, 128, 192), vm(4, 4, 64, 384),
        vm(4, 128, 768), vf(128, 768), vf(128, 768), vf(128, 1), vf(4, 128, 768), vf(4, 128, 768), vm(4, 128, 768),
        vf(128, 768), vm(4, 128, 768),
        vm(2, 64, 768), vm(2, 64, 768), vm(4, 128, 768), vf(128, 768), vm(4, 128, 768),
        vm(4, 128, 768), vm(4, 128, 768),
        vm(4, 128, 768), vf(4, 1, 768), vf(128, 768), vm(4, 128, 768), vm(4, 128, 192),
        vm(4, 128, 192), vm(4, 3, 128, 128), vm(3, 4, 128, 1024), vf(2, 512, 384), vm(512, 384),
        vm(512, 384), vm(4, 128, 576), vm(4, 128, 768), vm(4, 128, 768),
        vm(4, 2, 96, 768), vm(4, 96, 768), vm(4, 96, 384), vm(4, 96, 384), vm(4, 96, 384),
        vm(2, 2, 96, 384), vm(768, 768), vm(2, 192, 768), vm(192, 768), vm(192, 768), vf(192, 768),
        vm(192, 384), vm(192, 384),
        vm(2, 4, 48, 384), vm(4, 48, 384), vm(4, 48, 384), vm(4, 48, 384), vm(4, 48, 384),
        vm(2, 48, 384), vm(4, 6, 48, 384), vm(2, 6, 48, 384), vm(6, 48, 384), vm(6, 48, 384),
        vm(6, 48, 384), vm(2, 3, 48, 384),
        vf(8, 16, 128), vf(8, 16, 128), vf(16, 128), vf(16, 128), vf(16, 128), vf(16, 128),
        vf(4, 1, 192), vf(1, 192), vm(128, 768), vm(128, 768), vm(128, 768), vm(128, 768),
        vf(192, 288), vf(192, 96), vf(192, 384), vf(96, 768), vf(6, 96), vf(2, 96), vf(3, 128),
        pltpu.SMEM((2, 3), jnp.int32), pltpu.SMEM((1, 2), jnp.int32), pltpu.SMEM((1, 8), jnp.int32),
        vm(6, 96), vm(2, 96), vm(3, 128),
        pltpu.SemaphoreType.DMA((SENDS,)), pltpu.SemaphoreType.DMA((RECVS,)),
        pltpu.SemaphoreType.DMA((LOCALS,)),
    ]
    out = lambda kind, *dims: jax.ShapeDtypeStruct(dims, kind)
    shapes = (
        out(BF, 128, 768), out(BF, 128, 768), out(F32, 192, 288), out(F32, 192, 96),
        out(F32, 192, 384), out(F32, 96, 768), out(F32, 6, 96), out(F32, 2, 96), out(F32, 3, 128),
    )
    anywhere = pl.BlockSpec(memory_space=pl.ANY)
    results = pl.pallas_call(
        layer_kernel,
        out_shape=shapes,
        in_specs=[anywhere] * 12,
        out_specs=(anywhere,) * 9,
        scratch_shapes=scratch,
        compiler_params=pltpu.CompilerParams(
            collective_id=0, has_side_effects=True, vmem_limit_bytes=58 * 1024 * 1024
        ),
    )(
        random_blocks[0], global_blocks, document_lengths, biases, gains,
        expand_bias.reshape(3, 128), hidden[0], cotangent[0], project_in, project_out,
        expand_weight, shrink_weight.T,
    )
    results = pl.pallas_call(
        hand_over,
        out_shape=shapes,
        in_specs=[anywhere] * 9,
        out_specs=(anywhere,) * 9,
        scratch_shapes=[pltpu.VMEM(one.shape, one.dtype) for one in shapes]
        + [pltpu.SemaphoreType.DMA((9,))] * 2,
    )(*results)
    return (
        results[0][None], results[1][None], results[2], results[3], results[4], results[5].T,
        results[6], results[7], results[8].reshape(-1),
    )


def solution(mesh):
    small = tuple(mesh.shape[name] for name in ("ctx", "fsdp")) == (8, 4)
    return jax.shard_map(
        fast_shards if small else shards,
        mesh=mesh,
        in_specs=(
            P("fsdp", "ctx", None),
            P("fsdp", "ctx"),
            P("fsdp", "ctx"),
            P("fsdp", "ctx"),
            P("fsdp", "ctx"),
            P(None, "ctx"),
            P(None, "ctx"),
            P("ctx"),
            P("fsdp", "ctx", None),
            P("fsdp", None),
            P("fsdp", None),
            P("fsdp", "ctx", None),
        ),
        out_specs=(
            P("fsdp", "ctx", None),
            P("fsdp", "ctx", None),
            P("fsdp", "ctx"),
            P("fsdp", "ctx"),
            P("fsdp", "ctx"),
            P("fsdp", "ctx"),
            P(None, "ctx"),
            P(None, "ctx"),
            P("ctx"),
        ),
        check_vma=False,
    )
```
